32 devices in a mesh: dp: 32 (over z, y, x, core).
Axes of the slice: x: 2, y: 2, z: 4, core: 2. Of those that a mesh axis runs over, the one named last changes fastest.
Arguments:
- tokens: bfloat16 [12288, 2048], P('dp'), may hold values from -6 to 6
- segments: int32 [32, 384], P('dp'), may hold values from 0 to 2, never falling along the last dimension, each value on 1 to 192 neighbouring positions
- w_query: bfloat16 [2048, 2048], P('dp'), may hold values from -0.125 to 0.125
- w_key: bfloat16 [2048, 1024], P('dp'), may hold values from -0.125 to 0.125
- w_value: bfloat16 [2048, 1024], P('dp'), may hold values from -0.125 to 0.125
- w_out: bfloat16 [2048, 2048], P('dp'), may hold values from -0.75 to 0.75
- w_gate: bfloat16 [2048, 6144], P('dp'), may hold values from -0.125 to 0.125
- w_up: bfloat16 [2048, 6144], P('dp'), may hold values from -0.125 to 0.125
- w_down: bfloat16 [6144, 2048], P('dp'), may hold values from -0.078125 to 0.078125
- attn_gain: bfloat16 [2048], P('dp'), may hold values from 0.5 to 1.5
- mlp_gain: bfloat16 [2048], P('dp'), may hold values from 0.5 to 1.5
- query_gain: bfloat16 [128], P('dp'), may hold values from 0.25 to 1.75
- key_gain: bfloat16 [128], P('dp'), may hold values from 0.25 to 1.75
- cotangent: bfloat16 [12288, 2048], P('dp'), may hold values from -6 to 6
Outputs:
- output: bfloat16 [12288, 2048], P('dp')
- tokens_grad: bfloat16 [12288, 2048], P('dp')
- w_query_grad: float32 [2048, 2048], P('dp')
- w_key_grad: float32 [2048, 1024], P('dp')
- w_value_grad: float32 [2048, 1024], P('dp')
- w_out_grad: float32 [2048, 2048], P('dp')
- w_gate_grad: float32 [2048, 6144], P('dp')
- w_up_grad: float32 [2048, 6144], P('dp')
- w_down_grad: float32 [6144, 2048], P('dp')
- attn_gain_grad: float32 [2048], P('dp')
- mlp_gain_grad: float32 [2048], P('dp')
- query_gain_grad: float32 [128], P('dp')
- key_gain_grad: float32 [128], P('dp')
The draws below stay inside these ranges and needn't reach their ends.
Inputs may be any that keep to these rules, and one draw needn't show every extreme that they name: `segments`: document numbers never fall along a sequence and start at 0; each document spans 1 to 192 positions, and one spans exactly that many.
All inputs are finite; a program needn't handle non-finite values.
Results may differ from the reference program's by a relative error of at most 0.017.
Values may be sent and summed in bfloat16 or wider, within the bound.
A program may use at most 448 MiB of HBM per device.

```python
import math
import jax
import jax.numpy as jnp
import numpy as np
from jax import lax

D = 2048
H = 16
KVH = 8
HD = 128
FF = 6144
TOK_DEV = 384
SEQS = 32
TOKENS = 12288


def level_of(stream_key, shape, pieces, low, largest):
    level, own = 1.0, jax.random.fold_in(stream_key, 6)
    for position, parts in pieces:
        draws = jnp.exp(jax.random.uniform(jax.random.fold_in(own, position), (parts,), jnp.float32, low / len(pieces), largest / len(pieces)))
        level = level * jnp.repeat(draws, shape[position] // parts).reshape([-1 if axis == position else 1 for axis in range(len(shape))])
    return level


def profile(number_of, total, reach, skew):
    portions = [(1 << 20) // math.isqrt(grade ** skew) + 1 for grade in range(2, number_of + 1)]
    spare, given = total - reach - (number_of - 1), [1] * (number_of - 1)
    while spare > 0:
        free = [i for i in range(number_of - 1) if given[i] < reach]
        pool, budget = sum([portions[i] for i in free]), spare
        for i in free:
            more = min(reach - given[i], max(1, budget * portions[i] // pool), spare)
            given[i] = given[i] + more
            spare = spare - more
    return np.array([reach] + given)


def ragged(own_key, amount, total, limit, lean):
    if amount == 2:
        one = jax.random.randint(own_key, (), max(1, total - limit), min(limit, total - 1) + 1)
        return jnp.stack([one, total - one])
    tallies = jnp.asarray(profile(amount, total, limit, lean), jnp.int32)
    couples = (amount - 1) // 2
    giver, receiver = tallies[1:1 + 2 * couples:2], tallies[2:2 + 2 * couples:2]
    room = jnp.minimum(giver - 1, limit - receiver)
    shifted = jax.random.randint(jax.random.fold_in(own_key, 1), (couples,), 0, 1 << 20) % (room + 1)
    tallies = tallies.at[1:1 + 2 * couples:2].set(giver - shifted).at[2:2 + 2 * couples:2].set(receiver + shifted)
    return tallies[jax.random.permutation(jax.random.fold_in(own_key, 2), amount)]


def centred(key, shape, scale, reach, pieces=(), kind=jnp.bfloat16):
    array = scale * jax.random.normal(key, shape, jnp.float32)
    if pieces:
        array = array * level_of(key, shape, pieces, -0.22, 0.18)
    return jnp.clip(array, -reach, reach).astype(kind)


def setup_inputs(seed: int = 0) -> dict:
    key_list = jax.random.split(jax.random.key(seed), 15)
    return {
        "tokens": centred(key_list[0], (TOKENS, D), 1.0, 6.0, ((0, 32),)),
        "segments": jax.vmap(lambda own: jnp.searchsorted(jnp.cumsum(ragged(own, 3, TOK_DEV, TOK_DEV // 2, 2)), jnp.arange(TOK_DEV), side="right"))(jax.random.split(key_list[1], SEQS)).reshape((SEQS, TOK_DEV)).astype(jnp.int32),
        "w_query": centred(key_list[2], (D, H * HD), D ** -0.5, 0.125, ((0, 32),)),
        "w_key": centred(key_list[3], (D, KVH * HD), D ** -0.5, 0.125, ((0, 32),)),
        "w_value": centred(key_list[4], (D, KVH * HD), D ** -0.5, 0.125, ((0, 32),)),
        "w_out": centred(key_list[5], (H * HD, D), (D // 32) ** -0.5, 0.75, ((0, 32),)),
        "w_gate": centred(key_list[6], (D, FF), D ** -0.5, 0.125, ((0, 32),)),
        "w_up": centred(key_list[7], (D, FF), D ** -0.5, 0.125, ((0, 32),)),
        "w_down": centred(key_list[8], (FF, D), FF ** -0.5, 0.078125, ((0, 32),)),
        "attn_gain": jnp.clip(1.0 + 0.1 * jax.random.normal(key_list[9], (D,), jnp.float32), 0.5, 1.5).astype(jnp.bfloat16),
        "mlp_gain": jnp.clip(1.0 + 0.1 * jax.random.normal(key_list[10], (D,), jnp.float32), 0.5, 1.5).astype(jnp.bfloat16),
        "query_gain": jnp.clip(1.0 + 0.15 * jax.random.normal(key_list[11], (HD,), jnp.float32), 0.25, 1.75).astype(jnp.bfloat16),
        "key_gain": jnp.clip(1.0 + 0.15 * jax.random.normal(key_list[12], (HD,), jnp.float32), 0.25, 1.75).astype(jnp.bfloat16),
        "cotangent": centred(key_list[13], (TOKENS, D), 1.0, 6.0, ((0, 32),)),
    }


EPS = 1e-06
THETA = 1000000.0

@jax.custom_vjp
def low(v):
    return lax.optimization_barrier(v.astype(jnp.bfloat16)).astype(jnp.float32)

@jax.custom_vjp
def low_back(v):
    return v

def low_keep(v):
    return (low(v), None)

def reduced_precision_pass(kept, grad):
    return (grad,)

def back_keep(v):
    return (v, None)

def back_low(kept, grad):
    return (low(grad),)
low.defvjp(low_keep, reduced_precision_pass)
low_back.defvjp(back_keep, back_low)

def rms_norm(values, gain):
    return values * lax.rsqrt(lax.optimization_barrier(jnp.mean(values * values, axis=-1, keepdims=True)) + EPS) * gain

def swap_negate_halves(values):
    half = values.shape[-1] // 2
    return jnp.concatenate([-values[..., half:], values[..., :half]], axis=-1)

def rotary(values, cosine, sine):
    return values * cosine + swap_negate_halves(values) * sine

def project(activation_rows, weight_matrix):
    return jnp.einsum('gxf,fw->gxw', activation_rows, weight_matrix, precision=lax.Precision.HIGHEST)

def positions_of(segments):
    earlier = (segments[:, None, :] < segments[:, :, None]).astype(jnp.int32)
    index = jnp.arange(segments.shape[1], dtype=jnp.int32)
    return index[None, :] - lax.optimization_barrier(jnp.sum(earlier, axis=2))

def rope_tables(positions):
    half = HD // 2
    inverse = THETA ** (-(jnp.arange(half, dtype=jnp.float32) * 2.0 / HD))
    angle = positions.astype(jnp.float32)[..., None] * inverse
    cosine = jnp.concatenate([jnp.cos(angle), jnp.cos(angle)], axis=-1)
    sine = jnp.concatenate([jnp.sin(angle), jnp.sin(angle)], axis=-1)
    return (cosine, sine)

def forward(inputs, w_query, w_key, w_value, w_out, w_gate, w_up, w_down, attn_gain, mlp_gain, query_gain, key_gain, cosine, sine, allowed):
    seq_count, length, model_width = inputs.shape
    groups = H // KVH
    score_scale = HD ** (-0.5)
    normed_one = low(rms_norm(inputs, attn_gain))
    query_raw = low_back(project(normed_one, w_query)).reshape(seq_count, length, H, HD)
    key_raw = low_back(project(normed_one, w_key)).reshape(seq_count, length, KVH, HD)
    value_low = low(low_back(project(normed_one, w_value))).reshape(seq_count, length, KVH, HD)
    query_low = low(rotary(rms_norm(query_raw, query_gain), cosine, sine)).reshape(seq_count, length, KVH, groups, HD)
    key_low = low(rotary(rms_norm(key_raw, key_gain), cosine, sine))

    def attend(seq_block):
        queries, keys, values, mask = seq_block
        scores = low_back(jnp.einsum('ikgd,jkd->kgij', queries, keys, precision=lax.Precision.HIGHEST) * score_scale)
        masked = jnp.where(mask, scores, -1e+30)
        row_max = lax.optimization_barrier(jnp.max(masked, axis=-1, keepdims=True))
        power_term = jnp.exp(masked - row_max)
        probs_low = low(power_term / lax.optimization_barrier(jnp.sum(power_term, axis=-1, keepdims=True)))
        mixed = jnp.einsum('kgij,jkd->ikgd', probs_low, values, precision=lax.Precision.HIGHEST)
        return mixed.reshape(length, model_width)
    mixed_low = low(low_back(lax.map(jax.checkpoint(attend), (query_low, key_low, value_low, allowed))))
    after_attn = inputs + low_back(project(mixed_low, w_out))
    normed_two = low(rms_norm(after_attn, mlp_gain))
    gate_value = low_back(project(normed_two, w_gate))
    up_value = low_back(project(normed_two, w_up))
    hidden_low = low(jax.nn.silu(gate_value) * up_value)
    return after_attn + low_back(project(hidden_low, w_down))

def reference(tokens, segments, w_query, w_key, w_value, w_out, w_gate, w_up, w_down, attn_gain, mlp_gain, query_gain, key_gain, cotangent):
    seq_count = segments.shape[0]
    length = segments.shape[1]
    positions = positions_of(segments)
    cosine, sine = rope_tables(positions)
    cosine = cosine[:, :, None, :]
    sine = sine[:, :, None, :]
    index = jnp.arange(length, dtype=jnp.int32)
    allowed = (segments[:, :, None] == segments[:, None, :]) & (index[None, None, :] <= index[None, :, None])
    params = tuple((matrix.astype(jnp.float32) for matrix in (w_query, w_key, w_value, w_out, w_gate, w_up, w_down, attn_gain, mlp_gain, query_gain, key_gain)))
    inputs = tokens.astype(jnp.float32).reshape(seq_count, length, -1)

    def whole_layer(layer_input, *weights):
        return forward(layer_input, *weights, cosine, sine, allowed)
    output, backward = jax.vjp(whole_layer, inputs, *params)
    grads = backward(cotangent.astype(jnp.float32).reshape(seq_count, length, -1))
    width = tokens.shape[1]
    return (output.reshape(-1, width).astype(jnp.bfloat16), grads[0].reshape(-1, width).astype(jnp.bfloat16), grads[1], grads[2], grads[3], grads[4], grads[5], grads[6], grads[7], grads[8], grads[9], grads[10], grads[11])
```

```python
import jax
import jax.numpy as jnp
from jax import lax
from jax.sharding import PartitionSpec as P

H = 16
KVH = 8
HD = 128
TP = 4

EPS = 1e-06
THETA = 1000000.0

f32 = jnp.float32
bf16 = jnp.bfloat16


def positions_of(segments):
    earlier = (segments[:, None, :] < segments[:, :, None]).astype(jnp.int32)
    index = jnp.arange(segments.shape[1], dtype=jnp.int32)
    return index[None, :] - jnp.sum(earlier, axis=2)


def rope_tables(positions):
    half = HD // 2
    inverse = THETA ** (-(jnp.arange(half, dtype=f32) * 2.0 / HD))
    angle = positions.astype(f32)[..., None] * inverse
    cosine = jnp.concatenate([jnp.cos(angle), jnp.cos(angle)], axis=-1)
    sine = jnp.concatenate([jnp.sin(angle), jnp.sin(angle)], axis=-1)
    return (cosine, sine)


def rotary(values, cosine, sine):
    half = values.shape[-1] // 2
    turned = jnp.concatenate([-values[..., half:], values[..., :half]], axis=-1)
    return values * cosine + turned * sine


def rotary_back(grads, cosine, sine):
    half = grads.shape[-1] // 2
    scaled = grads * sine
    turned = jnp.concatenate([scaled[..., half:], -scaled[..., :half]], axis=-1)
    return grads * cosine + turned


def inverse_rms(values):
    return lax.rsqrt(jnp.mean(values * values, axis=-1, keepdims=True) + EPS)


def norm_back(values, inverse, gain, grad_normed):
    grad_scaled = grad_normed * gain
    inner = jnp.mean(grad_scaled * values, axis=-1, keepdims=True)
    grad_values = inverse * (grad_scaled - values * inverse * inverse * inner)
    gain_grad = jnp.sum((grad_normed * values * inverse).reshape(-1, values.shape[-1]), axis=0)
    return (grad_values, gain_grad)


def dot(a, b):
    return lax.dot_general(a, b, (((1,), (0,)), ((), ())), preferred_element_type=f32)


def dot_tn(a, b):
    return lax.dot_general(a, b, (((0,), (0,)), ((), ())), preferred_element_type=f32)


def dot_nt(a, b):
    return lax.dot_general(a, b, (((1,), (1,)), ((), ())), preferred_element_type=f32)


def make_body(n):
    m = n // (2 * TP)
    z_groups = [[g * 2 * TP + k for g in range(m)] for k in range(2 * TP)]

    def swap(v, bits):
        return lax.ppermute(v, "dp", [(a, a ^ bits) for a in range(n)])

    def gather_xy(v):
        h = v.shape[0] // 2
        x = swap(v, 2)
        y = swap(v, 4)
        d_low = swap(y[:h], 2)
        d_high = swap(x[h:], 4)
        return [v, x, y, jnp.concatenate([d_low, d_high])]

    def scatter_xy(p0, p1, p2, p3):
        h = p3.shape[0] // 2
        d_low = swap(p3[:h], 4)
        d_high = swap(p3[h:], 2)
        sx = jnp.concatenate([(p1[:h].astype(f32) + d_low.astype(f32)).astype(bf16), p1[h:]])
        sy = jnp.concatenate([p2[:h], (p2[h:].astype(f32) + d_high.astype(f32)).astype(bf16)])
        return p0 + swap(sx, 2).astype(f32) + swap(sy, 4).astype(f32)

    def gather_z(v):
        return lax.all_gather(v, "dp", axis=0, tiled=True, axis_index_groups=z_groups)

    def scatter_z(v):
        return lax.psum_scatter(
            v, "dp", scatter_dimension=0, tiled=True, axis_index_groups=z_groups
        )

    def body(
        tokens,
        segments,
        w_query,
        w_key,
        w_value,
        w_out,
        w_gate,
        w_up,
        w_down,
        attn_gain,
        mlp_gain,
        query_gain,
        key_gain,
        cotangent,
    ):
        me = lax.axis_index("dp")
        core = me % 2
        place = (me // 2) % TP
        length, width = tokens.shape
        rows = w_query.shape[0]
        ffr = w_down.shape[0]
        score_scale = HD ** (-0.5)

        def exchange(parts_at):
            got = [parts_at(place)]
            for k in range(1, TP):
                got.append(swap(parts_at(place ^ k), 2 * k))
            return got

        def absolute(got):
            stacked = jnp.stack(got)
            return [lax.dynamic_index_in_dim(stacked, place ^ a, 0, keepdims=False) for a in range(TP)]

        def by_core(own, other):
            return (jnp.where(core == 0, own, other), jnp.where(core == 0, other, own))

        def spread(w):
            mine = lax.dynamic_index_in_dim(w, core, 2, keepdims=False)
            other = lax.dynamic_index_in_dim(w, 1 - core, 2, keepdims=False)
            pair = jnp.concatenate(by_core(mine, swap(other, 1)))
            got = exchange(lambda p: lax.dynamic_index_in_dim(pair, p, 1, keepdims=False))
            return jnp.concatenate(absolute(got))

        def unspread(v):
            cut = v.reshape(TP, 2 * rows, v.shape[-1])
            got = exchange(lambda p: lax.dynamic_index_in_dim(cut, p, 0, keepdims=False))
            full = jnp.stack(absolute(got), axis=1)
            mine = lax.dynamic_slice_in_dim(full, core * rows, rows, 0)
            other = lax.dynamic_slice_in_dim(full, (1 - core) * rows, rows, 0)
            return jnp.stack(by_core(mine, swap(other, 1)), axis=2)

        gains = jnp.concatenate([attn_gain, mlp_gain, query_gain, key_gain])[None]
        bit = 1
        while bit < n:
            got = swap(gains, bit)
            upper = (me // bit) % 2 == 1
            gains = jnp.where(
                upper, jnp.concatenate([got, gains]), jnp.concatenate([gains, got])
            )
            bit *= 2
        hr = query_gain.shape[0]
        attn_scale = gains[:, :rows].reshape(-1).astype(f32)
        mlp_scale = gains[:, rows : 2 * rows].reshape(-1).astype(f32)
        query_scale = gains[:, 2 * rows : 2 * rows + hr].reshape(-1).astype(f32)
        key_scale = gains[:, 2 * rows + hr :].reshape(-1).astype(f32)

        attn_local = jnp.concatenate(
            [
                w_query.reshape(rows, TP, 2, -1),
                w_key.reshape(rows, TP, 2, -1),
                w_value.reshape(rows, TP, 2, -1),
                w_out.reshape(rows, TP, 2, -1),
            ],
            axis=3,
        )
        attn_own = gather_z(spread(attn_local))
        qn = w_query.shape[1] // (2 * TP)
        kn = w_key.shape[1] // (2 * TP)
        on = w_out.shape[1] // (2 * TP)
        pn = qn + 2 * kn
        proj_a = attn_own[:, :pn]
        proj_b = swap(proj_a, 1)
        out_cols = attn_own[:, pn:].reshape(TP, -1, on)
        out_got = exchange(lambda p: lax.dynamic_index_in_dim(out_cols, p, 0, keepdims=False))
        out_mine = jnp.stack(absolute(out_got), axis=1)
        out_full = jnp.stack(by_core(out_mine, swap(out_mine, 1)), axis=2).reshape(-1, width)
        out_a = lax.dynamic_slice_in_dim(out_full, core * qn, qn, 0)
        out_b = lax.dynamic_slice_in_dim(out_full, (1 - core) * qn, qn, 0)

        mlp_local = jnp.concatenate(
            [
                w_gate.reshape(rows, m, TP, 2, ffr).transpose(0, 2, 3, 1, 4).reshape(rows, TP, 2, -1),
                w_up.reshape(rows, m, TP, 2, ffr).transpose(0, 2, 3, 1, 4).reshape(rows, TP, 2, -1),
            ],
            axis=3,
        )
        mlp_a = gather_z(spread(mlp_local))
        mlp_b = swap(mlp_a, 1)
        down_a = gather_z(w_down)
        down_b = swap(down_a, 1)
        fn = down_a.shape[0]

        inputs_all = jnp.concatenate(gather_xy(tokens)).astype(f32)
        seg_all = jnp.concatenate([segments] + [swap(segments, 2 * k) for k in range(1, TP)])
        grad_all = jnp.concatenate(gather_xy(cotangent))

        index = jnp.arange(length, dtype=jnp.int32)
        allowed = (seg_all[:, :, None] == seg_all[:, None, :]) & (
            index[None, None, :] <= index[None, :, None]
        )
        allowed = allowed[:, None]
        cosine, sine = rope_tables(positions_of(seg_all))
        cosine = cosine[:, :, None, :]
        sine = sine[:, :, None, :]

        normed_one = (inputs_all * inverse_rms(inputs_all) * attn_scale).astype(bf16)

        def attend(proj):
            raw = dot(normed_one, proj).reshape(TP, length, pn)
            query_raw = raw[:, :, :qn].reshape(TP, length, qn // HD, HD)
            key_raw = raw[:, :, qn : qn + kn].reshape(TP, length, 1, HD)
            value_low = raw[:, :, qn + kn :].astype(bf16)
            query_inv = inverse_rms(query_raw)
            key_inv = inverse_rms(key_raw)
            query_low = rotary(query_raw * query_inv * query_scale, cosine, sine).astype(bf16)
            key_low = rotary(key_raw * key_inv * key_scale, cosine, sine).astype(bf16)[:, :, 0]
            scores = (
                jnp.einsum("sigd,sjd->sgij", query_low, key_low, preferred_element_type=f32)
                * score_scale
            )
            scores = jnp.where(allowed, scores, -1e30)
            row_max = jnp.max(scores, axis=-1, keepdims=True)
            power_term = jnp.exp(scores - row_max)
            row_total = jnp.sum(power_term, axis=-1, keepdims=True)
            log_total = row_max + jnp.log(row_total)
            probs_low = (power_term / row_total).astype(bf16)
            mixed = jnp.einsum("sgij,sjd->sigd", probs_low, value_low, preferred_element_type=f32)
            mixed_low = mixed.reshape(TP * length, qn).astype(bf16)
            kept = (query_raw, key_raw, value_low, query_inv, key_inv, query_low, key_low, log_total)
            return mixed_low, kept

        mixed_a, kept_a = attend(proj_a)
        mixed_b, kept_b = attend(proj_b)

        def part(v, k):
            return v[k * length : (k + 1) * length]

        def out_part(k):
            return dot(part(mixed_a, k), out_a) + dot(part(mixed_b, k), out_b)

        d3 = out_part(3).astype(bf16)
        d1 = out_part(1).astype(bf16)
        d2 = out_part(2).astype(bf16)
        inputs = tokens.astype(f32)
        after_attn = scatter_xy(inputs + out_part(0), d1, d2, d3)

        inv_two = inverse_rms(after_attn)
        normed_two = (after_attn * inv_two * mlp_scale).astype(bf16)
        normed_two_all = jnp.concatenate(gather_xy(normed_two))

        def feed(mlp, down):
            both = dot(normed_two_all, mlp)
            gate_value = both[:, :fn]
            up_value = both[:, fn:]
            sigmoid_gate = jax.nn.sigmoid(gate_value)
            hidden_low = (gate_value * sigmoid_gate * up_value).astype(bf16)
            grad_hidden = dot_nt(grad_all, down)
            grad_up = (grad_hidden * gate_value * sigmoid_gate).astype(bf16)
            grad_gate = (
                grad_hidden * up_value * sigmoid_gate * (1.0 + gate_value * (1.0 - sigmoid_gate))
            ).astype(bf16)
            return hidden_low, jnp.concatenate([grad_gate, grad_up], axis=1)

        hidden_a, grad_pre_a = feed(mlp_a, down_a)
        hidden_b, grad_pre_b = feed(mlp_b, down_b)

        def pre_part(k):
            return dot_nt(part(grad_pre_a, k), mlp_a) + dot_nt(part(grad_pre_b, k), mlp_b)

        e3 = pre_part(3).astype(bf16)
        e1 = pre_part(1).astype(bf16)
        e2 = pre_part(2).astype(bf16)
        grad_normed_two = scatter_xy(pre_part(0), e1, e2, e3)

        def core_sum(own, other):
            return (own + swap(other.astype(bf16), 1).astype(f32)).astype(bf16)

        down_shard = scatter_z(
            core_sum(dot_tn(hidden_a, grad_all), dot_tn(hidden_b, grad_all))
        ).astype(f32)

        def hidden_part(k):
            return dot(part(hidden_a, k), down_a) + dot(part(hidden_b, k), down_b)

        o3 = hidden_part(3).astype(bf16)
        o1 = hidden_part(1).astype(bf16)
        o2 = hidden_part(2).astype(bf16)
        output = scatter_xy(after_attn + hidden_part(0), o1, o2, o3).astype(bf16)

        mlp_rows = scatter_z(
            core_sum(dot_tn(normed_two_all, grad_pre_a), dot_tn(normed_two_all, grad_pre_b))
        )
        mlp_shard = unspread(mlp_rows).astype(f32)

        def ff_columns(v):
            return (
                v.reshape(rows, TP, 2, m, ffr).transpose(0, 3, 1, 2, 4).reshape(rows, w_gate.shape[1])
            )

        gate_shard = ff_columns(mlp_shard[..., :fn])
        up_shard = ff_columns(mlp_shard[..., fn:])

        grad_norm_two, mlp_gain_grad = norm_back(after_attn, inv_two, mlp_scale, grad_normed_two)
        grad_after = cotangent.astype(f32) + grad_norm_two
        grad_after_all = jnp.concatenate(gather_xy(grad_after.astype(bf16)))

        def attend_back(kept, out_rows):
            query_raw, key_raw, value_low, query_inv, key_inv, query_low, key_low, log_total = kept
            grad_mixed = dot_nt(grad_after_all, out_rows).astype(bf16)
            grad_mixed = grad_mixed.reshape(TP, length, qn // HD, HD)
            scores = (
                jnp.einsum("sigd,sjd->sgij", query_low, key_low, preferred_element_type=f32)
                * score_scale
            )
            probs = jnp.exp(jnp.where(allowed, scores, -1e30) - log_total)
            grad_value = jnp.einsum(
                "sgij,sigd->sjd", probs.astype(bf16), grad_mixed, preferred_element_type=f32
            ).astype(bf16)
            grad_probs = jnp.einsum(
                "sigd,sjd->sgij", grad_mixed, value_low, preferred_element_type=f32
            )
            row_delta = jnp.sum(probs * grad_probs, axis=-1, keepdims=True)
            grad_scores = (probs * (grad_probs - row_delta)).astype(bf16)
            grad_query_rot = (
                jnp.einsum("sgij,sjd->sigd", grad_scores, key_low, preferred_element_type=f32)
                * score_scale
            )
            grad_key_rot = (
                jnp.einsum("sgij,sigd->sjd", grad_scores, query_low, preferred_element_type=f32)
                * score_scale
            )[:, :, None]
            grad_query, query_gain_grad = norm_back(
                query_raw, query_inv, query_scale, rotary_back(grad_query_rot, cosine, sine)
            )
            grad_key, key_gain_grad = norm_back(
                key_raw, key_inv, key_scale, rotary_back(grad_key_rot, cosine, sine)
            )
            grad_proj = jnp.concatenate(
                [
                    grad_query.reshape(TP * length, qn).astype(bf16),
                    grad_key.reshape(TP * length, kn).astype(bf16),
                    grad_value.reshape(TP * length, kn),
                ],
                axis=1,
            )
            return grad_proj, query_gain_grad, key_gain_grad

        grad_proj_a, query_gain_a, key_gain_a = attend_back(kept_a, out_a)
        grad_proj_b, query_gain_b, key_gain_b = attend_back(kept_b, out_b)

        def proj_part(k):
            return dot_nt(part(grad_proj_a, k), proj_a) + dot_nt(part(grad_proj_b, k), proj_b)

        t3 = proj_part(3).astype(bf16)
        t1 = proj_part(1).astype(bf16)
        t2 = proj_part(2).astype(bf16)
        grad_normed_one = scatter_xy(proj_part(0), t1, t2, t3)

        out_rows_grad = jnp.concatenate(
            by_core(dot_tn(mixed_a, grad_after_all), dot_tn(mixed_b, grad_after_all))
        ).reshape(-1, TP, 2, on)
        out_sum = core_sum(
            lax.dynamic_index_in_dim(out_rows_grad, core, 2, keepdims=False),
            lax.dynamic_index_in_dim(out_rows_grad, 1 - core, 2, keepdims=False),
        )
        out_back = jnp.concatenate(
            absolute(exchange(lambda p: lax.dynamic_index_in_dim(out_sum, p, 1, keepdims=False)))
        )
        proj_sum = core_sum(dot_tn(normed_one, grad_proj_a), dot_tn(normed_one, grad_proj_b))
        attn_rows = scatter_z(jnp.concatenate([proj_sum, out_back], axis=1))
        attn_shard = unspread(attn_rows).astype(f32)
        query_shard = attn_shard[..., :qn].reshape(rows, -1)
        key_shard = attn_shard[..., qn : qn + kn].reshape(rows, -1)
        value_shard = attn_shard[..., qn + kn : pn].reshape(rows, -1)
        out_shard = attn_shard[..., pn:].reshape(rows, -1)

        grad_norm_one, attn_gain_grad = norm_back(
            inputs, inverse_rms(inputs), attn_scale, grad_normed_one
        )
        tokens_grad = (grad_after + grad_norm_one).astype(bf16)

        gain_grads = jnp.concatenate(
            [
                attn_gain_grad.reshape(n, -1),
                mlp_gain_grad.reshape(n, -1),
                (query_gain_a + query_gain_b).reshape(n, -1),
                (key_gain_a + key_gain_b).reshape(n, -1),
            ],
            axis=1,
        )
        bit = n // 2
        while bit:
            upper = (me // bit) % 2 == 1
            low, high = gain_grads[:bit], gain_grads[bit:]
            gain_grads = jnp.where(upper, high, low) + swap(jnp.where(upper, low, high), bit)
            bit //= 2
        gain_grads = gain_grads[0]

        return (
            output,
            tokens_grad,
            query_shard,
            key_shard,
            value_shard,
            out_shard,
            gate_shard,
            up_shard,
            down_shard,
            gain_grads[:rows],
            gain_grads[rows : 2 * rows],
            gain_grads[2 * rows : 2 * rows + hr],
            gain_grads[2 * rows + hr :],
        )

    return body


def solution(mesh):
    row = P("dp", None)
    flat = P("dp")
    return jax.shard_map(
        make_body(mesh.shape["dp"]),
        mesh=mesh,
        in_specs=(row,) * 9 + (flat,) * 4 + (row,),
        out_specs=(row,) * 9 + (flat,) * 4,
        check_vma=False,
    )
```

```python
import jax
import jax.numpy as jnp
from jax import lax
from jax.experimental import pallas as pl
from jax.experimental.pallas import tpu as pltpu
from jax.sharding import PartitionSpec as P

H = 16
KVH = 8
HD = 128
TP = 4

EPS = 1e-06
THETA = 1000000.0

f32 = jnp.float32
bf16 = jnp.bfloat16
MESH = pl.DeviceIdType.MESH


def positions_of(segments):
    earlier = (segments[:, None, :] < segments[:, :, None]).astype(jnp.int32)
    index = jnp.arange(segments.shape[1], dtype=jnp.int32)
    return index[None, :] - jnp.sum(earlier, axis=2)


def rope_tables(positions):
    half = HD // 2
    inverse = THETA ** (-(jnp.arange(half, dtype=f32) * 2.0 / HD))
    angle = positions.astype(f32)[..., None] * inverse
    cosine = jnp.concatenate([jnp.cos(angle), jnp.cos(angle)], axis=-1)
    sine = jnp.concatenate([jnp.sin(angle), jnp.sin(angle)], axis=-1)
    return (cosine, sine)


def inverse_rms(values):
    return lax.rsqrt(jnp.mean(values * values, axis=-1, keepdims=True) + EPS)


def norm_back(values, inverse, gain, grad_normed):
    grad_scaled = grad_normed * gain
    inner = jnp.mean(grad_scaled * values, axis=-1, keepdims=True)
    grad_values = inverse * (grad_scaled - values * inverse * inverse * inner)
    gain_grad = jnp.sum((grad_normed * values * inverse).reshape(-1, values.shape[-1]), axis=0)
    return (grad_values, gain_grad)


def dot(a, b):
    return lax.dot_general(a, b, (((1,), (0,)), ((), ())), preferred_element_type=f32)


def dot_tn(a, b):
    return lax.dot_general(a, b, (((0,), (0,)), ((), ())), preferred_element_type=f32)


def dot_nt(a, b):
    return lax.dot_general(a, b, (((1,), (1,)), ((), ())), preferred_element_type=f32)


def turn(v):
    return pltpu.roll(v, HD // 2, 1)


def heads_of(raw, cosine, sine, query_gain, key_gain):
    out = []
    for k, gain in ((0, query_gain), (1, query_gain), (2, key_gain)):
        v = raw[:, k * HD : (k + 1) * HD]
        inverse = inverse_rms(v)
        normed = v * inverse * gain
        out.append((v, inverse, (normed * cosine + turn(normed) * sine).astype(bf16)))
    return out, raw[:, 3 * HD :].astype(bf16)


def block_probs(qs, keys, starts, row0, score_scale):
    size, span = starts.shape[0], keys.shape[0]
    scores = dot_nt(qs, keys) * score_scale
    column = lax.broadcasted_iota(jnp.int32, (size, span), 1)
    row = lax.broadcasted_iota(jnp.int32, (size, span), 0) + row0
    allowed = (column >= starts) & (column <= row)
    allowed = jnp.concatenate([allowed, allowed], axis=0)
    scores = jnp.where(allowed, scores, -1e30)
    power_term = jnp.exp(scores - jnp.max(scores, axis=-1, keepdims=True))
    return power_term / jnp.sum(power_term, axis=-1, keepdims=True)


def attend_kernel(
    x_ref, pa_ref, pb_ref, cos_ref, sin_ref, start_ref, ag_ref, qg_ref, kg_ref,
    raw_ref, o_ref, a1_ref,
):
    length, width = x_ref.shape
    step = 128
    score_scale = HD ** (-0.5)

    @pl.loop(0, length // step)
    def _(t):
        sl = pl.ds(pl.multiple_of(t * step, step), step)
        x = x_ref[sl, :].astype(f32)
        a1_ref[sl, :] = (x * inverse_rms(x) * ag_ref[...]).astype(bf16)

    for h, p_ref in ((0, pa_ref), (1, pb_ref)):
        raw_ref[:, h * 4 * HD : (h + 1) * 4 * HD] = dot(a1_ref[...], p_ref[...])
        (q0, q1, k0), value = heads_of(
            raw_ref[:, h * 4 * HD : (h + 1) * 4 * HD], cos_ref[...], sin_ref[...], qg_ref[...], kg_ref[...]
        )
        for b in range(length // step):
            sl = slice(b * step, (b + 1) * step)
            span = (b + 1) * step
            qs = jnp.concatenate([q0[2][sl], q1[2][sl]], axis=0)
            probs = block_probs(qs, k0[2][:span], start_ref[sl, :], b * step, score_scale)
            mixed = dot(probs.astype(bf16), value[:span]).astype(bf16)
            o_ref[sl, 2 * h * HD : (2 * h + 1) * HD] = mixed[:step]
            o_ref[sl, (2 * h + 1) * HD : (2 * h + 2) * HD] = mixed[step:]


def partners(me):
    x = me + 2 - 4 * ((me // 2) % 2)
    y = me + 4 - 8 * ((me // 4) % 2)
    d = x + 4 - 8 * ((me // 4) % 2)
    return x, y, d, me + 1 - 2 * (me % 2)


def greet(devices):
    barrier = pltpu.get_barrier_semaphore()
    for device in devices:
        pl.semaphore_signal(barrier, inc=1, device_id=(device,), device_id_type=MESH)
    pl.semaphore_wait(barrier, len(devices))


def remote(src, dst, send, recv, device):
    return pltpu.make_async_remote_copy(
        src_ref=src, dst_ref=dst, send_sem=send, recv_sem=recv, device_id=(device,), device_id_type=MESH
    )


TILE = 512


class Scatter:
    def __init__(self, out, ebuf, rd, rxy, send, recv, x, y):
        self.out, self.ebuf, self.rd, self.rxy = out, ebuf, rd, rxy
        h = rd.shape[1]
        self.half = h
        self.low = remote(ebuf.at[0, pl.ds(0, h)], rd.at[0], send.at[0], recv.at[0], y)
        self.high = remote(ebuf.at[0, pl.ds(h, h)], rd.at[1], send.at[1], recv.at[1], x)
        self.to_x = remote(ebuf.at[1], rxy.at[0], send.at[2], recv.at[2], x)
        self.to_y = remote(ebuf.at[2], rxy.at[1], send.at[3], recv.at[3], y)

    def add(self, k, tile_of):
        h = self.half
        if k == 1:
            self.low.wait_recv()
        if k == 2:
            self.high.wait_recv()

        @pl.loop(0, self.out.shape[1] // TILE)
        def _(t):
            sl = pl.ds(pl.multiple_of(t * TILE, TILE), TILE)
            value = tile_of(sl)
            if k == 0:
                self.out[:, sl] = value
            elif k == 3:
                self.ebuf[0, :, sl] = value.astype(bf16)
            elif k == 1:
                self.ebuf[1, :h, sl] = (value[:h] + self.rd[0, :, sl].astype(f32)).astype(bf16)
                self.ebuf[1, h:, sl] = value[h:].astype(bf16)
            else:
                self.ebuf[2, :h, sl] = value[:h].astype(bf16)
                self.ebuf[2, h:, sl] = (value[h:] + self.rd[1, :, sl].astype(f32)).astype(bf16)

        if k == 3:
            self.low.start()
            self.high.start()
        if k == 1:
            self.to_x.start()
        if k == 2:
            self.to_y.start()

    def finish(self):
        self.to_x.wait_recv()
        self.to_y.wait_recv()

        @pl.loop(0, self.out.shape[1] // TILE)
        def _(t):
            sl = pl.ds(pl.multiple_of(t * TILE, TILE), TILE)
            self.out[:, sl] += self.rxy[0, :, sl].astype(f32) + self.rxy[1, :, sl].astype(f32)

        for copy in (self.low, self.high, self.to_x, self.to_y):
            copy.wait_send()


def scatter_scratch(length, width):
    return [
        pltpu.VMEM((3, length, width), bf16),
        pltpu.VMEM((2, length // 2, width), bf16),
        pltpu.VMEM((2, length, width), bf16),
        pltpu.SemaphoreType.DMA((4,)),
        pltpu.SemaphoreType.DMA((4,)),
    ]


def attend_back_kernel(
    gm_ref, raw_ref, a1_ref, pa_ref, pb_ref, cos_ref, sin_ref, start_ref, qg_ref, kg_ref,
    out_ref, sum_ref, dqg_ref, dkg_ref,
    gp_ref, dk_ref, dv_ref, acc_a, acc_b, heads, cbuf, crecv,
    ebuf, rd, rxy, rs_send, rs_recv, do_send, do_recv, do_own, c_send, c_recv,
):
    length = a1_ref.shape[0]
    step = 128
    score_scale = HD ** (-0.5)
    s = pl.program_id(0)
    me = lax.axis_index("dp")
    core = me % 2
    place = (me // 2) % TP
    x, y, d, sibling = partners(me)
    cols = 4 * HD

    def columns_of(device):
        return pl.ds(pl.multiple_of(((device // 2) % TP) * cols, cols), cols)

    incoming = [
        remote(gm_ref.at[:, columns_of(device)], heads.at[k], do_send.at[k - 1], do_recv.at[k - 1], device)
        for k, device in ((1, x), (2, y), (3, d))
    ]
    own = pltpu.make_async_copy(
        gm_ref.at[:, pl.ds(pl.multiple_of(place * cols, cols), cols)], heads.at[0], do_own
    )
    scatter = Scatter(out_ref, ebuf, rd, rxy, rs_send, rs_recv, x, y)
    across = remote(cbuf, crecv, c_send, c_recv, sibling)

    @pl.when(s == 0)
    def _():
        greet((x, y, d, sibling))
        for k in (2, 0, 1):
            incoming[k].start()
        own.start()
        for ref in (acc_a, acc_b, dqg_ref, dkg_ref):
            ref[...] = jnp.zeros_like(ref)
        incoming[2].wait_recv()

    @pl.when(s == 1)
    def _():
        incoming[0].wait_recv()

    @pl.when(s == 2)
    def _():
        incoming[1].wait_recv()

    @pl.when(s == 3)
    def _():
        own.wait()

    which = part_order(s)

    for h in range(2):
        col = h * 4 * HD
        side = core if h == 0 else 1 - core
        cosine, sine = cos_ref[...], sin_ref[...]
        (q0, q1, k0), value = heads_of(
            raw_ref[:, col : col + 4 * HD], cosine, sine, qg_ref[...], kg_ref[...]
        )
        dk_ref[...] = jnp.zeros_like(dk_ref)
        dv_ref[...] = jnp.zeros_like(dv_ref)
        parts = []
        for b in range(length // step):
            sl = slice(b * step, (b + 1) * step)
            span = (b + 1) * step
            qs = jnp.concatenate([q0[2][sl], q1[2][sl]], axis=0)
            gs = jnp.concatenate(
                [
                    heads[which, sl, pl.ds(pl.multiple_of((2 * side + g) * HD, HD), HD)]
                    for g in range(2)
                ],
                axis=0,
            )
            keys, values = k0[2][:span], value[:span]
            probs = block_probs(qs, keys, start_ref[sl, :], b * step, score_scale)
            dv_ref[:span, :] += dot_tn(probs.astype(bf16), gs)
            grad_probs = dot_nt(gs, values)
            delta = jnp.sum(probs * grad_probs, axis=-1, keepdims=True)
            grad_scores = (probs * (grad_probs - delta)).astype(bf16)
            dk_ref[:span, :] += dot_tn(grad_scores, qs)
            parts.append(dot(grad_scores, keys))
        dq0 = jnp.concatenate([p[:step] for p in parts], axis=0) * score_scale
        dq1 = jnp.concatenate([p[step:] for p in parts], axis=0) * score_scale
        for k, (raw, inverse, _), grad, gain_ref, dgain_ref in (
            (0, q0, dq0, qg_ref, dqg_ref),
            (1, q1, dq1, qg_ref, dqg_ref),
            (2, k0, dk_ref[...] * score_scale, kg_ref, dkg_ref),
        ):
            back = grad * cosine + turn(grad * sine)
            scaled = back * gain_ref[...]
            inner = jnp.mean(scaled * raw, axis=-1, keepdims=True)
            gp_ref[:, col + k * HD : col + (k + 1) * HD] = (
                inverse * (scaled - raw * inverse * inverse * inner)
            ).astype(bf16)
            dgain_ref[...] += jnp.sum(back * raw * inverse, axis=0, keepdims=True)
        gp_ref[:, col + 3 * HD : col + 4 * HD] = dv_ref[...].astype(bf16)

    half = 4 * HD

    def tile_of(sl):
        return dot_nt(gp_ref[:, :half], pa_ref[sl, :]) + dot_nt(gp_ref[:, half:], pb_ref[sl, :])

    for at, k in enumerate(ORDER):

        @pl.when(s == at)
        def _():
            scatter.add(k, tile_of)

    @pl.loop(0, acc_a.shape[0] // TILE)
    def _(t):
        sl = pl.ds(pl.multiple_of(t * TILE, TILE), TILE)
        acc_b[sl, :] += dot_tn(a1_ref[:, sl], gp_ref[:, half:])

    @pl.when(s == 3)
    def _():
        cbuf[...] = acc_b[...].astype(bf16)
        across.start()

    @pl.loop(0, acc_a.shape[0] // TILE)
    def _(t):
        sl = pl.ds(pl.multiple_of(t * TILE, TILE), TILE)
        acc_a[sl, :] += dot_tn(a1_ref[:, sl], gp_ref[:, :half])

    @pl.when(s == 3)
    def _():
        across.wait_recv()
        sum_ref[...] = (acc_a[...] + crecv[...].astype(f32)).astype(bf16)
        scatter.finish()
        across.wait_send()
        for copy in incoming:
            copy.wait_send()


def feed_back_kernel(
    gp_ref, wa_ref, wb_ref, a2_ref,
    out_ref, sum_ref, crecv_ref,
    gp, wa, wb, a2, cbuf, cgot, stage, loads, c_send, c_recv, g_sem, s_sem,
    ebuf, rd, rxy, rs_send, rs_recv,
):
    length = out_ref.shape[0]
    cols = wa.shape[1]
    rows = cbuf.shape[1]
    tiles = a2.shape[1] // rows
    x, y, d, sibling = partners(lax.axis_index("dp"))
    scatter = Scatter(out_ref, ebuf, rd, rxy, rs_send, rs_recv, x, y)

    def piece(k):
        sl = pl.ds(k * length, length)
        return pltpu.make_async_copy(gp_ref.at[sl], gp.at[sl], loads.at[k])

    load_a = pltpu.make_async_copy(wa_ref, wa, loads.at[4])
    load_b = pltpu.make_async_copy(wb_ref, wb, loads.at[5])
    load_x = pltpu.make_async_copy(a2_ref, a2, loads.at[6])
    piece(3).start()
    load_a.start()
    load_b.start()
    for k in (1, 2, 0):
        piece(k).start()
    load_x.start()
    greet((x, y, d, sibling))

    def rows_of(t):
        return pl.ds(pl.multiple_of(t * rows, rows), rows)

    def across(t):
        return remote(
            cbuf.at[t % 2], crecv_ref.at[rows_of(t)], c_send.at[t % 2], c_recv.at[t], sibling
        )

    def fetch(t):
        return pltpu.make_async_copy(crecv_ref.at[rows_of(t)], cgot.at[t % 2], g_sem.at[t % 2])

    def store(t):
        return pltpu.make_async_copy(stage.at[t % 2], sum_ref.at[rows_of(t)], s_sem.at[t % 2])

    def part_of(k):
        sl = slice(k * length, (k + 1) * length)

        def tile_of(cut):
            return dot_nt(gp[sl, :cols], wa[cut, :]) + dot_nt(gp[sl, cols:], wb[cut, :])

        return tile_of

    piece(3).wait()
    load_a.wait()
    load_b.wait()
    scatter.add(3, part_of(3))
    for k in (1, 2, 0):
        piece(k).wait()
    load_x.wait()

    @pl.loop(0, tiles)
    def _(t):
        @pl.when(t >= 2)
        def _():
            across(t - 2).wait_send()

        cbuf[t % 2] = dot_tn(a2[:, rows_of(t)], gp[:, cols:]).astype(bf16)
        across(t).start()

    for k in (1, 2, 0):
        scatter.add(k, part_of(k))

    @pl.loop(0, tiles)
    def _(t):
        across(t).wait_recv()
        fetch(t).start()

        @pl.when(t >= 2)
        def _():
            store(t - 2).wait()

        own = dot_tn(a2[:, rows_of(t)], gp[:, :cols])
        fetch(t).wait()
        stage[t % 2] = (own + cgot[t % 2].astype(f32)).astype(bf16)
        store(t).start()

    for t in (tiles - 2, tiles - 1):
        store(t).wait()
        across(t).wait_send()
    scatter.finish()


def feed_backward(gp, wa, wb, a2, length):
    tokens, width = a2.shape
    cols = wa.shape[1]
    rows = 256
    anywhere = pl.BlockSpec(memory_space=pl.ANY)
    return pl.pallas_call(
        feed_back_kernel,
        in_specs=[anywhere] * 4,
        out_specs=[pl.BlockSpec(memory_space=pltpu.VMEM), anywhere, anywhere],
        out_shape=[
            struct((length, width), f32),
            struct(wa.shape, bf16),
            struct(wa.shape, bf16),
        ],
        scratch_shapes=[
            pltpu.VMEM(gp.shape, bf16),
            pltpu.VMEM(wa.shape, bf16),
            pltpu.VMEM(wb.shape, bf16),
            pltpu.VMEM(a2.shape, bf16),
            pltpu.VMEM((2, rows, cols), bf16),
            pltpu.VMEM((2, rows, cols), bf16),
            pltpu.VMEM((2, rows, cols), bf16),
            pltpu.SemaphoreType.DMA((7,)),
            pltpu.SemaphoreType.DMA((2,)),
            pltpu.SemaphoreType.DMA((width // rows,)),
            pltpu.SemaphoreType.DMA((2,)),
            pltpu.SemaphoreType.DMA((2,)),
        ]
        + scatter_scratch(length, width),
        compiler_params=pltpu.CompilerParams(
            vmem_limit_bytes=60 << 20, collective_id=1, has_side_effects=True
        ),
        cost_estimate=pl.CostEstimate(
            flops=4 * tokens * width * cols * 2, bytes_accessed=30 << 20, transcendentals=0
        ),
        name="feed_backward",
    )(gp, wa, wb, a2)[:2]


ORDER = (3, 1, 2, 0)


def part_order(s):
    return 3 - 2 * s + 3 * (s // 2)


def rows_spec(length, cols):
    return pl.BlockSpec((length, cols), lambda s: (s, 0))


def whole_spec(shape):
    return pl.BlockSpec(shape, lambda s: (0, 0))


def struct(shape, dtype):
    return jax.ShapeDtypeStruct(shape, dtype)


def attend_forward(x, pa, pb, cosine, sine, starts, ag, qg, kg, length):
    tokens, width = x.shape
    fixed = [pa, pb]
    return pl.pallas_call(
        attend_kernel,
        grid=(tokens // length,),
        in_specs=[rows_spec(length, width)]
        + [whole_spec(w.shape) for w in fixed]
        + [rows_spec(length, HD), rows_spec(length, HD), rows_spec(length, 1)]
        + [whole_spec(g.shape) for g in (ag, qg, kg)],
        out_specs=[rows_spec(length, c) for c in (8 * HD, 4 * HD, width)],
        out_shape=[
            struct((tokens, 8 * HD), f32),
            struct((tokens, 4 * HD), bf16),
            struct((tokens, width), bf16),
        ],
        compiler_params=pltpu.CompilerParams(vmem_limit_bytes=48 << 20),
        cost_estimate=pl.CostEstimate(
            flops=2 * tokens * width * 8 * HD, bytes_accessed=30 << 20, transcendentals=0
        ),
        name="attend_forward",
    )(x, pa, pb, cosine, sine, starts, ag, qg, kg)


def attend_backward(gm, raw, a1, pa, pb, cosine, sine, starts, qg, kg, length):
    tokens, width = a1.shape

    def in_order(cols):
        return pl.BlockSpec((length, cols), lambda s: (part_order(s), 0))

    return pl.pallas_call(
        attend_back_kernel,
        grid=(TP,),
        in_specs=[pl.BlockSpec(memory_space=pl.ANY)]
        + [in_order(c) for c in (8 * HD, width)]
        + [whole_spec(w.shape) for w in (pa, pb)]
        + [in_order(HD), in_order(HD), in_order(1)]
        + [whole_spec(v.shape) for v in (qg, kg)],
        out_specs=[whole_spec((length, width)), whole_spec(pa.shape)]
        + [whole_spec(v.shape) for v in (qg, kg)],
        out_shape=[struct((length, width), f32), struct(pa.shape, bf16)]
        + [struct(v.shape, f32) for v in (qg, kg)],
        scratch_shapes=[
            pltpu.VMEM((length, 8 * HD), bf16),
            pltpu.VMEM((length, HD), f32),
            pltpu.VMEM((length, HD), f32),
            pltpu.VMEM(pa.shape, f32),
            pltpu.VMEM(pa.shape, f32),
            pltpu.VMEM((TP, length, 4 * HD), bf16),
            pltpu.VMEM(pa.shape, bf16),
            pltpu.VMEM(pa.shape, bf16),
        ]
        + scatter_scratch(length, width)
        + [
            pltpu.SemaphoreType.DMA((3,)),
            pltpu.SemaphoreType.DMA((3,)),
            pltpu.SemaphoreType.DMA,
            pltpu.SemaphoreType.DMA,
            pltpu.SemaphoreType.DMA,
        ],
        compiler_params=pltpu.CompilerParams(
            vmem_limit_bytes=58 << 20, collective_id=2, has_side_effects=True
        ),
        cost_estimate=pl.CostEstimate(
            flops=2 * tokens * width * 8 * HD, bytes_accessed=30 << 20, transcendentals=0
        ),
        name="attend_backward",
    )(gm, raw, a1, pa, pb, cosine, sine, starts, qg, kg)


def make_body(n):
    m = n // (2 * TP)
    z_groups = [[g * 2 * TP + k for g in range(m)] for k in range(2 * TP)]

    def swap(v, bits):
        return lax.ppermute(v, "dp", [(a, a ^ bits) for a in range(n)])

    def gather_xy(v):
        h = v.shape[0] // 2
        x = swap(v, 2)
        y = swap(v, 4)
        d_low = swap(y[:h], 2)
        d_high = swap(x[h:], 4)
        return [v, x, y, jnp.concatenate([d_low, d_high])]

    def scatter_xy(p0, p1, p2, p3):
        h = p3.shape[0] // 2
        d_low = swap(p3[:h], 4)
        d_high = swap(p3[h:], 2)
        sx = jnp.concatenate([(p1[:h].astype(f32) + d_low.astype(f32)).astype(bf16), p1[h:]])
        sy = jnp.concatenate([p2[:h], (p2[h:].astype(f32) + d_high.astype(f32)).astype(bf16)])
        return p0 + swap(sx, 2).astype(f32) + swap(sy, 4).astype(f32)

    def gather_z(v):
        return lax.all_gather(v, "dp", axis=0, tiled=True, axis_index_groups=z_groups)

    def scatter_z(v):
        return lax.psum_scatter(
            v, "dp", scatter_dimension=0, tiled=True, axis_index_groups=z_groups
        )

    def body(
        tokens,
        segments,
        w_query,
        w_key,
        w_value,
        w_out,
        w_gate,
        w_up,
        w_down,
        attn_gain,
        mlp_gain,
        query_gain,
        key_gain,
        cotangent,
    ):
        me = lax.axis_index("dp")
        core = me % 2
        place = (me // 2) % TP
        length, width = tokens.shape
        rows = w_query.shape[0]
        ffr = w_down.shape[0]

        def exchange(parts_at):
            got = [parts_at(place)]
            for k in range(1, TP):
                got.append(swap(parts_at(place ^ k), 2 * k))
            return got

        def absolute(got):
            stacked = jnp.stack(got)
            return [lax.dynamic_index_in_dim(stacked, place ^ a, 0, keepdims=False) for a in range(TP)]

        def by_core(own, other):
            return (jnp.where(core == 0, own, other), jnp.where(core == 0, other, own))

        def spread(w):
            mine = lax.dynamic_index_in_dim(w, core, 2, keepdims=False)
            other = lax.dynamic_index_in_dim(w, 1 - core, 2, keepdims=False)
            pair = jnp.concatenate(by_core(mine, swap(other, 1)))
            got = exchange(lambda p: lax.dynamic_index_in_dim(pair, p, 1, keepdims=False))
            return jnp.concatenate(absolute(got))

        def unspread(v):
            cut = v.reshape(TP, 2 * rows, v.shape[-1])
            got = exchange(lambda p: lax.dynamic_index_in_dim(cut, p, 0, keepdims=False))
            full = jnp.stack(absolute(got), axis=1)
            mine = lax.dynamic_slice_in_dim(full, core * rows, rows, 0)
            other = lax.dynamic_slice_in_dim(full, (1 - core) * rows, rows, 0)
            return jnp.stack(by_core(mine, swap(other, 1)), axis=2)

        attn_local = jnp.concatenate(
            [
                w_query.reshape(rows, TP, 2, -1),
                w_key.reshape(rows, TP, 2, -1),
                w_value.reshape(rows, TP, 2, -1),
                w_out.reshape(rows, TP, 2, -1),
            ],
            axis=3,
        )
        qn = w_query.shape[1] // (2 * TP)
        kn = w_key.shape[1] // (2 * TP)
        pn = qn + 2 * kn
        attn_in = spread(attn_local)

        gains = jnp.concatenate([attn_gain, mlp_gain, query_gain, key_gain])[None]
        gains, attn_in = lax.optimization_barrier((gains, attn_in))
        bit = 1
        while bit < n:
            got = swap(gains, bit)
            upper = (me // bit) % 2 == 1
            gains = jnp.where(
                upper, jnp.concatenate([got, gains]), jnp.concatenate([gains, got])
            )
            bit *= 2
        hr = query_gain.shape[0]
        attn_scale = gains[:, :rows].reshape(-1).astype(f32)
        mlp_scale = gains[:, rows : 2 * rows].reshape(-1).astype(f32)
        query_scale = gains[:, 2 * rows : 2 * rows + hr].reshape(-1).astype(f32)
        key_scale = gains[:, 2 * rows + hr :].reshape(-1).astype(f32)

        proj_a = gather_z(attn_in[:, :pn])
        proj_b = swap(proj_a, 1)
        out_in, proj_a = lax.optimization_barrier((attn_in[:, pn:], proj_a))
        out_cols = gather_z(out_in)

        tokens_in, attn_in = lax.optimization_barrier((tokens, attn_in))
        tokens_all = jnp.concatenate(gather_xy(tokens_in))

        mlp_local = jnp.concatenate(
            [
                w_gate.reshape(rows, m, TP, 2, ffr).transpose(0, 2, 3, 1, 4).reshape(rows, TP, 2, -1),
                w_up.reshape(rows, m, TP, 2, ffr).transpose(0, 2, 3, 1, 4).reshape(rows, TP, 2, -1),
            ],
            axis=3,
        )
        mlp_in = spread(mlp_local)
        mlp_in, out_cols = lax.optimization_barrier((mlp_in, out_cols))
        mlp_a = gather_z(mlp_in)
        mlp_b = swap(mlp_a, 1)
        down_local, proj_a = lax.optimization_barrier((w_down, proj_a))
        down_a = gather_z(down_local)
        down_b = swap(down_a, 1)
        fn = down_a.shape[0]

        out_got = [out_cols] + [swap(out_cols, 2 * k) for k in range(1, TP)]
        half_length = length // 2

        seg_all = jnp.concatenate([segments] + [swap(segments, 2 * k) for k in range(1, TP)])
        positions = positions_of(seg_all)
        cosine, sine = rope_tables(positions)
        sign = jnp.where(jnp.arange(HD) < HD // 2, -1.0, 1.0).astype(f32)
        cosine = cosine.reshape(-1, HD)
        sine = (sine * sign).reshape(-1, HD)
        starts = (jnp.arange(length, dtype=jnp.int32)[None] - positions).reshape(-1, 1)

        proj_a, out_cols, mlp_in = lax.optimization_barrier((proj_a, out_cols, mlp_in))
        raw, mixed, normed_one = attend_forward(
            tokens_all, proj_a, proj_b, cosine, sine, starts,
            attn_scale[None], query_scale[None], key_scale[None], length,
        )

        def part(v, k):
            return v[k * length : (k + 1) * length]

        def turn_halves(v):
            half = v.shape[1] // 2
            return jnp.where(core == 0, v, jnp.concatenate([v[:, half:], v[:, :half]], axis=1))

        mixed, out_got = lax.optimization_barrier((mixed, out_got))
        out_mine = jnp.stack(out_got)
        out_pair = by_core(out_mine, swap(out_mine, 1))
        out_full = jnp.concatenate(
            [
                lax.dynamic_index_in_dim(half, place ^ a, 0, keepdims=False)
                for a in range(TP)
                for half in out_pair
            ],
            axis=1,
        )
        mixed = turn_halves(mixed)
        heads = [part(mixed, 0)] + [swap(part(mixed, k), 2 * k) for k in range(1, TP)]
        mixed_own = jnp.concatenate(absolute(heads), axis=1)
        inputs = tokens.astype(f32)
        after_attn = inputs + dot(mixed_own, out_full)

        inv_two = inverse_rms(after_attn)
        normed_two = (after_attn * inv_two * mlp_scale).astype(bf16)
        normed_x, normed_y = swap(normed_two, 2), swap(normed_two, 4)
        normed_x, normed_y, cotangent_in = lax.optimization_barrier((normed_x, normed_y, cotangent))
        normed_two_all = jnp.concatenate(
            [
                normed_two,
                normed_x,
                normed_y,
                swap(normed_y[:half_length], 2),
                swap(normed_x[half_length:], 4),
            ]
        )
        grad_all = jnp.concatenate(gather_xy(cotangent_in))

        def feed(mlp):
            both = dot(normed_two_all, mlp)
            gate_value = both[:, :fn]
            up_value = both[:, fn:]
            sigmoid_gate = jax.nn.sigmoid(gate_value)
            return gate_value, up_value, (gate_value * sigmoid_gate * up_value).astype(bf16)

        def feed_back(gate_value, up_value, grads, down):
            sigmoid_gate = jax.nn.sigmoid(gate_value)
            grad_hidden = dot_nt(grads, down)
            grad_up = (grad_hidden * gate_value * sigmoid_gate).astype(bf16)
            grad_gate = (
                grad_hidden * up_value * sigmoid_gate * (1.0 + gate_value * (1.0 - sigmoid_gate))
            ).astype(bf16)
            return jnp.concatenate([grad_gate, grad_up], axis=1)

        def core_sum(own, other):
            return (own.astype(f32) + swap(other.astype(bf16), 1).astype(f32)).astype(bf16)

        down = jnp.concatenate([down_a, down_b])
        gate_a, up_a, hidden_a = feed(mlp_a)
        gate_b, up_b, hidden_b = feed(mlp_b)
        hidden = jnp.concatenate([hidden_a, hidden_b], axis=1)
        down_grad_b = dot_tn(hidden[:, fn:], grad_all).astype(bf16)
        down_sum = core_sum(dot_tn(hidden[:, :fn], grad_all), down_grad_b)
        down_sum, grad_all_two = lax.optimization_barrier((down_sum, grad_all))
        down_rows = scatter_z(down_sum)

        grad_pre = jnp.concatenate(
            [
                feed_back(gate_a, up_a, grad_all_two, down_a),
                feed_back(gate_b, up_b, grad_all_two, down_b),
            ],
            axis=1,
        )
        grad_normed_two, mlp_sum = feed_backward(grad_pre, mlp_a, mlp_b, normed_two_all, length)
        mlp_rows = scatter_z(mlp_sum)
        grad_normed_two, down_rows = lax.optimization_barrier((grad_normed_two, down_rows))
        down_shard = down_rows.astype(f32)

        grad_norm_two, mlp_gain_grad = norm_back(after_attn, inv_two, mlp_scale, grad_normed_two)
        grad_after = cotangent.astype(f32) + grad_norm_two
        grad_after_low = grad_after.astype(bf16)

        grad_mixed = dot_nt(grad_after_low, out_full).astype(bf16)
        grad_normed_one, proj_sum, query_gain_grad, key_gain_grad = attend_backward(
            grad_mixed, raw, normed_one, proj_a, proj_b, cosine, sine, starts,
            query_scale[None], key_scale[None], length,
        )
        proj_rows = scatter_z(proj_sum)
        grad_normed_one, mlp_rows, mixed_own, hidden = lax.optimization_barrier(
            (grad_normed_one, mlp_rows, mixed_own, hidden)
        )
        o3 = dot(part(hidden, 3), down).astype(bf16)
        o1 = dot(part(hidden, 1), down).astype(bf16)
        o2 = dot(part(hidden, 2), down).astype(bf16)
        o0 = after_attn + dot(part(hidden, 0), down)

        out_grad = dot_tn(mixed_own, grad_after_low).astype(bf16).reshape(width, TP, 2, -1)
        out_sum = core_sum(
            lax.dynamic_index_in_dim(out_grad, core, 2, keepdims=False),
            lax.dynamic_index_in_dim(out_grad, 1 - core, 2, keepdims=False),
        )
        out_got = exchange(lambda p: lax.dynamic_index_in_dim(out_sum, p, 1, keepdims=False))
        out_rows = scatter_z(sum(v.astype(f32) for v in out_got).astype(bf16))
        output = scatter_xy(o0, o1, o2, o3).astype(bf16)
        mlp_shard = unspread(mlp_rows).astype(f32)
        out_shard = unspread(out_rows).astype(f32).reshape(rows, -1)

        def ff_columns(v):
            return (
                v.reshape(rows, TP, 2, m, ffr).transpose(0, 3, 1, 2, 4).reshape(rows, w_gate.shape[1])
            )

        gate_shard = ff_columns(mlp_shard[..., :fn])
        up_shard = ff_columns(mlp_shard[..., fn:])

        proj_rows, gate_shard, up_shard = lax.optimization_barrier((proj_rows, gate_shard, up_shard))
        attn_shard = unspread(proj_rows).astype(f32)
        query_shard = attn_shard[..., :qn].reshape(rows, -1)
        key_shard = attn_shard[..., qn : qn + kn].reshape(rows, -1)
        value_shard = attn_shard[..., qn + kn :].reshape(rows, -1)

        grad_norm_one, attn_gain_grad = norm_back(
            inputs, inverse_rms(inputs), attn_scale, grad_normed_one
        )
        tokens_grad = (grad_after + grad_norm_one).astype(bf16)

        gain_grads = jnp.concatenate(
            [
                attn_gain_grad.reshape(n, -1),
                mlp_gain_grad.reshape(n, -1),
                query_gain_grad.reshape(n, -1),
                key_gain_grad.reshape(n, -1),
            ],
            axis=1,
        )
        bit = n // 2
        while bit:
            upper = (me // bit) % 2 == 1
            low, high = gain_grads[:bit], gain_grads[bit:]
            gain_grads = jnp.where(upper, high, low) + swap(jnp.where(upper, low, high), bit)
            bit //= 2
        gain_grads = gain_grads[0]

        return (
            output,
            tokens_grad,
            query_shard,
            key_shard,
            value_shard,
            out_shard,
            gate_shard,
            up_shard,
            down_shard,
            gain_grads[:rows],
            gain_grads[rows : 2 * rows],
            gain_grads[2 * rows : 2 * rows + hr],
            gain_grads[2 * rows + hr :],
        )

    return body


def solution(mesh):
    row = P("dp", None)
    flat = P("dp")
    return jax.shard_map(
        make_body(mesh.shape["dp"]),
        mesh=mesh,
        in_specs=(row,) * 9 + (flat,) * 4 + (row,),
        out_specs=(row,) * 9 + (flat,) * 4,
        check_vma=False,
    )
```

```python
import jax
import jax.numpy as jnp
from jax import lax
from jax.experimental import pallas as pl
from jax.experimental.pallas import tpu as pltpu
from jax.sharding import PartitionSpec as P

H = 16
KVH = 8
HD = 128
TP = 4

EPS = 1e-06
THETA = 1000000.0

f32 = jnp.float32
bf16 = jnp.bfloat16
MESH = pl.DeviceIdType.MESH


def positions_of(segments):
    earlier = (segments[:, None, :] < segments[:, :, None]).astype(jnp.int32)
    index = jnp.arange(segments.shape[1], dtype=jnp.int32)
    return index[None, :] - jnp.sum(earlier, axis=2)


def rope_tables(positions):
    half = HD // 2
    inverse = THETA ** (-(jnp.arange(half, dtype=f32) * 2.0 / HD))
    angle = positions.astype(f32)[..., None] * inverse
    cosine = jnp.concatenate([jnp.cos(angle), jnp.cos(angle)], axis=-1)
    sine = jnp.concatenate([jnp.sin(angle), jnp.sin(angle)], axis=-1)
    return (cosine, sine)


def inverse_rms(values):
    return lax.rsqrt(jnp.mean(values * values, axis=-1, keepdims=True) + EPS)


def norm_back(values, inverse, gain, grad_normed):
    grad_scaled = grad_normed * gain
    inner = jnp.mean(grad_scaled * values, axis=-1, keepdims=True)
    grad_values = inverse * (grad_scaled - values * inverse * inverse * inner)
    gain_grad = jnp.sum((grad_normed * values * inverse).reshape(-1, values.shape[-1]), axis=0)
    return (grad_values, gain_grad)


def dot(a, b):
    return lax.dot_general(a, b, (((1,), (0,)), ((), ())), preferred_element_type=f32)


def dot_tn(a, b):
    return lax.dot_general(a, b, (((0,), (0,)), ((), ())), preferred_element_type=f32)


def dot_nt(a, b):
    return lax.dot_general(a, b, (((1,), (1,)), ((), ())), preferred_element_type=f32)


def turn(v):
    return pltpu.roll(v, HD // 2, 1)


def heads_of(raw, cosine, sine, query_gain, key_gain):
    out = []
    for k, gain in ((0, query_gain), (1, query_gain), (2, key_gain)):
        v = raw[:, k * HD : (k + 1) * HD]
        inverse = inverse_rms(v)
        normed = v * inverse * gain
        out.append((v, inverse, (normed * cosine + turn(normed) * sine).astype(bf16)))
    return out, raw[:, 3 * HD :].astype(bf16)


def block_probs(qs, keys, starts, row0, score_scale):
    size, span = starts.shape[0], keys.shape[0]
    scores = dot_nt(qs, keys) * score_scale
    column = lax.broadcasted_iota(jnp.int32, (size, span), 1)
    row = lax.broadcasted_iota(jnp.int32, (size, span), 0) + row0
    allowed = (column >= starts) & (column <= row)
    allowed = jnp.concatenate([allowed, allowed], axis=0)
    scores = jnp.where(allowed, scores, -1e30)
    power_term = jnp.exp(scores - jnp.max(scores, axis=-1, keepdims=True))
    return power_term / jnp.sum(power_term, axis=-1, keepdims=True)


def partners(me):
    x = me + 2 - 4 * ((me // 2) % 2)
    y = me + 4 - 8 * ((me // 4) % 2)
    d = x + 4 - 8 * ((me // 4) % 2)
    return x, y, d, me + 1 - 2 * (me % 2)


def greet(devices):
    barrier = pltpu.get_barrier_semaphore()
    for device in devices:
        pl.semaphore_signal(barrier, inc=1, device_id=(device,), device_id_type=MESH)
    pl.semaphore_wait(barrier, len(devices))


def remote(src, dst, send, recv, device):
    return pltpu.make_async_remote_copy(
        src_ref=src, dst_ref=dst, send_sem=send, recv_sem=recv, device_id=(device,), device_id_type=MESH
    )


TILE = 512


class Scatter:
    def __init__(self, out, ebuf, rd, rxy, send, recv, x, y):
        self.out, self.ebuf, self.rd, self.rxy = out, ebuf, rd, rxy
        h = rd.shape[1]
        self.half = h
        self.low = remote(ebuf.at[0, pl.ds(0, h)], rd.at[0], send.at[0], recv.at[0], y)
        self.high = remote(ebuf.at[0, pl.ds(h, h)], rd.at[1], send.at[1], recv.at[1], x)
        self.to_x = remote(ebuf.at[1], rxy.at[0], send.at[2], recv.at[2], x)
        self.to_y = remote(ebuf.at[2], rxy.at[1], send.at[3], recv.at[3], y)

    def add(self, k, tile_of):
        h = self.half
        if k == 1:
            self.low.wait_recv()
        if k == 2:
            self.high.wait_recv()

        @pl.loop(0, self.out.shape[1] // TILE)
        def _(t):
            sl = pl.ds(pl.multiple_of(t * TILE, TILE), TILE)
            value = tile_of(sl)
            if k == 0:
                self.out[:, sl] = value
            elif k == 3:
                self.ebuf[0, :, sl] = value.astype(bf16)
            elif k == 1:
                self.ebuf[1, :h, sl] = (value[:h] + self.rd[0, :, sl].astype(f32)).astype(bf16)
                self.ebuf[1, h:, sl] = value[h:].astype(bf16)
            else:
                self.ebuf[2, :h, sl] = value[:h].astype(bf16)
                self.ebuf[2, h:, sl] = (value[h:] + self.rd[1, :, sl].astype(f32)).astype(bf16)

        if k == 3:
            self.low.start()
            self.high.start()
        if k == 1:
            self.to_x.start()
        if k == 2:
            self.to_y.start()

    def finish(self):
        self.to_x.wait_recv()
        self.to_y.wait_recv()

        @pl.loop(0, self.out.shape[1] // TILE)
        def _(t):
            sl = pl.ds(pl.multiple_of(t * TILE, TILE), TILE)
            self.out[:, sl] += self.rxy[0, :, sl].astype(f32) + self.rxy[1, :, sl].astype(f32)

        for copy in (self.low, self.high, self.to_x, self.to_y):
            copy.wait_send()


def scatter_scratch(length, width):
    return [
        pltpu.VMEM((3, length, width), bf16),
        pltpu.VMEM((2, length // 2, width), bf16),
        pltpu.VMEM((2, length, width), bf16),
        pltpu.SemaphoreType.DMA((4,)),
        pltpu.SemaphoreType.DMA((4,)),
    ]


def attend_back_kernel(
    gm_ref, raw_ref, a1_ref, pa_ref, pb_ref, cos_ref, sin_ref, start_ref, qg_ref, kg_ref,
    out_ref, sum_ref, dqg_ref, dkg_ref,
    gp_ref, dk_ref, dv_ref, acc_a, acc_b, heads, cbuf, crecv,
    ebuf, rd, rxy, rs_send, rs_recv, do_send, do_recv, do_own, c_send, c_recv,
):
    length = a1_ref.shape[0]
    step = 128
    score_scale = HD ** (-0.5)
    s = pl.program_id(0)
    me = lax.axis_index("dp")
    core = me % 2
    place = (me // 2) % TP
    x, y, d, sibling = partners(me)
    cols = 4 * HD

    def columns_of(device):
        return pl.ds(pl.multiple_of(((device // 2) % TP) * cols, cols), cols)

    incoming = [
        remote(gm_ref.at[:, columns_of(device)], heads.at[k], do_send.at[k - 1], do_recv.at[k - 1], device)
        for k, device in ((1, x), (2, y), (3, d))
    ]
    own = pltpu.make_async_copy(
        gm_ref.at[:, pl.ds(pl.multiple_of(place * cols, cols), cols)], heads.at[0], do_own
    )
    scatter = Scatter(out_ref, ebuf, rd, rxy, rs_send, rs_recv, x, y)
    across = remote(cbuf, crecv, c_send, c_recv, sibling)

    @pl.when(s == 0)
    def _():
        greet((x, y, d, sibling))
        for k in (2, 0, 1):
            incoming[k].start()
        own.start()
        for ref in (acc_a, acc_b, dqg_ref, dkg_ref):
            ref[...] = jnp.zeros_like(ref)
        incoming[2].wait_recv()

    @pl.when(s == 1)
    def _():
        incoming[0].wait_recv()

    @pl.when(s == 2)
    def _():
        incoming[1].wait_recv()

    @pl.when(s == 3)
    def _():
        own.wait()

    which = part_order(s)

    for h in range(2):
        col = h * 4 * HD
        side = core if h == 0 else 1 - core
        cosine, sine = cos_ref[...], sin_ref[...]
        (q0, q1, k0), value = heads_of(
            raw_ref[:, col : col + 4 * HD], cosine, sine, qg_ref[...], kg_ref[...]
        )
        dk_ref[...] = jnp.zeros_like(dk_ref)
        dv_ref[...] = jnp.zeros_like(dv_ref)
        parts = []
        for b in range(length // step):
            sl = slice(b * step, (b + 1) * step)
            span = (b + 1) * step
            qs = jnp.concatenate([q0[2][sl], q1[2][sl]], axis=0)
            gs = jnp.concatenate(
                [
                    heads[which, sl, pl.ds(pl.multiple_of((2 * side + g) * HD, HD), HD)]
                    for g in range(2)
                ],
                axis=0,
            )
            keys, values = k0[2][:span], value[:span]
            probs = block_probs(qs, keys, start_ref[sl, :], b * step, score_scale)
            dv_ref[:span, :] += dot_tn(probs.astype(bf16), gs)
            grad_probs = dot_nt(gs, values)
            delta = jnp.sum(probs * grad_probs, axis=-1, keepdims=True)
            grad_scores = (probs * (grad_probs - delta)).astype(bf16)
            dk_ref[:span, :] += dot_tn(grad_scores, qs)
            parts.append(dot(grad_scores, keys))
        dq0 = jnp.concatenate([p[:step] for p in parts], axis=0) * score_scale
        dq1 = jnp.concatenate([p[step:] for p in parts], axis=0) * score_scale
        for k, (raw, inverse, _), grad, gain_ref, dgain_ref in (
            (0, q0, dq0, qg_ref, dqg_ref),
            (1, q1, dq1, qg_ref, dqg_ref),
            (2, k0, dk_ref[...] * score_scale, kg_ref, dkg_ref),
        ):
            back = grad * cosine + turn(grad * sine)
            scaled = back * gain_ref[...]
            inner = jnp.mean(scaled * raw, axis=-1, keepdims=True)
            gp_ref[:, col + k * HD : col + (k + 1) * HD] = (
                inverse * (scaled - raw * inverse * inverse * inner)
            ).astype(bf16)
            dgain_ref[...] += jnp.sum(back * raw * inverse, axis=0, keepdims=True)
        gp_ref[:, col + 3 * HD : col + 4 * HD] = dv_ref[...].astype(bf16)

    half = 4 * HD

    def tile_of(sl):
        return dot_nt(gp_ref[:, :half], pa_ref[sl, :]) + dot_nt(gp_ref[:, half:], pb_ref[sl, :])

    for at, k in enumerate(ORDER):

        @pl.when(s == at)
        def _():
            scatter.add(k, tile_of)

    @pl.loop(0, acc_a.shape[0] // TILE)
    def _(t):
        sl = pl.ds(pl.multiple_of(t * TILE, TILE), TILE)
        acc_b[sl, :] += dot_tn(a1_ref[:, sl], gp_ref[:, half:])

    @pl.when(s == 3)
    def _():
        cbuf[...] = acc_b[...].astype(bf16)
        across.start()

    @pl.loop(0, acc_a.shape[0] // TILE)
    def _(t):
        sl = pl.ds(pl.multiple_of(t * TILE, TILE), TILE)
        acc_a[sl, :] += dot_tn(a1_ref[:, sl], gp_ref[:, :half])

    @pl.when(s == 3)
    def _():
        across.wait_recv()
        sum_ref[...] = (acc_a[...] + crecv[...].astype(f32)).astype(bf16)
        scatter.finish()
        across.wait_send()
        for copy in incoming:
            copy.wait_send()


CHUNK = 256


def feed_kernel(
    a2_ref, wa_ref, da_ref, g_ref,
    gate_ref, up_ref, hid_ref, wb_ref, db_ref, ga_ref, sum_ref,
    a2, wa, wb, g, hid, stage, cbuf, crecv,
    loads, x_send, x_recv, g_send, g_recv, s_sem, c_send, c_recv, keeps,
):
    tokens, width = a2.shape
    length = g_ref.shape[0]
    fn = wa.shape[1] // 2
    x, y, d, sibling = partners(lax.axis_index("dp"))
    h = length // 2

    def rows(k, offset=0, size=length):
        return g.at[pl.ds(k * length + offset, size)]

    load_x = pltpu.make_async_copy(a2_ref, a2, loads.at[0])
    load_w = pltpu.make_async_copy(wa_ref, wa, loads.at[1])
    load_g = pltpu.make_async_copy(g_ref, rows(0), loads.at[2])
    swap_w = remote(wa_ref, wb, x_send.at[0], x_recv.at[0], sibling)
    swap_d = remote(da_ref, db_ref, x_send.at[1], x_recv.at[1], sibling)
    g_x = remote(g_ref, rows(1), g_send.at[0], g_recv.at[0], x)
    g_y = remote(g_ref, rows(2), g_send.at[1], g_recv.at[1], y)
    g_low = remote(rows(2, 0, h), rows(3, 0, h), g_send.at[2], g_recv.at[2], x)
    g_high = remote(rows(1, h, h), rows(3, h, h), g_send.at[3], g_recv.at[3], y)
    keep_w = pltpu.make_async_copy(wb, wb_ref, keeps.at[0])
    keep_g = pltpu.make_async_copy(g, ga_ref, keeps.at[1])
    keep_h = pltpu.make_async_copy(hid, hid_ref, keeps.at[2])

    load_w.start()
    load_x.start()
    load_g.start()
    greet((x, y, d, sibling))
    g_x.start()
    g_y.start()
    swap_w.start()
    swap_d.start()

    per_half = fn // CHUNK
    span = 2 * length
    halves = tokens // span

    def store(i, which, ref):
        half = i // (per_half * halves)
        j = i % (per_half * halves)
        r, c = j // per_half, j % per_half
        return pltpu.make_async_copy(
            stage.at[i % 2, which],
            ref.at[
                pl.ds(pl.multiple_of(r * span, span), span),
                pl.ds(pl.multiple_of((half * per_half + c) * CHUNK, CHUNK), CHUNK),
            ],
            s_sem.at[i % 2, which],
        )

    def run(half, w):
        @pl.loop(0, per_half * halves)
        def _(j):
            i = j + half * per_half * halves

            @pl.when(i >= 2)
            def _():
                store(i - 2, 0, gate_ref).wait()
                store(i - 2, 1, up_ref).wait()

            r, c = j // per_half, j % per_half
            sl = pl.ds(pl.multiple_of(r * span, span), span)
            gate = dot(a2[sl, :], w[:, pl.ds(pl.multiple_of(c * CHUNK, CHUNK), CHUNK)])
            up = dot(a2[sl, :], w[:, pl.ds(pl.multiple_of(fn + c * CHUNK, CHUNK), CHUNK)])
            stage[i % 2, 0] = gate
            stage[i % 2, 1] = up
            hid[sl, pl.ds(pl.multiple_of((half * per_half + c) * CHUNK, CHUNK), CHUNK)] = (
                gate * jax.nn.sigmoid(gate) * up
            ).astype(bf16)
            store(i, 0, gate_ref).start()
            store(i, 1, up_ref).start()

    load_w.wait()
    load_x.wait()
    run(0, wa)
    swap_w.wait_recv()
    keep_w.start()
    run(1, wb)
    last = 2 * per_half * halves
    for i in (last - 2, last - 1):
        store(i, 0, gate_ref).wait()
        store(i, 1, up_ref).wait()
    keep_h.start()

    g_x.wait_recv()
    g_high.start()
    g_y.wait_recv()
    g_low.start()
    load_g.wait()
    g_low.wait_recv()
    g_high.wait_recv()
    keep_g.start()

    def across(t):
        return remote(cbuf.at[t], crecv.at[t], c_send.at[t], c_recv.at[t], sibling)

    @pl.loop(0, per_half)
    def _(t):
        cols = pl.ds(pl.multiple_of(fn + t * CHUNK, CHUNK), CHUNK)
        cbuf[t] = dot_tn(hid[:, cols], g[...]).astype(bf16)
        across(t).start()

    @pl.loop(0, per_half)
    def _(t):
        cols = pl.ds(pl.multiple_of(t * CHUNK, CHUNK), CHUNK)
        own = dot_tn(hid[:, cols], g[...])
        across(t).wait_recv()
        sum_ref[cols, :] = (own + crecv[t].astype(f32)).astype(bf16)

    for t in range(per_half):
        across(t).wait_send()
    swap_d.wait_recv()
    for copy in (swap_w, swap_d, g_x, g_y, g_low, g_high):
        copy.wait_send()
    for copy in (keep_w, keep_g, keep_h):
        copy.wait()


def feed_forward(a2, wa, da, g):
    tokens, width = a2.shape
    fn = da.shape[0]
    length = g.shape[0]
    anywhere = pl.BlockSpec(memory_space=pl.ANY)
    sem = pltpu.SemaphoreType.DMA
    return pl.pallas_call(
        feed_kernel,
        in_specs=[anywhere] * 4,
        out_specs=[anywhere] * 6 + [pl.BlockSpec(memory_space=pltpu.VMEM)],
        out_shape=[
            struct((tokens, 2 * fn), f32),
            struct((tokens, 2 * fn), f32),
            struct((tokens, 2 * fn), bf16),
            struct(wa.shape, bf16),
            struct(da.shape, bf16),
            struct((tokens, width), bf16),
            struct(da.shape, bf16),
        ],
        scratch_shapes=[
            pltpu.VMEM(a2.shape, bf16),
            pltpu.VMEM(wa.shape, bf16),
            pltpu.VMEM(wa.shape, bf16),
            pltpu.VMEM(a2.shape, bf16),
            pltpu.VMEM((tokens, 2 * fn), bf16),
            pltpu.VMEM((2, 2, 2 * length, CHUNK), f32),
            pltpu.VMEM((fn // CHUNK, CHUNK, width), bf16),
            pltpu.VMEM((fn // CHUNK, CHUNK, width), bf16),
            sem((3,)), sem((2,)), sem((2,)), sem((4,)), sem((4,)), sem((2, 2)),
            sem((fn // CHUNK,)), sem((fn // CHUNK,)), sem((3,)),
        ],
        compiler_params=pltpu.CompilerParams(
            vmem_limit_bytes=58 << 20, collective_id=4, has_side_effects=True
        ),
        cost_estimate=pl.CostEstimate(
            flops=4 * tokens * width * fn, bytes_accessed=30 << 20, transcendentals=0
        ),
        name="feed_forward",
    )(a2, wa, da, g)


def feed_back_kernel(
    gate_ref, up_ref, ga_ref, da_ref, db_ref, wa_ref, wb_ref, a2_ref,
    out_ref, sum_ref, crecv_ref,
    gp, wa, wb, a2, wd, uv, cbuf, cgot, stage, loads, u_sem, c_send, c_recv, g_sem, s_sem,
    ebuf, rd, rxy, rs_send, rs_recv,
):
    length = out_ref.shape[0]
    cols = wa.shape[1]
    fn = cols // 2
    rows = cbuf.shape[1]
    tiles = a2.shape[1] // rows
    x, y, d, sibling = partners(lax.axis_index("dp"))
    scatter = Scatter(out_ref, ebuf, rd, rxy, rs_send, rs_recv, x, y)

    def piece(k):
        sl = pl.ds(k * length, length)
        return pltpu.make_async_copy(ga_ref.at[sl], a2.at[sl], loads.at[k])

    load_a = pltpu.make_async_copy(wa_ref, wa, loads.at[4])
    load_b = pltpu.make_async_copy(wb_ref, wb, loads.at[5])
    load_da = pltpu.make_async_copy(da_ref, wd.at[pl.ds(0, fn)], loads.at[6])
    load_db = pltpu.make_async_copy(db_ref, wd.at[pl.ds(fn, fn)], loads.at[7])
    load_x = pltpu.make_async_copy(a2_ref, a2, loads.at[8])
    chunks = cols // CHUNK

    def fetch_uv(i, which, ref):
        return pltpu.make_async_copy(
            ref.at[
                pl.ds(pl.multiple_of(part_order(i // chunks) * length, length), length),
                pl.ds(pl.multiple_of((i % chunks) * CHUNK, CHUNK), CHUNK),
            ],
            uv.at[i % 2, which],
            u_sem.at[i % 2, which],
        )

    fetch_uv(0, 0, gate_ref).start()
    fetch_uv(0, 1, up_ref).start()
    piece(3).start()
    load_da.start()
    load_db.start()
    load_a.start()
    load_b.start()
    for k in (1, 2, 0):
        piece(k).start()
    greet((x, y, d, sibling))

    def rows_of(t):
        return pl.ds(pl.multiple_of(t * rows, rows), rows)

    def across(t):
        return remote(
            cbuf.at[t % 2], crecv_ref.at[rows_of(t)], c_send.at[t % 2], c_recv.at[t], sibling
        )

    def fetch(t):
        return pltpu.make_async_copy(crecv_ref.at[rows_of(t)], cgot.at[t % 2], g_sem.at[t % 2])

    def store(t):
        return pltpu.make_async_copy(stage.at[t % 2], sum_ref.at[rows_of(t)], s_sem.at[t % 2])

    def part_of(k):
        sl = slice(k * length, (k + 1) * length)

        def tile_of(cut):
            return dot_nt(gp[sl, :cols], wa[cut, :]) + dot_nt(gp[sl, cols:], wb[cut, :])

        return tile_of

    def inner(first, count):
        @pl.loop(first * chunks, (first + count) * chunks)
        def _(i):
            @pl.when(i + 1 < TP * chunks)
            def _():
                fetch_uv(i + 1, 0, gate_ref).start()
                fetch_uv(i + 1, 1, up_ref).start()

            sl = pl.ds(pl.multiple_of(part_order(i // chunks) * length, length), length)
            c = i % chunks
            half, at = c // (chunks // 2), c % (chunks // 2)
            grad_hidden = dot_nt(a2[sl, :], wd[pl.ds(pl.multiple_of(c * CHUNK, CHUNK), CHUNK), :])
            fetch_uv(i, 0, gate_ref).wait()
            fetch_uv(i, 1, up_ref).wait()
            gate, up = uv[i % 2, 0], uv[i % 2, 1]
            sig = jax.nn.sigmoid(gate)
            scaled = grad_hidden * sig
            to = half * cols + at * CHUNK
            gp[sl, pl.ds(pl.multiple_of(to, CHUNK), CHUNK)] = (
                scaled * up * (1.0 + gate * (1.0 - sig))
            ).astype(bf16)
            gp[sl, pl.ds(pl.multiple_of(to + fn, CHUNK), CHUNK)] = (scaled * gate).astype(bf16)

    piece(3).wait()
    load_da.wait()
    load_db.wait()
    inner(0, 1)
    load_a.wait()
    load_b.wait()
    scatter.add(3, part_of(3))
    for k in (1, 2, 0):
        piece(k).wait()
    inner(1, 3)
    load_x.start()
    scatter.add(1, part_of(1))
    scatter.add(2, part_of(2))
    load_x.wait()

    @pl.loop(0, tiles)
    def _(t):
        @pl.when(t >= 2)
        def _():
            across(t - 2).wait_send()

        cbuf[t % 2] = dot_tn(a2[:, rows_of(t)], gp[:, cols:]).astype(bf16)
        across(t).start()

    scatter.add(0, part_of(0))

    @pl.loop(0, tiles)
    def _(t):
        across(t).wait_recv()
        fetch(t).start()

        @pl.when(t >= 2)
        def _():
            store(t - 2).wait()

        own = dot_tn(a2[:, rows_of(t)], gp[:, :cols])
        fetch(t).wait()
        stage[t % 2] = (own + cgot[t % 2].astype(f32)).astype(bf16)
        store(t).start()

    for t in (tiles - 2, tiles - 1):
        store(t).wait()
        across(t).wait_send()
    scatter.finish()


def feed_backward(gate, up, ga, da, db, wa, wb, a2, length):
    tokens, width = a2.shape
    cols = wa.shape[1]
    rows = 256
    anywhere = pl.BlockSpec(memory_space=pl.ANY)
    sem = pltpu.SemaphoreType.DMA
    return pl.pallas_call(
        feed_back_kernel,
        in_specs=[anywhere] * 8,
        out_specs=[pl.BlockSpec(memory_space=pltpu.VMEM), anywhere, anywhere],
        out_shape=[
            struct((length, width), f32),
            struct(wa.shape, bf16),
            struct(wa.shape, bf16),
        ],
        scratch_shapes=[
            pltpu.VMEM((tokens, 2 * cols), bf16),
            pltpu.VMEM(wa.shape, bf16),
            pltpu.VMEM(wb.shape, bf16),
            pltpu.VMEM(a2.shape, bf16),
            pltpu.VMEM((cols, width), bf16),
            pltpu.VMEM((2, 2, length, CHUNK), f32),
            pltpu.VMEM((2, rows, cols), bf16),
            pltpu.VMEM((2, rows, cols), bf16),
            pltpu.VMEM((2, rows, cols), bf16),
            sem((9,)), sem((2, 2)), sem((2,)), sem((width // rows,)), sem((2,)), sem((2,)),
        ]
        + scatter_scratch(length, width),
        compiler_params=pltpu.CompilerParams(
            vmem_limit_bytes=62 << 20, collective_id=1, has_side_effects=True
        ),
        cost_estimate=pl.CostEstimate(
            flops=4 * tokens * width * cols, bytes_accessed=30 << 20, transcendentals=0
        ),
        name="feed_backward",
    )(gate, up, ga, da, db, wa, wb, a2)[:2]


ORDER = (3, 1, 2, 0)


def part_order(s):
    return 3 - 2 * s + 3 * (s // 2)


def rows_spec(length, cols):
    return pl.BlockSpec((length, cols), lambda s: (s, 0))


def whole_spec(shape):
    return pl.BlockSpec(shape, lambda s: (0, 0))


def struct(shape, dtype):
    return jax.ShapeDtypeStruct(shape, dtype)


def attend_kernel(
    x_ref, pa_ref, pb_ref, cos_ref, sin_ref, start_ref, ag_ref, mg_ref, qg_ref, kg_ref, wc_ref,
    raw_ref, a1_ref, mixed_ref, after_ref, wo_ref, a2_ref,
    heads, mix, wo, a2, o_send, o_recv, w_send, w_recv, s_send, s_recv, a_send, a_recv, local,
):
    length, width = x_ref.shape
    step = 128
    score_scale = HD ** (-0.5)
    s = pl.program_id(0)
    me = lax.axis_index("dp")
    core = me % 2
    place = (me // 2) % TP
    x, y, d, sibling = partners(me)
    near = (x, y, d)
    cols = 4 * HD
    block = wc_ref.shape[1]

    def block_of(device):
        return pl.ds(pl.multiple_of((device % (2 * TP)) * block, block), block)

    spread_out = [
        remote(wc_ref, wo.at[:, block_of(me)], w_send.at[i], w_recv.at[i], device)
        for i, device in enumerate(near)
    ]
    own_block = pltpu.make_async_copy(wc_ref, wo.at[:, block_of(me)], local.at[0])
    beside = [remote(wc_ref, wo.at[:, block_of(me)], s_send.at[3], s_recv.at[3], sibling)]
    onward = [
        remote(wo.at[:, block_of(device)], wo.at[:, block_of(device)], s_send.at[i], s_recv.at[i], sibling)
        for i, device in enumerate(near)
    ]
    mine = pl.ds(pl.multiple_of(place * cols, cols), cols)
    home = [
        remote(heads.at[i + 1], mix.at[:, mine], o_send.at[i], o_recv.at[i], device)
        for i, device in enumerate(near)
    ]
    h = length // 2
    a2_x = remote(a2.at[0], a2.at[1], a_send.at[0], a_recv.at[0], x)
    a2_y = remote(a2.at[0], a2.at[2], a_send.at[1], a_recv.at[1], y)
    a2_low = remote(a2.at[2, pl.ds(0, h)], a2.at[3, pl.ds(0, h)], a_send.at[2], a_recv.at[2], x)
    a2_high = remote(a2.at[1, pl.ds(h, h)], a2.at[3, pl.ds(h, h)], a_send.at[3], a_recv.at[3], y)
    keep = [
        pltpu.make_async_copy(a2.at[k], a2_ref.at[pl.ds(k * length, length)], local.at[1 + k])
        for k in range(TP)
    ]
    keep_out = pltpu.make_async_copy(wo, wo_ref, local.at[5])

    @pl.when(s == 0)
    def _():
        greet((x, y, d, sibling))
        for copy in spread_out + beside:
            copy.start()
        own_block.start()

    @pl.loop(0, length // step)
    def _(t):
        sl = pl.ds(pl.multiple_of(t * step, step), step)
        v = x_ref[sl, :].astype(f32)
        a1_ref[sl, :] = (v * inverse_rms(v) * ag_ref[...]).astype(bf16)

    which = part_order(s)
    for half, p_ref in ((0, pa_ref), (1, pb_ref)):
        side = core if half == 0 else 1 - core
        raw_ref[:, half * cols : (half + 1) * cols] = dot(a1_ref[...], p_ref[...])
        (q0, q1, k0), value = heads_of(
            raw_ref[:, half * cols : (half + 1) * cols], cos_ref[...], sin_ref[...], qg_ref[...], kg_ref[...]
        )
        for b in range(length // step):
            sl = slice(b * step, (b + 1) * step)
            span = (b + 1) * step
            qs = jnp.concatenate([q0[2][sl], q1[2][sl]], axis=0)
            probs = block_probs(qs, k0[2][:span], start_ref[sl, :], b * step, score_scale)
            mixed = dot(probs.astype(bf16), value[:span]).astype(bf16)
            for g in range(2):
                at = pl.ds(pl.multiple_of((2 * side + g) * HD, HD), HD)
                heads[which, sl, at] = mixed[g * step : (g + 1) * step]

    for at, k in enumerate(ORDER[:3]):

        @pl.when(s == at)
        def _():
            home[k - 1].start()

    @pl.when(s == 3)
    def _():
        mix[:, mine] = heads[0]
        for i in range(3):
            spread_out[i].wait_recv()
            onward[i].start()
        for copy in home:
            copy.wait_recv()
        own_block.wait()
        for copy in beside + onward:
            copy.wait_recv()
        keep_out.start()

        @pl.loop(0, width // TILE)
        def _(t):
            sl = pl.ds(pl.multiple_of(t * TILE, TILE), TILE)
            after_ref[:, sl] = x_ref[:, sl].astype(f32) + dot(mix[...], wo[:, sl])

        @pl.loop(0, length // step)
        def _(t):
            sl = pl.ds(pl.multiple_of(t * step, step), step)
            v = after_ref[sl, :]
            a2[0, sl, :] = (v * inverse_rms(v) * mg_ref[...]).astype(bf16)

        a2_x.start()
        a2_y.start()
        keep[0].start()
        mixed_ref[...] = mix[...]
        a2_x.wait_recv()
        a2_high.start()
        keep[1].start()
        a2_y.wait_recv()
        a2_low.start()
        keep[2].start()
        a2_high.wait_recv()
        a2_low.wait_recv()
        keep[3].start()
        for copy in spread_out + beside + onward + home + [a2_x, a2_y, a2_low, a2_high]:
            copy.wait_send()
        for copy in keep + [keep_out]:
            copy.wait()


def attend_forward(x, pa, pb, cosine, sine, starts, ag, mg, qg, kg, wc, length):
    tokens, width = x.shape
    anywhere = pl.BlockSpec(memory_space=pl.ANY)

    def in_order(cols):
        return pl.BlockSpec((length, cols), lambda s: (part_order(s), 0))

    return pl.pallas_call(
        attend_kernel,
        grid=(TP,),
        in_specs=[in_order(width)]
        + [whole_spec(w.shape) for w in (pa, pb)]
        + [in_order(HD), in_order(HD), in_order(1)]
        + [whole_spec(g.shape) for g in (ag, mg, qg, kg)]
        + [anywhere],
        out_specs=[in_order(8 * HD), in_order(width)]
        + [whole_spec((length, width))] * 2
        + [anywhere] * 2,
        out_shape=[
            struct((tokens, 8 * HD), f32),
            struct((tokens, width), bf16),
            struct((length, width), bf16),
            struct((length, width), f32),
            struct((wc.shape[0], width), bf16),
            struct((tokens, width), bf16),
        ],
        scratch_shapes=[
            pltpu.VMEM((TP, length, 4 * HD), bf16),
            pltpu.VMEM((length, width), bf16),
            pltpu.VMEM((wc.shape[0], width), bf16),
            pltpu.VMEM((TP, length, width), bf16),
            pltpu.SemaphoreType.DMA((3,)),
            pltpu.SemaphoreType.DMA((3,)),
            pltpu.SemaphoreType.DMA((3,)),
            pltpu.SemaphoreType.DMA((3,)),
            pltpu.SemaphoreType.DMA((4,)),
            pltpu.SemaphoreType.DMA((4,)),
            pltpu.SemaphoreType.DMA((4,)),
            pltpu.SemaphoreType.DMA((4,)),
            pltpu.SemaphoreType.DMA((6,)),
        ],
        compiler_params=pltpu.CompilerParams(
            vmem_limit_bytes=56 << 20, collective_id=3, has_side_effects=True
        ),
        cost_estimate=pl.CostEstimate(
            flops=2 * tokens * width * 8 * HD, bytes_accessed=30 << 20, transcendentals=0
        ),
        name="attend_forward",
    )(x, pa, pb, cosine, sine, starts, ag, mg, qg, kg, wc)


def attend_backward(gm, raw, a1, pa, pb, cosine, sine, starts, qg, kg, length):
    tokens, width = a1.shape

    def in_order(cols):
        return pl.BlockSpec((length, cols), lambda s: (part_order(s), 0))

    return pl.pallas_call(
        attend_back_kernel,
        grid=(TP,),
        in_specs=[pl.BlockSpec(memory_space=pl.ANY)]
        + [in_order(c) for c in (8 * HD, width)]
        + [whole_spec(w.shape) for w in (pa, pb)]
        + [in_order(HD), in_order(HD), in_order(1)]
        + [whole_spec(v.shape) for v in (qg, kg)],
        out_specs=[whole_spec((length, width)), whole_spec(pa.shape)]
        + [whole_spec(v.shape) for v in (qg, kg)],
        out_shape=[struct((length, width), f32), struct(pa.shape, bf16)]
        + [struct(v.shape, f32) for v in (qg, kg)],
        scratch_shapes=[
            pltpu.VMEM((length, 8 * HD), bf16),
            pltpu.VMEM((length, HD), f32),
            pltpu.VMEM((length, HD), f32),
            pltpu.VMEM(pa.shape, f32),
            pltpu.VMEM(pa.shape, f32),
            pltpu.VMEM((TP, length, 4 * HD), bf16),
            pltpu.VMEM(pa.shape, bf16),
            pltpu.VMEM(pa.shape, bf16),
        ]
        + scatter_scratch(length, width)
        + [
            pltpu.SemaphoreType.DMA((3,)),
            pltpu.SemaphoreType.DMA((3,)),
            pltpu.SemaphoreType.DMA,
            pltpu.SemaphoreType.DMA,
            pltpu.SemaphoreType.DMA,
        ],
        compiler_params=pltpu.CompilerParams(
            vmem_limit_bytes=58 << 20, collective_id=2, has_side_effects=True
        ),
        cost_estimate=pl.CostEstimate(
            flops=2 * tokens * width * 8 * HD, bytes_accessed=30 << 20, transcendentals=0
        ),
        name="attend_backward",
    )(gm, raw, a1, pa, pb, cosine, sine, starts, qg, kg)


def make_body(n):
    m = n // (2 * TP)
    z_groups = [[g * 2 * TP + k for g in range(m)] for k in range(2 * TP)]

    def swap(v, bits):
        return lax.ppermute(v, "dp", [(a, a ^ bits) for a in range(n)])

    def gather_xy(v):
        h = v.shape[0] // 2
        x = swap(v, 2)
        y = swap(v, 4)
        d_low = swap(y[:h], 2)
        d_high = swap(x[h:], 4)
        return [v, x, y, jnp.concatenate([d_low, d_high])]

    def scatter_xy(p0, p1, p2, p3):
        h = p3.shape[0] // 2
        d_low = swap(p3[:h], 4)
        d_high = swap(p3[h:], 2)
        sx = jnp.concatenate([(p1[:h].astype(f32) + d_low.astype(f32)).astype(bf16), p1[h:]])
        sy = jnp.concatenate([p2[:h], (p2[h:].astype(f32) + d_high.astype(f32)).astype(bf16)])
        return p0 + swap(sx, 2).astype(f32) + swap(sy, 4).astype(f32)

    def gather_z(v):
        return lax.all_gather(v, "dp", axis=0, tiled=True, axis_index_groups=z_groups)

    def scatter_z(v):
        return lax.psum_scatter(
            v, "dp", scatter_dimension=0, tiled=True, axis_index_groups=z_groups
        )

    def body(
        tokens,
        segments,
        w_query,
        w_key,
        w_value,
        w_out,
        w_gate,
        w_up,
        w_down,
        attn_gain,
        mlp_gain,
        query_gain,
        key_gain,
        cotangent,
    ):
        me = lax.axis_index("dp")
        core = me % 2
        place = (me // 2) % TP
        length, width = tokens.shape
        rows = w_query.shape[0]
        ffr = w_down.shape[0]

        def exchange(parts_at):
            got = [parts_at(place)]
            for k in range(1, TP):
                got.append(swap(parts_at(place ^ k), 2 * k))
            return got

        def absolute(got):
            stacked = jnp.stack(got)
            return [lax.dynamic_index_in_dim(stacked, place ^ a, 0, keepdims=False) for a in range(TP)]

        def by_core(own, other):
            return (jnp.where(core == 0, own, other), jnp.where(core == 0, other, own))

        def spread(w):
            mine = lax.dynamic_index_in_dim(w, core, 2, keepdims=False)
            other = lax.dynamic_index_in_dim(w, 1 - core, 2, keepdims=False)
            pair = jnp.concatenate(by_core(mine, swap(other, 1)))
            got = exchange(lambda p: lax.dynamic_index_in_dim(pair, p, 1, keepdims=False))
            return jnp.concatenate(absolute(got))

        def unspread(v):
            cut = v.reshape(TP, 2 * rows, v.shape[-1])
            got = exchange(lambda p: lax.dynamic_index_in_dim(cut, p, 0, keepdims=False))
            full = jnp.stack(absolute(got), axis=1)
            mine = lax.dynamic_slice_in_dim(full, core * rows, rows, 0)
            other = lax.dynamic_slice_in_dim(full, (1 - core) * rows, rows, 0)
            return jnp.stack(by_core(mine, swap(other, 1)), axis=2)

        attn_local = jnp.concatenate(
            [
                w_query.reshape(rows, TP, 2, -1),
                w_key.reshape(rows, TP, 2, -1),
                w_value.reshape(rows, TP, 2, -1),
                w_out.reshape(rows, TP, 2, -1),
            ],
            axis=3,
        )
        qn = w_query.shape[1] // (2 * TP)
        kn = w_key.shape[1] // (2 * TP)
        pn = qn + 2 * kn
        attn_in = spread(attn_local)

        gains = jnp.concatenate([attn_gain, mlp_gain, query_gain, key_gain])[None]
        gains, attn_in = lax.optimization_barrier((gains, attn_in))
        bit = 1
        while bit < n:
            got = swap(gains, bit)
            upper = (me // bit) % 2 == 1
            gains = jnp.where(
                upper, jnp.concatenate([got, gains]), jnp.concatenate([gains, got])
            )
            bit *= 2
        hr = query_gain.shape[0]
        attn_scale = gains[:, :rows].reshape(-1).astype(f32)
        mlp_scale = gains[:, rows : 2 * rows].reshape(-1).astype(f32)
        query_scale = gains[:, 2 * rows : 2 * rows + hr].reshape(-1).astype(f32)
        key_scale = gains[:, 2 * rows + hr :].reshape(-1).astype(f32)

        proj_a = gather_z(attn_in[:, :pn])
        proj_b = swap(proj_a, 1)
        out_in, proj_a = lax.optimization_barrier((attn_in[:, pn:], proj_a))
        out_cols = gather_z(out_in)

        tokens_in, attn_in = lax.optimization_barrier((tokens, attn_in))
        tokens_all = jnp.concatenate(gather_xy(tokens_in))

        mlp_local = jnp.concatenate(
            [
                w_gate.reshape(rows, m, TP, 2, ffr).transpose(0, 2, 3, 1, 4).reshape(rows, TP, 2, -1),
                w_up.reshape(rows, m, TP, 2, ffr).transpose(0, 2, 3, 1, 4).reshape(rows, TP, 2, -1),
            ],
            axis=3,
        )
        mlp_in = spread(mlp_local)
        mlp_in, out_cols = lax.optimization_barrier((mlp_in, out_cols))
        mlp_a = gather_z(mlp_in)
        down_local, proj_a = lax.optimization_barrier((w_down, proj_a))
        down_a = gather_z(down_local)
        fn = down_a.shape[0]

        seg_all = jnp.concatenate([segments] + [swap(segments, 2 * k) for k in range(1, TP)])
        positions = positions_of(seg_all)
        cosine, sine = rope_tables(positions)
        sign = jnp.where(jnp.arange(HD) < HD // 2, -1.0, 1.0).astype(f32)
        cosine = cosine.reshape(-1, HD)
        sine = (sine * sign).reshape(-1, HD)
        starts = (jnp.arange(length, dtype=jnp.int32)[None] - positions).reshape(-1, 1)

        proj_a, out_cols, mlp_in = lax.optimization_barrier((proj_a, out_cols, mlp_in))
        raw, normed_one, mixed_own, after_attn, out_full, normed_two_all = attend_forward(
            tokens_all, proj_a, proj_b, cosine, sine, starts,
            attn_scale[None], mlp_scale[None], query_scale[None], key_scale[None], out_cols, length,
        )

        def part(v, k):
            return v[k * length : (k + 1) * length]

        inputs = tokens.astype(f32)
        inv_two = inverse_rms(after_attn)
        mlp_a, down_a, normed_two_all = lax.optimization_barrier((mlp_a, down_a, normed_two_all))

        def core_sum(own, other):
            return (own.astype(f32) + swap(other.astype(bf16), 1).astype(f32)).astype(bf16)

        gate_value, up_value, hidden, mlp_b, down_b, grad_all, down_sum = feed_forward(
            normed_two_all, mlp_a, down_a, cotangent
        )
        down_rows = scatter_z(down_sum)
        grad_normed_two, mlp_sum = feed_backward(
            gate_value, up_value, grad_all, down_a, down_b, mlp_a, mlp_b, normed_two_all, length
        )
        mlp_rows = scatter_z(mlp_sum)
        grad_normed_two, down_rows = lax.optimization_barrier((grad_normed_two, down_rows))
        down_shard = down_rows.astype(f32)

        grad_norm_two, mlp_gain_grad = norm_back(after_attn, inv_two, mlp_scale, grad_normed_two)
        grad_after = cotangent.astype(f32) + grad_norm_two
        grad_after_low = grad_after.astype(bf16)

        grad_mixed = dot_nt(grad_after_low, out_full).astype(bf16)
        grad_normed_one, proj_sum, query_gain_grad, key_gain_grad = attend_backward(
            grad_mixed, raw, normed_one, proj_a, proj_b, cosine, sine, starts,
            query_scale[None], key_scale[None], length,
        )
        proj_rows = scatter_z(proj_sum)
        grad_normed_one, mlp_rows, mixed_own, hidden = lax.optimization_barrier(
            (grad_normed_one, mlp_rows, mixed_own, hidden)
        )
        down = jnp.concatenate([down_a, down_b])
        o3 = dot(part(hidden, 3), down).astype(bf16)
        o1 = dot(part(hidden, 1), down).astype(bf16)
        o2 = dot(part(hidden, 2), down).astype(bf16)
        o0 = after_attn + dot(part(hidden, 0), down)

        out_grad = dot_tn(mixed_own, grad_after_low).astype(bf16).reshape(width, TP, 2, -1)
        out_sum = core_sum(
            lax.dynamic_index_in_dim(out_grad, core, 2, keepdims=False),
            lax.dynamic_index_in_dim(out_grad, 1 - core, 2, keepdims=False),
        )
        out_got = exchange(lambda p: lax.dynamic_index_in_dim(out_sum, p, 1, keepdims=False))
        out_rows = scatter_z(sum(v.astype(f32) for v in out_got).astype(bf16))
        output = scatter_xy(o0, o1, o2, o3).astype(bf16)
        mlp_shard = unspread(mlp_rows).astype(f32)
        out_shard = unspread(out_rows).astype(f32).reshape(rows, -1)

        def ff_columns(v):
            return (
                v.reshape(rows, TP, 2, m, ffr).transpose(0, 3, 1, 2, 4).reshape(rows, w_gate.shape[1])
            )

        gate_shard = ff_columns(mlp_shard[..., :fn])
        up_shard = ff_columns(mlp_shard[..., fn:])

        proj_rows, gate_shard, up_shard = lax.optimization_barrier((proj_rows, gate_shard, up_shard))
        attn_shard = unspread(proj_rows).astype(f32)
        query_shard = attn_shard[..., :qn].reshape(rows, -1)
        key_shard = attn_shard[..., qn : qn + kn].reshape(rows, -1)
        value_shard = attn_shard[..., qn + kn :].reshape(rows, -1)

        grad_norm_one, attn_gain_grad = norm_back(
            inputs, inverse_rms(inputs), attn_scale, grad_normed_one
        )
        tokens_grad = (grad_after + grad_norm_one).astype(bf16)

        gain_grads = jnp.concatenate(
            [
                attn_gain_grad.reshape(n, -1),
                mlp_gain_grad.reshape(n, -1),
                query_gain_grad.reshape(n, -1),
                key_gain_grad.reshape(n, -1),
            ],
            axis=1,
        )
        bit = n // 2
        while bit:
            upper = (me // bit) % 2 == 1
            low, high = gain_grads[:bit], gain_grads[bit:]
            gain_grads = jnp.where(upper, high, low) + swap(jnp.where(upper, low, high), bit)
            bit //= 2
        gain_grads = gain_grads[0]

        return (
            output,
            tokens_grad,
            query_shard,
            key_shard,
            value_shard,
            out_shard,
            gate_shard,
            up_shard,
            down_shard,
            gain_grads[:rows],
            gain_grads[rows : 2 * rows],
            gain_grads[2 * rows : 2 * rows + hr],
            gain_grads[2 * rows + hr :],
        )

    return body


def solution(mesh):
    row = P("dp", None)
    flat = P("dp")
    return jax.shard_map(
        make_body(mesh.shape["dp"]),
        mesh=mesh,
        in_specs=(row,) * 9 + (flat,) * 4 + (row,),
        out_specs=(row,) * 9 + (flat,) * 4,
        check_vma=False,
    )
```

```python
import functools

import jax
import jax.numpy as jnp
from jax import lax
from jax.experimental import pallas as pl
from jax.experimental.pallas import tpu as pltpu
from jax.sharding import PartitionSpec as P

H = 16
KVH = 8
HD = 128
TP = 4

EPS = 1e-06
THETA = 1000000.0

f32 = jnp.float32
bf16 = jnp.bfloat16
MESH = pl.DeviceIdType.MESH


def positions_of(segments):
    earlier = (segments[:, None, :] < segments[:, :, None]).astype(jnp.int32)
    index = jnp.arange(segments.shape[1], dtype=jnp.int32)
    return index[None, :] - jnp.sum(earlier, axis=2)


def rope_tables(positions):
    half = HD // 2
    inverse = THETA ** (-(jnp.arange(half, dtype=f32) * 2.0 / HD))
    angle = positions.astype(f32)[..., None] * inverse
    cosine = jnp.concatenate([jnp.cos(angle), jnp.cos(angle)], axis=-1)
    sine = jnp.concatenate([jnp.sin(angle), jnp.sin(angle)], axis=-1)
    return (cosine, sine)


def inverse_rms(values):
    return lax.rsqrt(jnp.mean(values * values, axis=-1, keepdims=True) + EPS)


def norm_back(values, inverse, gain, grad_normed):
    grad_scaled = grad_normed * gain
    inner = jnp.mean(grad_scaled * values, axis=-1, keepdims=True)
    grad_values = inverse * (grad_scaled - values * inverse * inverse * inner)
    gain_grad = jnp.sum((grad_normed * values * inverse).reshape(-1, values.shape[-1]), axis=0)
    return (grad_values, gain_grad)


def dot(a, b):
    return lax.dot_general(a, b, (((1,), (0,)), ((), ())), preferred_element_type=f32)


def dot_tn(a, b):
    return lax.dot_general(a, b, (((0,), (0,)), ((), ())), preferred_element_type=f32)


def dot_nt(a, b):
    return lax.dot_general(a, b, (((1,), (1,)), ((), ())), preferred_element_type=f32)


def turn(v):
    return pltpu.roll(v, HD // 2, 1)


def heads_of(raw, cosine, sine, query_gain, key_gain):
    out = []
    for k, gain in ((0, query_gain), (1, query_gain), (2, key_gain)):
        v = raw[:, k * HD : (k + 1) * HD]
        inverse = inverse_rms(v)
        normed = v * inverse * gain
        out.append((v, inverse, (normed * cosine + turn(normed) * sine).astype(bf16)))
    return out, raw[:, 3 * HD :].astype(bf16)


def block_probs(qs, keys, starts, row0, score_scale):
    size, span = starts.shape[0], keys.shape[0]
    scores = dot_nt(qs, keys) * score_scale
    column = lax.broadcasted_iota(jnp.int32, (size, span), 1)
    row = lax.broadcasted_iota(jnp.int32, (size, span), 0) + row0
    allowed = (column >= starts) & (column <= row)
    allowed = jnp.concatenate([allowed, allowed], axis=0)
    scores = jnp.where(allowed, scores, -1e30)
    power_term = jnp.exp(scores - jnp.max(scores, axis=-1, keepdims=True))
    return power_term / jnp.sum(power_term, axis=-1, keepdims=True)


def partners(me):
    x = me + 2 - 4 * ((me // 2) % 2)
    y = me + 4 - 8 * ((me // 4) % 2)
    d = x + 4 - 8 * ((me // 4) % 2)
    return x, y, d, me + 1 - 2 * (me % 2)


def greet(devices):
    barrier = pltpu.get_barrier_semaphore()
    for device in devices:
        pl.semaphore_signal(barrier, inc=1, device_id=(device,), device_id_type=MESH)
    pl.semaphore_wait(barrier, len(devices))


def remote(src, dst, send, recv, device):
    return pltpu.make_async_remote_copy(
        src_ref=src, dst_ref=dst, send_sem=send, recv_sem=recv, device_id=(device,), device_id_type=MESH
    )


TILE = 512


class Scatter:
    def __init__(self, out, ebuf, rd, rxy, send, recv, x, y):
        self.out, self.ebuf, self.rd, self.rxy = out, ebuf, rd, rxy
        h = rd.shape[1]
        self.half = h
        self.low = remote(ebuf.at[0, pl.ds(0, h)], rd.at[0], send.at[0], recv.at[0], y)
        self.high = remote(ebuf.at[0, pl.ds(h, h)], rd.at[1], send.at[1], recv.at[1], x)
        self.to_x = remote(ebuf.at[1], rxy.at[0], send.at[2], recv.at[2], x)
        self.to_y = remote(ebuf.at[2], rxy.at[1], send.at[3], recv.at[3], y)

    def add(self, k, tile_of):
        h = self.half
        if k == 1:
            self.low.wait_recv()
        if k == 2:
            self.high.wait_recv()

        @pl.loop(0, self.out.shape[1] // TILE)
        def _(t):
            sl = pl.ds(pl.multiple_of(t * TILE, TILE), TILE)
            value = tile_of(sl)
            if k == 0:
                self.out[:, sl] = value
            elif k == 3:
                self.ebuf[0, :, sl] = value.astype(bf16)
            elif k == 1:
                self.ebuf[1, :h, sl] = (value[:h] + self.rd[0, :, sl].astype(f32)).astype(bf16)
                self.ebuf[1, h:, sl] = value[h:].astype(bf16)
            else:
                self.ebuf[2, :h, sl] = value[:h].astype(bf16)
                self.ebuf[2, h:, sl] = (value[h:] + self.rd[1, :, sl].astype(f32)).astype(bf16)

        if k == 3:
            self.low.start()
            self.high.start()
        if k == 1:
            self.to_x.start()
        if k == 2:
            self.to_y.start()

    def finish(self):
        self.to_x.wait_recv()
        self.to_y.wait_recv()

        @pl.loop(0, self.out.shape[1] // TILE)
        def _(t):
            sl = pl.ds(pl.multiple_of(t * TILE, TILE), TILE)
            self.out[:, sl] += self.rxy[0, :, sl].astype(f32) + self.rxy[1, :, sl].astype(f32)

        for copy in (self.low, self.high, self.to_x, self.to_y):
            copy.wait_send()


def scatter_scratch(length, width):
    return [
        pltpu.VMEM((3, length, width), bf16),
        pltpu.VMEM((2, length // 2, width), bf16),
        pltpu.VMEM((2, length, width), bf16),
        pltpu.SemaphoreType.DMA((4,)),
        pltpu.SemaphoreType.DMA((4,)),
    ]


def attend_back_kernel(
    gm_ref, raw_ref, a1_ref, pa_ref, pb_ref, cos_ref, sin_ref, start_ref, qg_ref, kg_ref, mix_ref, dy_ref,
    out_ref, sum_ref, dqg_ref, dkg_ref, ogot_ref, orecv_ref,
    gp_ref, dk_ref, dv_ref, acc_a, acc_b, heads, cbuf, crecv, oslot, ofetch,
    ebuf, rd, rxy, rs_send, rs_recv, do_send, do_recv, do_own, c_send, c_recv,
    oc_send, oc_recv, os_send, os_recv, o_local,
):
    length = a1_ref.shape[0]
    step = 128
    score_scale = HD ** (-0.5)
    s = pl.program_id(0)
    me = lax.axis_index("dp")
    core = me % 2
    place = (me // 2) % TP
    x, y, d, sibling = partners(me)
    cols = 4 * HD

    def columns_of(device):
        return pl.ds(pl.multiple_of(((device // 2) % TP) * cols, cols), cols)

    incoming = [
        remote(gm_ref.at[:, columns_of(device)], heads.at[k], do_send.at[k - 1], do_recv.at[k - 1], device)
        for k, device in ((1, x), (2, y), (3, d))
    ]
    own = pltpu.make_async_copy(
        gm_ref.at[:, pl.ds(pl.multiple_of(place * cols, cols), cols)], heads.at[0], do_own
    )
    scatter = Scatter(out_ref, ebuf, rd, rxy, rs_send, rs_recv, x, y)
    across = remote(cbuf, crecv, c_send, c_recv, sibling)
    block = oslot.shape[2]
    o_across = [
        remote(oslot.at[k], orecv_ref.at[k], oc_send.at[k], oc_recv.at[k], sibling) for k in range(TP)
    ]
    o_home = [
        remote(oslot.at[k], ogot_ref.at[k - 1], os_send.at[k - 1], os_recv.at[k - 1], device)
        for k, device in ((1, x), (2, y), (3, d))
    ]
    o_back = [
        pltpu.make_async_copy(ogot_ref.at[k - 1], oslot.at[k], o_local.at[k]) for k in range(1, TP)
    ]

    def out_block(k, side):
        device = (me, x, y, d)[k]
        at = ((device // 2) % TP) * 2 + side
        return pl.ds(pl.multiple_of(at * block, block), block)

    def out_tile(k, side, sl):
        return dot_tn(mix_ref[:, sl], dy_ref[:, out_block(k, side)])

    @pl.when(s == 0)
    def _():
        greet((x, y, d, sibling))
        for k in (2, 0, 1):
            incoming[k].start()
        own.start()
        for ref in (acc_a, acc_b, dqg_ref, dkg_ref):
            ref[...] = jnp.zeros_like(ref)
        for k in (3, 1, 2, 0):

            @pl.loop(0, oslot.shape[1] // TILE)
            def _(t):
                sl = pl.ds(pl.multiple_of(t * TILE, TILE), TILE)
                oslot[k, sl, :] = out_tile(k, 1 - core, sl).astype(bf16)

            o_across[k].start()
        incoming[2].wait_recv()

    @pl.when(s == 1)
    def _():
        for k in (3, 1, 2, 0):
            o_across[k].wait_send()
            o_across[k].wait_recv()
            fetch = pltpu.make_async_copy(orecv_ref.at[k], ofetch, o_local.at[0])
            fetch.start()
            fetch.wait()

            @pl.loop(0, oslot.shape[1] // TILE)
            def _(t):
                sl = pl.ds(pl.multiple_of(t * TILE, TILE), TILE)
                oslot[k, sl, :] = (out_tile(k, core, sl) + ofetch[sl, :].astype(f32)).astype(bf16)

            if k:
                o_home[k - 1].start()
        incoming[0].wait_recv()

    @pl.when(s == 2)
    def _():
        incoming[1].wait_recv()

    @pl.when(s == 3)
    def _():
        own.wait()

    which = part_order(s)

    for h in range(2):
        col = h * 4 * HD
        side = core if h == 0 else 1 - core
        cosine, sine = cos_ref[...], sin_ref[...]
        (q0, q1, k0), value = heads_of(
            raw_ref[:, col : col + 4 * HD], cosine, sine, qg_ref[...], kg_ref[...]
        )
        dk_ref[...] = jnp.zeros_like(dk_ref)
        dv_ref[...] = jnp.zeros_like(dv_ref)
        parts = []
        for b in range(length // step):
            sl = slice(b * step, (b + 1) * step)
            span = (b + 1) * step
            qs = jnp.concatenate([q0[2][sl], q1[2][sl]], axis=0)
            gs = jnp.concatenate(
                [
                    heads[which, sl, pl.ds(pl.multiple_of((2 * side + g) * HD, HD), HD)]
                    for g in range(2)
                ],
                axis=0,
            )
            keys, values = k0[2][:span], value[:span]
            probs = block_probs(qs, keys, start_ref[sl, :], b * step, score_scale)
            dv_ref[:span, :] += dot_tn(probs.astype(bf16), gs)
            grad_probs = dot_nt(gs, values)
            delta = jnp.sum(probs * grad_probs, axis=-1, keepdims=True)
            grad_scores = (probs * (grad_probs - delta)).astype(bf16)
            dk_ref[:span, :] += dot_tn(grad_scores, qs)
            parts.append(dot(grad_scores, keys))
        dq0 = jnp.concatenate([p[:step] for p in parts], axis=0) * score_scale
        dq1 = jnp.concatenate([p[step:] for p in parts], axis=0) * score_scale
        for k, (raw, inverse, _), grad, gain_ref, dgain_ref in (
            (0, q0, dq0, qg_ref, dqg_ref),
            (1, q1, dq1, qg_ref, dqg_ref),
            (2, k0, dk_ref[...] * score_scale, kg_ref, dkg_ref),
        ):
            back = grad * cosine + turn(grad * sine)
            scaled = back * gain_ref[...]
            inner = jnp.mean(scaled * raw, axis=-1, keepdims=True)
            gp_ref[:, col + k * HD : col + (k + 1) * HD] = (
                inverse * (scaled - raw * inverse * inverse * inner)
            ).astype(bf16)
            dgain_ref[...] += jnp.sum(back * raw * inverse, axis=0, keepdims=True)
        gp_ref[:, col + 3 * HD : col + 4 * HD] = dv_ref[...].astype(bf16)

    half = 4 * HD

    def tile_of(sl):
        return dot_nt(gp_ref[:, :half], pa_ref[sl, :]) + dot_nt(gp_ref[:, half:], pb_ref[sl, :])

    for at, k in enumerate(ORDER):

        @pl.when(s == at)
        def _():
            scatter.add(k, tile_of)

    @pl.loop(0, acc_a.shape[0] // TILE)
    def _(t):
        sl = pl.ds(pl.multiple_of(t * TILE, TILE), TILE)
        acc_b[sl, :] += dot_tn(a1_ref[:, sl], gp_ref[:, half:])

    @pl.when(s == 3)
    def _():
        cbuf[...] = acc_b[...].astype(bf16)
        across.start()

    @pl.loop(0, acc_a.shape[0] // TILE)
    def _(t):
        sl = pl.ds(pl.multiple_of(t * TILE, TILE), TILE)
        acc_a[sl, :] += dot_tn(a1_ref[:, sl], gp_ref[:, :half])

    @pl.when(s == 3)
    def _():
        proj = acc_a.shape[1]
        across.wait_recv()
        sum_ref[:, :proj] = (acc_a[...] + crecv[...].astype(f32)).astype(bf16)
        for copy, back in zip(o_home, o_back):
            copy.wait()
            back.start()
        for back in o_back:
            back.wait()

        @pl.loop(0, oslot.shape[1] // TILE)
        def _(t):
            sl = pl.ds(pl.multiple_of(t * TILE, TILE), TILE)
            total = oslot[0, sl, :].astype(f32)
            for k in range(1, TP):
                total += oslot[k, sl, :].astype(f32)
            sum_ref[sl, proj:] = total.astype(bf16)

        scatter.finish()
        across.wait_send()
        for copy in incoming:
            copy.wait_send()


CHUNK = 256


def feed_kernel(
    a2_ref, wa_ref, g_ref,
    gate_ref, up_ref, hid_ref, wb_ref, ga_ref, sum_ref,
    a2, wa, wb, g, hid, stage, cbuf, crecv,
    loads, x_send, x_recv, g_send, g_recv, s_sem, c_send, c_recv, keeps,
):
    tokens, width = a2.shape
    length = g_ref.shape[0]
    fn = wa.shape[1] // 2
    x, y, d, sibling = partners(lax.axis_index("dp"))
    h = length // 2

    def rows(k, offset=0, size=length):
        return g.at[pl.ds(k * length + offset, size)]

    load_x = pltpu.make_async_copy(a2_ref, a2, loads.at[0])
    load_w = pltpu.make_async_copy(wa_ref, wa, loads.at[1])
    load_g = pltpu.make_async_copy(g_ref, rows(0), loads.at[2])
    swap_w = remote(wa_ref, wb, x_send.at[0], x_recv.at[0], sibling)
    g_x = remote(g_ref, rows(1), g_send.at[0], g_recv.at[0], x)
    g_y = remote(g_ref, rows(2), g_send.at[1], g_recv.at[1], y)
    g_low = remote(rows(2, 0, h), rows(3, 0, h), g_send.at[2], g_recv.at[2], x)
    g_high = remote(rows(1, h, h), rows(3, h, h), g_send.at[3], g_recv.at[3], y)
    keep_w = pltpu.make_async_copy(wb, wb_ref, keeps.at[0])
    keep_g = pltpu.make_async_copy(g, ga_ref, keeps.at[1])
    keep_h = pltpu.make_async_copy(hid, hid_ref, keeps.at[2])

    load_w.start()
    load_x.start()
    load_g.start()
    greet((x, y, d, sibling))
    g_x.start()
    g_y.start()
    swap_w.start()

    per_half = fn // CHUNK
    span = 2 * length
    halves = tokens // span

    def store(i, which, ref):
        half = i // (per_half * halves)
        j = i % (per_half * halves)
        r, c = j // per_half, j % per_half
        return pltpu.make_async_copy(
            stage.at[i % 2, which],
            ref.at[
                pl.ds(pl.multiple_of(r * span, span), span),
                pl.ds(pl.multiple_of((half * per_half + c) * CHUNK, CHUNK), CHUNK),
            ],
            s_sem.at[i % 2, which],
        )

    def run(half, w):
        @pl.loop(0, per_half * halves)
        def _(j):
            i = j + half * per_half * halves

            @pl.when(i >= 2)
            def _():
                store(i - 2, 0, gate_ref).wait()
                store(i - 2, 1, up_ref).wait()

            r, c = j // per_half, j % per_half
            sl = pl.ds(pl.multiple_of(r * span, span), span)
            gate = dot(a2[sl, :], w[:, pl.ds(pl.multiple_of(c * CHUNK, CHUNK), CHUNK)])
            up = dot(a2[sl, :], w[:, pl.ds(pl.multiple_of(fn + c * CHUNK, CHUNK), CHUNK)])
            stage[i % 2, 0] = gate
            stage[i % 2, 1] = up
            hid[sl, pl.ds(pl.multiple_of((half * per_half + c) * CHUNK, CHUNK), CHUNK)] = (
                gate * jax.nn.sigmoid(gate) * up
            ).astype(bf16)
            store(i, 0, gate_ref).start()
            store(i, 1, up_ref).start()

    load_w.wait()
    load_x.wait()
    run(0, wa)
    swap_w.wait_recv()
    keep_w.start()
    run(1, wb)
    last = 2 * per_half * halves
    for i in (last - 2, last - 1):
        store(i, 0, gate_ref).wait()
        store(i, 1, up_ref).wait()
    keep_h.start()

    g_x.wait_recv()
    g_high.start()
    g_y.wait_recv()
    g_low.start()
    load_g.wait()
    g_low.wait_recv()
    g_high.wait_recv()
    keep_g.start()

    def across(t):
        return remote(cbuf.at[t], crecv.at[t], c_send.at[t], c_recv.at[t], sibling)

    @pl.loop(0, per_half)
    def _(t):
        cols = pl.ds(pl.multiple_of(fn + t * CHUNK, CHUNK), CHUNK)
        cbuf[t] = dot_tn(hid[:, cols], g[...]).astype(bf16)
        across(t).start()

    @pl.loop(0, per_half)
    def _(t):
        cols = pl.ds(pl.multiple_of(t * CHUNK, CHUNK), CHUNK)
        own = dot_tn(hid[:, cols], g[...])
        across(t).wait_recv()
        sum_ref[cols, :] = (own + crecv[t].astype(f32)).astype(bf16)

    for t in range(per_half):
        across(t).wait_send()
    for copy in (swap_w, g_x, g_y, g_low, g_high):
        copy.wait_send()
    for copy in (keep_w, keep_g, keep_h):
        copy.wait()


def feed_forward(a2, wa, g):
    tokens, width = a2.shape
    fn = wa.shape[1] // 2
    length = g.shape[0]
    anywhere = pl.BlockSpec(memory_space=pl.ANY)
    sem = pltpu.SemaphoreType.DMA
    return pl.pallas_call(
        feed_kernel,
        in_specs=[anywhere] * 3,
        out_specs=[anywhere] * 5 + [pl.BlockSpec(memory_space=pltpu.VMEM)],
        out_shape=[
            struct((tokens, 2 * fn), f32),
            struct((tokens, 2 * fn), f32),
            struct((tokens, 2 * fn), bf16),
            struct(wa.shape, bf16),
            struct((tokens, width), bf16),
            struct((fn, width), bf16),
        ],
        scratch_shapes=[
            pltpu.VMEM(a2.shape, bf16),
            pltpu.VMEM(wa.shape, bf16),
            pltpu.VMEM(wa.shape, bf16),
            pltpu.VMEM(a2.shape, bf16),
            pltpu.VMEM((tokens, 2 * fn), bf16),
            pltpu.VMEM((2, 2, 2 * length, CHUNK), f32),
            pltpu.VMEM((fn // CHUNK, CHUNK, width), bf16),
            pltpu.VMEM((fn // CHUNK, CHUNK, width), bf16),
            sem((3,)), sem((2,)), sem((2,)), sem((4,)), sem((4,)), sem((2, 2)),
            sem((fn // CHUNK,)), sem((fn // CHUNK,)), sem((3,)),
        ],
        compiler_params=pltpu.CompilerParams(
            vmem_limit_bytes=58 << 20, collective_id=4, has_side_effects=True
        ),
        cost_estimate=pl.CostEstimate(
            flops=4 * tokens * width * fn, bytes_accessed=30 << 20, transcendentals=0
        ),
        name="feed_forward",
    )(a2, wa, g)


def feed_back_kernel(
    gate_ref, up_ref, ga_ref, da_ref, wa_ref, wb_ref, a2_ref,
    out_ref, sum_ref, db_ref, crecv_ref,
    gp, wa, wb, a2, wd, uv, cbuf, cgot, stage, loads, u_sem, c_send, c_recv, g_sem, s_sem,
    d_send, d_recv,
    ebuf, rd, rxy, rs_send, rs_recv,
):
    length = out_ref.shape[0]
    cols = wa.shape[1]
    fn = cols // 2
    rows = cbuf.shape[1]
    tiles = a2.shape[1] // rows
    x, y, d, sibling = partners(lax.axis_index("dp"))
    scatter = Scatter(out_ref, ebuf, rd, rxy, rs_send, rs_recv, x, y)

    def piece(k):
        sl = pl.ds(k * length, length)
        return pltpu.make_async_copy(ga_ref.at[sl], a2.at[sl], loads.at[k])

    load_a = pltpu.make_async_copy(wa_ref, wa, loads.at[4])
    load_b = pltpu.make_async_copy(wb_ref, wb, loads.at[5])
    load_da = pltpu.make_async_copy(da_ref, wd.at[pl.ds(0, fn)], loads.at[6])
    swap_d = remote(da_ref, wd.at[pl.ds(fn, fn)], d_send, d_recv, sibling)
    keep_d = pltpu.make_async_copy(wd.at[pl.ds(fn, fn)], db_ref, loads.at[7])
    load_x = pltpu.make_async_copy(a2_ref, a2, loads.at[8])
    chunks = cols // CHUNK

    def fetch_uv(i, which, ref):
        return pltpu.make_async_copy(
            ref.at[
                pl.ds(pl.multiple_of(part_order(i // chunks) * length, length), length),
                pl.ds(pl.multiple_of((i % chunks) * CHUNK, CHUNK), CHUNK),
            ],
            uv.at[i % 2, which],
            u_sem.at[i % 2, which],
        )

    fetch_uv(0, 0, gate_ref).start()
    fetch_uv(0, 1, up_ref).start()
    piece(3).start()
    load_da.start()
    greet((x, y, d, sibling))
    swap_d.start()
    load_a.start()
    load_b.start()
    for k in (1, 2, 0):
        piece(k).start()

    def rows_of(t):
        return pl.ds(pl.multiple_of(t * rows, rows), rows)

    def across(t):
        return remote(
            cbuf.at[t % 2], crecv_ref.at[rows_of(t)], c_send.at[t % 2], c_recv.at[t], sibling
        )

    def fetch(t):
        return pltpu.make_async_copy(crecv_ref.at[rows_of(t)], cgot.at[t % 2], g_sem.at[t % 2])

    def store(t):
        return pltpu.make_async_copy(stage.at[t % 2], sum_ref.at[rows_of(t)], s_sem.at[t % 2])

    def part_of(k):
        sl = slice(k * length, (k + 1) * length)

        def tile_of(cut):
            return dot_nt(gp[sl, :cols], wa[cut, :]) + dot_nt(gp[sl, cols:], wb[cut, :])

        return tile_of

    def inner(first, count):
        @pl.loop(first * chunks, (first + count) * chunks)
        def _(i):
            @pl.when(i + 1 < TP * chunks)
            def _():
                fetch_uv(i + 1, 0, gate_ref).start()
                fetch_uv(i + 1, 1, up_ref).start()

            sl = pl.ds(pl.multiple_of(part_order(i // chunks) * length, length), length)
            c = i % chunks
            half, at = c // (chunks // 2), c % (chunks // 2)
            grad_hidden = dot_nt(a2[sl, :], wd[pl.ds(pl.multiple_of(c * CHUNK, CHUNK), CHUNK), :])
            fetch_uv(i, 0, gate_ref).wait()
            fetch_uv(i, 1, up_ref).wait()
            gate, up = uv[i % 2, 0], uv[i % 2, 1]
            sig = jax.nn.sigmoid(gate)
            scaled = grad_hidden * sig
            to = half * cols + at * CHUNK
            gp[sl, pl.ds(pl.multiple_of(to, CHUNK), CHUNK)] = (
                scaled * up * (1.0 + gate * (1.0 - sig))
            ).astype(bf16)
            gp[sl, pl.ds(pl.multiple_of(to + fn, CHUNK), CHUNK)] = (scaled * gate).astype(bf16)

    piece(3).wait()
    load_da.wait()
    swap_d.wait_recv()
    keep_d.start()
    inner(0, 1)
    load_a.wait()
    load_b.wait()
    scatter.add(3, part_of(3))
    for k in (1, 2, 0):
        piece(k).wait()
    inner(1, 3)
    load_x.start()
    scatter.add(1, part_of(1))
    scatter.add(2, part_of(2))
    load_x.wait()

    @pl.loop(0, tiles)
    def _(t):
        @pl.when(t >= 2)
        def _():
            across(t - 2).wait_send()

        cbuf[t % 2] = dot_tn(a2[:, rows_of(t)], gp[:, cols:]).astype(bf16)
        across(t).start()

    scatter.add(0, part_of(0))

    @pl.loop(0, tiles)
    def _(t):
        across(t).wait_recv()
        fetch(t).start()

        @pl.when(t >= 2)
        def _():
            store(t - 2).wait()

        own = dot_tn(a2[:, rows_of(t)], gp[:, :cols])
        fetch(t).wait()
        stage[t % 2] = (own + cgot[t % 2].astype(f32)).astype(bf16)
        store(t).start()

    for t in (tiles - 2, tiles - 1):
        store(t).wait()
        across(t).wait_send()
    swap_d.wait_send()
    keep_d.wait()
    scatter.finish()


def feed_backward(gate, up, ga, da, wa, wb, a2, length):
    tokens, width = a2.shape
    cols = wa.shape[1]
    rows = 256
    anywhere = pl.BlockSpec(memory_space=pl.ANY)
    sem = pltpu.SemaphoreType.DMA
    return pl.pallas_call(
        feed_back_kernel,
        in_specs=[anywhere] * 7,
        out_specs=[pl.BlockSpec(memory_space=pltpu.VMEM), anywhere, anywhere, anywhere],
        out_shape=[
            struct((length, width), f32),
            struct(wa.shape, bf16),
            struct(da.shape, bf16),
            struct(wa.shape, bf16),
        ],
        scratch_shapes=[
            pltpu.VMEM((tokens, 2 * cols), bf16),
            pltpu.VMEM(wa.shape, bf16),
            pltpu.VMEM(wb.shape, bf16),
            pltpu.VMEM(a2.shape, bf16),
            pltpu.VMEM((cols, width), bf16),
            pltpu.VMEM((2, 2, length, CHUNK), f32),
            pltpu.VMEM((2, rows, cols), bf16),
            pltpu.VMEM((2, rows, cols), bf16),
            pltpu.VMEM((2, rows, cols), bf16),
            sem((9,)), sem((2, 2)), sem((2,)), sem((width // rows,)), sem((2,)), sem((2,)),
            sem, sem,
        ]
        + scatter_scratch(length, width),
        compiler_params=pltpu.CompilerParams(
            vmem_limit_bytes=62 << 20, collective_id=1, has_side_effects=True
        ),
        cost_estimate=pl.CostEstimate(
            flops=4 * tokens * width * cols, bytes_accessed=30 << 20, transcendentals=0
        ),
        name="feed_backward",
    )(gate, up, ga, da, wa, wb, a2)[:3]


ORDER = (3, 1, 2, 0)


def part_order(s):
    return 3 - 2 * s + 3 * (s // 2)


def rows_spec(length, cols):
    return pl.BlockSpec((length, cols), lambda s: (s, 0))


def whole_spec(shape):
    return pl.BlockSpec(shape, lambda s: (0, 0))


def struct(shape, dtype):
    return jax.ShapeDtypeStruct(shape, dtype)


def everyone(me):
    size = 2 * TP
    base = me - me % size
    return [base + (me % size + i) % size for i in range(1, size)]


def spread_kernel(wq_ref, wk_ref, wv_ref, wo_ref, proj_ref, out_ref, send, recv, local):
    me = lax.axis_index("dp")
    size = 2 * TP
    rows = wq_ref.shape[0]
    here = pl.ds(pl.multiple_of((me % size) * rows, rows), rows)
    plan = []
    at = 0
    for ref in (wq_ref, wk_ref, wv_ref):
        width = ref.shape[1] // size
        plan.append((ref, width, proj_ref.at[here, pl.ds(at, width)]))
        at += width
    plan.append((wo_ref, wo_ref.shape[1] // size, out_ref.at[here]))

    def columns(ref, width, device):
        return ref.at[:, pl.ds(pl.multiple_of((device % size) * width, width), width)]

    others = everyone(me)
    own = [
        pltpu.make_async_copy(columns(ref, width, me), dst, local.at[t])
        for t, (ref, width, dst) in enumerate(plan)
    ]
    copies = [
        remote(columns(ref, width, device), dst, send.at[i, t], recv.at[i, t], device)
        for i, device in enumerate(others)
        for t, (ref, width, dst) in enumerate(plan)
    ]
    for copy in own:
        copy.start()
    greet(others)
    for copy in copies:
        copy.start()
    for copy in own + copies:
        copy.wait()


def spread_attention(wq, wk, wv, wo):
    size = 2 * TP
    rows = wq.shape[0]
    proj = (wq.shape[1] + wk.shape[1] + wv.shape[1]) // size
    anywhere = pl.BlockSpec(memory_space=pl.ANY)
    sem = pltpu.SemaphoreType.DMA
    return pl.pallas_call(
        spread_kernel,
        in_specs=[anywhere] * 4,
        out_specs=[anywhere] * 2,
        out_shape=[
            struct((size * rows, proj), bf16),
            struct((size * rows, wo.shape[1] // size), bf16),
        ],
        scratch_shapes=[sem((size - 1, 4)), sem((size - 1, 4)), sem((4,))],
        compiler_params=pltpu.CompilerParams(collective_id=5, has_side_effects=True),
        name="spread_attention",
    )(wq, wk, wv, wo)


def gather_kernel(
    x_ref, seg_ref, w_ref, x_all, seg_all, w_all, x_send, x_recv, s_send, s_recv, w_send, w_recv, local,
):
    me = lax.axis_index("dp")
    size = 2 * TP
    x, y, d, _ = partners(me)
    others = everyone(me)
    length = x_ref.shape[0]
    rows = w_ref.shape[1]
    h = length // 2
    here = pl.ds(pl.multiple_of((me % size) * rows, rows), rows)

    def place(k, offset=0, count=length):
        return x_all.at[pl.ds(k * length + offset, count)]

    own = [
        pltpu.make_async_copy(x_ref, place(0), local.at[0]),
        pltpu.make_async_copy(seg_ref, seg_all.at[0], local.at[1]),
        pltpu.make_async_copy(w_ref.at[me % size], w_all.at[here], local.at[2]),
    ]
    segs = [
        remote(seg_ref, seg_all.at[1 + k], s_send.at[k], s_recv.at[k], device)
        for k, device in enumerate((x, y, d))
    ]
    weights = [
        remote(w_ref.at[device % size], w_all.at[here], w_send.at[i], w_recv.at[i], device)
        for i, device in enumerate(others)
    ]
    to_x = remote(x_ref, place(1), x_send.at[0], x_recv.at[0], x)
    to_y = remote(x_ref, place(2), x_send.at[1], x_recv.at[1], y)
    low = remote(place(2, 0, h), place(3, 0, h), x_send.at[2], x_recv.at[2], x)
    high = remote(place(1, h, h), place(3, h, h), x_send.at[3], x_recv.at[3], y)
    for copy in own:
        copy.start()
    greet(others)
    for copy in segs + weights + [to_x, to_y]:
        copy.start()
    to_x.wait_recv()
    high.start()
    to_y.wait_recv()
    low.start()
    for copy in (to_x, to_y):
        copy.wait_send()
    for copy in own + segs + weights + [low, high]:
        copy.wait()


def gather_group(x, seg, w):
    size = 2 * TP
    anywhere = pl.BlockSpec(memory_space=pl.ANY)
    sem = pltpu.SemaphoreType.DMA
    return pl.pallas_call(
        gather_kernel,
        in_specs=[anywhere] * 3,
        out_specs=[anywhere] * 3,
        out_shape=[
            struct((TP * x.shape[0], x.shape[1]), bf16),
            struct((TP, *seg.shape), jnp.int32),
            struct((size * w.shape[1], w.shape[2]), bf16),
        ],
        scratch_shapes=[
            sem((4,)), sem((4,)), sem((3,)), sem((3,)), sem((size - 1,)), sem((size - 1,)), sem((3,)),
        ],
        compiler_params=pltpu.CompilerParams(collective_id=6, has_side_effects=True),
        name="gather_group",
    )(x, seg, w)


def attend_kernel(
    x_ref, pa_ref, pb_ref, cos_ref, sin_ref, start_ref, ag_ref, mg_ref, qg_ref, kg_ref, wc_ref,
    raw_ref, a1_ref, mixed_ref, after_ref, wo_ref, a2_ref,
    heads, mix, wo, a2, o_send, o_recv, w_send, w_recv, s_send, s_recv, a_send, a_recv, local,
):
    length, width = x_ref.shape
    step = 128
    score_scale = HD ** (-0.5)
    s = pl.program_id(0)
    me = lax.axis_index("dp")
    core = me % 2
    place = (me // 2) % TP
    x, y, d, sibling = partners(me)
    near = (x, y, d)
    cols = 4 * HD
    block = wc_ref.shape[1]

    def block_of(device):
        return pl.ds(pl.multiple_of((device % (2 * TP)) * block, block), block)

    spread_out = [
        remote(wc_ref, wo.at[:, block_of(me)], w_send.at[i], w_recv.at[i], device)
        for i, device in enumerate(near)
    ]
    own_block = pltpu.make_async_copy(wc_ref, wo.at[:, block_of(me)], local.at[0])
    beside = [remote(wc_ref, wo.at[:, block_of(me)], s_send.at[3], s_recv.at[3], sibling)]
    onward = [
        remote(wo.at[:, block_of(device)], wo.at[:, block_of(device)], s_send.at[i], s_recv.at[i], sibling)
        for i, device in enumerate(near)
    ]
    mine = pl.ds(pl.multiple_of(place * cols, cols), cols)
    home = [
        remote(heads.at[i + 1], mix.at[:, mine], o_send.at[i], o_recv.at[i], device)
        for i, device in enumerate(near)
    ]
    h = length // 2
    a2_x = remote(a2.at[0], a2.at[1], a_send.at[0], a_recv.at[0], x)
    a2_y = remote(a2.at[0], a2.at[2], a_send.at[1], a_recv.at[1], y)
    a2_low = remote(a2.at[2, pl.ds(0, h)], a2.at[3, pl.ds(0, h)], a_send.at[2], a_recv.at[2], x)
    a2_high = remote(a2.at[1, pl.ds(h, h)], a2.at[3, pl.ds(h, h)], a_send.at[3], a_recv.at[3], y)
    keep = [
        pltpu.make_async_copy(a2.at[k], a2_ref.at[pl.ds(k * length, length)], local.at[1 + k])
        for k in range(TP)
    ]
    keep_out = pltpu.make_async_copy(wo, wo_ref, local.at[5])

    @pl.when(s == 0)
    def _():
        greet((x, y, d, sibling))
        for copy in spread_out + beside:
            copy.start()
        own_block.start()

    @pl.loop(0, length // step)
    def _(t):
        sl = pl.ds(pl.multiple_of(t * step, step), step)
        v = x_ref[sl, :].astype(f32)
        a1_ref[sl, :] = (v * inverse_rms(v) * ag_ref[...]).astype(bf16)

    which = part_order(s)
    for half, p_ref in ((0, pa_ref), (1, pb_ref)):
        side = core if half == 0 else 1 - core
        raw_ref[:, half * cols : (half + 1) * cols] = dot(a1_ref[...], p_ref[...])
        (q0, q1, k0), value = heads_of(
            raw_ref[:, half * cols : (half + 1) * cols], cos_ref[...], sin_ref[...], qg_ref[...], kg_ref[...]
        )
        for b in range(length // step):
            sl = slice(b * step, (b + 1) * step)
            span = (b + 1) * step
            qs = jnp.concatenate([q0[2][sl], q1[2][sl]], axis=0)
            probs = block_probs(qs, k0[2][:span], start_ref[sl, :], b * step, score_scale)
            mixed = dot(probs.astype(bf16), value[:span]).astype(bf16)
            for g in range(2):
                at = pl.ds(pl.multiple_of((2 * side + g) * HD, HD), HD)
                heads[which, sl, at] = mixed[g * step : (g + 1) * step]

    for at, k in enumerate(ORDER[:3]):

        @pl.when(s == at)
        def _():
            home[k - 1].start()

    @pl.when(s == 3)
    def _():
        mix[:, mine] = heads[0]
        for i in range(3):
            spread_out[i].wait_recv()
            onward[i].start()
        for copy in home:
            copy.wait_recv()
        own_block.wait()
        for copy in beside + onward:
            copy.wait_recv()
        keep_out.start()

        @pl.loop(0, width // TILE)
        def _(t):
            sl = pl.ds(pl.multiple_of(t * TILE, TILE), TILE)
            after_ref[:, sl] = x_ref[:, sl].astype(f32) + dot(mix[...], wo[:, sl])

        @pl.loop(0, length // step)
        def _(t):
            sl = pl.ds(pl.multiple_of(t * step, step), step)
            v = after_ref[sl, :]
            a2[0, sl, :] = (v * inverse_rms(v) * mg_ref[...]).astype(bf16)

        a2_x.start()
        a2_y.start()
        keep[0].start()
        mixed_ref[...] = mix[...]
        a2_x.wait_recv()
        a2_high.start()
        keep[1].start()
        a2_y.wait_recv()
        a2_low.start()
        keep[2].start()
        a2_high.wait_recv()
        a2_low.wait_recv()
        keep[3].start()
        for copy in spread_out + beside + onward + home + [a2_x, a2_y, a2_low, a2_high]:
            copy.wait_send()
        for copy in keep + [keep_out]:
            copy.wait()


def attend_forward(x, pa, pb, cosine, sine, starts, ag, mg, qg, kg, wc, length):
    tokens, width = x.shape
    anywhere = pl.BlockSpec(memory_space=pl.ANY)

    def in_order(cols):
        return pl.BlockSpec((length, cols), lambda s: (part_order(s), 0))

    return pl.pallas_call(
        attend_kernel,
        grid=(TP,),
        in_specs=[in_order(width)]
        + [whole_spec(w.shape) for w in (pa, pb)]
        + [in_order(HD), in_order(HD), in_order(1)]
        + [whole_spec(g.shape) for g in (ag, mg, qg, kg)]
        + [anywhere],
        out_specs=[in_order(8 * HD), in_order(width)]
        + [whole_spec((length, width))] * 2
        + [anywhere] * 2,
        out_shape=[
            struct((tokens, 8 * HD), f32),
            struct((tokens, width), bf16),
            struct((length, width), bf16),
            struct((length, width), f32),
            struct((wc.shape[0], width), bf16),
            struct((tokens, width), bf16),
        ],
        scratch_shapes=[
            pltpu.VMEM((TP, length, 4 * HD), bf16),
            pltpu.VMEM((length, width), bf16),
            pltpu.VMEM((wc.shape[0], width), bf16),
            pltpu.VMEM((TP, length, width), bf16),
            pltpu.SemaphoreType.DMA((3,)),
            pltpu.SemaphoreType.DMA((3,)),
            pltpu.SemaphoreType.DMA((3,)),
            pltpu.SemaphoreType.DMA((3,)),
            pltpu.SemaphoreType.DMA((4,)),
            pltpu.SemaphoreType.DMA((4,)),
            pltpu.SemaphoreType.DMA((4,)),
            pltpu.SemaphoreType.DMA((4,)),
            pltpu.SemaphoreType.DMA((6,)),
        ],
        compiler_params=pltpu.CompilerParams(
            vmem_limit_bytes=56 << 20, collective_id=3, has_side_effects=True
        ),
        cost_estimate=pl.CostEstimate(
            flops=2 * tokens * width * 8 * HD, bytes_accessed=30 << 20, transcendentals=0
        ),
        name="attend_forward",
    )(x, pa, pb, cosine, sine, starts, ag, mg, qg, kg, wc)


def attend_backward(gm, raw, a1, pa, pb, cosine, sine, starts, qg, kg, mix, dy, length):
    tokens, width = a1.shape
    block = width // (2 * TP)
    anywhere = pl.BlockSpec(memory_space=pl.ANY)
    sem = pltpu.SemaphoreType.DMA

    def in_order(cols):
        return pl.BlockSpec((length, cols), lambda s: (part_order(s), 0))

    def once(v):
        return pl.BlockSpec(v.shape, lambda s: (0, 0), pipeline_mode=pl.Buffered(1))

    return pl.pallas_call(
        attend_back_kernel,
        grid=(TP,),
        in_specs=[anywhere]
        + [in_order(c) for c in (8 * HD, width)]
        + [once(w) for w in (pa, pb)]
        + [in_order(HD), in_order(HD), in_order(1)]
        + [whole_spec(v.shape) for v in (qg, kg)]
        + [once(v) for v in (mix, dy)],
        out_specs=[whole_spec((length, width)), whole_spec((width, pa.shape[1] + block))]
        + [whole_spec(v.shape) for v in (qg, kg)]
        + [anywhere] * 2,
        out_shape=[struct((length, width), f32), struct((width, pa.shape[1] + block), bf16)]
        + [struct(v.shape, f32) for v in (qg, kg)]
        + [struct((3, width, block), bf16), struct((TP, width, block), bf16)],
        scratch_shapes=[
            pltpu.VMEM((length, 8 * HD), bf16),
            pltpu.VMEM((length, HD), f32),
            pltpu.VMEM((length, HD), f32),
            pltpu.VMEM(pa.shape, f32),
            pltpu.VMEM(pa.shape, f32),
            pltpu.VMEM((TP, length, 4 * HD), bf16),
            pltpu.VMEM(pa.shape, bf16),
            pltpu.VMEM(pa.shape, bf16),
            pltpu.VMEM((TP, width, block), bf16),
            pltpu.VMEM((width, block), bf16),
        ]
        + scatter_scratch(length, width)
        + [sem((3,)), sem((3,)), sem, sem, sem, sem((TP,)), sem((TP,)), sem((3,)), sem((3,)), sem((TP,))],
        compiler_params=pltpu.CompilerParams(
            vmem_limit_bytes=60 << 20, collective_id=2, has_side_effects=True
        ),
        cost_estimate=pl.CostEstimate(
            flops=2 * tokens * width * 8 * HD, bytes_accessed=30 << 20, transcendentals=0
        ),
        name="attend_backward",
    )(gm, raw, a1, pa, pb, cosine, sine, starts, qg, kg, mix, dy)[:4]


def down_kernel(
    run, hid_ref, da_ref, db_ref, after_ref, rows_ref,
    out_ref, gate_ref, up_ref,
    hid, da, db, after, acc, pieces, loads, p_send, p_recv,
    ebuf, rd, rxy, rs_send, rs_recv,
):
    length = after.shape[0]
    fn = da.shape[0]
    size, rows, _ = pieces.shape
    me = lax.axis_index("dp")
    x, y, _, _ = partners(me)
    others = everyone(me)
    scatter = Scatter(acc, ebuf, rd, rxy, rs_send, rs_recv, x, y)

    def block(device):
        return rows_ref.at[pl.ds(pl.multiple_of((device % size) * rows, rows), rows)]

    own = pltpu.make_async_copy(block(me), pieces.at[me % size], loads.at[0])
    copies = [
        remote(block(device), pieces.at[me % size], p_send.at[i], p_recv.at[i], device)
        for i, device in enumerate(others)
    ]
    fills = [
        pltpu.make_async_copy(src, dst, loads.at[1 + i])
        for i, (src, dst) in enumerate(((hid_ref, hid), (da_ref, da), (db_ref, db), (after_ref, after)))
    ]
    for copy in fills:
        copy.start()
    own.start()
    greet(others)
    for copy in copies:
        copy.start()
    for copy in fills:
        copy.wait()

    def part_of(k):
        sl = slice(k * length, (k + 1) * length)

        def tile_of(cut):
            value = dot(hid[sl, :fn], da[:, cut]) + dot(hid[sl, fn:], db[:, cut])
            return value + after[:, cut] if k == 0 else value

        return tile_of

    for k in ORDER:
        scatter.add(k, part_of(k))
    own.wait()
    for copy in copies:
        copy.wait()
    for source in range(size):
        piece = pieces[source].astype(f32)
        for g in range(fn // run):
            to = (g * size + source) * run
            gate_ref[:, to : to + run] = piece[:, g * run : (g + 1) * run]
            up_ref[:, to : to + run] = piece[:, fn + g * run : fn + (g + 1) * run]
    scatter.finish()
    out_ref[...] = acc[...].astype(bf16)


def down_forward(hid, da, db, after, mlp_rows, run):
    length, width = after.shape
    size = 2 * TP
    rows, cols = mlp_rows.shape[0] // size, mlp_rows.shape[1]
    ff = size * cols // 2
    anywhere = pl.BlockSpec(memory_space=pl.ANY)
    vmem = pl.BlockSpec(memory_space=pltpu.VMEM)
    sem = pltpu.SemaphoreType.DMA
    return pl.pallas_call(
        functools.partial(down_kernel, run),
        in_specs=[anywhere] * 5,
        out_specs=[vmem] * 3,
        out_shape=[struct((length, width), bf16), struct((rows, ff), f32), struct((rows, ff), f32)],
        scratch_shapes=[
            pltpu.VMEM(hid.shape, bf16),
            pltpu.VMEM(da.shape, bf16),
            pltpu.VMEM(db.shape, bf16),
            pltpu.VMEM(after.shape, f32),
            pltpu.VMEM(after.shape, f32),
            pltpu.VMEM((size, rows, cols), bf16),
            sem((5,)), sem((size - 1,)), sem((size - 1,)),
        ]
        + scatter_scratch(length, width),
        compiler_params=pltpu.CompilerParams(
            vmem_limit_bytes=56 << 20, collective_id=7, has_side_effects=True
        ),
        cost_estimate=pl.CostEstimate(
            flops=2 * length * width * cols, bytes_accessed=30 << 20, transcendentals=0
        ),
        name="down_forward",
    )(hid, da, db, after, mlp_rows)


def return_kernel(rows_ref, q_ref, k_ref, v_ref, o_ref, pieces, send, recv, local):
    size, rows, _ = pieces.shape
    me = lax.axis_index("dp")
    others = everyone(me)

    def block(device):
        return rows_ref.at[pl.ds(pl.multiple_of((device % size) * rows, rows), rows)]

    own = pltpu.make_async_copy(block(me), pieces.at[me % size], local)
    copies = [
        remote(block(device), pieces.at[me % size], send.at[i], recv.at[i], device)
        for i, device in enumerate(others)
    ]
    own.start()
    greet(others)
    for copy in copies:
        copy.start()
    own.wait()
    for copy in copies:
        copy.wait()
    for source in range(size):
        at = 0
        for ref in (q_ref, k_ref, v_ref, o_ref):
            width = ref.shape[1] // size
            ref[:, source * width : (source + 1) * width] = pieces[source, :, at : at + width].astype(f32)
            at += width


def return_attention(attn_rows, widths):
    size = 2 * TP
    rows, cols = attn_rows.shape[0] // size, attn_rows.shape[1]
    sem = pltpu.SemaphoreType.DMA
    return pl.pallas_call(
        return_kernel,
        in_specs=[pl.BlockSpec(memory_space=pl.ANY)],
        out_specs=[pl.BlockSpec(memory_space=pltpu.VMEM)] * 4,
        out_shape=[struct((rows, w), f32) for w in widths],
        scratch_shapes=[
            pltpu.VMEM((size, rows, cols), bf16), sem((size - 1,)), sem((size - 1,)), sem,
        ],
        compiler_params=pltpu.CompilerParams(collective_id=8, has_side_effects=True),
        name="return_attention",
    )(attn_rows)


def make_body(n):
    m = n // (2 * TP)
    z_groups = [[g * 2 * TP + k for g in range(m)] for k in range(2 * TP)]

    def swap(v, bits):
        return lax.ppermute(v, "dp", [(a, a ^ bits) for a in range(n)])

    def gather_xy(v):
        h = v.shape[0] // 2
        x = swap(v, 2)
        y = swap(v, 4)
        d_low = swap(y[:h], 2)
        d_high = swap(x[h:], 4)
        return [v, x, y, jnp.concatenate([d_low, d_high])]

    def scatter_xy(p0, p1, p2, p3):
        h = p3.shape[0] // 2
        d_low = swap(p3[:h], 4)
        d_high = swap(p3[h:], 2)
        sx = jnp.concatenate([(p1[:h].astype(f32) + d_low.astype(f32)).astype(bf16), p1[h:]])
        sy = jnp.concatenate([p2[:h], (p2[h:].astype(f32) + d_high.astype(f32)).astype(bf16)])
        return p0 + swap(sx, 2).astype(f32) + swap(sy, 4).astype(f32)

    def gather_z(v):
        return lax.all_gather(v, "dp", axis=0, tiled=True, axis_index_groups=z_groups)

    def scatter_z(v):
        return lax.psum_scatter(
            v, "dp", scatter_dimension=0, tiled=True, axis_index_groups=z_groups
        )

    def body(
        tokens,
        segments,
        w_query,
        w_key,
        w_value,
        w_out,
        w_gate,
        w_up,
        w_down,
        attn_gain,
        mlp_gain,
        query_gain,
        key_gain,
        cotangent,
    ):
        me = lax.axis_index("dp")
        core = me % 2
        place = (me // 2) % TP
        length, width = tokens.shape
        rows = w_query.shape[0]
        ffr = w_down.shape[0]

        qn = w_query.shape[1] // (2 * TP)
        kn = w_key.shape[1] // (2 * TP)
        pn = qn + 2 * kn
        proj_in, out_in = spread_attention(w_query, w_key, w_value, w_out)

        gains = jnp.concatenate([attn_gain, mlp_gain, query_gain, key_gain])[None]
        gains, proj_in = lax.optimization_barrier((gains, proj_in))
        bit = 1
        while bit < n:
            got = swap(gains, bit)
            upper = (me // bit) % 2 == 1
            gains = jnp.where(
                upper, jnp.concatenate([got, gains]), jnp.concatenate([gains, got])
            )
            bit *= 2
        hr = query_gain.shape[0]
        attn_scale = gains[:, :rows].reshape(-1).astype(f32)
        mlp_scale = gains[:, rows : 2 * rows].reshape(-1).astype(f32)
        query_scale = gains[:, 2 * rows : 2 * rows + hr].reshape(-1).astype(f32)
        key_scale = gains[:, 2 * rows + hr :].reshape(-1).astype(f32)

        proj_a = gather_z(proj_in)
        out_cols = gather_z(out_in)

        def ff_slices(w):
            return w.reshape(rows, m, 2 * TP, ffr).transpose(2, 0, 1, 3).reshape(2 * TP, rows, -1)

        mlp_local = jnp.concatenate([ff_slices(w_gate), ff_slices(w_up)], axis=2)
        mlp_local, tokens_in, proj_in = lax.optimization_barrier((mlp_local, tokens, proj_in))

        tokens_all, seg_all, mlp_in = gather_group(tokens_in, segments, mlp_local)
        mlp_a = gather_z(mlp_in)
        tokens_all, proj_a, out_cols = lax.optimization_barrier((tokens_all, proj_a, out_cols))
        proj_b = swap(proj_a, 1)
        seg_all = seg_all[:, 0]
        positions = positions_of(seg_all)
        cosine, sine = rope_tables(positions)
        sign = jnp.where(jnp.arange(HD) < HD // 2, -1.0, 1.0).astype(f32)
        cosine = cosine.reshape(-1, HD)
        sine = (sine * sign).reshape(-1, HD)
        starts = (jnp.arange(length, dtype=jnp.int32)[None] - positions).reshape(-1, 1)

        raw, normed_one, mixed_own, after_attn, out_full, normed_two_all = attend_forward(
            tokens_all, proj_a, proj_b, cosine, sine, starts,
            attn_scale[None], mlp_scale[None], query_scale[None], key_scale[None], out_cols, length,
        )

        def part(v, k):
            return v[k * length : (k + 1) * length]

        inputs = tokens.astype(f32)
        inv_two = inverse_rms(after_attn)
        mlp_a, normed_two_all, down_local = lax.optimization_barrier((mlp_a, normed_two_all, w_down))
        down_a = gather_z(down_local)
        fn = down_a.shape[0]

        gate_value, up_value, hidden, mlp_b, grad_all, down_sum = feed_forward(
            normed_two_all, mlp_a, cotangent
        )
        down_rows = scatter_z(down_sum)
        grad_normed_two, mlp_sum, down_b = feed_backward(
            gate_value, up_value, grad_all, down_a, mlp_a, mlp_b, normed_two_all, length
        )
        mlp_rows = scatter_z(mlp_sum)
        grad_normed_two, down_rows = lax.optimization_barrier((grad_normed_two, down_rows))
        down_shard = down_rows.astype(f32)

        grad_norm_two, mlp_gain_grad = norm_back(after_attn, inv_two, mlp_scale, grad_normed_two)
        grad_after = cotangent.astype(f32) + grad_norm_two
        grad_after_low = grad_after.astype(bf16)

        grad_mixed = dot_nt(grad_after_low, out_full).astype(bf16)
        grad_normed_one, attn_sum, query_gain_grad, key_gain_grad = attend_backward(
            grad_mixed, raw, normed_one, proj_a, proj_b, cosine, sine, starts,
            query_scale[None], key_scale[None], mixed_own, grad_after_low, length,
        )
        attn_rows = scatter_z(attn_sum)
        grad_normed_one, mlp_rows, hidden = lax.optimization_barrier(
            (grad_normed_one, mlp_rows, hidden)
        )
        output, gate_shard, up_shard = down_forward(hidden, down_a, down_b, after_attn, mlp_rows, ffr)
        attn_rows, output = lax.optimization_barrier((attn_rows, output))
        query_shard, key_shard, value_shard, out_shard = return_attention(
            attn_rows, [w.shape[1] for w in (w_query, w_key, w_value, w_out)]
        )

        grad_norm_one, attn_gain_grad = norm_back(
            inputs, inverse_rms(inputs), attn_scale, grad_normed_one
        )
        tokens_grad = (grad_after + grad_norm_one).astype(bf16)

        gain_grads = jnp.concatenate(
            [
                attn_gain_grad.reshape(n, -1),
                mlp_gain_grad.reshape(n, -1),
                query_gain_grad.reshape(n, -1),
                key_gain_grad.reshape(n, -1),
            ],
            axis=1,
        )
        bit = n // 2
        while bit:
            upper = (me // bit) % 2 == 1
            low, high = gain_grads[:bit], gain_grads[bit:]
            gain_grads = jnp.where(upper, high, low) + swap(jnp.where(upper, low, high), bit)
            bit //= 2
        gain_grads = gain_grads[0]

        return (
            output,
            tokens_grad,
            query_shard,
            key_shard,
            value_shard,
            out_shard,
            gate_shard,
            up_shard,
            down_shard,
            gain_grads[:rows],
            gain_grads[rows : 2 * rows],
            gain_grads[2 * rows : 2 * rows + hr],
            gain_grads[2 * rows + hr :],
        )

    return body


def solution(mesh):
    row = P("dp", None)
    flat = P("dp")
    return jax.shard_map(
        make_body(mesh.shape["dp"]),
        mesh=mesh,
        in_specs=(row,) * 9 + (flat,) * 4 + (row,),
        out_specs=(row,) * 9 + (flat,) * 4,
        check_vma=False,
    )
```

```python
import functools

import jax
import jax.numpy as jnp
from jax import lax
from jax.experimental import pallas as pl
from jax.experimental.pallas import tpu as pltpu
from jax.sharding import PartitionSpec as P

H = 16
KVH = 8
HD = 128
TP = 4

EPS = 1e-06
THETA = 1000000.0

f32 = jnp.float32
bf16 = jnp.bfloat16
MESH = pl.DeviceIdType.MESH


def inverse_rms(values):
    return lax.rsqrt(jnp.mean(values * values, axis=-1, keepdims=True) + EPS)


def norm_back(values, inverse, gain, grad_normed):
    grad_scaled = grad_normed * gain
    inner = jnp.mean(grad_scaled * values, axis=-1, keepdims=True)
    grad_values = inverse * (grad_scaled - values * inverse * inverse * inner)
    gain_grad = jnp.sum((grad_normed * values * inverse).reshape(-1, values.shape[-1]), axis=0)
    return (grad_values, gain_grad)


def dot(a, b):
    return lax.dot_general(a, b, (((1,), (0,)), ((), ())), preferred_element_type=f32)


def dot_tn(a, b):
    return lax.dot_general(a, b, (((0,), (0,)), ((), ())), preferred_element_type=f32)


def dot_nt(a, b):
    return lax.dot_general(a, b, (((1,), (1,)), ((), ())), preferred_element_type=f32)


def turn(v):
    return pltpu.roll(v, HD // 2, 1)


def heads_of(raw, cosine, sine, query_gain, key_gain):
    out = []
    for k, gain in ((0, query_gain), (1, query_gain), (2, key_gain)):
        v = raw[:, k * HD : (k + 1) * HD]
        inverse = inverse_rms(v)
        normed = v * inverse * gain
        out.append((v, inverse, (normed * cosine + turn(normed) * sine).astype(bf16)))
    return out, raw[:, 3 * HD :].astype(bf16)


def block_probs(qs, keys, starts, row0, score_scale):
    size, span = starts.shape[0], keys.shape[0]
    scores = dot_nt(qs, keys) * score_scale
    column = lax.broadcasted_iota(jnp.int32, (size, span), 1)
    row = lax.broadcasted_iota(jnp.int32, (size, span), 0) + row0
    allowed = (column >= starts) & (column <= row)
    allowed = jnp.concatenate([allowed, allowed], axis=0)
    scores = jnp.where(allowed, scores, -1e30)
    power_term = jnp.exp(scores - jnp.max(scores, axis=-1, keepdims=True))
    return power_term / jnp.sum(power_term, axis=-1, keepdims=True)


def partners(me):
    x = me + 2 - 4 * ((me // 2) % 2)
    y = me + 4 - 8 * ((me // 4) % 2)
    d = x + 4 - 8 * ((me // 4) % 2)
    return x, y, d, me + 1 - 2 * (me % 2)


def greet(devices):
    barrier = pltpu.get_barrier_semaphore()
    for device in devices:
        pl.semaphore_signal(barrier, inc=1, device_id=(device,), device_id_type=MESH)
    pl.semaphore_wait(barrier, len(devices))


def remote(src, dst, send, recv, device):
    return pltpu.make_async_remote_copy(
        src_ref=src, dst_ref=dst, send_sem=send, recv_sem=recv, device_id=(device,), device_id_type=MESH
    )


TILE = 512


class Scatter:
    def __init__(self, out, ebuf, rd, rxy, send, recv, x, y):
        self.out, self.ebuf, self.rd, self.rxy = out, ebuf, rd, rxy
        h = rd.shape[1]
        self.half = h
        self.low = remote(ebuf.at[0, pl.ds(0, h)], rd.at[0], send.at[0], recv.at[0], y)
        self.high = remote(ebuf.at[0, pl.ds(h, h)], rd.at[1], send.at[1], recv.at[1], x)
        self.to_x = remote(ebuf.at[1], rxy.at[0], send.at[2], recv.at[2], x)
        self.to_y = remote(ebuf.at[2], rxy.at[1], send.at[3], recv.at[3], y)

    def add(self, k, tile_of):
        h = self.half
        if k == 1:
            self.low.wait_recv()
        if k == 2:
            self.high.wait_recv()

        @pl.loop(0, self.out.shape[1] // TILE)
        def _(t):
            sl = pl.ds(pl.multiple_of(t * TILE, TILE), TILE)
            value = tile_of(sl)
            if k == 0:
                self.out[:, sl] = value
            elif k == 3:
                self.ebuf[0, :, sl] = value.astype(bf16)
            elif k == 1:
                self.ebuf[1, :h, sl] = (value[:h] + self.rd[0, :, sl].astype(f32)).astype(bf16)
                self.ebuf[1, h:, sl] = value[h:].astype(bf16)
            else:
                self.ebuf[2, :h, sl] = value[:h].astype(bf16)
                self.ebuf[2, h:, sl] = (value[h:] + self.rd[1, :, sl].astype(f32)).astype(bf16)

        if k == 3:
            self.low.start()
            self.high.start()
        if k == 1:
            self.to_x.start()
        if k == 2:
            self.to_y.start()

    def finish(self):
        self.to_x.wait_recv()
        self.to_y.wait_recv()

        @pl.loop(0, self.out.shape[1] // TILE)
        def _(t):
            sl = pl.ds(pl.multiple_of(t * TILE, TILE), TILE)
            self.out[:, sl] += self.rxy[0, :, sl].astype(f32) + self.rxy[1, :, sl].astype(f32)

        for copy in (self.low, self.high, self.to_x, self.to_y):
            copy.wait_send()


def scatter_scratch(length, width):
    return [
        pltpu.VMEM((3, length, width), bf16),
        pltpu.VMEM((2, length // 2, width), bf16),
        pltpu.VMEM((2, length, width), bf16),
        pltpu.SemaphoreType.DMA((4,)),
        pltpu.SemaphoreType.DMA((4,)),
    ]


def attend_back_kernel(
    gm_ref, raw_ref, a1_ref, pa_ref, pb_ref, cos_ref, sin_ref, start_ref, qg_ref, kg_ref, mix_ref, dy_ref,
    out_ref, sum_ref, dqg_ref, dkg_ref, ogot_ref, orecv_ref,
    gp_ref, dk_ref, dv_ref, acc_a, acc_b, heads, cbuf, crecv, oslot, ofetch,
    ebuf, rd, rxy, rs_send, rs_recv, do_send, do_recv, do_own, c_send, c_recv,
    oc_send, oc_recv, os_send, os_recv, o_local,
):
    length = a1_ref.shape[0]
    step = 128
    score_scale = HD ** (-0.5)
    s = pl.program_id(0)
    me = lax.axis_index("dp")
    core = me % 2
    place = (me // 2) % TP
    x, y, d, sibling = partners(me)
    cols = 4 * HD

    def columns_of(device):
        return pl.ds(pl.multiple_of(((device // 2) % TP) * cols, cols), cols)

    incoming = [
        remote(gm_ref.at[:, columns_of(device)], heads.at[k], do_send.at[k - 1], do_recv.at[k - 1], device)
        for k, device in ((1, x), (2, y), (3, d))
    ]
    own = pltpu.make_async_copy(
        gm_ref.at[:, pl.ds(pl.multiple_of(place * cols, cols), cols)], heads.at[0], do_own
    )
    scatter = Scatter(out_ref, ebuf, rd, rxy, rs_send, rs_recv, x, y)
    across = remote(cbuf, crecv, c_send, c_recv, sibling)
    block = oslot.shape[2]
    o_across = [
        remote(oslot.at[k], orecv_ref.at[k], oc_send.at[k], oc_recv.at[k], sibling) for k in range(TP)
    ]
    tall = oslot.shape[1] // 2
    o_low = remote(
        oslot.at[3, pl.ds(0, tall)], ogot_ref.at[2, pl.ds(0, tall)], os_send.at[2], os_recv.at[2], y
    )
    o_high = remote(
        oslot.at[3, pl.ds(tall, tall)], ogot_ref.at[2, pl.ds(tall, tall)], os_send.at[3], os_recv.at[3], x
    )
    o_home = [
        remote(oslot.at[k], ogot_ref.at[k - 1], os_send.at[k - 1], os_recv.at[k - 1], device)
        for k, device in ((1, x), (2, y))
    ]
    o_back = [
        pltpu.make_async_copy(ogot_ref.at[k - 1], oslot.at[k], o_local.at[k]) for k in range(1, 3)
    ]

    def out_block(k, side):
        device = (me, x, y, d)[k]
        at = ((device // 2) % TP) * 2 + side
        return pl.ds(pl.multiple_of(at * block, block), block)

    def out_tile(k, side, sl):
        return dot_tn(mix_ref[:, sl], dy_ref[:, out_block(k, side)])

    @pl.when(s == 0)
    def _():
        greet((x, y, d, sibling))
        for k in (2, 0, 1):
            incoming[k].start()
        own.start()
        for ref in (acc_a, acc_b, dqg_ref, dkg_ref):
            ref[...] = jnp.zeros_like(ref)
        for k in (3, 1, 2, 0):

            @pl.loop(0, oslot.shape[1] // TILE)
            def _(t):
                sl = pl.ds(pl.multiple_of(t * TILE, TILE), TILE)
                oslot[k, sl, :] = out_tile(k, 1 - core, sl).astype(bf16)

            o_across[k].start()
        incoming[2].wait_recv()

    @pl.when(s == 1)
    def _():
        for k in (3, 1, 2, 0):
            o_across[k].wait_send()
            o_across[k].wait_recv()
            fetch = pltpu.make_async_copy(orecv_ref.at[k], ofetch, o_local.at[0])
            fetch.start()
            fetch.wait()

            @pl.loop(0, oslot.shape[1] // TILE)
            def _(t):
                sl = pl.ds(pl.multiple_of(t * TILE, TILE), TILE)
                oslot[k, sl, :] = (out_tile(k, core, sl) + ofetch[sl, :].astype(f32)).astype(bf16)

            if k == 3:
                o_low.start()
                o_high.start()
        incoming[0].wait_recv()

    @pl.when(s == 2)
    def _():
        for copy, k, offset in ((o_low, 1, 0), (o_high, 2, tall)):
            copy.wait_recv()
            fetch = pltpu.make_async_copy(
                ogot_ref.at[2, pl.ds(offset, tall)], ofetch.at[pl.ds(0, tall)], o_local.at[0]
            )
            fetch.start()
            fetch.wait()

            @pl.loop(0, tall // TILE)
            def _(t):
                sl = pl.ds(pl.multiple_of(t * TILE, TILE), TILE)
                to = pl.ds(pl.multiple_of(offset + t * TILE, TILE), TILE)
                oslot[k, to, :] = (oslot[k, to, :].astype(f32) + ofetch[sl, :].astype(f32)).astype(bf16)

            o_home[k - 1].start()
        incoming[1].wait_recv()

    @pl.when(s == 3)
    def _():
        own.wait()

    which = part_order(s)

    for h in range(2):
        col = h * 4 * HD
        side = core if h == 0 else 1 - core
        cosine, sine = cos_ref[...], sin_ref[...]
        (q0, q1, k0), value = heads_of(
            raw_ref[:, col : col + 4 * HD], cosine, sine, qg_ref[...], kg_ref[...]
        )
        dk_ref[...] = jnp.zeros_like(dk_ref)
        dv_ref[...] = jnp.zeros_like(dv_ref)
        parts = []
        for b in range(length // step):
            sl = slice(b * step, (b + 1) * step)
            span = (b + 1) * step
            qs = jnp.concatenate([q0[2][sl], q1[2][sl]], axis=0)
            gs = jnp.concatenate(
                [
                    heads[which, sl, pl.ds(pl.multiple_of((2 * side + g) * HD, HD), HD)]
                    for g in range(2)
                ],
                axis=0,
            )
            keys, values = k0[2][:span], value[:span]
            probs = block_probs(qs, keys, start_ref[sl, :], b * step, score_scale)
            dv_ref[:span, :] += dot_tn(probs.astype(bf16), gs)
            grad_probs = dot_nt(gs, values)
            delta = jnp.sum(probs * grad_probs, axis=-1, keepdims=True)
            grad_scores = (probs * (grad_probs - delta)).astype(bf16)
            dk_ref[:span, :] += dot_tn(grad_scores, qs)
            parts.append(dot(grad_scores, keys))
        dq0 = jnp.concatenate([p[:step] for p in parts], axis=0) * score_scale
        dq1 = jnp.concatenate([p[step:] for p in parts], axis=0) * score_scale
        for k, (raw, inverse, _), grad, gain_ref, dgain_ref in (
            (0, q0, dq0, qg_ref, dqg_ref),
            (1, q1, dq1, qg_ref, dqg_ref),
            (2, k0, dk_ref[...] * score_scale, kg_ref, dkg_ref),
        ):
            back = grad * cosine + turn(grad * sine)
            scaled = back * gain_ref[...]
            inner = jnp.mean(scaled * raw, axis=-1, keepdims=True)
            gp_ref[:, col + k * HD : col + (k + 1) * HD] = (
                inverse * (scaled - raw * inverse * inverse * inner)
            ).astype(bf16)
            dgain_ref[...] += jnp.sum(back * raw * inverse, axis=0, keepdims=True)
        gp_ref[:, col + 3 * HD : col + 4 * HD] = dv_ref[...].astype(bf16)

    half = 4 * HD

    def tile_of(sl):
        return dot_nt(gp_ref[:, :half], pa_ref[sl, :]) + dot_nt(gp_ref[:, half:], pb_ref[sl, :])

    for at, k in enumerate(ORDER):

        @pl.when(s == at)
        def _():
            scatter.add(k, tile_of)

    @pl.loop(0, acc_a.shape[0] // TILE)
    def _(t):
        sl = pl.ds(pl.multiple_of(t * TILE, TILE), TILE)
        acc_b[sl, :] += dot_tn(a1_ref[:, sl], gp_ref[:, half:])

    @pl.when(s == 3)
    def _():
        cbuf[...] = acc_b[...].astype(bf16)
        across.start()

    @pl.loop(0, acc_a.shape[0] // TILE)
    def _(t):
        sl = pl.ds(pl.multiple_of(t * TILE, TILE), TILE)
        acc_a[sl, :] += dot_tn(a1_ref[:, sl], gp_ref[:, :half])

    @pl.when(s == 3)
    def _():
        proj = acc_a.shape[1]
        across.wait_recv()
        sum_ref[:, :proj] = (acc_a[...] + crecv[...].astype(f32)).astype(bf16)
        o_low.wait_send()
        o_high.wait_send()
        for copy, back in zip(o_home, o_back):
            copy.wait()
            back.start()
        for back in o_back:
            back.wait()

        @pl.loop(0, oslot.shape[1] // TILE)
        def _(t):
            sl = pl.ds(pl.multiple_of(t * TILE, TILE), TILE)
            total = oslot[0, sl, :].astype(f32)
            for k in range(1, 3):
                total += oslot[k, sl, :].astype(f32)
            sum_ref[sl, proj:] = total.astype(bf16)

        scatter.finish()
        across.wait_send()
        for copy in incoming:
            copy.wait_send()


CHUNK = 256


def feed_kernel(
    a2_ref, wa_ref, g_ref,
    gate_ref, up_ref, hid_ref, wb_ref, ga_ref, sum_ref,
    a2, wa, wb, g, hid, stage, cbuf, crecv,
    loads, x_send, x_recv, g_send, g_recv, s_sem, c_send, c_recv, keeps,
):
    tokens, width = a2.shape
    length = g_ref.shape[0]
    fn = wa.shape[1] // 2
    x, y, d, sibling = partners(lax.axis_index("dp"))
    h = length // 2

    def rows(k, offset=0, size=length):
        return g.at[pl.ds(k * length + offset, size)]

    load_x = pltpu.make_async_copy(a2_ref, a2, loads.at[0])
    load_w = pltpu.make_async_copy(wa_ref, wa, loads.at[1])
    load_g = pltpu.make_async_copy(g_ref, rows(0), loads.at[2])
    swap_w = remote(wa_ref, wb, x_send.at[0], x_recv.at[0], sibling)
    g_x = remote(g_ref, rows(1), g_send.at[0], g_recv.at[0], x)
    g_y = remote(g_ref, rows(2), g_send.at[1], g_recv.at[1], y)
    g_low = remote(rows(2, 0, h), rows(3, 0, h), g_send.at[2], g_recv.at[2], x)
    g_high = remote(rows(1, h, h), rows(3, h, h), g_send.at[3], g_recv.at[3], y)
    keep_w = pltpu.make_async_copy(wb, wb_ref, keeps.at[0])
    keep_g = pltpu.make_async_copy(g, ga_ref, keeps.at[1])
    keep_h = pltpu.make_async_copy(hid, hid_ref, keeps.at[2])

    load_w.start()
    load_x.start()
    load_g.start()
    greet((x, y, d, sibling))
    g_x.start()
    g_y.start()
    swap_w.start()

    per_half = fn // CHUNK
    span = 2 * length
    halves = tokens // span

    def store(i, which, ref):
        half = i // (per_half * halves)
        j = i % (per_half * halves)
        r, c = j // per_half, j % per_half
        return pltpu.make_async_copy(
            stage.at[i % 2, which],
            ref.at[
                pl.ds(pl.multiple_of(r * span, span), span),
                pl.ds(pl.multiple_of((half * per_half + c) * CHUNK, CHUNK), CHUNK),
            ],
            s_sem.at[i % 2, which],
        )

    def run(half, w):
        @pl.loop(0, per_half * halves)
        def _(j):
            i = j + half * per_half * halves

            @pl.when(i >= 2)
            def _():
                store(i - 2, 0, gate_ref).wait()
                store(i - 2, 1, up_ref).wait()

            r, c = j // per_half, j % per_half
            sl = pl.ds(pl.multiple_of(r * span, span), span)
            gate = dot(a2[sl, :], w[:, pl.ds(pl.multiple_of(c * CHUNK, CHUNK), CHUNK)])
            up = dot(a2[sl, :], w[:, pl.ds(pl.multiple_of(fn + c * CHUNK, CHUNK), CHUNK)])
            stage[i % 2, 0] = gate
            stage[i % 2, 1] = up
            hid[sl, pl.ds(pl.multiple_of((half * per_half + c) * CHUNK, CHUNK), CHUNK)] = (
                gate * jax.nn.sigmoid(gate) * up
            ).astype(bf16)
            store(i, 0, gate_ref).start()
            store(i, 1, up_ref).start()

    load_w.wait()
    load_x.wait()
    run(0, wa)
    swap_w.wait_recv()
    keep_w.start()
    run(1, wb)
    last = 2 * per_half * halves
    for i in (last - 2, last - 1):
        store(i, 0, gate_ref).wait()
        store(i, 1, up_ref).wait()
    keep_h.start()

    g_x.wait_recv()
    g_high.start()
    g_y.wait_recv()
    g_low.start()
    load_g.wait()
    g_low.wait_recv()
    g_high.wait_recv()
    keep_g.start()

    def across(t):
        return remote(cbuf.at[t], crecv.at[t], c_send.at[t], c_recv.at[t], sibling)

    @pl.loop(0, per_half)
    def _(t):
        cols = pl.ds(pl.multiple_of(fn + t * CHUNK, CHUNK), CHUNK)
        cbuf[t] = dot_tn(hid[:, cols], g[...]).astype(bf16)
        across(t).start()

    @pl.loop(0, per_half)
    def _(t):
        cols = pl.ds(pl.multiple_of(t * CHUNK, CHUNK), CHUNK)
        own = dot_tn(hid[:, cols], g[...])
        across(t).wait_recv()
        sum_ref[cols, :] = (own + crecv[t].astype(f32)).astype(bf16)

    for t in range(per_half):
        across(t).wait_send()
    for copy in (swap_w, g_x, g_y, g_low, g_high):
        copy.wait_send()
    for copy in (keep_w, keep_g, keep_h):
        copy.wait()


def feed_forward(a2, wa, g):
    tokens, width = a2.shape
    fn = wa.shape[1] // 2
    length = g.shape[0]
    anywhere = pl.BlockSpec(memory_space=pl.ANY)
    sem = pltpu.SemaphoreType.DMA
    return pl.pallas_call(
        feed_kernel,
        in_specs=[anywhere] * 3,
        out_specs=[anywhere] * 5 + [pl.BlockSpec(memory_space=pltpu.VMEM)],
        out_shape=[
            struct((tokens, 2 * fn), f32),
            struct((tokens, 2 * fn), f32),
            struct((tokens, 2 * fn), bf16),
            struct(wa.shape, bf16),
            struct((tokens, width), bf16),
            struct((fn, width), bf16),
        ],
        scratch_shapes=[
            pltpu.VMEM(a2.shape, bf16),
            pltpu.VMEM(wa.shape, bf16),
            pltpu.VMEM(wa.shape, bf16),
            pltpu.VMEM(a2.shape, bf16),
            pltpu.VMEM((tokens, 2 * fn), bf16),
            pltpu.VMEM((2, 2, 2 * length, CHUNK), f32),
            pltpu.VMEM((fn // CHUNK, CHUNK, width), bf16),
            pltpu.VMEM((fn // CHUNK, CHUNK, width), bf16),
            sem((3,)), sem((2,)), sem((2,)), sem((4,)), sem((4,)), sem((2, 2)),
            sem((fn // CHUNK,)), sem((fn // CHUNK,)), sem((3,)),
        ],
        compiler_params=pltpu.CompilerParams(
            vmem_limit_bytes=58 << 20, collective_id=4, has_side_effects=True
        ),
        cost_estimate=pl.CostEstimate(
            flops=4 * tokens * width * fn, bytes_accessed=30 << 20, transcendentals=0
        ),
        name="feed_forward",
    )(a2, wa, g)


def feed_back_kernel(
    gate_ref, up_ref, ga_ref, da_ref, wa_ref, wb_ref, a2_ref,
    out_ref, sum_ref, db_ref, crecv_ref,
    gp, wa, wb, a2, wd, uv, cbuf, cgot, stage, loads, u_sem, c_send, c_recv, g_sem, s_sem,
    d_send, d_recv,
    ebuf, rd, rxy, rs_send, rs_recv,
):
    length = out_ref.shape[0]
    cols = wa.shape[1]
    fn = cols // 2
    rows = cbuf.shape[1]
    tiles = a2.shape[1] // rows
    x, y, d, sibling = partners(lax.axis_index("dp"))
    scatter = Scatter(out_ref, ebuf, rd, rxy, rs_send, rs_recv, x, y)

    def piece(k):
        sl = pl.ds(k * length, length)
        return pltpu.make_async_copy(ga_ref.at[sl], a2.at[sl], loads.at[k])

    load_a = pltpu.make_async_copy(wa_ref, wa, loads.at[4])
    load_b = pltpu.make_async_copy(wb_ref, wb, loads.at[5])
    load_da = pltpu.make_async_copy(da_ref, wd.at[pl.ds(0, fn)], loads.at[6])
    swap_d = remote(da_ref, wd.at[pl.ds(fn, fn)], d_send, d_recv, sibling)
    keep_d = pltpu.make_async_copy(wd.at[pl.ds(fn, fn)], db_ref, loads.at[7])
    load_x = pltpu.make_async_copy(a2_ref, a2, loads.at[8])
    per_half = fn // CHUNK
    steps = 2 * TP * per_half

    def step_of(i):
        return part_order(i // (2 * per_half)), i % (2 * per_half)

    def fetch_uv(i, which, ref):
        part, c = step_of(i)
        return pltpu.make_async_copy(
            ref.at[
                pl.ds(pl.multiple_of(part * length, length), length),
                pl.ds(pl.multiple_of(c * CHUNK, CHUNK), CHUNK),
            ],
            uv.at[i % 2, which],
            u_sem.at[i % 2, which],
        )

    fetch_uv(0, 0, gate_ref).start()
    fetch_uv(0, 1, up_ref).start()
    piece(3).start()
    load_da.start()
    greet((x, y, d, sibling))
    swap_d.start()
    load_a.start()
    load_b.start()
    for k in (1, 2, 0):
        piece(k).start()

    def rows_of(t):
        return pl.ds(pl.multiple_of(t * rows, rows), rows)

    def across(t):
        return remote(
            cbuf.at[t % 2], crecv_ref.at[rows_of(t)], c_send.at[t % 2], c_recv.at[t], sibling
        )

    def fetch(t):
        return pltpu.make_async_copy(crecv_ref.at[rows_of(t)], cgot.at[t % 2], g_sem.at[t % 2])

    def store(t):
        return pltpu.make_async_copy(stage.at[t % 2], sum_ref.at[rows_of(t)], s_sem.at[t % 2])

    def part_of(k):
        sl = slice(k * length, (k + 1) * length)

        def tile_of(cut):
            return dot_nt(gp[sl, :cols], wa[cut, :]) + dot_nt(gp[sl, cols:], wb[cut, :])

        return tile_of

    def inner(first, end):
        @pl.loop(first, end)
        def _(i):
            @pl.when(i + 1 < steps)
            def _():
                fetch_uv(i + 1, 0, gate_ref).start()
                fetch_uv(i + 1, 1, up_ref).start()

            part, c = step_of(i)
            sl = pl.ds(pl.multiple_of(part * length, length), length)
            half, at = c // per_half, c % per_half
            grad_hidden = dot_nt(a2[sl, :], wd[pl.ds(pl.multiple_of(c * CHUNK, CHUNK), CHUNK), :])
            fetch_uv(i, 0, gate_ref).wait()
            fetch_uv(i, 1, up_ref).wait()
            gate, up = uv[i % 2, 0], uv[i % 2, 1]
            sig = jax.nn.sigmoid(gate)
            scaled = grad_hidden * sig
            to = half * cols + at * CHUNK
            gp[sl, pl.ds(pl.multiple_of(to, CHUNK), CHUNK)] = (
                scaled * up * (1.0 + gate * (1.0 - sig))
            ).astype(bf16)
            gp[sl, pl.ds(pl.multiple_of(to + fn, CHUNK), CHUNK)] = (scaled * gate).astype(bf16)

    piece(3).wait()
    load_da.wait()
    inner(0, per_half)
    swap_d.wait_recv()
    keep_d.start()
    inner(per_half, 2 * per_half)
    load_a.wait()
    load_b.wait()
    scatter.add(3, part_of(3))
    for k in (1, 2, 0):
        piece(k).wait()
    inner(2 * per_half, steps)
    load_x.start()
    scatter.add(1, part_of(1))
    scatter.add(2, part_of(2))
    load_x.wait()

    @pl.loop(0, tiles)
    def _(t):
        @pl.when(t >= 2)
        def _():
            across(t - 2).wait_send()

        cbuf[t % 2] = dot_tn(a2[:, rows_of(t)], gp[:, cols:]).astype(bf16)
        across(t).start()

    scatter.add(0, part_of(0))

    @pl.loop(0, tiles)
    def _(t):
        across(t).wait_recv()
        fetch(t).start()

        @pl.when(t >= 2)
        def _():
            store(t - 2).wait()

        own = dot_tn(a2[:, rows_of(t)], gp[:, :cols])
        fetch(t).wait()
        stage[t % 2] = (own + cgot[t % 2].astype(f32)).astype(bf16)
        store(t).start()

    for t in (tiles - 2, tiles - 1):
        store(t).wait()
        across(t).wait_send()
    swap_d.wait_send()
    keep_d.wait()
    scatter.finish()


def feed_backward(gate, up, ga, da, wa, wb, a2, length):
    tokens, width = a2.shape
    cols = wa.shape[1]
    rows = 256
    anywhere = pl.BlockSpec(memory_space=pl.ANY)
    sem = pltpu.SemaphoreType.DMA
    return pl.pallas_call(
        feed_back_kernel,
        in_specs=[anywhere] * 7,
        out_specs=[pl.BlockSpec(memory_space=pltpu.VMEM), anywhere, anywhere, anywhere],
        out_shape=[
            struct((length, width), f32),
            struct(wa.shape, bf16),
            struct(da.shape, bf16),
            struct(wa.shape, bf16),
        ],
        scratch_shapes=[
            pltpu.VMEM((tokens, 2 * cols), bf16),
            pltpu.VMEM(wa.shape, bf16),
            pltpu.VMEM(wb.shape, bf16),
            pltpu.VMEM(a2.shape, bf16),
            pltpu.VMEM((cols, width), bf16),
            pltpu.VMEM((2, 2, length, CHUNK), f32),
            pltpu.VMEM((2, rows, cols), bf16),
            pltpu.VMEM((2, rows, cols), bf16),
            pltpu.VMEM((2, rows, cols), bf16),
            sem((9,)), sem((2, 2)), sem((2,)), sem((width // rows,)), sem((2,)), sem((2,)),
            sem, sem,
        ]
        + scatter_scratch(length, width),
        compiler_params=pltpu.CompilerParams(
            vmem_limit_bytes=62 << 20, collective_id=1, has_side_effects=True
        ),
        cost_estimate=pl.CostEstimate(
            flops=4 * tokens * width * cols, bytes_accessed=30 << 20, transcendentals=0
        ),
        name="feed_backward",
    )(gate, up, ga, da, wa, wb, a2)[:3]


ORDER = (3, 1, 2, 0)


def part_order(s):
    return 3 - 2 * s + 3 * (s // 2)


def rows_spec(length, cols):
    return pl.BlockSpec((length, cols), lambda s: (s, 0))


def whole_spec(shape):
    return pl.BlockSpec(shape, lambda s: (0, 0))


def struct(shape, dtype):
    return jax.ShapeDtypeStruct(shape, dtype)


def everyone(me):
    size = 2 * TP
    base = me - me % size
    return [base + (me % size + i) % size for i in range(1, size)]


def spread_kernel(
    wq_ref, wk_ref, wv_ref, wo_ref, gain_ref, seg_ref,
    all_ref, gains_ref, segs_ref,
    send, recv, local, s_send, s_recv,
):
    me = lax.axis_index("dp")
    size = 2 * TP
    rows = wq_ref.shape[0]
    here = pl.ds(pl.multiple_of((me % size) * rows, rows), rows)
    plan = []
    at = 0
    for ref in (wq_ref, wk_ref, wv_ref, wo_ref):
        width = ref.shape[1] // size
        plan.append((ref, width, all_ref.at[here, pl.ds(at, width)]))
        at += width

    def columns(ref, width, device):
        return ref.at[:, pl.ds(pl.multiple_of((device % size) * width, width), width)]

    others = everyone(me)
    gains_here = gains_ref.at[me % size]
    own = [
        pltpu.make_async_copy(columns(ref, width, me), dst, local.at[t])
        for t, (ref, width, dst) in enumerate(plan)
    ] + [
        pltpu.make_async_copy(gain_ref, gains_here, local.at[4]),
        pltpu.make_async_copy(seg_ref, segs_ref.at[0], local.at[5]),
    ]
    copies = [
        remote(columns(ref, width, device), dst, send.at[i, t], recv.at[i, t], device)
        for i, device in enumerate(others)
        for t, (ref, width, dst) in enumerate(plan)
    ]
    copies += [
        remote(gain_ref, gains_here, send.at[i, 4], recv.at[i, 4], device)
        for i, device in enumerate(others)
    ]
    copies += [
        remote(seg_ref, segs_ref.at[1 + k], s_send.at[k], s_recv.at[k], device)
        for k, device in enumerate(partners(me)[:3])
    ]
    for copy in own:
        copy.start()
    greet(others)
    for copy in copies:
        copy.start()
    for copy in own + copies:
        copy.wait()


def spread_attention(wq, wk, wv, wo, gain, seg):
    size = 2 * TP
    rows = wq.shape[0]
    cols = (wq.shape[1] + wk.shape[1] + wv.shape[1] + wo.shape[1]) // size
    anywhere = pl.BlockSpec(memory_space=pl.ANY)
    sem = pltpu.SemaphoreType.DMA
    return pl.pallas_call(
        spread_kernel,
        in_specs=[anywhere] * 6,
        out_specs=[anywhere] * 3,
        out_shape=[
            struct((size * rows, cols), bf16),
            struct((size, *gain.shape), f32),
            struct((TP, *seg.shape), jnp.int32),
        ],
        scratch_shapes=[sem((size - 1, 5)), sem((size - 1, 5)), sem((6,)), sem((3,)), sem((3,))],
        compiler_params=pltpu.CompilerParams(collective_id=5, has_side_effects=True),
        name="spread_attention",
    )(wq, wk, wv, wo, gain, seg)


def gather_kernel(
    run, seg_ref, rate_ref, x_ref, gate_ref, up_ref,
    cos_ref, sin_ref, start_ref, x_all, w_all,
    w_ref, flat, wide, x_send, x_recv, w_send, w_recv, local,
):
    me = lax.axis_index("dp")
    size = 2 * TP
    x, y, d, _ = partners(me)
    others = everyone(me)
    length = x_ref.shape[0]
    rows = w_ref.shape[1]
    h = length // 2
    here = pl.ds(pl.multiple_of((me % size) * rows, rows), rows)

    def place(k, offset=0, count=length):
        return x_all.at[pl.ds(k * length + offset, count)]

    own = [
        pltpu.make_async_copy(x_ref, place(0), local.at[0]),
        pltpu.make_async_copy(w_ref.at[me % size], w_all.at[here], local.at[1]),
    ]
    fills = [
        pltpu.make_async_copy(ref, flat.at[i], local.at[2 + i]) for i, ref in enumerate((gate_ref, up_ref))
    ]
    weights = [
        remote(w_ref.at[device % size], w_all.at[here], w_send.at[i], w_recv.at[i], device)
        for i, device in enumerate(others)
    ]
    to_x = remote(x_ref, place(1), x_send.at[0], x_recv.at[0], x)
    to_y = remote(x_ref, place(2), x_send.at[1], x_recv.at[1], y)
    low = remote(place(2, 0, h), place(3, 0, h), x_send.at[2], x_recv.at[2], x)
    high = remote(place(1, h, h), place(3, h, h), x_send.at[3], x_recv.at[3], y)
    for copy in fills + own[:1]:
        copy.start()
    greet(others)
    for copy in (to_x, to_y):
        copy.start()
    for copy in fills:
        copy.wait()
    half = wide.shape[1] // 2
    values = [flat[i].astype(f32) for i in range(2)]
    for s in range(size):
        for i in range(2):
            for g in range(half // run):
                at = (g * size + s) * run
                wide[:, i * half + g * run : i * half + (g + 1) * run] = values[i][:, at : at + run]
        w_ref[s] = wide[...].astype(bf16)
    for copy in own[1:] + weights:
        copy.start()

    row = lax.broadcasted_iota(jnp.int32, (length, length), 0)
    column = lax.broadcasted_iota(jnp.int32, (length, length), 1)
    for k in range(TP):
        label = jnp.broadcast_to(seg_ref[k].astype(f32), (length, length))
        mine = jnp.sum(jnp.where(row == column, label, 0.0), axis=1, keepdims=True)
        start = jnp.sum(jnp.where(label < mine, 1.0, 0.0), axis=1, keepdims=True)
        position = lax.broadcasted_iota(jnp.int32, (length, 1), 0).astype(f32) - start
        angle = position * rate_ref[0:1, :]
        sl = pl.ds(k * length, length)
        cos_ref[sl, :] = jnp.cos(angle)
        sin_ref[sl, :] = jnp.sin(angle) * rate_ref[1:2, :]
        start_ref[sl, :] = start.astype(jnp.int32)

    to_x.wait_recv()
    high.start()
    to_y.wait_recv()
    low.start()
    for copy in (to_x, to_y):
        copy.wait_send()
    for copy in own + weights + [low, high]:
        copy.wait()


def gather_group(seg, rates, x, gate, up, run):
    size = 2 * TP
    rows, cols = gate.shape[0], 2 * gate.shape[1] // size
    anywhere = pl.BlockSpec(memory_space=pl.ANY)
    vmem = pl.BlockSpec(memory_space=pltpu.VMEM)
    sem = pltpu.SemaphoreType.DMA
    return pl.pallas_call(
        functools.partial(gather_kernel, run),
        in_specs=[vmem] * 2 + [anywhere] * 3,
        out_specs=[vmem] * 3 + [anywhere] * 2,
        out_shape=[
            struct((TP * x.shape[0], HD), f32),
            struct((TP * x.shape[0], HD), f32),
            struct((TP * x.shape[0], 1), jnp.int32),
            struct((TP * x.shape[0], x.shape[1]), bf16),
            struct((size * rows, cols), bf16),
        ],
        scratch_shapes=[
            pltpu.VMEM((size, rows, cols), bf16),
            pltpu.VMEM((2, *gate.shape), bf16),
            pltpu.VMEM((rows, cols), f32),
            sem((4,)), sem((4,)), sem((size - 1,)), sem((size - 1,)), sem((4,)),
        ],
        compiler_params=pltpu.CompilerParams(
            vmem_limit_bytes=32 << 20, collective_id=6, has_side_effects=True
        ),
        name="gather_group",
    )(seg, rates, x, gate, up)


def attend_kernel(
    x_ref, pa_ref, cos_ref, sin_ref, start_ref, ag_ref, mg_ref, qg_ref, kg_ref, wc_ref,
    raw_ref, a1_ref, mixed_ref, after_ref, pb_out, wo_ref, a2_ref,
    pb_ref, heads, mix, wo, a2, p_send, p_recv, o_send, o_recv, w_send, w_recv, s_send, s_recv, a_send, a_recv, local,
):
    length, width = x_ref.shape
    step = 128
    score_scale = HD ** (-0.5)
    s = pl.program_id(0)
    me = lax.axis_index("dp")
    core = me % 2
    place = (me // 2) % TP
    x, y, d, sibling = partners(me)
    near = (x, y, d)
    cols = 4 * HD
    block = wc_ref.shape[1]

    def block_of(device):
        return pl.ds(pl.multiple_of((device % (2 * TP)) * block, block), block)

    tall = wo.shape[0] // 2
    spread_out = [
        remote(wc_ref, wo.at[:, block_of(me)], w_send.at[i], w_recv.at[i], device)
        for i, device in enumerate(near[:2])
    ]

    def passed(device, offset, i, to):
        ref = wo.at[pl.ds(offset, tall), block_of(device)]
        return remote(ref, ref, w_send.at[i], w_recv.at[i], to)

    pass_on = [passed(x, tall, 2, y), passed(y, 0, 3, x)]
    own_block = pltpu.make_async_copy(wc_ref, wo.at[:, block_of(me)], local.at[0])
    beside = [remote(wc_ref, wo.at[:, block_of(me)], s_send.at[3], s_recv.at[3], sibling)]
    onward = [
        remote(wo.at[:, block_of(device)], wo.at[:, block_of(device)], s_send.at[i], s_recv.at[i], sibling)
        for i, device in enumerate(near)
    ]
    mine = pl.ds(pl.multiple_of(place * cols, cols), cols)
    home = [
        remote(heads.at[i + 1], mix.at[:, mine], o_send.at[i], o_recv.at[i], device)
        for i, device in enumerate(near)
    ]
    h = length // 2
    a2_x = remote(a2.at[0], a2.at[1], a_send.at[0], a_recv.at[0], x)
    a2_y = remote(a2.at[0], a2.at[2], a_send.at[1], a_recv.at[1], y)
    a2_low = remote(a2.at[2, pl.ds(0, h)], a2.at[3, pl.ds(0, h)], a_send.at[2], a_recv.at[2], x)
    a2_high = remote(a2.at[1, pl.ds(h, h)], a2.at[3, pl.ds(h, h)], a_send.at[3], a_recv.at[3], y)
    keep = [
        pltpu.make_async_copy(a2.at[k], a2_ref.at[pl.ds(k * length, length)], local.at[1 + k])
        for k in range(TP)
    ]
    keep_out = pltpu.make_async_copy(wo, wo_ref, local.at[5])
    keep_b = pltpu.make_async_copy(pb_ref, pb_out, local.at[6])
    swap_p = remote(pa_ref, pb_ref, p_send, p_recv, sibling)

    @pl.when(s == 0)
    def _():
        greet((x, y, d, sibling))
        for copy in [swap_p] + spread_out + beside:
            copy.start()
        own_block.start()

    @pl.when(s == 3)
    def _():
        for i in range(2):
            spread_out[i].wait_recv()
            pass_on[i].start()
            onward[i].start()

    @pl.loop(0, length // step)
    def _(t):
        sl = pl.ds(pl.multiple_of(t * step, step), step)
        v = x_ref[sl, :].astype(f32)
        a1_ref[sl, :] = (v * inverse_rms(v) * ag_ref[...]).astype(bf16)

    which = part_order(s)
    for half, p_ref in ((0, pa_ref), (1, pb_ref)):
        side = core if half == 0 else 1 - core
        if half:

            @pl.when(s == 0)
            def _():
                swap_p.wait_recv()
                keep_b.start()

        raw_ref[:, half * cols : (half + 1) * cols] = dot(a1_ref[...], p_ref[...])
        (q0, q1, k0), value = heads_of(
            raw_ref[:, half * cols : (half + 1) * cols], cos_ref[...], sin_ref[...], qg_ref[...], kg_ref[...]
        )
        for b in range(length // step):
            sl = slice(b * step, (b + 1) * step)
            span = (b + 1) * step
            qs = jnp.concatenate([q0[2][sl], q1[2][sl]], axis=0)
            probs = block_probs(qs, k0[2][:span], start_ref[sl, :], b * step, score_scale)
            mixed = dot(probs.astype(bf16), value[:span]).astype(bf16)
            for g in range(2):
                at = pl.ds(pl.multiple_of((2 * side + g) * HD, HD), HD)
                heads[which, sl, at] = mixed[g * step : (g + 1) * step]

    for at, k in enumerate(ORDER[:3]):

        @pl.when(s == at)
        def _():
            home[k - 1].start()

    @pl.when(s == 3)
    def _():
        mix[:, mine] = heads[0]
        for copy in pass_on:
            copy.wait_recv()
        onward[2].start()
        for copy in home:
            copy.wait_recv()
        own_block.wait()
        for copy in beside + onward:
            copy.wait_recv()
        keep_out.start()

        @pl.loop(0, width // TILE)
        def _(t):
            sl = pl.ds(pl.multiple_of(t * TILE, TILE), TILE)
            after_ref[:, sl] = x_ref[:, sl].astype(f32) + dot(mix[...], wo[:, sl])

        @pl.loop(0, length // step)
        def _(t):
            sl = pl.ds(pl.multiple_of(t * step, step), step)
            v = after_ref[sl, :]
            a2[0, sl, :] = (v * inverse_rms(v) * mg_ref[...]).astype(bf16)

        a2_x.start()
        a2_y.start()
        keep[0].start()
        mixed_ref[...] = mix[...]
        a2_x.wait_recv()
        a2_high.start()
        keep[1].start()
        a2_y.wait_recv()
        a2_low.start()
        keep[2].start()
        a2_high.wait_recv()
        a2_low.wait_recv()
        keep[3].start()
        for copy in spread_out + pass_on + beside + onward + home + [a2_x, a2_y, a2_low, a2_high]:
            copy.wait_send()
        swap_p.wait_send()
        for copy in keep + [keep_out, keep_b]:
            copy.wait()


def attend_forward(x, pa, cosine, sine, starts, ag, mg, qg, kg, wc, length):
    tokens, width = x.shape
    anywhere = pl.BlockSpec(memory_space=pl.ANY)

    def in_order(cols):
        return pl.BlockSpec((length, cols), lambda s: (part_order(s), 0))

    return pl.pallas_call(
        attend_kernel,
        grid=(TP,),
        in_specs=[in_order(width), pl.BlockSpec(pa.shape, lambda s: (0, 0), pipeline_mode=pl.Buffered(1))]
        + [in_order(HD), in_order(HD), in_order(1)]
        + [whole_spec(g.shape) for g in (ag, mg, qg, kg)]
        + [anywhere],
        out_specs=[in_order(8 * HD), in_order(width)]
        + [whole_spec((length, width))] * 2
        + [anywhere] * 3,
        out_shape=[
            struct((tokens, 8 * HD), f32),
            struct((tokens, width), bf16),
            struct((length, width), bf16),
            struct((length, width), f32),
            struct(pa.shape, bf16),
            struct((wc.shape[0], width), bf16),
            struct((tokens, width), bf16),
        ],
        scratch_shapes=[
            pltpu.VMEM(pa.shape, bf16),
            pltpu.VMEM((TP, length, 4 * HD), bf16),
            pltpu.VMEM((length, width), bf16),
            pltpu.VMEM((wc.shape[0], width), bf16),
            pltpu.VMEM((TP, length, width), bf16),
            pltpu.SemaphoreType.DMA,
            pltpu.SemaphoreType.DMA,
            pltpu.SemaphoreType.DMA((3,)),
            pltpu.SemaphoreType.DMA((3,)),
            pltpu.SemaphoreType.DMA((4,)),
            pltpu.SemaphoreType.DMA((4,)),
            pltpu.SemaphoreType.DMA((4,)),
            pltpu.SemaphoreType.DMA((4,)),
            pltpu.SemaphoreType.DMA((4,)),
            pltpu.SemaphoreType.DMA((4,)),
            pltpu.SemaphoreType.DMA((7,)),
        ],
        compiler_params=pltpu.CompilerParams(
            vmem_limit_bytes=56 << 20, collective_id=3, has_side_effects=True
        ),
        cost_estimate=pl.CostEstimate(
            flops=2 * tokens * width * 8 * HD, bytes_accessed=30 << 20, transcendentals=0
        ),
        name="attend_forward",
    )(x, pa, cosine, sine, starts, ag, mg, qg, kg, wc)


def attend_backward(gm, raw, a1, pa, pb, cosine, sine, starts, qg, kg, mix, dy, length):
    tokens, width = a1.shape
    block = width // (2 * TP)
    anywhere = pl.BlockSpec(memory_space=pl.ANY)
    sem = pltpu.SemaphoreType.DMA

    def in_order(cols):
        return pl.BlockSpec((length, cols), lambda s: (part_order(s), 0))

    def once(v):
        return pl.BlockSpec(v.shape, lambda s: (0, 0), pipeline_mode=pl.Buffered(1))

    return pl.pallas_call(
        attend_back_kernel,
        grid=(TP,),
        in_specs=[anywhere]
        + [in_order(c) for c in (8 * HD, width)]
        + [once(w) for w in (pa, pb)]
        + [in_order(HD), in_order(HD), in_order(1)]
        + [whole_spec(v.shape) for v in (qg, kg)]
        + [once(v) for v in (mix, dy)],
        out_specs=[whole_spec((length, width)), whole_spec((width, pa.shape[1] + block))]
        + [whole_spec(v.shape) for v in (qg, kg)]
        + [anywhere] * 2,
        out_shape=[struct((length, width), f32), struct((width, pa.shape[1] + block), bf16)]
        + [struct(v.shape, f32) for v in (qg, kg)]
        + [struct((3, width, block), bf16), struct((TP, width, block), bf16)],
        scratch_shapes=[
            pltpu.VMEM((length, 8 * HD), bf16),
            pltpu.VMEM((length, HD), f32),
            pltpu.VMEM((length, HD), f32),
            pltpu.VMEM(pa.shape, f32),
            pltpu.VMEM(pa.shape, f32),
            pltpu.VMEM((TP, length, 4 * HD), bf16),
            pltpu.VMEM(pa.shape, bf16),
            pltpu.VMEM(pa.shape, bf16),
            pltpu.VMEM((TP, width, block), bf16),
            pltpu.VMEM((width, block), bf16),
        ]
        + scatter_scratch(length, width)
        + [sem((3,)), sem((3,)), sem, sem, sem, sem((TP,)), sem((TP,)), sem((4,)), sem((4,)), sem((TP,))],
        compiler_params=pltpu.CompilerParams(
            vmem_limit_bytes=60 << 20, collective_id=2, has_side_effects=True
        ),
        cost_estimate=pl.CostEstimate(
            flops=2 * tokens * width * 8 * HD, bytes_accessed=30 << 20, transcendentals=0
        ),
        name="attend_backward",
    )(gm, raw, a1, pa, pb, cosine, sine, starts, qg, kg, mix, dy)[:4]


def down_kernel(
    run, hid_ref, da_ref, db_ref, after_ref, rows_ref, gains_ref,
    out_ref, gate_ref, up_ref, total_ref,
    hid, da, db, after, acc, pieces, gains, loads, p_send, p_recv, g_send, g_recv,
    ebuf, rd, rxy, rs_send, rs_recv,
):
    length = after.shape[0]
    fn = da.shape[0]
    size, rows, _ = pieces.shape
    me = lax.axis_index("dp")
    x, y, _, _ = partners(me)
    others = everyone(me)
    scatter = Scatter(acc, ebuf, rd, rxy, rs_send, rs_recv, x, y)

    def block(device):
        return rows_ref.at[pl.ds(pl.multiple_of((device % size) * rows, rows), rows)]

    own = pltpu.make_async_copy(block(me), pieces.at[me % size], loads.at[0])
    copies = [
        remote(block(device), pieces.at[me % size], p_send.at[i], p_recv.at[i], device)
        for i, device in enumerate(others)
    ]
    own_gains = pltpu.make_async_copy(gains_ref.at[me % size], gains.at[me % size], loads.at[5])
    gain_copies = [
        remote(gains_ref.at[device % size], gains.at[me % size], g_send.at[i], g_recv.at[i], device)
        for i, device in enumerate(others)
    ]
    fills = [
        pltpu.make_async_copy(src, dst, loads.at[1 + i])
        for i, (src, dst) in enumerate(((hid_ref, hid), (da_ref, da), (db_ref, db), (after_ref, after)))
    ]
    for copy in fills:
        copy.start()
    own.start()
    own_gains.start()
    greet(others)
    for copy in gain_copies:
        copy.start()
    for copy in fills:
        copy.wait()

    def part_of(k):
        sl = slice(k * length, (k + 1) * length)

        def tile_of(cut):
            value = dot(hid[sl, :fn], da[:, cut]) + dot(hid[sl, fn:], db[:, cut])
            return value + after[:, cut] if k == 0 else value

        return tile_of

    for k in ORDER[:3]:
        scatter.add(k, part_of(k))
    for copy in copies:
        copy.start()
    scatter.add(0, part_of(0))
    own_gains.wait()
    for copy in gain_copies:
        copy.wait()
    total_ref[...] = jnp.sum(gains[...], axis=0)
    own.wait()
    for copy in copies:
        copy.wait()
    for source in range(size):
        piece = pieces[source].astype(f32)
        for g in range(fn // run):
            to = (g * size + source) * run
            gate_ref[:, to : to + run] = piece[:, g * run : (g + 1) * run]
            up_ref[:, to : to + run] = piece[:, fn + g * run : fn + (g + 1) * run]
    scatter.finish()
    out_ref[...] = acc[...].astype(bf16)


def down_forward(hid, da, db, after, mlp_rows, gains, run):
    length, width = after.shape
    size = 2 * TP
    rows, cols = mlp_rows.shape[0] // size, mlp_rows.shape[1]
    ff = size * cols // 2
    anywhere = pl.BlockSpec(memory_space=pl.ANY)
    vmem = pl.BlockSpec(memory_space=pltpu.VMEM)
    sem = pltpu.SemaphoreType.DMA
    return pl.pallas_call(
        functools.partial(down_kernel, run),
        in_specs=[anywhere] * 6,
        out_specs=[vmem] * 4,
        out_shape=[
            struct((length, width), bf16),
            struct((rows, ff), f32),
            struct((rows, ff), f32),
            struct(gains.shape[1:], f32),
        ],
        scratch_shapes=[
            pltpu.VMEM(hid.shape, bf16),
            pltpu.VMEM(da.shape, bf16),
            pltpu.VMEM(db.shape, bf16),
            pltpu.VMEM(after.shape, f32),
            pltpu.VMEM(after.shape, f32),
            pltpu.VMEM((size, rows, cols), bf16),
            pltpu.VMEM(gains.shape, f32),
            sem((6,)), sem((size - 1,)), sem((size - 1,)), sem((size - 1,)), sem((size - 1,)),
        ]
        + scatter_scratch(length, width),
        compiler_params=pltpu.CompilerParams(
            vmem_limit_bytes=56 << 20, collective_id=7, has_side_effects=True
        ),
        cost_estimate=pl.CostEstimate(
            flops=2 * length * width * cols, bytes_accessed=30 << 20, transcendentals=0
        ),
        name="down_forward",
    )(hid, da, db, after, mlp_rows, gains)


def return_kernel(rows_ref, q_ref, k_ref, v_ref, o_ref, pieces, send, recv, local):
    size, rows, _ = pieces.shape
    me = lax.axis_index("dp")
    others = everyone(me)

    def block(device):
        return rows_ref.at[pl.ds(pl.multiple_of((device % size) * rows, rows), rows)]

    own = pltpu.make_async_copy(block(me), pieces.at[me % size], local)
    copies = [
        remote(block(device), pieces.at[me % size], send.at[i], recv.at[i], device)
        for i, device in enumerate(others)
    ]
    own.start()
    greet(others)
    for copy in copies:
        copy.start()
    own.wait()
    for copy in copies:
        copy.wait()
    for source in range(size):
        at = 0
        for ref in (q_ref, k_ref, v_ref, o_ref):
            width = ref.shape[1] // size
            ref[:, source * width : (source + 1) * width] = pieces[source, :, at : at + width].astype(f32)
            at += width


def return_attention(attn_rows, widths):
    size = 2 * TP
    rows, cols = attn_rows.shape[0] // size, attn_rows.shape[1]
    sem = pltpu.SemaphoreType.DMA
    return pl.pallas_call(
        return_kernel,
        in_specs=[pl.BlockSpec(memory_space=pl.ANY)],
        out_specs=[pl.BlockSpec(memory_space=pltpu.VMEM)] * 4,
        out_shape=[struct((rows, w), f32) for w in widths],
        scratch_shapes=[
            pltpu.VMEM((size, rows, cols), bf16), sem((size - 1,)), sem((size - 1,)), sem,
        ],
        compiler_params=pltpu.CompilerParams(collective_id=8, has_side_effects=True),
        name="return_attention",
    )(attn_rows)


def make_body(n):
    m = n // (2 * TP)
    z_groups = [[g * 2 * TP + k for g in range(m)] for k in range(2 * TP)]

    def swap(v, bits):
        return lax.ppermute(v, "dp", [(a, a ^ bits) for a in range(n)])

    def gather_xy(v):
        h = v.shape[0] // 2
        x = swap(v, 2)
        y = swap(v, 4)
        d_low = swap(y[:h], 2)
        d_high = swap(x[h:], 4)
        return [v, x, y, jnp.concatenate([d_low, d_high])]

    def scatter_xy(p0, p1, p2, p3):
        h = p3.shape[0] // 2
        d_low = swap(p3[:h], 4)
        d_high = swap(p3[h:], 2)
        sx = jnp.concatenate([(p1[:h].astype(f32) + d_low.astype(f32)).astype(bf16), p1[h:]])
        sy = jnp.concatenate([p2[:h], (p2[h:].astype(f32) + d_high.astype(f32)).astype(bf16)])
        return p0 + swap(sx, 2).astype(f32) + swap(sy, 4).astype(f32)

    def gather_z(v):
        return lax.all_gather(v, "dp", axis=0, tiled=True, axis_index_groups=z_groups)

    def scatter_z(v):
        return lax.psum_scatter(
            v, "dp", scatter_dimension=0, tiled=True, axis_index_groups=z_groups
        )

    def body(
        tokens,
        segments,
        w_query,
        w_key,
        w_value,
        w_out,
        w_gate,
        w_up,
        w_down,
        attn_gain,
        mlp_gain,
        query_gain,
        key_gain,
        cotangent,
    ):
        me = lax.axis_index("dp")
        core = me % 2
        place = (me // 2) % TP
        length, width = tokens.shape
        rows = w_query.shape[0]
        ffr = w_down.shape[0]

        qn = w_query.shape[1] // (2 * TP)
        kn = w_key.shape[1] // (2 * TP)
        pn = qn + 2 * kn
        hr = query_gain.shape[0]
        gains = jnp.concatenate([attn_gain, mlp_gain, query_gain, key_gain]).astype(f32)
        count = gains.shape[0]
        padded = -(-count // 256) * 256
        attn_in, gains, seg_all = spread_attention(
            w_query, w_key, w_value, w_out, jnp.pad(gains, (0, padded - count))[None], segments
        )

        depth, wide = attn_in.shape
        gain_rows = gains.astype(bf16).reshape(-1, padded)
        below = jnp.pad(gain_rows, ((0, -gain_rows.shape[0] % 16), (0, wide - padded)))
        attn_all = gather_z(jnp.concatenate([attn_in, below])).reshape(m, -1, wide)
        tokens_in, _ = lax.optimization_barrier((tokens, attn_in))

        rate = THETA ** (-(jnp.arange(HD // 2, dtype=f32) * 2.0 / HD))
        sign = jnp.where(jnp.arange(HD) < HD // 2, -1.0, 1.0).astype(f32)
        rates = jnp.stack([jnp.concatenate([rate, rate]), sign])
        cosine, sine, starts, tokens_all, mlp_in = gather_group(
            seg_all, rates, tokens_in, w_gate, w_up, ffr
        )
        mlp_a = gather_z(mlp_in)
        tokens_all, attn_all = lax.optimization_barrier((tokens_all, attn_all))
        proj_a = attn_all[:, :depth, :pn].reshape(-1, pn)
        out_cols = attn_all[:, :depth, pn:].reshape(-1, wide - pn)
        gains = attn_all[:, depth : depth + gain_rows.shape[0], :padded].reshape(n, padded)
        attn_scale = gains[:, :rows].reshape(-1).astype(f32)
        mlp_scale = gains[:, rows : 2 * rows].reshape(-1).astype(f32)
        query_scale = gains[:, 2 * rows : 2 * rows + hr].reshape(-1).astype(f32)
        key_scale = gains[:, 2 * rows + hr : count].reshape(-1).astype(f32)

        raw, normed_one, mixed_own, after_attn, proj_b, out_full, normed_two_all = attend_forward(
            tokens_all, proj_a, cosine, sine, starts,
            attn_scale[None], mlp_scale[None], query_scale[None], key_scale[None], out_cols, length,
        )

        def part(v, k):
            return v[k * length : (k + 1) * length]

        inputs = tokens.astype(f32)
        inv_two = inverse_rms(after_attn)
        mlp_a, normed_two_all, down_local = lax.optimization_barrier((mlp_a, normed_two_all, w_down))
        down_a = gather_z(down_local)
        fn = down_a.shape[0]

        gate_value, up_value, hidden, mlp_b, grad_all, down_sum = feed_forward(
            normed_two_all, mlp_a, cotangent
        )
        down_rows = scatter_z(down_sum)
        grad_normed_two, mlp_sum, down_b = feed_backward(
            gate_value, up_value, grad_all, down_a, mlp_a, mlp_b, normed_two_all, length
        )
        mlp_rows = scatter_z(mlp_sum)
        grad_normed_two, down_rows = lax.optimization_barrier((grad_normed_two, down_rows))
        down_shard = down_rows.astype(f32)

        grad_norm_two, mlp_gain_grad = norm_back(after_attn, inv_two, mlp_scale, grad_normed_two)
        grad_after = cotangent.astype(f32) + grad_norm_two
        grad_after_low = grad_after.astype(bf16)

        grad_mixed = dot_nt(grad_after_low, out_full).astype(bf16)
        grad_normed_one, attn_sum, query_gain_grad, key_gain_grad = attend_backward(
            grad_mixed, raw, normed_one, proj_a, proj_b, cosine, sine, starts,
            query_scale[None], key_scale[None], mixed_own, grad_after_low, length,
        )
        attn_rows = scatter_z(attn_sum)
        grad_norm_one, attn_gain_grad = norm_back(
            inputs, inverse_rms(inputs), attn_scale, grad_normed_one
        )
        tokens_grad = (grad_after + grad_norm_one).astype(bf16)

        gain_grads = jnp.concatenate(
            [
                attn_gain_grad.reshape(m, 2 * TP, -1),
                mlp_gain_grad.reshape(m, 2 * TP, -1),
                query_gain_grad.reshape(m, 2 * TP, -1),
                key_gain_grad.reshape(m, 2 * TP, -1),
                jnp.zeros((m, 2 * TP, padded - count), f32),
            ],
            axis=2,
        ).transpose(1, 0, 2)
        output, gate_shard, up_shard, gain_sums = down_forward(
            hidden, down_a, down_b, after_attn, mlp_rows, gain_grads, ffr
        )
        bit = m // 2
        while bit:
            upper = (me // (2 * TP * bit)) % 2 == 1
            low, high = gain_sums[:bit], gain_sums[bit:]
            gain_sums = jnp.where(upper, high, low) + swap(
                jnp.where(upper, low, high), 2 * TP * bit
            )
            bit //= 2
        gain_grads = gain_sums[0]
        attn_rows, output = lax.optimization_barrier((attn_rows, output))
        query_shard, key_shard, value_shard, out_shard = return_attention(
            attn_rows, [w.shape[1] for w in (w_query, w_key, w_value, w_out)]
        )

        return (
            output,
            tokens_grad,
            query_shard,
            key_shard,
            value_shard,
            out_shard,
            gate_shard,
            up_shard,
            down_shard,
            gain_grads[:rows],
            gain_grads[rows : 2 * rows],
            gain_grads[2 * rows : 2 * rows + hr],
            gain_grads[2 * rows + hr : count],
        )

    return body


def solution(mesh):
    row = P("dp", None)
    flat = P("dp")
    return jax.shard_map(
        make_body(mesh.shape["dp"]),
        mesh=mesh,
        in_specs=(row,) * 9 + (flat,) * 4 + (row,),
        out_specs=(row,) * 9 + (flat,) * 4,
        check_vma=False,
    )
```

```python
import functools

import jax
import jax.numpy as jnp
from jax import lax
from jax.experimental import pallas as pl
from jax.experimental.pallas import tpu as pltpu
from jax.sharding import PartitionSpec as P

H = 16
KVH = 8
HD = 128
TP = 4

EPS = 1e-06
THETA = 1000000.0

f32 = jnp.float32
bf16 = jnp.bfloat16
MESH = pl.DeviceIdType.MESH


def inverse_rms(values):
    return lax.rsqrt(jnp.mean(values * values, axis=-1, keepdims=True) + EPS)


def norm_back(values, inverse, gain, grad_normed):
    grad_scaled = grad_normed * gain
    inner = jnp.mean(grad_scaled * values, axis=-1, keepdims=True)
    grad_values = inverse * (grad_scaled - values * inverse * inverse * inner)
    gain_grad = jnp.sum((grad_normed * values * inverse).reshape(-1, values.shape[-1]), axis=0)
    return (grad_values, gain_grad)


def dot(a, b):
    return lax.dot_general(a, b, (((1,), (0,)), ((), ())), preferred_element_type=f32)


def dot_tn(a, b):
    return lax.dot_general(a, b, (((0,), (0,)), ((), ())), preferred_element_type=f32)


def dot_nt(a, b):
    return lax.dot_general(a, b, (((1,), (1,)), ((), ())), preferred_element_type=f32)


def turn(v):
    return pltpu.roll(v, HD // 2, 1)


def heads_of(raw, cosine, sine, query_gain, key_gain):
    out = []
    for k, gain in ((0, query_gain), (1, query_gain), (2, key_gain)):
        v = raw[:, k * HD : (k + 1) * HD]
        inverse = inverse_rms(v)
        normed = v * inverse * gain
        out.append((v, inverse, (normed * cosine + turn(normed) * sine).astype(bf16)))
    return out, raw[:, 3 * HD :].astype(bf16)


def block_probs(qs, keys, starts, row0, score_scale):
    size, span = starts.shape[0], keys.shape[0]
    scores = dot_nt(qs, keys) * score_scale
    column = lax.broadcasted_iota(jnp.int32, (size, span), 1)
    row = lax.broadcasted_iota(jnp.int32, (size, span), 0) + row0
    allowed = (column >= starts) & (column <= row)
    allowed = jnp.concatenate([allowed, allowed], axis=0)
    scores = jnp.where(allowed, scores, -1e30)
    power_term = jnp.exp(scores - jnp.max(scores, axis=-1, keepdims=True))
    return power_term / jnp.sum(power_term, axis=-1, keepdims=True)


def partners(me):
    x = me + 2 - 4 * ((me // 2) % 2)
    y = me + 4 - 8 * ((me // 4) % 2)
    d = x + 4 - 8 * ((me // 4) % 2)
    return x, y, d, me + 1 - 2 * (me % 2)


def greet(devices):
    barrier = pltpu.get_barrier_semaphore()
    for device in devices:
        pl.semaphore_signal(barrier, inc=1, device_id=(device,), device_id_type=MESH)
    pl.semaphore_wait(barrier, len(devices))


def remote(src, dst, send, recv, device):
    return pltpu.make_async_remote_copy(
        src_ref=src, dst_ref=dst, send_sem=send, recv_sem=recv, device_id=(device,), device_id_type=MESH
    )


TILE = 512


class Scatter:
    def __init__(self, out, ebuf, rd, rxy, send, recv, x, y):
        self.out, self.ebuf, self.rd, self.rxy = out, ebuf, rd, rxy
        length, width = out.shape
        h = length // 2
        self.half = h
        self.span = width // 2

        def pair(i, src, dst, rows, device):
            copies = []
            for c in range(2):
                cols = pl.ds(c * self.span, self.span)
                copies.append(
                    remote(
                        src[0].at[src[1], pl.ds(src[2], rows), cols],
                        dst[0].at[dst[1], pl.ds(dst[2], rows), cols],
                        send.at[i, c],
                        recv.at[i, c],
                        device,
                    )
                )
            return copies

        self.low = pair(0, (ebuf, 0, 0), (rd, 0, 0), h, y)
        self.high = pair(1, (ebuf, 0, h), (rd, 1, 0), h, x)
        self.to_x = pair(2, (ebuf, 1, 0), (rxy, 0, 0), length, x)
        self.to_y = pair(3, (ebuf, 2, 0), (rxy, 1, 0), length, y)

    def add(self, k, tile_of):
        h = self.half
        tiles = self.span // TILE
        for c in range(2):
            if k == 1:
                self.low[c].wait_recv()
            if k == 2:
                self.high[c].wait_recv()

            @pl.loop(c * tiles, (c + 1) * tiles)
            def _(t):
                sl = pl.ds(pl.multiple_of(t * TILE, TILE), TILE)
                value = tile_of(sl)
                if k == 0:
                    self.out[:, sl] = value
                elif k == 3:
                    self.ebuf[0, :, sl] = value.astype(bf16)
                elif k == 1:
                    self.ebuf[1, :h, sl] = (value[:h] + self.rd[0, :, sl].astype(f32)).astype(bf16)
                    self.ebuf[1, h:, sl] = value[h:].astype(bf16)
                else:
                    self.ebuf[2, :h, sl] = value[:h].astype(bf16)
                    self.ebuf[2, h:, sl] = (value[h:] + self.rd[1, :, sl].astype(f32)).astype(bf16)

            if k == 3:
                self.low[c].start()
                self.high[c].start()
            if k == 1:
                self.to_x[c].start()
            if k == 2:
                self.to_y[c].start()

    def finish(self):
        tiles = self.span // TILE
        for c in range(2):
            self.to_x[c].wait_recv()
            self.to_y[c].wait_recv()

            @pl.loop(c * tiles, (c + 1) * tiles)
            def _(t):
                sl = pl.ds(pl.multiple_of(t * TILE, TILE), TILE)
                self.out[:, sl] += self.rxy[0, :, sl].astype(f32) + self.rxy[1, :, sl].astype(f32)

        for copy in self.low + self.high + self.to_x + self.to_y:
            copy.wait_send()


def scatter_scratch(length, width):
    return [
        pltpu.VMEM((3, length, width), bf16),
        pltpu.VMEM((2, length // 2, width), bf16),
        pltpu.VMEM((2, length, width), bf16),
        pltpu.SemaphoreType.DMA((4, 2)),
        pltpu.SemaphoreType.DMA((4, 2)),
    ]


def attend_back_kernel(
    gm_ref, raw_ref, a1_ref, pa_ref, pb_ref, cos_ref, sin_ref, start_ref, qg_ref, kg_ref, mix_ref, dy_ref,
    out_ref, sum_ref, dqg_ref, dkg_ref, ogot_ref, orecv_ref,
    gp_ref, dk_ref, dv_ref, acc_a, acc_b, heads, cbuf, crecv, oslot, ofetch,
    ebuf, rd, rxy, rs_send, rs_recv, do_send, do_recv, do_own, c_send, c_recv,
    oc_send, oc_recv, os_send, os_recv, o_local,
):
    length = a1_ref.shape[0]
    step = 128
    score_scale = HD ** (-0.5)
    s = pl.program_id(0)
    me = lax.axis_index("dp")
    core = me % 2
    place = (me // 2) % TP
    x, y, d, sibling = partners(me)
    cols = 4 * HD

    def columns_of(device):
        return pl.ds(pl.multiple_of(((device // 2) % TP) * cols, cols), cols)

    incoming = [
        remote(gm_ref.at[:, columns_of(device)], heads.at[k], do_send.at[k - 1], do_recv.at[k - 1], device)
        for k, device in ((1, x), (2, y), (3, d))
    ]
    own = pltpu.make_async_copy(
        gm_ref.at[:, pl.ds(pl.multiple_of(place * cols, cols), cols)], heads.at[0], do_own
    )
    scatter = Scatter(out_ref, ebuf, rd, rxy, rs_send, rs_recv, x, y)
    across = remote(cbuf, crecv, c_send, c_recv, sibling)
    block = oslot.shape[2]
    o_across = [
        remote(oslot.at[k], orecv_ref.at[k], oc_send.at[k], oc_recv.at[k], sibling) for k in range(TP)
    ]
    tall = oslot.shape[1] // 2
    o_low = remote(
        oslot.at[3, pl.ds(0, tall)], ogot_ref.at[2, pl.ds(0, tall)], os_send.at[2], os_recv.at[2], y
    )
    o_high = remote(
        oslot.at[3, pl.ds(tall, tall)], ogot_ref.at[2, pl.ds(tall, tall)], os_send.at[3], os_recv.at[3], x
    )
    o_home = [
        remote(oslot.at[k], ogot_ref.at[k - 1], os_send.at[k - 1], os_recv.at[k - 1], device)
        for k, device in ((1, x), (2, y))
    ]
    o_back = [
        pltpu.make_async_copy(ogot_ref.at[k - 1], oslot.at[k], o_local.at[k]) for k in range(1, 3)
    ]

    def out_block(k, side):
        device = (me, x, y, d)[k]
        at = ((device // 2) % TP) * 2 + side
        return pl.ds(pl.multiple_of(at * block, block), block)

    def out_tile(k, side, sl):
        return dot_tn(mix_ref[:, sl], dy_ref[:, out_block(k, side)])

    @pl.when(s == 0)
    def _():
        greet((x, y, d, sibling))
        for k in (2, 0, 1):
            incoming[k].start()
        own.start()
        for ref in (acc_a, acc_b, dqg_ref, dkg_ref):
            ref[...] = jnp.zeros_like(ref)
        for k in (3, 1, 2, 0):

            @pl.loop(0, oslot.shape[1] // TILE)
            def _(t):
                sl = pl.ds(pl.multiple_of(t * TILE, TILE), TILE)
                oslot[k, sl, :] = out_tile(k, 1 - core, sl).astype(bf16)

            o_across[k].start()
        incoming[2].wait_recv()

    @pl.when(s == 1)
    def _():
        for k in (3, 1, 2, 0):
            o_across[k].wait_send()
            o_across[k].wait_recv()
            fetch = pltpu.make_async_copy(orecv_ref.at[k], ofetch, o_local.at[0])
            fetch.start()
            fetch.wait()

            @pl.loop(0, oslot.shape[1] // TILE)
            def _(t):
                sl = pl.ds(pl.multiple_of(t * TILE, TILE), TILE)
                oslot[k, sl, :] = (out_tile(k, core, sl) + ofetch[sl, :].astype(f32)).astype(bf16)

            if k == 3:
                o_low.start()
                o_high.start()
        incoming[0].wait_recv()

    @pl.when(s == 2)
    def _():
        for copy, k, offset in ((o_low, 1, 0), (o_high, 2, tall)):
            copy.wait_recv()
            fetch = pltpu.make_async_copy(
                ogot_ref.at[2, pl.ds(offset, tall)], ofetch.at[pl.ds(0, tall)], o_local.at[0]
            )
            fetch.start()
            fetch.wait()

            @pl.loop(0, tall // TILE)
            def _(t):
                sl = pl.ds(pl.multiple_of(t * TILE, TILE), TILE)
                to = pl.ds(pl.multiple_of(offset + t * TILE, TILE), TILE)
                oslot[k, to, :] = (oslot[k, to, :].astype(f32) + ofetch[sl, :].astype(f32)).astype(bf16)

            o_home[k - 1].start()
        incoming[1].wait_recv()

    @pl.when(s == 3)
    def _():
        own.wait()

    which = part_order(s)

    for h in range(2):
        col = h * 4 * HD
        side = core if h == 0 else 1 - core
        cosine, sine = cos_ref[...], sin_ref[...]
        (q0, q1, k0), value = heads_of(
            raw_ref[:, col : col + 4 * HD], cosine, sine, qg_ref[...], kg_ref[...]
        )
        dk_ref[...] = jnp.zeros_like(dk_ref)
        dv_ref[...] = jnp.zeros_like(dv_ref)
        parts = []
        for b in range(length // step):
            sl = slice(b * step, (b + 1) * step)
            span = (b + 1) * step
            qs = jnp.concatenate([q0[2][sl], q1[2][sl]], axis=0)
            gs = jnp.concatenate(
                [
                    heads[which, sl, pl.ds(pl.multiple_of((2 * side + g) * HD, HD), HD)]
                    for g in range(2)
                ],
                axis=0,
            )
            keys, values = k0[2][:span], value[:span]
            probs = block_probs(qs, keys, start_ref[sl, :], b * step, score_scale)
            dv_ref[:span, :] += dot_tn(probs.astype(bf16), gs)
            grad_probs = dot_nt(gs, values)
            delta = jnp.sum(probs * grad_probs, axis=-1, keepdims=True)
            grad_scores = (probs * (grad_probs - delta)).astype(bf16)
            dk_ref[:span, :] += dot_tn(grad_scores, qs)
            parts.append(dot(grad_scores, keys))
        dq0 = jnp.concatenate([p[:step] for p in parts], axis=0) * score_scale
        dq1 = jnp.concatenate([p[step:] for p in parts], axis=0) * score_scale
        for k, (raw, inverse, _), grad, gain_ref, dgain_ref in (
            (0, q0, dq0, qg_ref, dqg_ref),
            (1, q1, dq1, qg_ref, dqg_ref),
            (2, k0, dk_ref[...] * score_scale, kg_ref, dkg_ref),
        ):
            back = grad * cosine + turn(grad * sine)
            scaled = back * gain_ref[...]
            inner = jnp.mean(scaled * raw, axis=-1, keepdims=True)
            gp_ref[:, col + k * HD : col + (k + 1) * HD] = (
                inverse * (scaled - raw * inverse * inverse * inner)
            ).astype(bf16)
            dgain_ref[...] += jnp.sum(back * raw * inverse, axis=0, keepdims=True)
        gp_ref[:, col + 3 * HD : col + 4 * HD] = dv_ref[...].astype(bf16)

    half = 4 * HD

    def tile_of(sl):
        return dot_nt(gp_ref[:, :half], pa_ref[sl, :]) + dot_nt(gp_ref[:, half:], pb_ref[sl, :])

    for at, k in enumerate(ORDER):

        @pl.when(s == at)
        def _():
            scatter.add(k, tile_of)

    @pl.loop(0, acc_a.shape[0] // TILE)
    def _(t):
        sl = pl.ds(pl.multiple_of(t * TILE, TILE), TILE)
        acc_b[sl, :] += dot_tn(a1_ref[:, sl], gp_ref[:, half:])

    @pl.when(s == 3)
    def _():
        cbuf[...] = acc_b[...].astype(bf16)
        across.start()

    @pl.loop(0, acc_a.shape[0] // TILE)
    def _(t):
        sl = pl.ds(pl.multiple_of(t * TILE, TILE), TILE)
        acc_a[sl, :] += dot_tn(a1_ref[:, sl], gp_ref[:, :half])

    @pl.when(s == 3)
    def _():
        proj = acc_a.shape[1]
        across.wait_recv()
        sum_ref[:, :proj] = (acc_a[...] + crecv[...].astype(f32)).astype(bf16)
        o_low.wait_send()
        o_high.wait_send()
        for copy, back in zip(o_home, o_back):
            copy.wait()
            back.start()
        for back in o_back:
            back.wait()

        @pl.loop(0, oslot.shape[1] // TILE)
        def _(t):
            sl = pl.ds(pl.multiple_of(t * TILE, TILE), TILE)
            total = oslot[0, sl, :].astype(f32)
            for k in range(1, 3):
                total += oslot[k, sl, :].astype(f32)
            sum_ref[sl, proj:] = total.astype(bf16)

        scatter.finish()
        across.wait_send()
        for copy in incoming:
            copy.wait_send()


CHUNK = 256


def feed_kernel(
    a2_ref, wa_ref, g_ref,
    gate_ref, up_ref, hid_ref, wb_ref, ga_ref, sum_ref,
    a2, wa, wb, g, hid, stage, cbuf, crecv, acc,
    loads, x_send, x_recv, g_send, g_recv, s_sem, c_send, c_recv, keeps,
):
    tokens, width = a2.shape
    length = g_ref.shape[0]
    fn = wa.shape[1] // 2
    x, y, d, sibling = partners(lax.axis_index("dp"))
    h = length // 2

    def rows(k, offset=0, size=length):
        return g.at[pl.ds(k * length + offset, size)]

    load_x = pltpu.make_async_copy(a2_ref, a2, loads.at[0])
    load_w = pltpu.make_async_copy(wa_ref, wa, loads.at[1])
    load_g = pltpu.make_async_copy(g_ref, rows(0), loads.at[2])
    swap_w = remote(wa_ref, wb, x_send.at[0], x_recv.at[0], sibling)
    g_x = remote(g_ref, rows(1), g_send.at[0], g_recv.at[0], x)
    g_y = remote(g_ref, rows(2), g_send.at[1], g_recv.at[1], y)
    g_low = remote(rows(2, 0, h), rows(3, 0, h), g_send.at[2], g_recv.at[2], x)
    g_high = remote(rows(1, h, h), rows(3, h, h), g_send.at[3], g_recv.at[3], y)
    keep_w = pltpu.make_async_copy(wb, wb_ref, keeps.at[0])
    keep_g = pltpu.make_async_copy(g, ga_ref, keeps.at[1])
    keep_h = pltpu.make_async_copy(hid, hid_ref, keeps.at[2])

    load_w.start()
    load_x.start()
    load_g.start()
    greet((x, y, d, sibling))
    g_x.start()
    g_y.start()
    swap_w.start()

    per_half = fn // CHUNK
    span = 2 * length
    halves = tokens // span

    def store(i, which, ref):
        half = i // (per_half * halves)
        j = i % (per_half * halves)
        r, c = j // per_half, j % per_half
        return pltpu.make_async_copy(
            stage.at[i % 2, which],
            ref.at[
                pl.ds(pl.multiple_of(r * span, span), span),
                pl.ds(pl.multiple_of((half * per_half + c) * CHUNK, CHUNK), CHUNK),
            ],
            s_sem.at[i % 2, which],
        )

    def run(half, w):
        @pl.loop(0, per_half * halves)
        def _(j):
            i = j + half * per_half * halves

            @pl.when(i >= 2)
            def _():
                store(i - 2, 0, gate_ref).wait()
                store(i - 2, 1, up_ref).wait()

            r, c = j // per_half, j % per_half
            sl = pl.ds(pl.multiple_of(r * span, span), span)
            gate = dot(a2[sl, :], w[:, pl.ds(pl.multiple_of(c * CHUNK, CHUNK), CHUNK)])
            up = dot(a2[sl, :], w[:, pl.ds(pl.multiple_of(fn + c * CHUNK, CHUNK), CHUNK)])
            stage[i % 2, 0] = gate.astype(bf16)
            stage[i % 2, 1] = up.astype(bf16)
            hid[sl, pl.ds(pl.multiple_of((half * per_half + c) * CHUNK, CHUNK), CHUNK)] = (
                gate * jax.nn.sigmoid(gate) * up
            ).astype(bf16)
            store(i, 0, gate_ref).start()
            store(i, 1, up_ref).start()

    load_w.wait()
    load_x.wait()
    run(0, wa)
    swap_w.wait_recv()
    keep_w.start()
    run(1, wb)
    last = 2 * per_half * halves
    for i in (last - 2, last - 1):
        store(i, 0, gate_ref).wait()
        store(i, 1, up_ref).wait()
    keep_h.start()

    g_x.wait_recv()
    g_high.start()
    g_y.wait_recv()
    g_low.start()
    load_g.wait()
    near = pl.ds(0, 3 * length)
    far = pl.ds(3 * length, length)

    @pl.loop(0, 2 * per_half)
    def _(t):
        cols = pl.ds(pl.multiple_of(t * CHUNK, CHUNK), CHUNK)
        acc[t] = dot_tn(hid[near, cols], g[near, :])

    g_low.wait_recv()
    g_high.wait_recv()
    keep_g.start()

    def across(t):
        return remote(cbuf.at[t], crecv.at[t], c_send.at[t], c_recv.at[t], sibling)

    @pl.loop(0, per_half)
    def _(t):
        cols = pl.ds(pl.multiple_of(fn + t * CHUNK, CHUNK), CHUNK)
        cbuf[t] = (acc[per_half + t] + dot_tn(hid[far, cols], g[far, :])).astype(bf16)
        across(t).start()

    @pl.loop(0, per_half)
    def _(t):
        cols = pl.ds(pl.multiple_of(t * CHUNK, CHUNK), CHUNK)
        own = acc[t] + dot_tn(hid[far, cols], g[far, :])
        across(t).wait_recv()
        sum_ref[cols, :] = (own + crecv[t].astype(f32)).astype(bf16)

    for t in range(per_half):
        across(t).wait_send()
    for copy in (swap_w, g_x, g_y, g_low, g_high):
        copy.wait_send()
    for copy in (keep_w, keep_g, keep_h):
        copy.wait()


def feed_forward(a2, wa, g):
    tokens, width = a2.shape
    fn = wa.shape[1] // 2
    length = g.shape[0]
    anywhere = pl.BlockSpec(memory_space=pl.ANY)
    sem = pltpu.SemaphoreType.DMA
    return pl.pallas_call(
        feed_kernel,
        in_specs=[anywhere] * 3,
        out_specs=[anywhere] * 5 + [pl.BlockSpec(memory_space=pltpu.VMEM)],
        out_shape=[
            struct((tokens, 2 * fn), bf16),
            struct((tokens, 2 * fn), bf16),
            struct((tokens, 2 * fn), bf16),
            struct(wa.shape, bf16),
            struct((tokens, width), bf16),
            struct((fn, width), bf16),
        ],
        scratch_shapes=[
            pltpu.VMEM(a2.shape, bf16),
            pltpu.VMEM(wa.shape, bf16),
            pltpu.VMEM(wa.shape, bf16),
            pltpu.VMEM(a2.shape, bf16),
            pltpu.VMEM((tokens, 2 * fn), bf16),
            pltpu.VMEM((2, 2, 2 * length, CHUNK), bf16),
            pltpu.VMEM((fn // CHUNK, CHUNK, width), bf16),
            pltpu.VMEM((fn // CHUNK, CHUNK, width), bf16),
            pltpu.VMEM((2 * fn // CHUNK, CHUNK, width), f32),
            sem((3,)), sem((2,)), sem((2,)), sem((4,)), sem((4,)), sem((2, 2)),
            sem((fn // CHUNK,)), sem((fn // CHUNK,)), sem((3,)),
        ],
        compiler_params=pltpu.CompilerParams(
            vmem_limit_bytes=58 << 20, collective_id=4, has_side_effects=True
        ),
        cost_estimate=pl.CostEstimate(
            flops=4 * tokens * width * fn, bytes_accessed=30 << 20, transcendentals=0
        ),
        name="feed_forward",
    )(a2, wa, g)


def feed_back_kernel(
    gate_ref, up_ref, ga_ref, da_ref, wa_ref, wb_ref, a2_ref,
    out_ref, sum_ref, db_ref, crecv_ref,
    gp, wa, wb, a2, wd, uv, cbuf, cgot, stage, loads, u_sem, c_send, c_recv, g_sem, s_sem,
    d_send, d_recv,
    ebuf, rd, rxy, rs_send, rs_recv,
):
    length = out_ref.shape[0]
    cols = wa.shape[1]
    fn = cols // 2
    rows = cbuf.shape[1]
    tiles = a2.shape[1] // rows
    x, y, d, sibling = partners(lax.axis_index("dp"))
    scatter = Scatter(out_ref, ebuf, rd, rxy, rs_send, rs_recv, x, y)

    def piece(k):
        sl = pl.ds(k * length, length)
        return pltpu.make_async_copy(ga_ref.at[sl], a2.at[sl], loads.at[k])

    load_a = pltpu.make_async_copy(wa_ref, wa, loads.at[4])
    load_b = pltpu.make_async_copy(wb_ref, wb, loads.at[5])
    load_da = pltpu.make_async_copy(da_ref, wd.at[pl.ds(0, fn)], loads.at[6])
    swap_d = remote(da_ref, wd.at[pl.ds(fn, fn)], d_send, d_recv, sibling)
    keep_d = pltpu.make_async_copy(wd.at[pl.ds(fn, fn)], db_ref, loads.at[7])
    load_x = pltpu.make_async_copy(a2_ref, a2, loads.at[8])
    steps = 2 * TP

    def step_of(i):
        return part_order(i // 2), i % 2

    def fetch_uv(i, which, ref):
        part, c = step_of(i)
        return pltpu.make_async_copy(
            ref.at[
                pl.ds(pl.multiple_of(part * length, length), length),
                pl.ds(pl.multiple_of(c * fn, CHUNK), fn),
            ],
            uv.at[i % 2, which],
            u_sem.at[i % 2, which],
        )

    fetch_uv(0, 0, gate_ref).start()
    fetch_uv(0, 1, up_ref).start()
    piece(3).start()
    load_da.start()
    greet((x, y, d, sibling))
    swap_d.start()
    load_a.start()
    load_b.start()
    for k in (1, 2, 0):
        piece(k).start()

    def rows_of(t):
        return pl.ds(pl.multiple_of(t * rows, rows), rows)

    def across(t):
        return remote(
            cbuf.at[t % 2], crecv_ref.at[rows_of(t)], c_send.at[t % 2], c_recv.at[t], sibling
        )

    def fetch(t):
        return pltpu.make_async_copy(crecv_ref.at[rows_of(t)], cgot.at[t % 2], g_sem.at[t % 2])

    def store(t):
        return pltpu.make_async_copy(stage.at[t % 2], sum_ref.at[rows_of(t)], s_sem.at[t % 2])

    def part_of(k):
        sl = slice(k * length, (k + 1) * length)

        def tile_of(cut):
            return dot_nt(gp[sl, :cols], wa[cut, :]) + dot_nt(gp[sl, cols:], wb[cut, :])

        return tile_of

    def inner(first, end):
        @pl.loop(first, end)
        def _(i):
            @pl.when(i + 1 < steps)
            def _():
                fetch_uv(i + 1, 0, gate_ref).start()
                fetch_uv(i + 1, 1, up_ref).start()

            part, half = step_of(i)
            sl = pl.ds(pl.multiple_of(part * length, length), length)
            fetch_uv(i, 0, gate_ref).wait()
            fetch_uv(i, 1, up_ref).wait()
            for at in range(0, fn, CHUNK):
                cut = slice(at, at + CHUNK)
                rows_at = pl.ds(pl.multiple_of(half * fn + at, CHUNK), CHUNK)
                grad_hidden = dot_nt(a2[sl, :], wd[rows_at, :])
                gate = uv[i % 2, 0, :, cut].astype(f32)
                up = uv[i % 2, 1, :, cut].astype(f32)
                sig = jax.nn.sigmoid(gate)
                scaled = grad_hidden * sig
                to = half * cols + at
                gp[sl, pl.ds(pl.multiple_of(to, CHUNK), CHUNK)] = (
                    scaled * up * (1.0 + gate * (1.0 - sig))
                ).astype(bf16)
                gp[sl, pl.ds(pl.multiple_of(to + fn, CHUNK), CHUNK)] = (scaled * gate).astype(bf16)

    piece(3).wait()
    load_da.wait()
    inner(0, 1)
    swap_d.wait_recv()
    keep_d.start()
    inner(1, 2)
    load_a.wait()
    load_b.wait()
    scatter.add(3, part_of(3))
    for k in (1, 2, 0):
        piece(k).wait()
    inner(2, steps)
    load_x.start()
    scatter.add(1, part_of(1))
    scatter.add(2, part_of(2))
    load_x.wait()

    @pl.loop(0, tiles)
    def _(t):
        @pl.when(t >= 2)
        def _():
            across(t - 2).wait_send()

        cbuf[t % 2] = dot_tn(a2[:, rows_of(t)], gp[:, cols:]).astype(bf16)
        across(t).start()

    scatter.add(0, part_of(0))

    @pl.loop(0, tiles)
    def _(t):
        across(t).wait_recv()
        fetch(t).start()

        @pl.when(t >= 2)
        def _():
            store(t - 2).wait()

        own = dot_tn(a2[:, rows_of(t)], gp[:, :cols])
        fetch(t).wait()
        stage[t % 2] = (own + cgot[t % 2].astype(f32)).astype(bf16)
        store(t).start()

    for t in (tiles - 2, tiles - 1):
        store(t).wait()
        across(t).wait_send()
    swap_d.wait_send()
    keep_d.wait()
    scatter.finish()


def feed_backward(gate, up, ga, da, wa, wb, a2, length):
    tokens, width = a2.shape
    cols = wa.shape[1]
    rows = 256
    anywhere = pl.BlockSpec(memory_space=pl.ANY)
    sem = pltpu.SemaphoreType.DMA
    return pl.pallas_call(
        feed_back_kernel,
        in_specs=[anywhere] * 7,
        out_specs=[pl.BlockSpec(memory_space=pltpu.VMEM), anywhere, anywhere, anywhere],
        out_shape=[
            struct((length, width), f32),
            struct(wa.shape, bf16),
            struct(da.shape, bf16),
            struct(wa.shape, bf16),
        ],
        scratch_shapes=[
            pltpu.VMEM((tokens, 2 * cols), bf16),
            pltpu.VMEM(wa.shape, bf16),
            pltpu.VMEM(wb.shape, bf16),
            pltpu.VMEM(a2.shape, bf16),
            pltpu.VMEM((cols, width), bf16),
            pltpu.VMEM((2, 2, length, cols // 2), bf16),
            pltpu.VMEM((2, rows, cols), bf16),
            pltpu.VMEM((2, rows, cols), bf16),
            pltpu.VMEM((2, rows, cols), bf16),
            sem((9,)), sem((2, 2)), sem((2,)), sem((width // rows,)), sem((2,)), sem((2,)),
            sem, sem,
        ]
        + scatter_scratch(length, width),
        compiler_params=pltpu.CompilerParams(
            vmem_limit_bytes=62 << 20, collective_id=1, has_side_effects=True
        ),
        cost_estimate=pl.CostEstimate(
            flops=4 * tokens * width * cols, bytes_accessed=30 << 20, transcendentals=0
        ),
        name="feed_backward",
    )(gate, up, ga, da, wa, wb, a2)[:3]


ORDER = (3, 1, 2, 0)


def part_order(s):
    return 3 - 2 * s + 3 * (s // 2)


def rows_spec(length, cols):
    return pl.BlockSpec((length, cols), lambda s: (s, 0))


def whole_spec(shape):
    return pl.BlockSpec(shape, lambda s: (0, 0))


def struct(shape, dtype):
    return jax.ShapeDtypeStruct(shape, dtype)


def everyone(me):
    size = 2 * TP
    base = me - me % size
    return [base + (me % size + i) % size for i in range(1, size)]


def spread_kernel(
    wq_ref, wk_ref, wv_ref, wo_ref, gain_ref, seg_ref,
    all_ref, gains_ref, segs_ref,
    send, recv, local, s_send, s_recv,
):
    me = lax.axis_index("dp")
    size = 2 * TP
    rows = wq_ref.shape[0]
    here = pl.ds(pl.multiple_of((me % size) * rows, rows), rows)
    plan = []
    at = 0
    for ref in (wq_ref, wk_ref, wv_ref, wo_ref):
        width = ref.shape[1] // size
        plan.append((ref, width, all_ref.at[here, pl.ds(at, width)]))
        at += width

    def columns(ref, width, device):
        return ref.at[:, pl.ds(pl.multiple_of((device % size) * width, width), width)]

    others = everyone(me)
    gains_here = gains_ref.at[me % size]
    own = [
        pltpu.make_async_copy(columns(ref, width, me), dst, local.at[t])
        for t, (ref, width, dst) in enumerate(plan)
    ] + [
        pltpu.make_async_copy(gain_ref, gains_here, local.at[4]),
        pltpu.make_async_copy(seg_ref, segs_ref.at[0], local.at[5]),
    ]
    copies = [
        remote(columns(ref, width, device), dst, send.at[i, t], recv.at[i, t], device)
        for i, device in enumerate(others)
        for t, (ref, width, dst) in enumerate(plan)
    ]
    copies += [
        remote(gain_ref, gains_here, send.at[i, 4], recv.at[i, 4], device)
        for i, device in enumerate(others)
    ]
    copies += [
        remote(seg_ref, segs_ref.at[1 + k], s_send.at[k], s_recv.at[k], device)
        for k, device in enumerate(partners(me)[:3])
    ]
    for copy in own:
        copy.start()
    greet(others)
    for copy in copies:
        copy.start()
    for copy in own + copies:
        copy.wait()


def spread_attention(wq, wk, wv, wo, gain, seg):
    size = 2 * TP
    rows = wq.shape[0]
    cols = (wq.shape[1] + wk.shape[1] + wv.shape[1] + wo.shape[1]) // size
    anywhere = pl.BlockSpec(memory_space=pl.ANY)
    sem = pltpu.SemaphoreType.DMA
    return pl.pallas_call(
        spread_kernel,
        in_specs=[anywhere] * 6,
        out_specs=[anywhere] * 3,
        out_shape=[
            struct((size * rows, cols), bf16),
            struct((size, *gain.shape), f32),
            struct((TP, *seg.shape), jnp.int32),
        ],
        scratch_shapes=[sem((size - 1, 5)), sem((size - 1, 5)), sem((6,)), sem((3,)), sem((3,))],
        compiler_params=pltpu.CompilerParams(collective_id=5, has_side_effects=True),
        name="spread_attention",
    )(wq, wk, wv, wo, gain, seg)


def gather_kernel(
    run, seg_ref, rate_ref, x_ref, gate_ref, up_ref,
    cos_ref, sin_ref, start_ref, x_all, w_all,
    w_ref, flat, wide, x_send, x_recv, w_send, w_recv, local,
):
    me = lax.axis_index("dp")
    size = 2 * TP
    x, y, d, _ = partners(me)
    others = everyone(me)
    length = x_ref.shape[0]
    rows = w_ref.shape[1]
    h = length // 2
    here = pl.ds(pl.multiple_of((me % size) * rows, rows), rows)

    def place(k, offset=0, count=length):
        return x_all.at[pl.ds(k * length + offset, count)]

    own = [
        pltpu.make_async_copy(x_ref, place(0), local.at[0]),
        pltpu.make_async_copy(w_ref.at[me % size], w_all.at[here], local.at[1]),
    ]
    fills = [
        pltpu.make_async_copy(ref, flat.at[i], local.at[2 + i]) for i, ref in enumerate((gate_ref, up_ref))
    ]
    weights = [
        remote(w_ref.at[device % size], w_all.at[here], w_send.at[i], w_recv.at[i], device)
        for i, device in enumerate(others)
    ]
    to_x = remote(x_ref, place(1), x_send.at[0], x_recv.at[0], x)
    to_y = remote(x_ref, place(2), x_send.at[1], x_recv.at[1], y)
    low = remote(place(2, 0, h), place(3, 0, h), x_send.at[2], x_recv.at[2], x)
    high = remote(place(1, h, h), place(3, h, h), x_send.at[3], x_recv.at[3], y)
    for copy in fills + own[:1]:
        copy.start()
    greet(others)
    for copy in (to_x, to_y):
        copy.start()
    for copy in fills:
        copy.wait()
    half = wide.shape[1] // 2
    values = [flat[i].astype(f32) for i in range(2)]
    for s in range(size):
        for i in range(2):
            for g in range(half // run):
                at = (g * size + s) * run
                wide[:, i * half + g * run : i * half + (g + 1) * run] = values[i][:, at : at + run]
        w_ref[s] = wide[...].astype(bf16)
    for copy in own[1:] + weights:
        copy.start()

    row = lax.broadcasted_iota(jnp.int32, (length, length), 0)
    column = lax.broadcasted_iota(jnp.int32, (length, length), 1)
    for k in range(TP):
        label = jnp.broadcast_to(seg_ref[k].astype(f32), (length, length))
        mine = jnp.sum(jnp.where(row == column, label, 0.0), axis=1, keepdims=True)
        start = jnp.sum(jnp.where(label < mine, 1.0, 0.0), axis=1, keepdims=True)
        position = lax.broadcasted_iota(jnp.int32, (length, 1), 0).astype(f32) - start
        angle = position * rate_ref[0:1, :]
        sl = pl.ds(k * length, length)
        cos_ref[sl, :] = jnp.cos(angle)
        sin_ref[sl, :] = jnp.sin(angle) * rate_ref[1:2, :]
        start_ref[sl, :] = start.astype(jnp.int32)

    to_x.wait_recv()
    high.start()
    to_y.wait_recv()
    low.start()
    for copy in (to_x, to_y):
        copy.wait_send()
    for copy in own + weights + [low, high]:
        copy.wait()


def gather_group(seg, rates, x, gate, up, run):
    size = 2 * TP
    rows, cols = gate.shape[0], 2 * gate.shape[1] // size
    anywhere = pl.BlockSpec(memory_space=pl.ANY)
    vmem = pl.BlockSpec(memory_space=pltpu.VMEM)
    sem = pltpu.SemaphoreType.DMA
    return pl.pallas_call(
        functools.partial(gather_kernel, run),
        in_specs=[vmem] * 2 + [anywhere] * 3,
        out_specs=[vmem] * 3 + [anywhere] * 2,
        out_shape=[
            struct((TP * x.shape[0], HD), f32),
            struct((TP * x.shape[0], HD), f32),
            struct((TP * x.shape[0], 1), jnp.int32),
            struct((TP * x.shape[0], x.shape[1]), bf16),
            struct((size * rows, cols), bf16),
        ],
        scratch_shapes=[
            pltpu.VMEM((size, rows, cols), bf16),
            pltpu.VMEM((2, *gate.shape), bf16),
            pltpu.VMEM((rows, cols), f32),
            sem((4,)), sem((4,)), sem((size - 1,)), sem((size - 1,)), sem((4,)),
        ],
        compiler_params=pltpu.CompilerParams(
            vmem_limit_bytes=32 << 20, collective_id=6, has_side_effects=True
        ),
        name="gather_group",
    )(seg, rates, x, gate, up)


def attend_kernel(
    x_ref, cos_ref, sin_ref, start_ref, ag_ref, mg_ref, qg_ref, kg_ref, all_ref,
    raw_ref, a1_ref, mixed_ref, after_ref, inv_ref, pa_out, pb_out, wo_ref, a2_ref,
    pa_ref, pb_ref, fill, heads, mix, wo, a2, p_send, p_recv, o_send, o_recv, w_send, w_recv, s_send, s_recv, a_send, a_recv, local,
):
    length, width = x_ref.shape
    step = 128
    score_scale = HD ** (-0.5)
    s = pl.program_id(0)
    me = lax.axis_index("dp")
    core = me % 2
    place = (me // 2) % TP
    x, y, d, sibling = partners(me)
    near = (x, y, d)
    cols = 4 * HD
    proj = pa_ref.shape[1]
    block = all_ref.shape[2] - proj
    planes = all_ref.shape[0]
    deep = pa_ref.shape[0] // planes

    def block_of(device):
        return pl.ds(pl.multiple_of((device % (2 * TP)) * block, block), block)

    own_out = wo.at[:, block_of(me)]
    fills = []
    for g in range(planes):
        at = pl.ds(g * deep, deep)
        fills.append(
            pltpu.make_async_copy(
                all_ref.at[g, pl.ds(0, deep), pl.ds(0, proj)], pa_ref.at[at], fill.at[g, 0]
            )
        )
        fills.append(
            pltpu.make_async_copy(
                all_ref.at[g, pl.ds(0, deep), pl.ds(proj, block)], wo.at[at, block_of(me)], fill.at[g, 1]
            )
        )

    tall = wo.shape[0] // 2
    spread_out = [
        remote(own_out, own_out, w_send.at[i], w_recv.at[i], device)
        for i, device in enumerate(near[:2])
    ]

    def passed(device, offset, i, to):
        ref = wo.at[pl.ds(offset, tall), block_of(device)]
        return remote(ref, ref, w_send.at[i], w_recv.at[i], to)

    pass_on = [passed(x, tall, 2, y), passed(y, 0, 3, x)]
    beside = [remote(own_out, own_out, s_send.at[3], s_recv.at[3], sibling)]
    onward = [
        remote(wo.at[:, block_of(device)], wo.at[:, block_of(device)], s_send.at[i], s_recv.at[i], sibling)
        for i, device in enumerate(near)
    ]
    mine = pl.ds(pl.multiple_of(place * cols, cols), cols)
    home = [
        remote(heads.at[i + 1], mix.at[:, mine], o_send.at[i], o_recv.at[i], device)
        for i, device in enumerate(near)
    ]
    h = length // 2
    a2_x = remote(a2.at[0], a2.at[1], a_send.at[0], a_recv.at[0], x)
    a2_y = remote(a2.at[0], a2.at[2], a_send.at[1], a_recv.at[1], y)
    a2_low = remote(a2.at[2, pl.ds(0, h)], a2.at[3, pl.ds(0, h)], a_send.at[2], a_recv.at[2], x)
    a2_high = remote(a2.at[1, pl.ds(h, h)], a2.at[3, pl.ds(h, h)], a_send.at[3], a_recv.at[3], y)
    keep = [
        pltpu.make_async_copy(a2.at[k], a2_ref.at[pl.ds(k * length, length)], local.at[1 + k])
        for k in range(TP)
    ]
    keep_out = pltpu.make_async_copy(wo, wo_ref, local.at[5])
    keep_b = pltpu.make_async_copy(pb_ref, pb_out, local.at[6])
    keep_a = pltpu.make_async_copy(pa_ref, pa_out, local.at[0])
    swap_p = remote(pa_ref, pb_ref, p_send, p_recv, sibling)

    @pl.when(s == 0)
    def _():
        for copy in fills:
            copy.start()
        greet((x, y, d, sibling))
        for copy in fills:
            copy.wait()
        for copy in [swap_p] + spread_out + beside:
            copy.start()
        keep_a.start()

    @pl.when(s == 3)
    def _():
        for i in range(2):
            spread_out[i].wait_recv()
            pass_on[i].start()
            onward[i].start()

    @pl.loop(0, length // step)
    def _(t):
        sl = pl.ds(pl.multiple_of(t * step, step), step)
        v = x_ref[sl, :].astype(f32)
        a1_ref[sl, :] = (v * inverse_rms(v) * ag_ref[...]).astype(bf16)

    which = part_order(s)
    for half, p_ref in ((0, pa_ref), (1, pb_ref)):
        side = core if half == 0 else 1 - core
        if half:

            @pl.when(s == 0)
            def _():
                swap_p.wait_recv()
                keep_b.start()

        raw_ref[:, half * cols : (half + 1) * cols] = dot(a1_ref[...], p_ref[...])
        (q0, q1, k0), value = heads_of(
            raw_ref[:, half * cols : (half + 1) * cols], cos_ref[...], sin_ref[...], qg_ref[...], kg_ref[...]
        )
        for b in range(length // step):
            sl = slice(b * step, (b + 1) * step)
            span = (b + 1) * step
            qs = jnp.concatenate([q0[2][sl], q1[2][sl]], axis=0)
            probs = block_probs(qs, k0[2][:span], start_ref[sl, :], b * step, score_scale)
            mixed = dot(probs.astype(bf16), value[:span]).astype(bf16)
            for g in range(2):
                at = pl.ds(pl.multiple_of((2 * side + g) * HD, HD), HD)
                heads[which, sl, at] = mixed[g * step : (g + 1) * step]

    for at, k in enumerate(ORDER[:3]):

        @pl.when(s == at)
        def _():
            home[k - 1].start()

    @pl.when(s == 3)
    def _():
        mix[:, mine] = heads[0]
        for copy in pass_on:
            copy.wait_recv()
        onward[2].start()
        for copy in home:
            copy.wait_recv()
        for copy in beside + onward:
            copy.wait_recv()
        keep_out.start()

        @pl.loop(0, width // TILE)
        def _(t):
            sl = pl.ds(pl.multiple_of(t * TILE, TILE), TILE)
            after_ref[:, sl] = x_ref[:, sl].astype(f32) + dot(mix[...], wo[:, sl])

        @pl.loop(0, length // step)
        def _(t):
            sl = pl.ds(pl.multiple_of(t * step, step), step)
            v = after_ref[sl, :]
            inverse = inverse_rms(v)
            inv_ref[sl, :] = inverse
            a2[0, sl, :] = (v * inverse * mg_ref[...]).astype(bf16)

        a2_x.start()
        a2_y.start()
        keep[0].start()
        mixed_ref[...] = mix[...]
        a2_x.wait_recv()
        a2_high.start()
        keep[1].start()
        a2_y.wait_recv()
        a2_low.start()
        keep[2].start()
        a2_high.wait_recv()
        a2_low.wait_recv()
        keep[3].start()
        for copy in spread_out + pass_on + beside + onward + home + [a2_x, a2_y, a2_low, a2_high]:
            copy.wait_send()
        swap_p.wait_send()
        for copy in keep + [keep_out, keep_a, keep_b]:
            copy.wait()


def attend_forward(x, cosine, sine, starts, ag, mg, qg, kg, weights, depth, proj, length):
    tokens, width = x.shape
    planes = weights.shape[0]
    total = planes * depth
    anywhere = pl.BlockSpec(memory_space=pl.ANY)

    def in_order(cols):
        return pl.BlockSpec((length, cols), lambda s: (part_order(s), 0))

    return pl.pallas_call(
        attend_kernel,
        grid=(TP,),
        in_specs=[in_order(width)]
        + [in_order(HD), in_order(HD), in_order(1)]
        + [whole_spec(g.shape) for g in (ag, mg, qg, kg)]
        + [anywhere],
        out_specs=[in_order(8 * HD), in_order(width)]
        + [whole_spec((length, width))] * 2
        + [whole_spec((length, 1))]
        + [anywhere] * 4,
        out_shape=[
            struct((tokens, 8 * HD), f32),
            struct((tokens, width), bf16),
            struct((length, width), bf16),
            struct((length, width), f32),
            struct((length, 1), f32),
            struct((total, proj), bf16),
            struct((total, proj), bf16),
            struct((total, width), bf16),
            struct((tokens, width), bf16),
        ],
        scratch_shapes=[
            pltpu.VMEM((total, proj), bf16),
            pltpu.VMEM((total, proj), bf16),
            pltpu.SemaphoreType.DMA((planes, 2)),
            pltpu.VMEM((TP, length, 4 * HD), bf16),
            pltpu.VMEM((length, width), bf16),
            pltpu.VMEM((total, width), bf16),
            pltpu.VMEM((TP, length, width), bf16),
            pltpu.SemaphoreType.DMA,
            pltpu.SemaphoreType.DMA,
            pltpu.SemaphoreType.DMA((3,)),
            pltpu.SemaphoreType.DMA((3,)),
            pltpu.SemaphoreType.DMA((4,)),
            pltpu.SemaphoreType.DMA((4,)),
            pltpu.SemaphoreType.DMA((4,)),
            pltpu.SemaphoreType.DMA((4,)),
            pltpu.SemaphoreType.DMA((4,)),
            pltpu.SemaphoreType.DMA((4,)),
            pltpu.SemaphoreType.DMA((7,)),
        ],
        compiler_params=pltpu.CompilerParams(
            vmem_limit_bytes=56 << 20, collective_id=3, has_side_effects=True
        ),
        cost_estimate=pl.CostEstimate(
            flops=2 * tokens * width * 8 * HD, bytes_accessed=30 << 20, transcendentals=0
        ),
        name="attend_forward",
    )(x, cosine, sine, starts, ag, mg, qg, kg, weights)


def between_kernel(
    grad_ref, after_ref, inv_ref, gain_ref, cot_ref, w_ref,
    sum_ref, dy_ref, dgain_ref, heads_ref,
):
    length = after_ref.shape[0]
    step = 128

    @pl.when(pl.program_id(0) == 0)
    def _():
        dgain_ref[...] = jnp.zeros_like(dgain_ref)

        @pl.loop(0, length // step)
        def _(t):
            sl = pl.ds(pl.multiple_of(t * step, step), step)
            grad, values, inverse = grad_ref[sl, :], after_ref[sl, :], inv_ref[sl, :]
            scaled = grad * gain_ref[...]
            inner = jnp.mean(scaled * values, axis=-1, keepdims=True)
            total = cot_ref[sl, :].astype(f32) + inverse * (scaled - values * inverse * inverse * inner)
            sum_ref[sl, :] = total
            dy_ref[sl, :] = total.astype(bf16)
            dgain_ref[...] += jnp.sum(grad * values * inverse, axis=0, keepdims=True)

    heads_ref[...] = dot_nt(dy_ref[...], w_ref[...]).astype(bf16)


def between(grad, after, inverse, gain, cot, w):
    length, width = after.shape
    block = 256

    def once(v):
        return pl.BlockSpec(v.shape, lambda s: (0, 0), pipeline_mode=pl.Buffered(1))

    return pl.pallas_call(
        between_kernel,
        grid=(w.shape[0] // block,),
        in_specs=[once(v) for v in (grad, after, inverse, gain, cot)]
        + [pl.BlockSpec((block, width), lambda s: (s, 0))],
        out_specs=[whole_spec((length, width))] * 2
        + [whole_spec((1, width)), pl.BlockSpec((length, block), lambda s: (0, s))],
        out_shape=[
            struct((length, width), f32),
            struct((length, width), bf16),
            struct((1, width), f32),
            struct((length, w.shape[0]), bf16),
        ],
        compiler_params=pltpu.CompilerParams(vmem_limit_bytes=40 << 20),
        cost_estimate=pl.CostEstimate(
            flops=2 * length * width * w.shape[0], bytes_accessed=24 << 20, transcendentals=0
        ),
        name="between",
    )(grad, after, inverse, gain, cot, w)


def attend_backward(gm, raw, a1, pa, pb, cosine, sine, starts, qg, kg, mix, dy, length):
    tokens, width = a1.shape
    block = width // (2 * TP)
    anywhere = pl.BlockSpec(memory_space=pl.ANY)
    sem = pltpu.SemaphoreType.DMA

    def in_order(cols):
        return pl.BlockSpec((length, cols), lambda s: (part_order(s), 0))

    def once(v):
        return pl.BlockSpec(v.shape, lambda s: (0, 0), pipeline_mode=pl.Buffered(1))

    return pl.pallas_call(
        attend_back_kernel,
        grid=(TP,),
        in_specs=[anywhere]
        + [in_order(c) for c in (8 * HD, width)]
        + [once(w) for w in (pa, pb)]
        + [in_order(HD), in_order(HD), in_order(1)]
        + [whole_spec(v.shape) for v in (qg, kg)]
        + [once(v) for v in (mix, dy)],
        out_specs=[whole_spec((length, width)), whole_spec((width, pa.shape[1] + block))]
        + [whole_spec(v.shape) for v in (qg, kg)]
        + [anywhere] * 2,
        out_shape=[struct((length, width), f32), struct((width, pa.shape[1] + block), bf16)]
        + [struct(v.shape, f32) for v in (qg, kg)]
        + [struct((3, width, block), bf16), struct((TP, width, block), bf16)],
        scratch_shapes=[
            pltpu.VMEM((length, 8 * HD), bf16),
            pltpu.VMEM((length, HD), f32),
            pltpu.VMEM((length, HD), f32),
            pltpu.VMEM(pa.shape, f32),
            pltpu.VMEM(pa.shape, f32),
            pltpu.VMEM((TP, length, 4 * HD), bf16),
            pltpu.VMEM(pa.shape, bf16),
            pltpu.VMEM(pa.shape, bf16),
            pltpu.VMEM((TP, width, block), bf16),
            pltpu.VMEM((width, block), bf16),
        ]
        + scatter_scratch(length, width)
        + [sem((3,)), sem((3,)), sem, sem, sem, sem((TP,)), sem((TP,)), sem((4,)), sem((4,)), sem((TP,))],
        compiler_params=pltpu.CompilerParams(
            vmem_limit_bytes=60 << 20, collective_id=2, has_side_effects=True
        ),
        cost_estimate=pl.CostEstimate(
            flops=2 * tokens * width * 8 * HD, bytes_accessed=30 << 20, transcendentals=0
        ),
        name="attend_backward",
    )(gm, raw, a1, pa, pb, cosine, sine, starts, qg, kg, mix, dy)[:4]


def down_kernel(
    run, hid_ref, da_ref, db_ref, after_ref, rows_ref, gains_ref, near_ref, back_ref,
    out_ref, gate_ref, up_ref, total_ref, tokens_ref,
    hid, da, db, after, acc, pieces, gains, near, back, loads, p_send, p_recv, g_send, g_recv,
    ebuf, rd, rxy, rs_send, rs_recv,
):
    length = after.shape[0]
    fn = da.shape[0]
    size, rows, _ = pieces.shape
    me = lax.axis_index("dp")
    x, y, _, _ = partners(me)
    others = everyone(me)
    scatter = Scatter(acc, ebuf, rd, rxy, rs_send, rs_recv, x, y)

    def block(device):
        return rows_ref.at[pl.ds(pl.multiple_of((device % size) * rows, rows), rows)]

    own = pltpu.make_async_copy(block(me), pieces.at[me % size], loads.at[0])
    copies = [
        remote(block(device), pieces.at[me % size], p_send.at[i], p_recv.at[i], device)
        for i, device in enumerate(others)
    ]
    own_gains = pltpu.make_async_copy(gains_ref.at[me % size], gains.at[me % size], loads.at[5])
    gain_copies = [
        remote(gains_ref.at[device % size], gains.at[me % size], g_send.at[i], g_recv.at[i], device)
        for i, device in enumerate(others)
    ]
    fills = [
        pltpu.make_async_copy(src, dst, loads.at[1 + i])
        for i, (src, dst) in enumerate(((hid_ref, hid), (da_ref, da), (db_ref, db), (after_ref, after)))
    ]
    extra = [
        pltpu.make_async_copy(near_ref, near, loads.at[6]),
        pltpu.make_async_copy(back_ref, back, loads.at[7]),
    ]
    for copy in fills:
        copy.start()
    own.start()
    own_gains.start()
    for copy in extra:
        copy.start()
    greet(others)
    for copy in gain_copies:
        copy.start()
    for copy in fills:
        copy.wait()

    def part_of(k):
        sl = slice(k * length, (k + 1) * length)

        def tile_of(cut):
            value = dot(hid[sl, :fn], da[:, cut]) + dot(hid[sl, fn:], db[:, cut])
            return value + after[:, cut] if k == 0 else value

        return tile_of

    for k in ORDER[:3]:
        scatter.add(k, part_of(k))
    for copy in copies:
        copy.start()
    scatter.add(0, part_of(0))
    for copy in extra:
        copy.wait()

    @pl.loop(0, near.shape[1] // TILE)
    def _(t):
        sl = pl.ds(pl.multiple_of(t * TILE, TILE), TILE)
        tokens_ref[:, sl] = (near[:, sl] + back[:, sl]).astype(bf16)

    own_gains.wait()
    for copy in gain_copies:
        copy.wait()
    total = jnp.sum(gains[...], axis=0)
    for g in range(total.shape[0]):
        total_ref[g] = total[g : g + 1]
    own.wait()
    for copy in copies:
        copy.wait()
    for source in range(size):
        piece = pieces[source].astype(f32)
        for g in range(fn // run):
            to = (g * size + source) * run
            gate_ref[:, to : to + run] = piece[:, g * run : (g + 1) * run]
            up_ref[:, to : to + run] = piece[:, fn + g * run : fn + (g + 1) * run]
    scatter.finish()
    out_ref[...] = acc[...].astype(bf16)


def down_forward(hid, da, db, after, mlp_rows, gains, near, back, run):
    length, width = after.shape
    size = 2 * TP
    rows, cols = mlp_rows.shape[0] // size, mlp_rows.shape[1]
    ff = size * cols // 2
    anywhere = pl.BlockSpec(memory_space=pl.ANY)
    vmem = pl.BlockSpec(memory_space=pltpu.VMEM)
    sem = pltpu.SemaphoreType.DMA
    return pl.pallas_call(
        functools.partial(down_kernel, run),
        in_specs=[anywhere] * 8,
        out_specs=[vmem] * 5,
        out_shape=[
            struct((length, width), bf16),
            struct((rows, ff), f32),
            struct((rows, ff), f32),
            struct((gains.shape[1], 1, gains.shape[2]), f32),
            struct((length, width), bf16),
        ],
        scratch_shapes=[
            pltpu.VMEM(hid.shape, bf16),
            pltpu.VMEM(da.shape, bf16),
            pltpu.VMEM(db.shape, bf16),
            pltpu.VMEM(after.shape, f32),
            pltpu.VMEM(after.shape, f32),
            pltpu.VMEM((size, rows, cols), bf16),
            pltpu.VMEM(gains.shape, f32),
            pltpu.VMEM(after.shape, f32),
            pltpu.VMEM(after.shape, f32),
            sem((8,)), sem((size - 1,)), sem((size - 1,)), sem((size - 1,)), sem((size - 1,)),
        ]
        + scatter_scratch(length, width),
        compiler_params=pltpu.CompilerParams(
            vmem_limit_bytes=56 << 20, collective_id=7, has_side_effects=True
        ),
        cost_estimate=pl.CostEstimate(
            flops=2 * length * width * cols, bytes_accessed=30 << 20, transcendentals=0
        ),
        name="down_forward",
    )(hid, da, db, after, mlp_rows, gains, near, back)


def return_kernel(
    rows_ref, gains_ref, q_ref, k_ref, v_ref, o_ref, total_ref, pieces, gains, send, recv, local, g_send, g_recv,
):
    size, rows, _ = pieces.shape
    me = lax.axis_index("dp")
    others = everyone(me)

    def block(device):
        return rows_ref.at[pl.ds(pl.multiple_of((device % size) * rows, rows), rows)]

    planes = gains.shape[0]
    plane = me // size
    column = [(plane + i) % planes for i in range(1, planes)]
    own = [
        pltpu.make_async_copy(block(me), pieces.at[me % size], local.at[0]),
        pltpu.make_async_copy(gains_ref.at[plane], gains.at[plane], local.at[1]),
    ]
    copies = [
        remote(block(device), pieces.at[me % size], send.at[i], recv.at[i], device)
        for i, device in enumerate(others)
    ]
    copies += [
        remote(gains_ref.at[to], gains.at[plane], g_send.at[i], g_recv.at[i], to * size + me % size)
        for i, to in enumerate(column)
    ]
    for copy in own:
        copy.start()
    greet(others + [to * size + me % size for to in column])
    for copy in copies:
        copy.start()
    for copy in own + copies:
        copy.wait()
    total_ref[...] = jnp.sum(gains[...], axis=0)
    for source in range(size):
        at = 0
        for ref in (q_ref, k_ref, v_ref, o_ref):
            width = ref.shape[1] // size
            ref[:, source * width : (source + 1) * width] = pieces[source, :, at : at + width].astype(f32)
            at += width


def return_attention(attn_rows, gains, widths):
    size = 2 * TP
    rows, cols = attn_rows.shape[0] // size, attn_rows.shape[1]
    sem = pltpu.SemaphoreType.DMA
    return pl.pallas_call(
        return_kernel,
        in_specs=[pl.BlockSpec(memory_space=pl.ANY)] * 2,
        out_specs=[pl.BlockSpec(memory_space=pltpu.VMEM)] * 5,
        out_shape=[struct((rows, w), f32) for w in widths] + [struct(gains.shape[1:], f32)],
        scratch_shapes=[
            pltpu.VMEM((size, rows, cols), bf16),
            pltpu.VMEM(gains.shape, f32),
            sem((size - 1,)), sem((size - 1,)), sem((2,)),
            sem((gains.shape[0] - 1,)), sem((gains.shape[0] - 1,)),
        ],
        compiler_params=pltpu.CompilerParams(collective_id=8, has_side_effects=True),
        name="return_attention",
    )(attn_rows, gains)


def make_body(n):
    m = n // (2 * TP)
    z_groups = [[g * 2 * TP + k for g in range(m)] for k in range(2 * TP)]

    def swap(v, bits):
        return lax.ppermute(v, "dp", [(a, a ^ bits) for a in range(n)])

    def gather_xy(v):
        h = v.shape[0] // 2
        x = swap(v, 2)
        y = swap(v, 4)
        d_low = swap(y[:h], 2)
        d_high = swap(x[h:], 4)
        return [v, x, y, jnp.concatenate([d_low, d_high])]

    def scatter_xy(p0, p1, p2, p3):
        h = p3.shape[0] // 2
        d_low = swap(p3[:h], 4)
        d_high = swap(p3[h:], 2)
        sx = jnp.concatenate([(p1[:h].astype(f32) + d_low.astype(f32)).astype(bf16), p1[h:]])
        sy = jnp.concatenate([p2[:h], (p2[h:].astype(f32) + d_high.astype(f32)).astype(bf16)])
        return p0 + swap(sx, 2).astype(f32) + swap(sy, 4).astype(f32)

    def gather_z(v):
        return lax.all_gather(v, "dp", axis=0, tiled=True, axis_index_groups=z_groups)

    def scatter_z(v):
        return lax.psum_scatter(
            v, "dp", scatter_dimension=0, tiled=True, axis_index_groups=z_groups
        )

    def body(
        tokens,
        segments,
        w_query,
        w_key,
        w_value,
        w_out,
        w_gate,
        w_up,
        w_down,
        attn_gain,
        mlp_gain,
        query_gain,
        key_gain,
        cotangent,
    ):
        me = lax.axis_index("dp")
        core = me % 2
        place = (me // 2) % TP
        length, width = tokens.shape
        rows = w_query.shape[0]
        ffr = w_down.shape[0]

        qn = w_query.shape[1] // (2 * TP)
        kn = w_key.shape[1] // (2 * TP)
        pn = qn + 2 * kn
        hr = query_gain.shape[0]
        gains = jnp.concatenate([attn_gain, mlp_gain, query_gain, key_gain]).astype(f32)
        count = gains.shape[0]
        padded = -(-count // 256) * 256
        attn_in, gains, seg_all = spread_attention(
            w_query, w_key, w_value, w_out, jnp.pad(gains, (0, padded - count))[None], segments
        )

        depth, wide = attn_in.shape
        gain_rows = gains.astype(bf16).reshape(-1, padded)
        below = jnp.pad(gain_rows, ((0, -gain_rows.shape[0] % 16), (0, wide - padded)))
        attn_all = gather_z(jnp.concatenate([attn_in, below])).reshape(m, -1, wide)
        tokens_in, _ = lax.optimization_barrier((tokens, attn_in))

        rate = THETA ** (-(jnp.arange(HD // 2, dtype=f32) * 2.0 / HD))
        sign = jnp.where(jnp.arange(HD) < HD // 2, -1.0, 1.0).astype(f32)
        rates = jnp.stack([jnp.concatenate([rate, rate]), sign])
        cosine, sine, starts, tokens_all, mlp_in = gather_group(
            seg_all, rates, tokens_in, w_gate, w_up, ffr
        )
        mlp_a = gather_z(mlp_in)
        tokens_all, attn_all = lax.optimization_barrier((tokens_all, attn_all))
        gains = attn_all[:, depth : depth + gain_rows.shape[0], :padded].reshape(n, padded)
        attn_scale = gains[:, :rows].reshape(-1).astype(f32)
        mlp_scale = gains[:, rows : 2 * rows].reshape(-1).astype(f32)
        query_scale = gains[:, 2 * rows : 2 * rows + hr].reshape(-1).astype(f32)
        key_scale = gains[:, 2 * rows + hr : count].reshape(-1).astype(f32)

        (
            raw, normed_one, mixed_own, after_attn, inv_two, proj_a, proj_b, out_full, normed_two_all
        ) = attend_forward(
            tokens_all, cosine, sine, starts, attn_scale[None], mlp_scale[None],
            query_scale[None], key_scale[None], attn_all, depth, pn, length,
        )

        inputs = tokens.astype(f32)
        mlp_a, normed_two_all, down_local = lax.optimization_barrier((mlp_a, normed_two_all, w_down))
        down_a = gather_z(down_local)
        fn = down_a.shape[0]

        gate_value, up_value, hidden, mlp_b, grad_all, down_sum = feed_forward(
            normed_two_all, mlp_a, cotangent
        )
        down_rows = scatter_z(down_sum)
        grad_normed_two, mlp_sum, down_b = feed_backward(
            gate_value, up_value, grad_all, down_a, mlp_a, mlp_b, normed_two_all, length
        )
        mlp_rows = scatter_z(mlp_sum)
        grad_normed_two, down_rows = lax.optimization_barrier((grad_normed_two, down_rows))
        down_shard = down_rows.astype(f32)

        grad_after, grad_after_low, mlp_gain_grad, grad_mixed = between(
            grad_normed_two, after_attn, inv_two, mlp_scale[None], cotangent, out_full
        )

        grad_normed_one, attn_sum, query_gain_grad, key_gain_grad = attend_backward(
            grad_mixed, raw, normed_one, proj_a, proj_b, cosine, sine, starts,
            query_scale[None], key_scale[None], mixed_own, grad_after_low, length,
        )
        attn_rows = scatter_z(attn_sum)
        grad_norm_one, attn_gain_grad = norm_back(
            inputs, inverse_rms(inputs), attn_scale, grad_normed_one
        )

        gain_grads = jnp.concatenate(
            [
                attn_gain_grad.reshape(m, 2 * TP, -1),
                mlp_gain_grad.reshape(m, 2 * TP, -1),
                query_gain_grad.reshape(m, 2 * TP, -1),
                key_gain_grad.reshape(m, 2 * TP, -1),
                jnp.zeros((m, 2 * TP, padded - count), f32),
            ],
            axis=2,
        ).transpose(1, 0, 2)
        output, gate_shard, up_shard, gain_sums, tokens_grad = down_forward(
            hidden, down_a, down_b, after_attn, mlp_rows, gain_grads, grad_after, grad_norm_one, ffr
        )
        attn_rows, output = lax.optimization_barrier((attn_rows, output))
        query_shard, key_shard, value_shard, out_shard, gain_grads = return_attention(
            attn_rows, gain_sums, [w.shape[1] for w in (w_query, w_key, w_value, w_out)]
        )

        gain_grads = gain_grads[0]

        return (
            output,
            tokens_grad,
            query_shard,
            key_shard,
            value_shard,
            out_shard,
            gate_shard,
            up_shard,
            down_shard,
            gain_grads[:rows],
            gain_grads[rows : 2 * rows],
            gain_grads[2 * rows : 2 * rows + hr],
            gain_grads[2 * rows + hr : count],
        )

    return body


def solution(mesh):
    row = P("dp", None)
    flat = P("dp")
    return jax.shard_map(
        make_body(mesh.shape["dp"]),
        mesh=mesh,
        in_specs=(row,) * 9 + (flat,) * 4 + (row,),
        out_specs=(row,) * 9 + (flat,) * 4,
        check_vma=False,
    )
```

```python
import functools

import jax
import jax.numpy as jnp
from jax import lax
from jax.experimental import pallas as pl
from jax.experimental.pallas import tpu as pltpu
from jax.sharding import PartitionSpec as P

H = 16
KVH = 8
HD = 128
TP = 4

EPS = 1e-06
THETA = 1000000.0

f32 = jnp.float32
bf16 = jnp.bfloat16
MESH = pl.DeviceIdType.MESH


def inverse_rms(values):
    return lax.rsqrt(jnp.mean(values * values, axis=-1, keepdims=True) + EPS)


def dot(a, b):
    return lax.dot_general(a, b, (((1,), (0,)), ((), ())), preferred_element_type=f32)


def dot_tn(a, b):
    return lax.dot_general(a, b, (((0,), (0,)), ((), ())), preferred_element_type=f32)


def dot_nt(a, b):
    return lax.dot_general(a, b, (((1,), (1,)), ((), ())), preferred_element_type=f32)


def turn(v):
    return pltpu.roll(v, HD // 2, 1)


def heads_of(raw, cosine, sine, query_gain, key_gain):
    out = []
    for k, gain in ((0, query_gain), (1, query_gain), (2, key_gain)):
        v = raw[:, k * HD : (k + 1) * HD]
        inverse = inverse_rms(v)
        normed = v * inverse * gain
        out.append((v, inverse, (normed * cosine + turn(normed) * sine).astype(bf16)))
    return out, raw[:, 3 * HD :].astype(bf16)


def block_probs(qs, keys, starts, row0, score_scale):
    size, span = starts.shape[0], keys.shape[0]
    scores = dot_nt(qs, keys) * score_scale
    column = lax.broadcasted_iota(jnp.int32, (size, span), 1)
    row = lax.broadcasted_iota(jnp.int32, (size, span), 0) + row0
    allowed = (column >= starts) & (column <= row)
    allowed = jnp.concatenate([allowed, allowed], axis=0)
    scores = jnp.where(allowed, scores, -1e30)
    power_term = jnp.exp(scores - jnp.max(scores, axis=-1, keepdims=True))
    return power_term / jnp.sum(power_term, axis=-1, keepdims=True)


def partners(me):
    x = me + 2 - 4 * ((me // 2) % 2)
    y = me + 4 - 8 * ((me // 4) % 2)
    d = x + 4 - 8 * ((me // 4) % 2)
    return x, y, d, me + 1 - 2 * (me % 2)


def greet(devices):
    barrier = pltpu.get_barrier_semaphore()
    for device in devices:
        pl.semaphore_signal(barrier, inc=1, device_id=(device,), device_id_type=MESH)
    pl.semaphore_wait(barrier, len(devices))


def remote(src, dst, send, recv, device):
    return pltpu.make_async_remote_copy(
        src_ref=src, dst_ref=dst, send_sem=send, recv_sem=recv, device_id=(device,), device_id_type=MESH
    )


TILE = 512


class Scatter:
    def __init__(self, out, ebuf, rd, rxy, send, recv, x, y):
        self.out, self.ebuf, self.rd, self.rxy = out, ebuf, rd, rxy
        length, width = out.shape
        h = length // 2
        self.half = h
        self.span = width // 2

        def pair(i, src, dst, rows, device):
            copies = []
            for c in range(2):
                cols = pl.ds(c * self.span, self.span)
                copies.append(
                    remote(
                        src[0].at[src[1], pl.ds(src[2], rows), cols],
                        dst[0].at[dst[1], pl.ds(dst[2], rows), cols],
                        send.at[i, c],
                        recv.at[i, c],
                        device,
                    )
                )
            return copies

        self.low = pair(0, (ebuf, 0, 0), (rd, 0, 0), h, y)
        self.high = pair(1, (ebuf, 0, h), (rd, 1, 0), h, x)
        self.to_x = pair(2, (ebuf, 1, 0), (rxy, 0, 0), length, x)
        self.to_y = pair(3, (ebuf, 2, 0), (rxy, 1, 0), length, y)

    def add(self, k, tile_of):
        h = self.half
        tiles = self.span // TILE
        for c in range(2):
            if k == 1:
                self.low[c].wait_recv()
            if k == 2:
                self.high[c].wait_recv()

            @pl.loop(c * tiles, (c + 1) * tiles)
            def _(t):
                sl = pl.ds(pl.multiple_of(t * TILE, TILE), TILE)
                value = tile_of(sl)
                if k == 0:
                    self.out[:, sl] = value
                elif k == 3:
                    self.ebuf[0, :, sl] = value.astype(bf16)
                elif k == 1:
                    self.ebuf[1, :h, sl] = (value[:h] + self.rd[0, :, sl].astype(f32)).astype(bf16)
                    self.ebuf[1, h:, sl] = value[h:].astype(bf16)
                else:
                    self.ebuf[2, :h, sl] = value[:h].astype(bf16)
                    self.ebuf[2, h:, sl] = (value[h:] + self.rd[1, :, sl].astype(f32)).astype(bf16)

            if k == 3:
                self.low[c].start()
                self.high[c].start()
            if k == 1:
                self.to_x[c].start()
            if k == 2:
                self.to_y[c].start()

    def finish(self):
        tiles = self.span // TILE
        for c in range(2):
            self.to_x[c].wait_recv()
            self.to_y[c].wait_recv()

            @pl.loop(c * tiles, (c + 1) * tiles)
            def _(t):
                sl = pl.ds(pl.multiple_of(t * TILE, TILE), TILE)
                self.out[:, sl] += self.rxy[0, :, sl].astype(f32) + self.rxy[1, :, sl].astype(f32)

        for copy in self.low + self.high + self.to_x + self.to_y:
            copy.wait_send()


def scatter_scratch(length, width):
    return [
        pltpu.VMEM((3, length, width), bf16),
        pltpu.VMEM((2, length // 2, width), bf16),
        pltpu.VMEM((2, length, width), bf16),
        pltpu.SemaphoreType.DMA((4, 2)),
        pltpu.SemaphoreType.DMA((4, 2)),
    ]


def attend_back_kernel(
    gm_ref, raw_ref, a1_ref, pa_ref, pb_ref, cos_ref, sin_ref, start_ref, qg_ref, kg_ref, mix_ref, dy_ref,
    out_ref, sum_ref, dqg_ref, dkg_ref, ogot_ref, orecv_ref,
    gp_ref, dk_ref, dv_ref, acc_a, acc_b, heads, cbuf, crecv, oslot, ofetch,
    ebuf, rd, rxy, rs_send, rs_recv, do_send, do_recv, do_own, c_send, c_recv,
    oc_send, oc_recv, os_send, os_recv, o_local,
):
    length = a1_ref.shape[0]
    step = 128
    score_scale = HD ** (-0.5)
    s = pl.program_id(0)
    me = lax.axis_index("dp")
    core = me % 2
    place = (me // 2) % TP
    x, y, d, sibling = partners(me)
    cols = 4 * HD

    def columns_of(device):
        return pl.ds(pl.multiple_of(((device // 2) % TP) * cols, cols), cols)

    incoming = [
        remote(gm_ref.at[:, columns_of(device)], heads.at[k], do_send.at[k - 1], do_recv.at[k - 1], device)
        for k, device in ((1, x), (2, y), (3, d))
    ]
    own = pltpu.make_async_copy(
        gm_ref.at[:, pl.ds(pl.multiple_of(place * cols, cols), cols)], heads.at[0], do_own
    )
    scatter = Scatter(out_ref, ebuf, rd, rxy, rs_send, rs_recv, x, y)
    across = remote(cbuf, crecv, c_send, c_recv, sibling)
    block = oslot.shape[2]
    o_across = [
        remote(oslot.at[k], orecv_ref.at[k], oc_send.at[k], oc_recv.at[k], sibling) for k in range(TP)
    ]
    tall = oslot.shape[1] // 2
    o_low = remote(
        oslot.at[3, pl.ds(0, tall)], ogot_ref.at[2, pl.ds(0, tall)], os_send.at[2], os_recv.at[2], y
    )
    o_high = remote(
        oslot.at[3, pl.ds(tall, tall)], ogot_ref.at[2, pl.ds(tall, tall)], os_send.at[3], os_recv.at[3], x
    )
    o_home = [
        remote(oslot.at[k], ogot_ref.at[k - 1], os_send.at[k - 1], os_recv.at[k - 1], device)
        for k, device in ((1, x), (2, y))
    ]
    o_back = [
        pltpu.make_async_copy(ogot_ref.at[k - 1], oslot.at[k], o_local.at[k]) for k in range(1, 3)
    ]

    def out_block(k, side):
        device = (me, x, y, d)[k]
        at = ((device // 2) % TP) * 2 + side
        return pl.ds(pl.multiple_of(at * block, block), block)

    def out_tile(k, side, sl):
        return dot_tn(mix_ref[:, sl], dy_ref[:, out_block(k, side)])

    @pl.when(s == 0)
    def _():
        greet((x, y, d, sibling))
        for k in (2, 0, 1):
            incoming[k].start()
        own.start()
        for ref in (acc_a, acc_b, dqg_ref, dkg_ref):
            ref[...] = jnp.zeros_like(ref)
        for k in (3, 1, 2, 0):

            @pl.loop(0, oslot.shape[1] // TILE)
            def _(t):
                sl = pl.ds(pl.multiple_of(t * TILE, TILE), TILE)
                oslot[k, sl, :] = out_tile(k, 1 - core, sl).astype(bf16)

            o_across[k].start()
        incoming[2].wait_recv()

    @pl.when(s == 1)
    def _():
        for k in (3, 1, 2, 0):
            o_across[k].wait_send()
            o_across[k].wait_recv()
            fetch = pltpu.make_async_copy(orecv_ref.at[k], ofetch, o_local.at[0])
            fetch.start()
            fetch.wait()

            @pl.loop(0, oslot.shape[1] // TILE)
            def _(t):
                sl = pl.ds(pl.multiple_of(t * TILE, TILE), TILE)
                oslot[k, sl, :] = (out_tile(k, core, sl) + ofetch[sl, :].astype(f32)).astype(bf16)

            if k == 3:
                o_low.start()
                o_high.start()
        incoming[0].wait_recv()

    @pl.when(s == 2)
    def _():
        for copy, k, offset in ((o_low, 1, 0), (o_high, 2, tall)):
            copy.wait_recv()
            fetch = pltpu.make_async_copy(
                ogot_ref.at[2, pl.ds(offset, tall)], ofetch.at[pl.ds(0, tall)], o_local.at[0]
            )
            fetch.start()
            fetch.wait()

            @pl.loop(0, tall // TILE)
            def _(t):
                sl = pl.ds(pl.multiple_of(t * TILE, TILE), TILE)
                to = pl.ds(pl.multiple_of(offset + t * TILE, TILE), TILE)
                oslot[k, to, :] = (oslot[k, to, :].astype(f32) + ofetch[sl, :].astype(f32)).astype(bf16)

            o_home[k - 1].start()
        incoming[1].wait_recv()

    @pl.when(s == 3)
    def _():
        own.wait()

    which = part_order(s)

    for h in range(2):
        col = h * 4 * HD
        side = core if h == 0 else 1 - core
        cosine, sine = cos_ref[...], sin_ref[...]
        (q0, q1, k0), value = heads_of(
            raw_ref[:, col : col + 4 * HD], cosine, sine, qg_ref[...], kg_ref[...]
        )
        dk_ref[...] = jnp.zeros_like(dk_ref)
        dv_ref[...] = jnp.zeros_like(dv_ref)
        parts = []
        for b in range(length // step):
            sl = slice(b * step, (b + 1) * step)
            span = (b + 1) * step
            qs = jnp.concatenate([q0[2][sl], q1[2][sl]], axis=0)
            gs = jnp.concatenate(
                [
                    heads[which, sl, pl.ds(pl.multiple_of((2 * side + g) * HD, HD), HD)]
                    for g in range(2)
                ],
                axis=0,
            )
            keys, values = k0[2][:span], value[:span]
            probs = block_probs(qs, keys, start_ref[sl, :], b * step, score_scale)
            dv_ref[:span, :] += dot_tn(probs.astype(bf16), gs)
            grad_probs = dot_nt(gs, values)
            delta = jnp.sum(probs * grad_probs, axis=-1, keepdims=True)
            grad_scores = (probs * (grad_probs - delta)).astype(bf16)
            dk_ref[:span, :] += dot_tn(grad_scores, qs)
            parts.append(dot(grad_scores, keys))
        dq0 = jnp.concatenate([p[:step] for p in parts], axis=0) * score_scale
        dq1 = jnp.concatenate([p[step:] for p in parts], axis=0) * score_scale
        for k, (raw, inverse, _), grad, gain_ref, dgain_ref in (
            (0, q0, dq0, qg_ref, dqg_ref),
            (1, q1, dq1, qg_ref, dqg_ref),
            (2, k0, dk_ref[...] * score_scale, kg_ref, dkg_ref),
        ):
            back = grad * cosine + turn(grad * sine)
            scaled = back * gain_ref[...]
            inner = jnp.mean(scaled * raw, axis=-1, keepdims=True)
            gp_ref[:, col + k * HD : col + (k + 1) * HD] = (
                inverse * (scaled - raw * inverse * inverse * inner)
            ).astype(bf16)
            dgain_ref[...] += jnp.sum(back * raw * inverse, axis=0, keepdims=True)
        gp_ref[:, col + 3 * HD : col + 4 * HD] = dv_ref[...].astype(bf16)

    half = 4 * HD

    def tile_of(sl):
        return dot_nt(gp_ref[:, :half], pa_ref[sl, :]) + dot_nt(gp_ref[:, half:], pb_ref[sl, :])

    for at, k in enumerate(ORDER):

        @pl.when(s == at)
        def _():
            scatter.add(k, tile_of)

    @pl.loop(0, acc_a.shape[0] // TILE)
    def _(t):
        sl = pl.ds(pl.multiple_of(t * TILE, TILE), TILE)
        acc_b[sl, :] += dot_tn(a1_ref[:, sl], gp_ref[:, half:])

    @pl.when(s == 3)
    def _():
        cbuf[...] = acc_b[...].astype(bf16)
        across.start()

    @pl.loop(0, acc_a.shape[0] // TILE)
    def _(t):
        sl = pl.ds(pl.multiple_of(t * TILE, TILE), TILE)
        acc_a[sl, :] += dot_tn(a1_ref[:, sl], gp_ref[:, :half])

    @pl.when(s == 3)
    def _():
        proj = acc_a.shape[1]
        across.wait_recv()
        sum_ref[:, :proj] = (acc_a[...] + crecv[...].astype(f32)).astype(bf16)
        o_low.wait_send()
        o_high.wait_send()
        for copy, back in zip(o_home, o_back):
            copy.wait()
            back.start()
        for back in o_back:
            back.wait()

        @pl.loop(0, oslot.shape[1] // TILE)
        def _(t):
            sl = pl.ds(pl.multiple_of(t * TILE, TILE), TILE)
            total = oslot[0, sl, :].astype(f32)
            for k in range(1, 3):
                total += oslot[k, sl, :].astype(f32)
            sum_ref[sl, proj:] = total.astype(bf16)

        scatter.finish()
        across.wait_send()
        for copy in incoming:
            copy.wait_send()


CHUNK = 256


def feed_kernel(
    a2_ref, wa_ref, g_ref,
    gate_ref, up_ref, hid_ref, wb_ref, ga_ref, sum_ref,
    a2, wa, wb, g, hid, stage, cbuf, crecv, acc,
    loads, x_send, x_recv, g_send, g_recv, s_sem, c_send, c_recv, keeps,
):
    tokens, width = a2.shape
    length = g_ref.shape[0]
    fn = wa.shape[1] // 2
    x, y, d, sibling = partners(lax.axis_index("dp"))
    h = length // 2

    def rows(k, offset=0, size=length):
        return g.at[pl.ds(k * length + offset, size)]

    load_x = pltpu.make_async_copy(a2_ref, a2, loads.at[0])
    load_w = pltpu.make_async_copy(wa_ref, wa, loads.at[1])
    load_g = pltpu.make_async_copy(g_ref, rows(0), loads.at[2])
    swap_w = remote(wa_ref, wb, x_send.at[0], x_recv.at[0], sibling)
    g_x = remote(g_ref, rows(1), g_send.at[0], g_recv.at[0], x)
    g_y = remote(g_ref, rows(2), g_send.at[1], g_recv.at[1], y)
    g_low = remote(rows(2, 0, h), rows(3, 0, h), g_send.at[2], g_recv.at[2], x)
    g_high = remote(rows(1, h, h), rows(3, h, h), g_send.at[3], g_recv.at[3], y)
    keep_w = pltpu.make_async_copy(wb, wb_ref, keeps.at[0])
    keep_g = pltpu.make_async_copy(g, ga_ref, keeps.at[1])
    keep_h = pltpu.make_async_copy(hid, hid_ref, keeps.at[2])

    load_w.start()
    load_x.start()
    load_g.start()
    greet((x, y, d, sibling))
    g_x.start()
    g_y.start()
    swap_w.start()

    per_half = fn // CHUNK
    span = 2 * length
    halves = tokens // span

    def store(i, which, ref):
        half = i // (per_half * halves)
        j = i % (per_half * halves)
        r, c = j // per_half, j % per_half
        return pltpu.make_async_copy(
            stage.at[i % 2, which],
            ref.at[
                pl.ds(pl.multiple_of(r * span, span), span),
                pl.ds(pl.multiple_of((half * per_half + c) * CHUNK, CHUNK), CHUNK),
            ],
            s_sem.at[i % 2, which],
        )

    def run(half, w):
        @pl.loop(0, per_half * halves)
        def _(j):
            i = j + half * per_half * halves

            @pl.when(i >= 2)
            def _():
                store(i - 2, 0, gate_ref).wait()
                store(i - 2, 1, up_ref).wait()

            r, c = j // per_half, j % per_half
            sl = pl.ds(pl.multiple_of(r * span, span), span)
            gate = dot(a2[sl, :], w[:, pl.ds(pl.multiple_of(c * CHUNK, CHUNK), CHUNK)])
            up = dot(a2[sl, :], w[:, pl.ds(pl.multiple_of(fn + c * CHUNK, CHUNK), CHUNK)])
            stage[i % 2, 0] = gate.astype(bf16)
            stage[i % 2, 1] = up.astype(bf16)
            hid[sl, pl.ds(pl.multiple_of((half * per_half + c) * CHUNK, CHUNK), CHUNK)] = (
                gate * jax.nn.sigmoid(gate) * up
            ).astype(bf16)
            store(i, 0, gate_ref).start()
            store(i, 1, up_ref).start()

    load_w.wait()
    load_x.wait()
    run(0, wa)
    swap_w.wait_recv()
    keep_w.start()
    run(1, wb)
    last = 2 * per_half * halves
    for i in (last - 2, last - 1):
        store(i, 0, gate_ref).wait()
        store(i, 1, up_ref).wait()
    keep_h.start()

    g_x.wait_recv()
    g_high.start()
    g_y.wait_recv()
    g_low.start()
    load_g.wait()
    near = pl.ds(0, 3 * length)
    far = pl.ds(3 * length, length)

    @pl.loop(0, 2 * per_half)
    def _(t):
        cols = pl.ds(pl.multiple_of(t * CHUNK, CHUNK), CHUNK)
        acc[t] = dot_tn(hid[near, cols], g[near, :])

    g_low.wait_recv()
    g_high.wait_recv()
    keep_g.start()

    def across(t):
        return remote(cbuf.at[t], crecv.at[t], c_send.at[t], c_recv.at[t], sibling)

    @pl.loop(0, per_half)
    def _(t):
        cols = pl.ds(pl.multiple_of(fn + t * CHUNK, CHUNK), CHUNK)
        cbuf[t] = (acc[per_half + t] + dot_tn(hid[far, cols], g[far, :])).astype(bf16)
        across(t).start()

    @pl.loop(0, per_half)
    def _(t):
        cols = pl.ds(pl.multiple_of(t * CHUNK, CHUNK), CHUNK)
        own = acc[t] + dot_tn(hid[far, cols], g[far, :])
        across(t).wait_recv()
        sum_ref[cols, :] = (own + crecv[t].astype(f32)).astype(bf16)

    for t in range(per_half):
        across(t).wait_send()
    for copy in (swap_w, g_x, g_y, g_low, g_high):
        copy.wait_send()
    for copy in (keep_w, keep_g, keep_h):
        copy.wait()


def feed_forward(a2, wa, g):
    tokens, width = a2.shape
    fn = wa.shape[1] // 2
    length = g.shape[0]
    anywhere = pl.BlockSpec(memory_space=pl.ANY)
    sem = pltpu.SemaphoreType.DMA
    return pl.pallas_call(
        feed_kernel,
        in_specs=[anywhere] * 3,
        out_specs=[anywhere] * 5 + [pl.BlockSpec(memory_space=pltpu.VMEM)],
        out_shape=[
            struct((tokens, 2 * fn), bf16),
            struct((tokens, 2 * fn), bf16),
            struct((tokens, 2 * fn), bf16),
            struct(wa.shape, bf16),
            struct((tokens, width), bf16),
            struct((fn, width), bf16),
        ],
        scratch_shapes=[
            pltpu.VMEM(a2.shape, bf16),
            pltpu.VMEM(wa.shape, bf16),
            pltpu.VMEM(wa.shape, bf16),
            pltpu.VMEM(a2.shape, bf16),
            pltpu.VMEM((tokens, 2 * fn), bf16),
            pltpu.VMEM((2, 2, 2 * length, CHUNK), bf16),
            pltpu.VMEM((fn // CHUNK, CHUNK, width), bf16),
            pltpu.VMEM((fn // CHUNK, CHUNK, width), bf16),
            pltpu.VMEM((2 * fn // CHUNK, CHUNK, width), f32),
            sem((3,)), sem((2,)), sem((2,)), sem((4,)), sem((4,)), sem((2, 2)),
            sem((fn // CHUNK,)), sem((fn // CHUNK,)), sem((3,)),
        ],
        compiler_params=pltpu.CompilerParams(
            vmem_limit_bytes=58 << 20, collective_id=4, has_side_effects=True
        ),
        cost_estimate=pl.CostEstimate(
            flops=4 * tokens * width * fn, bytes_accessed=30 << 20, transcendentals=0
        ),
        name="feed_forward",
    )(a2, wa, g)


def feed_back_kernel(
    gate_ref, up_ref, ga_ref, da_ref, wa_ref, wb_ref, a2_ref,
    out_ref, sum_ref, db_ref, crecv_ref,
    gp, wa, wb, a2, wd, uv, cbuf, cgot, stage, loads, u_sem, c_send, c_recv, g_sem, s_sem,
    d_send, d_recv,
    ebuf, rd, rxy, rs_send, rs_recv,
):
    length = out_ref.shape[0]
    cols = wa.shape[1]
    fn = cols // 2
    rows = cbuf.shape[1]
    tiles = a2.shape[1] // rows
    x, y, d, sibling = partners(lax.axis_index("dp"))
    scatter = Scatter(out_ref, ebuf, rd, rxy, rs_send, rs_recv, x, y)

    def piece(k):
        sl = pl.ds(k * length, length)
        return pltpu.make_async_copy(ga_ref.at[sl], a2.at[sl], loads.at[k])

    load_a = pltpu.make_async_copy(wa_ref, wa, loads.at[4])
    load_b = pltpu.make_async_copy(wb_ref, wb, loads.at[5])
    load_da = pltpu.make_async_copy(da_ref, wd.at[pl.ds(0, fn)], loads.at[6])
    swap_d = remote(da_ref, wd.at[pl.ds(fn, fn)], d_send, d_recv, sibling)
    keep_d = pltpu.make_async_copy(wd.at[pl.ds(fn, fn)], db_ref, loads.at[7])
    load_x = pltpu.make_async_copy(a2_ref, a2, loads.at[8])
    steps = 2 * TP

    def step_of(i):
        return part_order(i // 2), i % 2

    def fetch_uv(i, which, ref):
        part, c = step_of(i)
        return pltpu.make_async_copy(
            ref.at[
                pl.ds(pl.multiple_of(part * length, length), length),
                pl.ds(pl.multiple_of(c * fn, CHUNK), fn),
            ],
            uv.at[i % 2, which],
            u_sem.at[i % 2, which],
        )

    fetch_uv(0, 0, gate_ref).start()
    fetch_uv(0, 1, up_ref).start()
    piece(3).start()
    load_da.start()
    greet((x, y, d, sibling))
    swap_d.start()
    load_a.start()
    load_b.start()
    for k in (1, 2, 0):
        piece(k).start()

    def rows_of(t):
        return pl.ds(pl.multiple_of(t * rows, rows), rows)

    def across(t):
        return remote(
            cbuf.at[t % 2], crecv_ref.at[rows_of(t)], c_send.at[t % 2], c_recv.at[t], sibling
        )

    def fetch(t):
        return pltpu.make_async_copy(crecv_ref.at[rows_of(t)], cgot.at[t % 2], g_sem.at[t % 2])

    def store(t):
        return pltpu.make_async_copy(stage.at[t % 2], sum_ref.at[rows_of(t)], s_sem.at[t % 2])

    def part_of(k):
        sl = slice(k * length, (k + 1) * length)

        def tile_of(cut):
            return dot_nt(gp[sl, :cols], wa[cut, :]) + dot_nt(gp[sl, cols:], wb[cut, :])

        return tile_of

    def inner(first, end):
        @pl.loop(first, end)
        def _(i):
            @pl.when(i + 1 < steps)
            def _():
                fetch_uv(i + 1, 0, gate_ref).start()
                fetch_uv(i + 1, 1, up_ref).start()

            part, half = step_of(i)
            sl = pl.ds(pl.multiple_of(part * length, length), length)
            fetch_uv(i, 0, gate_ref).wait()
            fetch_uv(i, 1, up_ref).wait()
            for at in range(0, fn, CHUNK):
                cut = slice(at, at + CHUNK)
                rows_at = pl.ds(pl.multiple_of(half * fn + at, CHUNK), CHUNK)
                grad_hidden = dot_nt(a2[sl, :], wd[rows_at, :])
                gate = uv[i % 2, 0, :, cut].astype(f32)
                up = uv[i % 2, 1, :, cut].astype(f32)
                sig = jax.nn.sigmoid(gate)
                scaled = grad_hidden * sig
                to = half * cols + at
                gp[sl, pl.ds(pl.multiple_of(to, CHUNK), CHUNK)] = (
                    scaled * up * (1.0 + gate * (1.0 - sig))
                ).astype(bf16)
                gp[sl, pl.ds(pl.multiple_of(to + fn, CHUNK), CHUNK)] = (scaled * gate).astype(bf16)

    piece(3).wait()
    load_da.wait()
    inner(0, 1)
    swap_d.wait_recv()
    keep_d.start()
    inner(1, 2)
    load_a.wait()
    load_b.wait()
    scatter.add(3, part_of(3))
    for k in (1, 2, 0):
        piece(k).wait()
    inner(2, steps)
    load_x.start()
    scatter.add(1, part_of(1))
    scatter.add(2, part_of(2))
    load_x.wait()

    @pl.loop(0, tiles)
    def _(t):
        @pl.when(t >= 2)
        def _():
            across(t - 2).wait_send()

        cbuf[t % 2] = dot_tn(a2[:, rows_of(t)], gp[:, cols:]).astype(bf16)
        across(t).start()

    scatter.add(0, part_of(0))

    @pl.loop(0, tiles)
    def _(t):
        across(t).wait_recv()
        fetch(t).start()

        @pl.when(t >= 2)
        def _():
            store(t - 2).wait()

        own = dot_tn(a2[:, rows_of(t)], gp[:, :cols])
        fetch(t).wait()
        stage[t % 2] = (own + cgot[t % 2].astype(f32)).astype(bf16)
        store(t).start()

    for t in (tiles - 2, tiles - 1):
        store(t).wait()
        across(t).wait_send()
    swap_d.wait_send()
    keep_d.wait()
    scatter.finish()


def feed_backward(gate, up, ga, da, wa, wb, a2, length):
    tokens, width = a2.shape
    cols = wa.shape[1]
    rows = 256
    anywhere = pl.BlockSpec(memory_space=pl.ANY)
    sem = pltpu.SemaphoreType.DMA
    return pl.pallas_call(
        feed_back_kernel,
        in_specs=[anywhere] * 7,
        out_specs=[pl.BlockSpec(memory_space=pltpu.VMEM), anywhere, anywhere, anywhere],
        out_shape=[
            struct((length, width), f32),
            struct(wa.shape, bf16),
            struct(da.shape, bf16),
            struct(wa.shape, bf16),
        ],
        scratch_shapes=[
            pltpu.VMEM((tokens, 2 * cols), bf16),
            pltpu.VMEM(wa.shape, bf16),
            pltpu.VMEM(wb.shape, bf16),
            pltpu.VMEM(a2.shape, bf16),
            pltpu.VMEM((cols, width), bf16),
            pltpu.VMEM((2, 2, length, cols // 2), bf16),
            pltpu.VMEM((2, rows, cols), bf16),
            pltpu.VMEM((2, rows, cols), bf16),
            pltpu.VMEM((2, rows, cols), bf16),
            sem((9,)), sem((2, 2)), sem((2,)), sem((width // rows,)), sem((2,)), sem((2,)),
            sem, sem,
        ]
        + scatter_scratch(length, width),
        compiler_params=pltpu.CompilerParams(
            vmem_limit_bytes=62 << 20, collective_id=1, has_side_effects=True
        ),
        cost_estimate=pl.CostEstimate(
            flops=4 * tokens * width * cols, bytes_accessed=30 << 20, transcendentals=0
        ),
        name="feed_backward",
    )(gate, up, ga, da, wa, wb, a2)[:3]


ORDER = (3, 1, 2, 0)


def part_order(s):
    return 3 - 2 * s + 3 * (s // 2)


def rows_spec(length, cols):
    return pl.BlockSpec((length, cols), lambda s: (s, 0))


def whole_spec(shape):
    return pl.BlockSpec(shape, lambda s: (0, 0))


def struct(shape, dtype):
    return jax.ShapeDtypeStruct(shape, dtype)


def everyone(me):
    size = 2 * TP
    base = me - me % size
    return [base + (me % size + i) % size for i in range(1, size)]


def spread_kernel(
    wq_ref, wk_ref, wv_ref, wo_ref, gain_ref, seg_ref,
    all_ref, gains_ref, segs_ref,
    send, recv, local, s_send, s_recv,
):
    me = lax.axis_index("dp")
    size = 2 * TP
    rows = wq_ref.shape[0]
    here = pl.ds(pl.multiple_of((me % size) * rows, rows), rows)
    plan = []
    at = 0
    for ref in (wq_ref, wk_ref, wv_ref, wo_ref):
        width = ref.shape[1] // size
        plan.append((ref, width, all_ref.at[here, pl.ds(at, width)]))
        at += width

    def columns(ref, width, device):
        return ref.at[:, pl.ds(pl.multiple_of((device % size) * width, width), width)]

    others = everyone(me)
    gains_here = gains_ref.at[me % size]
    own = [
        pltpu.make_async_copy(columns(ref, width, me), dst, local.at[t])
        for t, (ref, width, dst) in enumerate(plan)
    ] + [
        pltpu.make_async_copy(gain_ref, gains_here, local.at[4]),
        pltpu.make_async_copy(seg_ref, segs_ref.at[0], local.at[5]),
    ]
    copies = [
        remote(columns(ref, width, device), dst, send.at[i, t], recv.at[i, t], device)
        for i, device in enumerate(others)
        for t, (ref, width, dst) in enumerate(plan)
    ]
    copies += [
        remote(gain_ref, gains_here, send.at[i, 4], recv.at[i, 4], device)
        for i, device in enumerate(others)
    ]
    copies += [
        remote(seg_ref, segs_ref.at[1 + k], s_send.at[k], s_recv.at[k], device)
        for k, device in enumerate(partners(me)[:3])
    ]
    for copy in own:
        copy.start()
    greet(others)
    for copy in copies:
        copy.start()
    for copy in own + copies:
        copy.wait()


def spread_attention(wq, wk, wv, wo, gain, seg):
    size = 2 * TP
    rows = wq.shape[0]
    cols = (wq.shape[1] + wk.shape[1] + wv.shape[1] + wo.shape[1]) // size
    anywhere = pl.BlockSpec(memory_space=pl.ANY)
    sem = pltpu.SemaphoreType.DMA
    return pl.pallas_call(
        spread_kernel,
        in_specs=[anywhere] * 6,
        out_specs=[anywhere] * 3,
        out_shape=[
            struct((size * rows, cols), bf16),
            struct((size, *gain.shape), f32),
            struct((TP, *seg.shape), jnp.int32),
        ],
        scratch_shapes=[sem((size - 1, 5)), sem((size - 1, 5)), sem((6,)), sem((3,)), sem((3,))],
        compiler_params=pltpu.CompilerParams(collective_id=5, has_side_effects=True),
        name="spread_attention",
    )(wq, wk, wv, wo, gain, seg)


def gather_kernel(
    run, seg_ref, rate_ref, x_ref, gate_ref, up_ref,
    cos_ref, sin_ref, start_ref, x_all, w_all,
    w_ref, flat, wide, xs, x_send, x_recv, w_send, w_recv, local,
):
    me = lax.axis_index("dp")
    size = 2 * TP
    x, y, d, _ = partners(me)
    others = everyone(me)
    length = x_ref.shape[0]
    rows = w_ref.shape[1]
    h = length // 2
    here = pl.ds(pl.multiple_of((me % size) * rows, rows), rows)

    def place(k, offset=0, count=length):
        return x_all.at[pl.ds(k * length + offset, count)]

    own = [
        pltpu.make_async_copy(xs, place(0), local.at[0]),
        pltpu.make_async_copy(w_ref.at[me % size], w_all.at[here], local.at[1]),
    ]
    fills = [
        pltpu.make_async_copy(ref, flat.at[i], local.at[2 + i]) for i, ref in enumerate((gate_ref, up_ref))
    ]
    weights = [
        remote(w_ref.at[device % size], w_all.at[here], w_send.at[i], w_recv.at[i], device)
        for i, device in enumerate(others)
    ]
    to_x = remote(xs, place(1), x_send.at[0], x_recv.at[0], x)
    to_y = remote(xs, place(2), x_send.at[1], x_recv.at[1], y)
    load_x = pltpu.make_async_copy(x_ref, xs, local.at[4])
    low = remote(place(2, 0, h), place(3, 0, h), x_send.at[2], x_recv.at[2], x)
    high = remote(place(1, h, h), place(3, h, h), x_send.at[3], x_recv.at[3], y)
    for copy in [load_x] + fills:
        copy.start()
    greet(others)
    load_x.wait()
    for copy in (to_x, to_y, own[0]):
        copy.start()
    for copy in fills:
        copy.wait()
    half = wide.shape[1] // 2
    values = [flat[i].astype(f32) for i in range(2)]
    for s in range(size):
        for i in range(2):
            for g in range(half // run):
                at = (g * size + s) * run
                wide[:, i * half + g * run : i * half + (g + 1) * run] = values[i][:, at : at + run]
        w_ref[s] = wide[...].astype(bf16)
    for copy in own[1:] + weights:
        copy.start()

    row = lax.broadcasted_iota(jnp.int32, (length, length), 0)
    column = lax.broadcasted_iota(jnp.int32, (length, length), 1)
    for k in range(TP):
        label = jnp.broadcast_to(seg_ref[k].astype(f32), (length, length))
        mine = jnp.sum(jnp.where(row == column, label, 0.0), axis=1, keepdims=True)
        start = jnp.sum(jnp.where(label < mine, 1.0, 0.0), axis=1, keepdims=True)
        position = lax.broadcasted_iota(jnp.int32, (length, 1), 0).astype(f32) - start
        angle = position * rate_ref[0:1, :]
        sl = pl.ds(k * length, length)
        cos_ref[sl, :] = jnp.cos(angle)
        sin_ref[sl, :] = jnp.sin(angle) * rate_ref[1:2, :]
        start_ref[sl, :] = start.astype(jnp.int32)

    to_x.wait_recv()
    high.start()
    to_y.wait_recv()
    low.start()
    for copy in (to_x, to_y):
        copy.wait_send()
    for copy in own + weights + [low, high]:
        copy.wait()


def gather_group(seg, rates, x, gate, up, run):
    size = 2 * TP
    rows, cols = gate.shape[0], 2 * gate.shape[1] // size
    anywhere = pl.BlockSpec(memory_space=pl.ANY)
    vmem = pl.BlockSpec(memory_space=pltpu.VMEM)
    sem = pltpu.SemaphoreType.DMA
    return pl.pallas_call(
        functools.partial(gather_kernel, run),
        in_specs=[vmem] * 2 + [anywhere] * 3,
        out_specs=[vmem] * 3 + [anywhere] * 2,
        out_shape=[
            struct((TP * x.shape[0], HD), f32),
            struct((TP * x.shape[0], HD), f32),
            struct((TP * x.shape[0], 1), jnp.int32),
            struct((TP * x.shape[0], x.shape[1]), bf16),
            struct((size * rows, cols), bf16),
        ],
        scratch_shapes=[
            pltpu.VMEM((size, rows, cols), bf16),
            pltpu.VMEM((2, *gate.shape), bf16),
            pltpu.VMEM((rows, cols), f32),
            pltpu.VMEM(x.shape, bf16),
            sem((4,)), sem((4,)), sem((size - 1,)), sem((size - 1,)), sem((5,)),
        ],
        compiler_params=pltpu.CompilerParams(
            vmem_limit_bytes=60 << 20, collective_id=6, has_side_effects=True
        ),
        name="gather_group",
    )(seg, rates, x, gate, up)


def attend_kernel(
    x_ref, cos_ref, sin_ref, start_ref, ag_ref, mg_ref, qg_ref, kg_ref, all_ref,
    raw_ref, a1_ref, mixed_ref, after_ref, inv_ref, pa_out, pb_out, wo_ref, a2_ref,
    pa_ref, pb_ref, fill, heads, mix, wo, a2, p_send, p_recv, o_send, o_recv, w_send, w_recv, s_send, s_recv, a_send, a_recv, local,
):
    length, width = x_ref.shape
    step = 128
    score_scale = HD ** (-0.5)
    s = pl.program_id(0)
    me = lax.axis_index("dp")
    core = me % 2
    place = (me // 2) % TP
    x, y, d, sibling = partners(me)
    near = (x, y, d)
    cols = 4 * HD
    proj = pa_ref.shape[1]
    block = all_ref.shape[2] - proj
    planes = all_ref.shape[0]
    deep = pa_ref.shape[0] // planes

    def block_of(device):
        return pl.ds(pl.multiple_of((device % (2 * TP)) * block, block), block)

    own_out = wo.at[:, block_of(me)]
    fills = []
    for g in range(planes):
        at = pl.ds(g * deep, deep)
        fills.append(
            pltpu.make_async_copy(
                all_ref.at[g, pl.ds(0, deep), pl.ds(0, proj)], pa_ref.at[at], fill.at[g, 0]
            )
        )
        fills.append(
            pltpu.make_async_copy(
                all_ref.at[g, pl.ds(0, deep), pl.ds(proj, block)], wo.at[at, block_of(me)], fill.at[g, 1]
            )
        )

    tall = wo.shape[0] // 2
    spread_out = [
        remote(own_out, own_out, w_send.at[i], w_recv.at[i], device)
        for i, device in enumerate(near[:2])
    ]

    def passed(device, offset, i, to):
        ref = wo.at[pl.ds(offset, tall), block_of(device)]
        return remote(ref, ref, w_send.at[i], w_recv.at[i], to)

    pass_on = [passed(x, tall, 2, y), passed(y, 0, 3, x)]
    beside = [remote(own_out, own_out, s_send.at[3], s_recv.at[3], sibling)]
    onward = [
        remote(wo.at[:, block_of(device)], wo.at[:, block_of(device)], s_send.at[i], s_recv.at[i], sibling)
        for i, device in enumerate(near)
    ]
    mine = pl.ds(pl.multiple_of(place * cols, cols), cols)
    home = [
        remote(heads.at[i + 1], mix.at[:, mine], o_send.at[i], o_recv.at[i], device)
        for i, device in enumerate(near)
    ]
    h = length // 2
    a2_x = remote(a2.at[0], a2.at[1], a_send.at[0], a_recv.at[0], x)
    a2_y = remote(a2.at[0], a2.at[2], a_send.at[1], a_recv.at[1], y)
    a2_low = remote(a2.at[2, pl.ds(0, h)], a2.at[3, pl.ds(0, h)], a_send.at[2], a_recv.at[2], x)
    a2_high = remote(a2.at[1, pl.ds(h, h)], a2.at[3, pl.ds(h, h)], a_send.at[3], a_recv.at[3], y)
    keep = [
        pltpu.make_async_copy(a2.at[k], a2_ref.at[pl.ds(k * length, length)], local.at[1 + k])
        for k in range(TP)
    ]
    keep_out = pltpu.make_async_copy(wo, wo_ref, local.at[5])
    keep_b = pltpu.make_async_copy(pb_ref, pb_out, local.at[6])
    keep_a = pltpu.make_async_copy(pa_ref, pa_out, local.at[0])
    swap_p = remote(pa_ref, pb_ref, p_send, p_recv, sibling)

    @pl.when(s == 0)
    def _():
        for copy in fills:
            copy.start()
        greet((x, y, d, sibling))
        for copy in fills:
            copy.wait()
        for copy in [swap_p] + spread_out + beside:
            copy.start()
        keep_a.start()

    @pl.when(s == 3)
    def _():
        for i in range(2):
            spread_out[i].wait_recv()
            pass_on[i].start()
            onward[i].start()

    @pl.loop(0, length // step)
    def _(t):
        sl = pl.ds(pl.multiple_of(t * step, step), step)
        v = x_ref[sl, :].astype(f32)
        a1_ref[sl, :] = (v * inverse_rms(v) * ag_ref[...]).astype(bf16)

    which = part_order(s)
    for half, p_ref in ((0, pa_ref), (1, pb_ref)):
        side = core if half == 0 else 1 - core
        if half:

            @pl.when(s == 0)
            def _():
                swap_p.wait_recv()
                keep_b.start()

        raw_ref[:, half * cols : (half + 1) * cols] = dot(a1_ref[...], p_ref[...])
        (q0, q1, k0), value = heads_of(
            raw_ref[:, half * cols : (half + 1) * cols], cos_ref[...], sin_ref[...], qg_ref[...], kg_ref[...]
        )
        for b in range(length // step):
            sl = slice(b * step, (b + 1) * step)
            span = (b + 1) * step
            qs = jnp.concatenate([q0[2][sl], q1[2][sl]], axis=0)
            probs = block_probs(qs, k0[2][:span], start_ref[sl, :], b * step, score_scale)
            mixed = dot(probs.astype(bf16), value[:span]).astype(bf16)
            for g in range(2):
                at = pl.ds(pl.multiple_of((2 * side + g) * HD, HD), HD)
                heads[which, sl, at] = mixed[g * step : (g + 1) * step]

    for at, k in enumerate(ORDER[:3]):

        @pl.when(s == at)
        def _():
            home[k - 1].start()

    @pl.when(s == 3)
    def _():
        mix[:, mine] = heads[0]
        for copy in pass_on:
            copy.wait_recv()
        onward[2].start()
        for copy in home:
            copy.wait_recv()
        for copy in beside + onward:
            copy.wait_recv()
        keep_out.start()

        @pl.loop(0, width // TILE)
        def _(t):
            sl = pl.ds(pl.multiple_of(t * TILE, TILE), TILE)
            after_ref[:, sl] = x_ref[:, sl].astype(f32) + dot(mix[...], wo[:, sl])

        @pl.loop(0, length // step)
        def _(t):
            sl = pl.ds(pl.multiple_of(t * step, step), step)
            v = after_ref[sl, :]
            inverse = inverse_rms(v)
            inv_ref[sl, :] = inverse
            a2[0, sl, :] = (v * inverse * mg_ref[...]).astype(bf16)

        a2_x.start()
        a2_y.start()
        keep[0].start()
        mixed_ref[...] = mix[...]
        a2_x.wait_recv()
        a2_high.start()
        keep[1].start()
        a2_y.wait_recv()
        a2_low.start()
        keep[2].start()
        a2_high.wait_recv()
        a2_low.wait_recv()
        keep[3].start()
        for copy in spread_out + pass_on + beside + onward + home + [a2_x, a2_y, a2_low, a2_high]:
            copy.wait_send()
        swap_p.wait_send()
        for copy in keep + [keep_out, keep_a, keep_b]:
            copy.wait()


def attend_forward(x, cosine, sine, starts, ag, mg, qg, kg, weights, depth, proj, length):
    tokens, width = x.shape
    planes = weights.shape[0]
    total = planes * depth
    anywhere = pl.BlockSpec(memory_space=pl.ANY)

    def in_order(cols):
        return pl.BlockSpec((length, cols), lambda s: (part_order(s), 0))

    return pl.pallas_call(
        attend_kernel,
        grid=(TP,),
        in_specs=[in_order(width)]
        + [in_order(HD), in_order(HD), in_order(1)]
        + [whole_spec(g.shape) for g in (ag, mg, qg, kg)]
        + [anywhere],
        out_specs=[in_order(8 * HD), in_order(width)]
        + [whole_spec((length, width))] * 2
        + [whole_spec((length, 1))]
        + [anywhere] * 4,
        out_shape=[
            struct((tokens, 8 * HD), f32),
            struct((tokens, width), bf16),
            struct((length, width), bf16),
            struct((length, width), f32),
            struct((length, 1), f32),
            struct((total, proj), bf16),
            struct((total, proj), bf16),
            struct((total, width), bf16),
            struct((tokens, width), bf16),
        ],
        scratch_shapes=[
            pltpu.VMEM((total, proj), bf16),
            pltpu.VMEM((total, proj), bf16),
            pltpu.SemaphoreType.DMA((planes, 2)),
            pltpu.VMEM((TP, length, 4 * HD), bf16),
            pltpu.VMEM((length, width), bf16),
            pltpu.VMEM((total, width), bf16),
            pltpu.VMEM((TP, length, width), bf16),
            pltpu.SemaphoreType.DMA,
            pltpu.SemaphoreType.DMA,
            pltpu.SemaphoreType.DMA((3,)),
            pltpu.SemaphoreType.DMA((3,)),
            pltpu.SemaphoreType.DMA((4,)),
            pltpu.SemaphoreType.DMA((4,)),
            pltpu.SemaphoreType.DMA((4,)),
            pltpu.SemaphoreType.DMA((4,)),
            pltpu.SemaphoreType.DMA((4,)),
            pltpu.SemaphoreType.DMA((4,)),
            pltpu.SemaphoreType.DMA((7,)),
        ],
        compiler_params=pltpu.CompilerParams(
            vmem_limit_bytes=56 << 20, collective_id=3, has_side_effects=True
        ),
        cost_estimate=pl.CostEstimate(
            flops=2 * tokens * width * 8 * HD, bytes_accessed=30 << 20, transcendentals=0
        ),
        name="attend_forward",
    )(x, cosine, sine, starts, ag, mg, qg, kg, weights)


def between_kernel(
    grad_ref, after_ref, inv_ref, gain_ref, cot_ref, w_ref,
    sum_ref, dy_ref, dgain_ref, heads_ref,
):
    length = after_ref.shape[0]
    step = 128

    @pl.when(pl.program_id(0) == 0)
    def _():
        dgain_ref[...] = jnp.zeros_like(dgain_ref)

        @pl.loop(0, length // step)
        def _(t):
            sl = pl.ds(pl.multiple_of(t * step, step), step)
            grad, values, inverse = grad_ref[sl, :], after_ref[sl, :], inv_ref[sl, :]
            scaled = grad * gain_ref[...]
            inner = jnp.mean(scaled * values, axis=-1, keepdims=True)
            total = cot_ref[sl, :].astype(f32) + inverse * (scaled - values * inverse * inverse * inner)
            sum_ref[sl, :] = total
            dy_ref[sl, :] = total.astype(bf16)
            dgain_ref[...] += jnp.sum(grad * values * inverse, axis=0, keepdims=True)

    heads_ref[...] = dot_nt(dy_ref[...], w_ref[...]).astype(bf16)


def between(grad, after, inverse, gain, cot, w):
    length, width = after.shape
    block = 256

    def once(v):
        return pl.BlockSpec(v.shape, lambda s: (0, 0), pipeline_mode=pl.Buffered(1))

    return pl.pallas_call(
        between_kernel,
        grid=(w.shape[0] // block,),
        in_specs=[once(v) for v in (grad, after, inverse, gain, cot)]
        + [pl.BlockSpec((block, width), lambda s: (s, 0))],
        out_specs=[whole_spec((length, width))] * 2
        + [whole_spec((1, width)), pl.BlockSpec((length, block), lambda s: (0, s))],
        out_shape=[
            struct((length, width), f32),
            struct((length, width), bf16),
            struct((1, width), f32),
            struct((length, w.shape[0]), bf16),
        ],
        compiler_params=pltpu.CompilerParams(vmem_limit_bytes=60 << 20),
        cost_estimate=pl.CostEstimate(
            flops=2 * length * width * w.shape[0], bytes_accessed=24 << 20, transcendentals=0
        ),
        name="between",
    )(grad, after, inverse, gain, cot, w)


def attend_backward(gm, raw, a1, pa, pb, cosine, sine, starts, qg, kg, mix, dy, length):
    tokens, width = a1.shape
    block = width // (2 * TP)
    anywhere = pl.BlockSpec(memory_space=pl.ANY)
    sem = pltpu.SemaphoreType.DMA

    def in_order(cols):
        return pl.BlockSpec((length, cols), lambda s: (part_order(s), 0))

    def once(v):
        return pl.BlockSpec(v.shape, lambda s: (0, 0), pipeline_mode=pl.Buffered(1))

    return pl.pallas_call(
        attend_back_kernel,
        grid=(TP,),
        in_specs=[anywhere]
        + [in_order(c) for c in (8 * HD, width)]
        + [once(w) for w in (pa, pb)]
        + [in_order(HD), in_order(HD), in_order(1)]
        + [whole_spec(v.shape) for v in (qg, kg)]
        + [once(v) for v in (mix, dy)],
        out_specs=[whole_spec((length, width)), whole_spec((width, pa.shape[1] + block))]
        + [whole_spec(v.shape) for v in (qg, kg)]
        + [anywhere] * 2,
        out_shape=[struct((length, width), f32), struct((width, pa.shape[1] + block), bf16)]
        + [struct(v.shape, f32) for v in (qg, kg)]
        + [struct((3, width, block), bf16), struct((TP, width, block), bf16)],
        scratch_shapes=[
            pltpu.VMEM((length, 8 * HD), bf16),
            pltpu.VMEM((length, HD), f32),
            pltpu.VMEM((length, HD), f32),
            pltpu.VMEM(pa.shape, f32),
            pltpu.VMEM(pa.shape, f32),
            pltpu.VMEM((TP, length, 4 * HD), bf16),
            pltpu.VMEM(pa.shape, bf16),
            pltpu.VMEM(pa.shape, bf16),
            pltpu.VMEM((TP, width, block), bf16),
            pltpu.VMEM((width, block), bf16),
        ]
        + scatter_scratch(length, width)
        + [sem((3,)), sem((3,)), sem, sem, sem, sem((TP,)), sem((TP,)), sem((4,)), sem((4,)), sem((TP,))],
        compiler_params=pltpu.CompilerParams(
            vmem_limit_bytes=60 << 20, collective_id=2, has_side_effects=True
        ),
        cost_estimate=pl.CostEstimate(
            flops=2 * tokens * width * 8 * HD, bytes_accessed=30 << 20, transcendentals=0
        ),
        name="attend_backward",
    )(gm, raw, a1, pa, pb, cosine, sine, starts, qg, kg, mix, dy)[:4]


def down_kernel(
    run, hid_ref, da_ref, db_ref, after_ref, rows_ref, gains_ref, near_ref, back_ref, x_ref, ag_ref, down_ref,
    out_ref, gate_ref, up_ref, total_ref, tokens_ref, wide_ref,
    hid, da, db, after, acc, pieces, gains, near, back, xs, down, loads, p_send, p_recv, g_send, g_recv,
    ebuf, rd, rxy, rs_send, rs_recv,
):
    length = after.shape[0]
    fn = da.shape[0]
    size, rows, _ = pieces.shape
    me = lax.axis_index("dp")
    x, y, _, _ = partners(me)
    others = everyone(me)
    scatter = Scatter(acc, ebuf, rd, rxy, rs_send, rs_recv, x, y)

    def block(device):
        return rows_ref.at[pl.ds(pl.multiple_of((device % size) * rows, rows), rows)]

    own = pltpu.make_async_copy(block(me), pieces.at[me % size], loads.at[0])
    copies = [
        remote(block(device), pieces.at[me % size], p_send.at[i], p_recv.at[i], device)
        for i, device in enumerate(others)
    ]
    own_gains = pltpu.make_async_copy(gains_ref.at[me % size], gains.at[me % size], loads.at[5])
    gain_copies = [
        remote(gains_ref.at[device % size], gains.at[me % size], g_send.at[i], g_recv.at[i], device)
        for i, device in enumerate(others)
    ]
    fills = [
        pltpu.make_async_copy(src, dst, loads.at[1 + i])
        for i, (src, dst) in enumerate(((hid_ref, hid), (da_ref, da), (db_ref, db), (after_ref, after)))
    ]
    extra = [
        pltpu.make_async_copy(near_ref, near, loads.at[6]),
        pltpu.make_async_copy(back_ref, back, loads.at[7]),
        pltpu.make_async_copy(x_ref, xs, loads.at[8]),
        pltpu.make_async_copy(down_ref, down, loads.at[9]),
    ]
    for copy in fills:
        copy.start()
    own.start()
    own_gains.start()
    for copy in extra:
        copy.start()
    greet(others)
    for copy in gain_copies:
        copy.start()
    for copy in fills:
        copy.wait()

    def part_of(k):
        sl = slice(k * length, (k + 1) * length)

        def tile_of(cut):
            value = dot(hid[sl, :fn], da[:, cut]) + dot(hid[sl, fn:], db[:, cut])
            return value + after[:, cut] if k == 0 else value

        return tile_of

    for k in ORDER[:3]:
        scatter.add(k, part_of(k))
    for copy in copies:
        copy.start()
    scatter.add(0, part_of(0))
    for copy in extra:
        copy.wait()

    step = 128

    @pl.loop(0, length // step)
    def _(t):
        sl = pl.ds(pl.multiple_of(t * step, step), step)
        values = xs[sl, :].astype(f32)
        inverse = inverse_rms(values)
        scaled = back[sl, :] * ag_ref[...]
        inner = jnp.mean(scaled * values, axis=-1, keepdims=True)
        tokens_ref[sl, :] = (
            near[sl, :] + inverse * (scaled - values * inverse * inverse * inner)
        ).astype(bf16)

    wide_ref[...] = down[...].astype(f32)
    own_gains.wait()
    for copy in gain_copies:
        copy.wait()
    total = jnp.sum(gains[...], axis=0)
    for g in range(total.shape[0]):
        total_ref[g] = total[g : g + 1]
    own.wait()
    for copy in copies:
        copy.wait()
    for source in range(size):
        piece = pieces[source].astype(f32)
        for g in range(fn // run):
            to = (g * size + source) * run
            gate_ref[:, to : to + run] = piece[:, g * run : (g + 1) * run]
            up_ref[:, to : to + run] = piece[:, fn + g * run : fn + (g + 1) * run]
    scatter.finish()
    out_ref[...] = acc[...].astype(bf16)


def down_forward(hid, da, db, after, mlp_rows, gains, near, back, x, ag, down, run):
    length, width = after.shape
    size = 2 * TP
    rows, cols = mlp_rows.shape[0] // size, mlp_rows.shape[1]
    ff = size * cols // 2
    anywhere = pl.BlockSpec(memory_space=pl.ANY)
    vmem = pl.BlockSpec(memory_space=pltpu.VMEM)
    sem = pltpu.SemaphoreType.DMA
    return pl.pallas_call(
        functools.partial(down_kernel, run),
        in_specs=[anywhere] * 9 + [vmem, anywhere],
        out_specs=[vmem] * 6,
        out_shape=[
            struct((length, width), bf16),
            struct((rows, ff), f32),
            struct((rows, ff), f32),
            struct((gains.shape[1], 1, gains.shape[2]), f32),
            struct((length, width), bf16),
            struct(down.shape, f32),
        ],
        scratch_shapes=[
            pltpu.VMEM(hid.shape, bf16),
            pltpu.VMEM(da.shape, bf16),
            pltpu.VMEM(db.shape, bf16),
            pltpu.VMEM(after.shape, f32),
            pltpu.VMEM(after.shape, f32),
            pltpu.VMEM((size, rows, cols), bf16),
            pltpu.VMEM(gains.shape, f32),
            pltpu.VMEM(after.shape, f32),
            pltpu.VMEM(after.shape, f32),
            pltpu.VMEM(x.shape, bf16),
            pltpu.VMEM(down.shape, bf16),
            sem((10,)), sem((size - 1,)), sem((size - 1,)), sem((size - 1,)), sem((size - 1,)),
        ]
        + scatter_scratch(length, width),
        compiler_params=pltpu.CompilerParams(
            vmem_limit_bytes=56 << 20, collective_id=7, has_side_effects=True
        ),
        cost_estimate=pl.CostEstimate(
            flops=2 * length * width * cols, bytes_accessed=30 << 20, transcendentals=0
        ),
        name="down_forward",
    )(hid, da, db, after, mlp_rows, gains, near, back, x, ag, down)


def return_kernel(
    rows_ref, gains_ref, q_ref, k_ref, v_ref, o_ref, total_ref, pieces, gains, send, recv, local, g_send, g_recv,
):
    size, rows, _ = pieces.shape
    me = lax.axis_index("dp")
    others = everyone(me)

    def block(device):
        return rows_ref.at[pl.ds(pl.multiple_of((device % size) * rows, rows), rows)]

    planes = gains.shape[0]
    plane = me // size
    column = [(plane + i) % planes for i in range(1, planes)]
    own = [
        pltpu.make_async_copy(block(me), pieces.at[me % size], local.at[0]),
        pltpu.make_async_copy(gains_ref.at[plane], gains.at[plane], local.at[1]),
    ]
    copies = [
        remote(block(device), pieces.at[me % size], send.at[i], recv.at[i], device)
        for i, device in enumerate(others)
    ]
    copies += [
        remote(gains_ref.at[to], gains.at[plane], g_send.at[i], g_recv.at[i], to * size + me % size)
        for i, to in enumerate(column)
    ]
    for copy in own:
        copy.start()
    greet(others + [to * size + me % size for to in column])
    for copy in copies:
        copy.start()
    for copy in own + copies:
        copy.wait()
    total_ref[...] = jnp.sum(gains[...], axis=0)
    for source in range(size):
        at = 0
        for ref in (q_ref, k_ref, v_ref, o_ref):
            width = ref.shape[1] // size
            ref[:, source * width : (source + 1) * width] = pieces[source, :, at : at + width].astype(f32)
            at += width


def return_attention(attn_rows, gains, widths):
    size = 2 * TP
    rows, cols = attn_rows.shape[0] // size, attn_rows.shape[1]
    sem = pltpu.SemaphoreType.DMA
    return pl.pallas_call(
        return_kernel,
        in_specs=[pl.BlockSpec(memory_space=pl.ANY)] * 2,
        out_specs=[pl.BlockSpec(memory_space=pltpu.VMEM)] * 5,
        out_shape=[struct((rows, w), f32) for w in widths] + [struct(gains.shape[1:], f32)],
        scratch_shapes=[
            pltpu.VMEM((size, rows, cols), bf16),
            pltpu.VMEM(gains.shape, f32),
            sem((size - 1,)), sem((size - 1,)), sem((2,)),
            sem((gains.shape[0] - 1,)), sem((gains.shape[0] - 1,)),
        ],
        compiler_params=pltpu.CompilerParams(collective_id=8, has_side_effects=True),
        name="return_attention",
    )(attn_rows, gains)


def make_body(n):
    m = n // (2 * TP)
    z_groups = [[g * 2 * TP + k for g in range(m)] for k in range(2 * TP)]

    def swap(v, bits):
        return lax.ppermute(v, "dp", [(a, a ^ bits) for a in range(n)])

    def gather_xy(v):
        h = v.shape[0] // 2
        x = swap(v, 2)
        y = swap(v, 4)
        d_low = swap(y[:h], 2)
        d_high = swap(x[h:], 4)
        return [v, x, y, jnp.concatenate([d_low, d_high])]

    def scatter_xy(p0, p1, p2, p3):
        h = p3.shape[0] // 2
        d_low = swap(p3[:h], 4)
        d_high = swap(p3[h:], 2)
        sx = jnp.concatenate([(p1[:h].astype(f32) + d_low.astype(f32)).astype(bf16), p1[h:]])
        sy = jnp.concatenate([p2[:h], (p2[h:].astype(f32) + d_high.astype(f32)).astype(bf16)])
        return p0 + swap(sx, 2).astype(f32) + swap(sy, 4).astype(f32)

    def gather_z(v):
        return lax.all_gather(v, "dp", axis=0, tiled=True, axis_index_groups=z_groups)

    def scatter_z(v):
        return lax.psum_scatter(
            v, "dp", scatter_dimension=0, tiled=True, axis_index_groups=z_groups
        )

    def body(
        tokens,
        segments,
        w_query,
        w_key,
        w_value,
        w_out,
        w_gate,
        w_up,
        w_down,
        attn_gain,
        mlp_gain,
        query_gain,
        key_gain,
        cotangent,
    ):
        me = lax.axis_index("dp")
        core = me % 2
        place = (me // 2) % TP
        length, width = tokens.shape
        rows = w_query.shape[0]
        ffr = w_down.shape[0]

        qn = w_query.shape[1] // (2 * TP)
        kn = w_key.shape[1] // (2 * TP)
        pn = qn + 2 * kn
        hr = query_gain.shape[0]
        gains = jnp.concatenate([attn_gain, mlp_gain, query_gain, key_gain]).astype(f32)
        count = gains.shape[0]
        padded = -(-count // 256) * 256
        attn_in, gains, seg_all = spread_attention(
            w_query, w_key, w_value, w_out, jnp.pad(gains, (0, padded - count))[None], segments
        )

        depth, wide = attn_in.shape
        gain_rows = gains.astype(bf16).reshape(-1, padded)
        below = jnp.pad(gain_rows, ((0, -gain_rows.shape[0] % 16), (0, wide - padded)))
        attn_all = gather_z(jnp.concatenate([attn_in, below])).reshape(m, -1, wide)
        tokens_in, _ = lax.optimization_barrier((tokens, attn_in))

        rate = THETA ** (-(jnp.arange(HD // 2, dtype=f32) * 2.0 / HD))
        sign = jnp.where(jnp.arange(HD) < HD // 2, -1.0, 1.0).astype(f32)
        rates = jnp.stack([jnp.concatenate([rate, rate]), sign])
        cosine, sine, starts, tokens_all, mlp_in = gather_group(
            seg_all, rates, tokens_in, w_gate, w_up, ffr
        )
        mlp_a = gather_z(mlp_in)
        tokens_all, attn_all = lax.optimization_barrier((tokens_all, attn_all))
        gains = attn_all[:, depth : depth + gain_rows.shape[0], :padded].reshape(n, padded)
        attn_scale = gains[:, :rows].reshape(-1).astype(f32)
        mlp_scale = gains[:, rows : 2 * rows].reshape(-1).astype(f32)
        query_scale = gains[:, 2 * rows : 2 * rows + hr].reshape(-1).astype(f32)
        key_scale = gains[:, 2 * rows + hr : count].reshape(-1).astype(f32)

        (
            raw, normed_one, mixed_own, after_attn, inv_two, proj_a, proj_b, out_full, normed_two_all
        ) = attend_forward(
            tokens_all, cosine, sine, starts, attn_scale[None], mlp_scale[None],
            query_scale[None], key_scale[None], attn_all, depth, pn, length,
        )

        inputs = tokens.astype(f32)
        mlp_a, normed_two_all, down_local = lax.optimization_barrier((mlp_a, normed_two_all, w_down))
        down_a = gather_z(down_local)
        fn = down_a.shape[0]

        gate_value, up_value, hidden, mlp_b, grad_all, down_sum = feed_forward(
            normed_two_all, mlp_a, cotangent
        )
        down_rows = scatter_z(down_sum)
        grad_normed_two, mlp_sum, down_b = feed_backward(
            gate_value, up_value, grad_all, down_a, mlp_a, mlp_b, normed_two_all, length
        )
        mlp_rows = scatter_z(mlp_sum)
        grad_normed_two, down_rows = lax.optimization_barrier((grad_normed_two, down_rows))

        grad_after, grad_after_low, mlp_gain_grad, grad_mixed = between(
            grad_normed_two, after_attn, inv_two, mlp_scale[None], cotangent, out_full
        )

        grad_normed_one, attn_sum, query_gain_grad, key_gain_grad = attend_backward(
            grad_mixed, raw, normed_one, proj_a, proj_b, cosine, sine, starts,
            query_scale[None], key_scale[None], mixed_own, grad_after_low, length,
        )
        attn_rows = scatter_z(attn_sum)
        attn_gain_grad = jnp.sum(grad_normed_one * inputs * inverse_rms(inputs), axis=0)

        gain_grads = jnp.concatenate(
            [
                attn_gain_grad.reshape(m, 2 * TP, -1),
                mlp_gain_grad.reshape(m, 2 * TP, -1),
                query_gain_grad.reshape(m, 2 * TP, -1),
                key_gain_grad.reshape(m, 2 * TP, -1),
                jnp.zeros((m, 2 * TP, padded - count), f32),
            ],
            axis=2,
        ).transpose(1, 0, 2)
        output, gate_shard, up_shard, gain_sums, tokens_grad, down_shard = down_forward(
            hidden, down_a, down_b, after_attn, mlp_rows, gain_grads, grad_after, grad_normed_one,
            tokens, attn_scale[None], down_rows, ffr,
        )
        attn_rows, output = lax.optimization_barrier((attn_rows, output))
        query_shard, key_shard, value_shard, out_shard, gain_grads = return_attention(
            attn_rows, gain_sums, [w.shape[1] for w in (w_query, w_key, w_value, w_out)]
        )

        gain_grads = gain_grads[0]

        return (
            output,
            tokens_grad,
            query_shard,
            key_shard,
            value_shard,
            out_shard,
            gate_shard,
            up_shard,
            down_shard,
            gain_grads[:rows],
            gain_grads[rows : 2 * rows],
            gain_grads[2 * rows : 2 * rows + hr],
            gain_grads[2 * rows + hr : count],
        )

    return body


def solution(mesh):
    row = P("dp", None)
    flat = P("dp")
    return jax.shard_map(
        make_body(mesh.shape["dp"]),
        mesh=mesh,
        in_specs=(row,) * 9 + (flat,) * 4 + (row,),
        out_specs=(row,) * 9 + (flat,) * 4,
        check_vma=False,
    )
```

```python
import functools

import jax
import jax.numpy as jnp
from jax import lax
from jax.experimental import pallas as pl
from jax.experimental.pallas import tpu as pltpu
from jax.sharding import PartitionSpec as P

H = 16
KVH = 8
HD = 128
TP = 4

EPS = 1e-06
THETA = 1000000.0

f32 = jnp.float32
bf16 = jnp.bfloat16
MESH = pl.DeviceIdType.MESH


def inverse_rms(values):
    return lax.rsqrt(jnp.mean(values * values, axis=-1, keepdims=True) + EPS)


def dot(a, b):
    return lax.dot_general(a, b, (((1,), (0,)), ((), ())), preferred_element_type=f32)


def dot_tn(a, b):
    return lax.dot_general(a, b, (((0,), (0,)), ((), ())), preferred_element_type=f32)


def dot_nt(a, b):
    return lax.dot_general(a, b, (((1,), (1,)), ((), ())), preferred_element_type=f32)


def turn(v):
    return pltpu.roll(v, HD // 2, 1)


def heads_of(raw, cosine, sine, query_gain, key_gain):
    out = []
    for k, gain in ((0, query_gain), (1, query_gain), (2, key_gain)):
        v = raw[:, k * HD : (k + 1) * HD]
        inverse = inverse_rms(v)
        normed = v * inverse * gain
        out.append((v, inverse, (normed * cosine + turn(normed) * sine).astype(bf16)))
    return out, raw[:, 3 * HD :].astype(bf16)


def block_probs(qs, keys, starts, row0, score_scale):
    size, span = starts.shape[0], keys.shape[0]
    scores = dot_nt(qs, keys) * score_scale
    column = lax.broadcasted_iota(jnp.int32, (size, span), 1)
    row = lax.broadcasted_iota(jnp.int32, (size, span), 0) + row0
    allowed = (column >= starts) & (column <= row)
    allowed = jnp.concatenate([allowed, allowed], axis=0)
    scores = jnp.where(allowed, scores, -1e30)
    power_term = jnp.exp(scores - jnp.max(scores, axis=-1, keepdims=True))
    return power_term / jnp.sum(power_term, axis=-1, keepdims=True)


def partners(me):
    x = me + 2 - 4 * ((me // 2) % 2)
    y = me + 4 - 8 * ((me // 4) % 2)
    d = x + 4 - 8 * ((me // 4) % 2)
    return x, y, d, me + 1 - 2 * (me % 2)


def greet(devices):
    barrier = pltpu.get_barrier_semaphore()
    for device in devices:
        pl.semaphore_signal(barrier, inc=1, device_id=(device,), device_id_type=MESH)
    pl.semaphore_wait(barrier, len(devices))


def remote(src, dst, send, recv, device):
    return pltpu.make_async_remote_copy(
        src_ref=src, dst_ref=dst, send_sem=send, recv_sem=recv, device_id=(device,), device_id_type=MESH
    )


TILE = 512


class Scatter:
    def __init__(self, out, ebuf, rd, rxy, send, recv, x, y):
        self.out, self.ebuf, self.rd, self.rxy = out, ebuf, rd, rxy
        length, width = out.shape
        h = length // 2
        self.half = h
        self.span = width // 2

        def pair(i, src, dst, rows, device):
            copies = []
            for c in range(2):
                cols = pl.ds(c * self.span, self.span)
                copies.append(
                    remote(
                        src[0].at[src[1], pl.ds(src[2], rows), cols],
                        dst[0].at[dst[1], pl.ds(dst[2], rows), cols],
                        send.at[i, c],
                        recv.at[i, c],
                        device,
                    )
                )
            return copies

        self.low = pair(0, (ebuf, 0, 0), (rd, 0, 0), h, y)
        self.high = pair(1, (ebuf, 0, h), (rd, 1, 0), h, x)
        self.to_x = pair(2, (ebuf, 1, 0), (rxy, 0, 0), length, x)
        self.to_y = pair(3, (ebuf, 2, 0), (rxy, 1, 0), length, y)

    def add(self, k, tile_of):
        h = self.half
        tiles = self.span // TILE
        for c in range(2):
            if k == 1:
                self.low[c].wait_recv()
            if k == 2:
                self.high[c].wait_recv()

            @pl.loop(c * tiles, (c + 1) * tiles)
            def _(t):
                sl = pl.ds(pl.multiple_of(t * TILE, TILE), TILE)
                value = tile_of(sl)
                if k == 0:
                    self.out[:, sl] = value
                elif k == 3:
                    self.ebuf[0, :, sl] = value.astype(bf16)
                elif k == 1:
                    self.ebuf[1, :h, sl] = (value[:h] + self.rd[0, :, sl].astype(f32)).astype(bf16)
                    self.ebuf[1, h:, sl] = value[h:].astype(bf16)
                else:
                    self.ebuf[2, :h, sl] = value[:h].astype(bf16)
                    self.ebuf[2, h:, sl] = (value[h:] + self.rd[1, :, sl].astype(f32)).astype(bf16)

            if k == 3:
                self.low[c].start()
                self.high[c].start()
            if k == 1:
                self.to_x[c].start()
            if k == 2:
                self.to_y[c].start()

    def finish(self):
        tiles = self.span // TILE
        for c in range(2):
            self.to_x[c].wait_recv()
            self.to_y[c].wait_recv()

            @pl.loop(c * tiles, (c + 1) * tiles)
            def _(t):
                sl = pl.ds(pl.multiple_of(t * TILE, TILE), TILE)
                self.out[:, sl] += self.rxy[0, :, sl].astype(f32) + self.rxy[1, :, sl].astype(f32)

        for copy in self.low + self.high + self.to_x + self.to_y:
            copy.wait_send()


def scatter_scratch(length, width):
    return [
        pltpu.VMEM((3, length, width), bf16),
        pltpu.VMEM((2, length // 2, width), bf16),
        pltpu.VMEM((2, length, width), bf16),
        pltpu.SemaphoreType.DMA((4, 2)),
        pltpu.SemaphoreType.DMA((4, 2)),
    ]


def attend_back_kernel(
    heads, raw_ref, a1_ref, pa_ref, pb_ref, cos_ref, sin_ref, start_ref, qg_ref, kg_ref, mix_ref, dy_ref, orecv_ref,
    out_ref, sum_ref, dqg_ref, dkg_ref, ogot_ref,
    gp_ref, dk_ref, dv_ref, acc_a, acc_b, cbuf, crecv, oslot, ofetch,
    ebuf, rd, rxy, rs_send, rs_recv, c_send, c_recv, os_send, os_recv, o_local,
):
    length = a1_ref.shape[0]
    step = 128
    score_scale = HD ** (-0.5)
    s = pl.program_id(0)
    me = lax.axis_index("dp")
    core = me % 2
    x, y, d, sibling = partners(me)
    scatter = Scatter(out_ref, ebuf, rd, rxy, rs_send, rs_recv, x, y)
    across = remote(cbuf, crecv, c_send, c_recv, sibling)
    block = oslot.shape[2]
    tall = oslot.shape[1] // 2
    o_low = remote(
        oslot.at[3, pl.ds(0, tall)], ogot_ref.at[2, pl.ds(0, tall)], os_send.at[2], os_recv.at[2], y
    )
    o_high = remote(
        oslot.at[3, pl.ds(tall, tall)], ogot_ref.at[2, pl.ds(tall, tall)], os_send.at[3], os_recv.at[3], x
    )
    o_home = [
        remote(oslot.at[k], ogot_ref.at[k - 1], os_send.at[k - 1], os_recv.at[k - 1], device)
        for k, device in ((1, x), (2, y))
    ]
    o_back = [
        pltpu.make_async_copy(ogot_ref.at[k - 1], oslot.at[k], o_local.at[k]) for k in range(1, 3)
    ]

    def out_block(k, side):
        device = (me, x, y, d)[k]
        at = ((device // 2) % TP) * 2 + side
        return pl.ds(pl.multiple_of(at * block, block), block)

    def out_tile(k, side, sl):
        return dot_tn(mix_ref[:, sl], dy_ref[:, out_block(k, side)])

    @pl.when(s == 0)
    def _():
        greet((x, y, d, sibling))
        for ref in (acc_a, acc_b, dqg_ref, dkg_ref):
            ref[...] = jnp.zeros_like(ref)
        for k in (3, 1, 2, 0):
            fetch = pltpu.make_async_copy(orecv_ref.at[k], ofetch, o_local.at[0])
            fetch.start()
            fetch.wait()

            @pl.loop(0, oslot.shape[1] // TILE)
            def _(t):
                sl = pl.ds(pl.multiple_of(t * TILE, TILE), TILE)
                oslot[k, sl, :] = (out_tile(k, core, sl) + ofetch[sl, :].astype(f32)).astype(bf16)

            if k == 3:
                o_low.start()
                o_high.start()

    @pl.when(s == 1)
    def _():
        for copy, k, offset in ((o_low, 1, 0), (o_high, 2, tall)):
            copy.wait_recv()
            fetch = pltpu.make_async_copy(
                ogot_ref.at[2, pl.ds(offset, tall)], ofetch.at[pl.ds(0, tall)], o_local.at[0]
            )
            fetch.start()
            fetch.wait()

            @pl.loop(0, tall // TILE)
            def _(t):
                sl = pl.ds(pl.multiple_of(t * TILE, TILE), TILE)
                to = pl.ds(pl.multiple_of(offset + t * TILE, TILE), TILE)
                oslot[k, to, :] = (oslot[k, to, :].astype(f32) + ofetch[sl, :].astype(f32)).astype(bf16)

            o_home[k - 1].start()

    which = part_order(s)

    for h in range(2):
        col = h * 4 * HD
        side = core if h == 0 else 1 - core
        cosine, sine = cos_ref[...], sin_ref[...]
        (q0, q1, k0), value = heads_of(
            raw_ref[:, col : col + 4 * HD], cosine, sine, qg_ref[...], kg_ref[...]
        )
        dk_ref[...] = jnp.zeros_like(dk_ref)
        dv_ref[...] = jnp.zeros_like(dv_ref)
        parts = []
        for b in range(length // step):
            sl = slice(b * step, (b + 1) * step)
            span = (b + 1) * step
            qs = jnp.concatenate([q0[2][sl], q1[2][sl]], axis=0)
            gs = jnp.concatenate(
                [
                    heads[which, sl, pl.ds(pl.multiple_of((2 * side + g) * HD, HD), HD)]
                    for g in range(2)
                ],
                axis=0,
            )
            keys, values = k0[2][:span], value[:span]
            probs = block_probs(qs, keys, start_ref[sl, :], b * step, score_scale)
            dv_ref[:span, :] += dot_tn(probs.astype(bf16), gs)
            grad_probs = dot_nt(gs, values)
            delta = jnp.sum(probs * grad_probs, axis=-1, keepdims=True)
            grad_scores = (probs * (grad_probs - delta)).astype(bf16)
            dk_ref[:span, :] += dot_tn(grad_scores, qs)
            parts.append(dot(grad_scores, keys))
        dq0 = jnp.concatenate([p[:step] for p in parts], axis=0) * score_scale
        dq1 = jnp.concatenate([p[step:] for p in parts], axis=0) * score_scale
        for k, (raw, inverse, _), grad, gain_ref, dgain_ref in (
            (0, q0, dq0, qg_ref, dqg_ref),
            (1, q1, dq1, qg_ref, dqg_ref),
            (2, k0, dk_ref[...] * score_scale, kg_ref, dkg_ref),
        ):
            back = grad * cosine + turn(grad * sine)
            scaled = back * gain_ref[...]
            inner = jnp.mean(scaled * raw, axis=-1, keepdims=True)
            gp_ref[:, col + k * HD : col + (k + 1) * HD] = (
                inverse * (scaled - raw * inverse * inverse * inner)
            ).astype(bf16)
            dgain_ref[...] += jnp.sum(back * raw * inverse, axis=0, keepdims=True)
        gp_ref[:, col + 3 * HD : col + 4 * HD] = dv_ref[...].astype(bf16)

    half = 4 * HD

    def tile_of(sl):
        return dot_nt(gp_ref[:, :half], pa_ref[sl, :]) + dot_nt(gp_ref[:, half:], pb_ref[sl, :])

    for at, k in enumerate(ORDER):

        @pl.when(s == at)
        def _():
            scatter.add(k, tile_of)

    @pl.loop(0, acc_a.shape[0] // TILE)
    def _(t):
        sl = pl.ds(pl.multiple_of(t * TILE, TILE), TILE)
        acc_b[sl, :] += dot_tn(a1_ref[:, sl], gp_ref[:, half:])

    @pl.when(s == 3)
    def _():
        cbuf[...] = acc_b[...].astype(bf16)
        across.start()

    @pl.loop(0, acc_a.shape[0] // TILE)
    def _(t):
        sl = pl.ds(pl.multiple_of(t * TILE, TILE), TILE)
        acc_a[sl, :] += dot_tn(a1_ref[:, sl], gp_ref[:, :half])

    @pl.when(s == 3)
    def _():
        proj = acc_a.shape[1]
        across.wait_recv()
        sum_ref[:, :proj] = (acc_a[...] + crecv[...].astype(f32)).astype(bf16)
        o_low.wait_send()
        o_high.wait_send()
        for copy, back in zip(o_home, o_back):
            copy.wait()
            back.start()
        for back in o_back:
            back.wait()

        @pl.loop(0, oslot.shape[1] // TILE)
        def _(t):
            sl = pl.ds(pl.multiple_of(t * TILE, TILE), TILE)
            total = oslot[0, sl, :].astype(f32)
            for k in range(1, 3):
                total += oslot[k, sl, :].astype(f32)
            sum_ref[sl, proj:] = total.astype(bf16)

        scatter.finish()
        across.wait_send()


CHUNK = 256


def feed_kernel(
    a2_ref, wa_ref, g_ref,
    gate_ref, up_ref, hid_ref, wb_ref, ga_ref, sum_ref,
    a2, wa, wb, g, hid, stage, cbuf, crecv, acc,
    loads, x_send, x_recv, g_send, g_recv, s_sem, c_send, c_recv, keeps,
):
    tokens, width = a2.shape
    length = g_ref.shape[0]
    fn = wa.shape[1] // 2
    x, y, d, sibling = partners(lax.axis_index("dp"))
    h = length // 2

    def rows(k, offset=0, size=length):
        return g.at[pl.ds(k * length + offset, size)]

    load_x = pltpu.make_async_copy(a2_ref, a2, loads.at[0])
    load_w = pltpu.make_async_copy(wa_ref, wa, loads.at[1])
    load_g = pltpu.make_async_copy(g_ref, rows(0), loads.at[2])
    swap_w = remote(wa_ref, wb, x_send.at[0], x_recv.at[0], sibling)
    g_x = remote(g_ref, rows(1), g_send.at[0], g_recv.at[0], x)
    g_y = remote(g_ref, rows(2), g_send.at[1], g_recv.at[1], y)
    g_low = remote(rows(2, 0, h), rows(3, 0, h), g_send.at[2], g_recv.at[2], x)
    g_high = remote(rows(1, h, h), rows(3, h, h), g_send.at[3], g_recv.at[3], y)
    keep_w = pltpu.make_async_copy(wb, wb_ref, keeps.at[0])
    keep_g = pltpu.make_async_copy(g, ga_ref, keeps.at[1])
    keep_h = pltpu.make_async_copy(hid, hid_ref, keeps.at[2])

    load_w.start()
    load_x.start()
    load_g.start()
    greet((x, y, d, sibling))
    g_x.start()
    g_y.start()
    swap_w.start()

    per_half = fn // CHUNK
    span = 2 * length
    halves = tokens // span

    def store(i, which, ref):
        half = i // (per_half * halves)
        j = i % (per_half * halves)
        r, c = j // per_half, j % per_half
        return pltpu.make_async_copy(
            stage.at[i % 2, which],
            ref.at[
                pl.ds(pl.multiple_of(r * span, span), span),
                pl.ds(pl.multiple_of((half * per_half + c) * CHUNK, CHUNK), CHUNK),
            ],
            s_sem.at[i % 2, which],
        )

    def run(half, w):
        @pl.loop(0, per_half * halves)
        def _(j):
            i = j + half * per_half * halves

            @pl.when(i >= 2)
            def _():
                store(i - 2, 0, gate_ref).wait()
                store(i - 2, 1, up_ref).wait()

            r, c = j // per_half, j % per_half
            sl = pl.ds(pl.multiple_of(r * span, span), span)
            gate = dot(a2[sl, :], w[:, pl.ds(pl.multiple_of(c * CHUNK, CHUNK), CHUNK)])
            up = dot(a2[sl, :], w[:, pl.ds(pl.multiple_of(fn + c * CHUNK, CHUNK), CHUNK)])
            stage[i % 2, 0] = gate.astype(bf16)
            stage[i % 2, 1] = up.astype(bf16)
            hid[sl, pl.ds(pl.multiple_of((half * per_half + c) * CHUNK, CHUNK), CHUNK)] = (
                gate * jax.nn.sigmoid(gate) * up
            ).astype(bf16)
            store(i, 0, gate_ref).start()
            store(i, 1, up_ref).start()

    load_w.wait()
    load_x.wait()
    run(0, wa)
    swap_w.wait_recv()
    keep_w.start()
    run(1, wb)
    last = 2 * per_half * halves
    for i in (last - 2, last - 1):
        store(i, 0, gate_ref).wait()
        store(i, 1, up_ref).wait()
    keep_h.start()

    g_x.wait_recv()
    g_high.start()
    g_y.wait_recv()
    g_low.start()
    load_g.wait()
    near = pl.ds(0, 3 * length)
    far = pl.ds(3 * length, length)

    @pl.loop(0, 2 * per_half)
    def _(t):
        cols = pl.ds(pl.multiple_of(t * CHUNK, CHUNK), CHUNK)
        acc[t] = dot_tn(hid[near, cols], g[near, :])

    g_low.wait_recv()
    g_high.wait_recv()
    keep_g.start()

    def across(t):
        return remote(cbuf.at[t], crecv.at[t], c_send.at[t], c_recv.at[t], sibling)

    @pl.loop(0, per_half)
    def _(t):
        cols = pl.ds(pl.multiple_of(fn + t * CHUNK, CHUNK), CHUNK)
        cbuf[t] = (acc[per_half + t] + dot_tn(hid[far, cols], g[far, :])).astype(bf16)
        across(t).start()

    @pl.loop(0, per_half)
    def _(t):
        cols = pl.ds(pl.multiple_of(t * CHUNK, CHUNK), CHUNK)
        own = acc[t] + dot_tn(hid[far, cols], g[far, :])
        across(t).wait_recv()
        sum_ref[cols, :] = (own + crecv[t].astype(f32)).astype(bf16)

    for t in range(per_half):
        across(t).wait_send()
    for copy in (swap_w, g_x, g_y, g_low, g_high):
        copy.wait_send()
    for copy in (keep_w, keep_g, keep_h):
        copy.wait()


def feed_forward(a2, wa, g):
    tokens, width = a2.shape
    fn = wa.shape[1] // 2
    length = g.shape[0]
    anywhere = pl.BlockSpec(memory_space=pl.ANY)
    sem = pltpu.SemaphoreType.DMA
    return pl.pallas_call(
        feed_kernel,
        in_specs=[anywhere] * 3,
        out_specs=[anywhere] * 5 + [pl.BlockSpec(memory_space=pltpu.VMEM)],
        out_shape=[
            struct((tokens, 2 * fn), bf16),
            struct((tokens, 2 * fn), bf16),
            struct((tokens, 2 * fn), bf16),
            struct(wa.shape, bf16),
            struct((tokens, width), bf16),
            struct((fn, width), bf16),
        ],
        scratch_shapes=[
            pltpu.VMEM(a2.shape, bf16),
            pltpu.VMEM(wa.shape, bf16),
            pltpu.VMEM(wa.shape, bf16),
            pltpu.VMEM(a2.shape, bf16),
            pltpu.VMEM((tokens, 2 * fn), bf16),
            pltpu.VMEM((2, 2, 2 * length, CHUNK), bf16),
            pltpu.VMEM((fn // CHUNK, CHUNK, width), bf16),
            pltpu.VMEM((fn // CHUNK, CHUNK, width), bf16),
            pltpu.VMEM((2 * fn // CHUNK, CHUNK, width), f32),
            sem((3,)), sem((2,)), sem((2,)), sem((4,)), sem((4,)), sem((2, 2)),
            sem((fn // CHUNK,)), sem((fn // CHUNK,)), sem((3,)),
        ],
        compiler_params=pltpu.CompilerParams(
            vmem_limit_bytes=58 << 20, collective_id=4, has_side_effects=True
        ),
        cost_estimate=pl.CostEstimate(
            flops=4 * tokens * width * fn, bytes_accessed=30 << 20, transcendentals=0
        ),
        name="feed_forward",
    )(a2, wa, g)


def feed_back_kernel(
    gate_ref, up_ref, ga_ref, da_ref, wa_ref, wb_ref, a2_ref,
    out_ref, sum_ref, db_ref, crecv_ref,
    gp, wa, wb, a2, wd, uv, cbuf, cgot, stage, loads, u_sem, c_send, c_recv, g_sem, s_sem,
    d_send, d_recv,
    ebuf, rd, rxy, rs_send, rs_recv,
):
    length = out_ref.shape[0]
    cols = wa.shape[1]
    fn = cols // 2
    rows = cbuf.shape[1]
    tiles = a2.shape[1] // rows
    x, y, d, sibling = partners(lax.axis_index("dp"))
    scatter = Scatter(out_ref, ebuf, rd, rxy, rs_send, rs_recv, x, y)

    def piece(k):
        sl = pl.ds(k * length, length)
        return pltpu.make_async_copy(ga_ref.at[sl], a2.at[sl], loads.at[k])

    load_a = pltpu.make_async_copy(wa_ref, wa, loads.at[4])
    load_b = pltpu.make_async_copy(wb_ref, wb, loads.at[5])
    load_da = pltpu.make_async_copy(da_ref, wd.at[pl.ds(0, fn)], loads.at[6])
    swap_d = remote(da_ref, wd.at[pl.ds(fn, fn)], d_send, d_recv, sibling)
    keep_d = pltpu.make_async_copy(wd.at[pl.ds(fn, fn)], db_ref, loads.at[7])
    load_x = pltpu.make_async_copy(a2_ref, a2, loads.at[8])
    steps = 2 * TP

    def step_of(i):
        return part_order(i // 2), i % 2

    def fetch_uv(i, which, ref):
        part, c = step_of(i)
        return pltpu.make_async_copy(
            ref.at[
                pl.ds(pl.multiple_of(part * length, length), length),
                pl.ds(pl.multiple_of(c * fn, CHUNK), fn),
            ],
            uv.at[i % 2, which],
            u_sem.at[i % 2, which],
        )

    fetch_uv(0, 0, gate_ref).start()
    fetch_uv(0, 1, up_ref).start()
    piece(3).start()
    load_da.start()
    greet((x, y, d, sibling))
    swap_d.start()
    load_a.start()
    load_b.start()
    for k in (1, 2, 0):
        piece(k).start()

    def rows_of(t):
        return pl.ds(pl.multiple_of(t * rows, rows), rows)

    def across(t):
        return remote(
            cbuf.at[t % 2], crecv_ref.at[rows_of(t)], c_send.at[t % 2], c_recv.at[t], sibling
        )

    def fetch(t):
        return pltpu.make_async_copy(crecv_ref.at[rows_of(t)], cgot.at[t % 2], g_sem.at[t % 2])

    def store(t):
        return pltpu.make_async_copy(stage.at[t % 2], sum_ref.at[rows_of(t)], s_sem.at[t % 2])

    def part_of(k):
        sl = slice(k * length, (k + 1) * length)

        def tile_of(cut):
            return dot_nt(gp[sl, :cols], wa[cut, :]) + dot_nt(gp[sl, cols:], wb[cut, :])

        return tile_of

    def inner(first, end):
        @pl.loop(first, end)
        def _(i):
            @pl.when(i + 1 < steps)
            def _():
                fetch_uv(i + 1, 0, gate_ref).start()
                fetch_uv(i + 1, 1, up_ref).start()

            part, half = step_of(i)
            sl = pl.ds(pl.multiple_of(part * length, length), length)
            fetch_uv(i, 0, gate_ref).wait()
            fetch_uv(i, 1, up_ref).wait()
            for at in range(0, fn, CHUNK):
                cut = slice(at, at + CHUNK)
                rows_at = pl.ds(pl.multiple_of(half * fn + at, CHUNK), CHUNK)
                grad_hidden = dot_nt(a2[sl, :], wd[rows_at, :])
                gate = uv[i % 2, 0, :, cut].astype(f32)
                up = uv[i % 2, 1, :, cut].astype(f32)
                sig = jax.nn.sigmoid(gate)
                scaled = grad_hidden * sig
                to = half * cols + at
                gp[sl, pl.ds(pl.multiple_of(to, CHUNK), CHUNK)] = (
                    scaled * up * (1.0 + gate * (1.0 - sig))
                ).astype(bf16)
                gp[sl, pl.ds(pl.multiple_of(to + fn, CHUNK), CHUNK)] = (scaled * gate).astype(bf16)

    piece(3).wait()
    load_da.wait()
    inner(0, 1)
    swap_d.wait_recv()
    keep_d.start()
    inner(1, 2)
    load_a.wait()
    load_b.wait()
    scatter.add(3, part_of(3))
    for k in (1, 2, 0):
        piece(k).wait()
    inner(2, steps)
    load_x.start()
    scatter.add(1, part_of(1))
    scatter.add(2, part_of(2))
    load_x.wait()

    @pl.loop(0, tiles)
    def _(t):
        @pl.when(t >= 2)
        def _():
            across(t - 2).wait_send()

        cbuf[t % 2] = dot_tn(a2[:, rows_of(t)], gp[:, cols:]).astype(bf16)
        across(t).start()

    scatter.add(0, part_of(0))

    @pl.loop(0, tiles)
    def _(t):
        across(t).wait_recv()
        fetch(t).start()

        @pl.when(t >= 2)
        def _():
            store(t - 2).wait()

        own = dot_tn(a2[:, rows_of(t)], gp[:, :cols])
        fetch(t).wait()
        stage[t % 2] = (own + cgot[t % 2].astype(f32)).astype(bf16)
        store(t).start()

    for t in (tiles - 2, tiles - 1):
        store(t).wait()
        across(t).wait_send()
    swap_d.wait_send()
    keep_d.wait()
    scatter.finish()


def feed_backward(gate, up, ga, da, wa, wb, a2, length):
    tokens, width = a2.shape
    cols = wa.shape[1]
    rows = 256
    anywhere = pl.BlockSpec(memory_space=pl.ANY)
    sem = pltpu.SemaphoreType.DMA
    return pl.pallas_call(
        feed_back_kernel,
        in_specs=[anywhere] * 7,
        out_specs=[pl.BlockSpec(memory_space=pltpu.VMEM), anywhere, anywhere, anywhere],
        out_shape=[
            struct((length, width), f32),
            struct(wa.shape, bf16),
            struct(da.shape, bf16),
            struct(wa.shape, bf16),
        ],
        scratch_shapes=[
            pltpu.VMEM((tokens, 2 * cols), bf16),
            pltpu.VMEM(wa.shape, bf16),
            pltpu.VMEM(wb.shape, bf16),
            pltpu.VMEM(a2.shape, bf16),
            pltpu.VMEM((cols, width), bf16),
            pltpu.VMEM((2, 2, length, cols // 2), bf16),
            pltpu.VMEM((2, rows, cols), bf16),
            pltpu.VMEM((2, rows, cols), bf16),
            pltpu.VMEM((2, rows, cols), bf16),
            sem((9,)), sem((2, 2)), sem((2,)), sem((width // rows,)), sem((2,)), sem((2,)),
            sem, sem,
        ]
        + scatter_scratch(length, width),
        compiler_params=pltpu.CompilerParams(
            vmem_limit_bytes=62 << 20, collective_id=1, has_side_effects=True
        ),
        cost_estimate=pl.CostEstimate(
            flops=4 * tokens * width * cols, bytes_accessed=30 << 20, transcendentals=0
        ),
        name="feed_backward",
    )(gate, up, ga, da, wa, wb, a2)[:3]


ORDER = (3, 1, 2, 0)


def part_order(s):
    return 3 - 2 * s + 3 * (s // 2)


def rows_spec(length, cols):
    return pl.BlockSpec((length, cols), lambda s: (s, 0))


def whole_spec(shape):
    return pl.BlockSpec(shape, lambda s: (0, 0))


def struct(shape, dtype):
    return jax.ShapeDtypeStruct(shape, dtype)


def everyone(me):
    size = 2 * TP
    base = me - me % size
    return [base + (me % size + i) % size for i in range(1, size)]


def spread_kernel(
    wq_ref, wk_ref, wv_ref, wo_ref, gain_ref, seg_ref,
    all_ref, gains_ref, segs_ref,
    send, recv, local, s_send, s_recv,
):
    me = lax.axis_index("dp")
    size = 2 * TP
    rows = wq_ref.shape[0]
    here = pl.ds(pl.multiple_of((me % size) * rows, rows), rows)
    plan = []
    at = 0
    for ref in (wq_ref, wk_ref, wv_ref, wo_ref):
        width = ref.shape[1] // size
        plan.append((ref, width, all_ref.at[here, pl.ds(at, width)]))
        at += width

    def columns(ref, width, device):
        return ref.at[:, pl.ds(pl.multiple_of((device % size) * width, width), width)]

    others = everyone(me)
    gains_here = gains_ref.at[me % size]
    own = [
        pltpu.make_async_copy(columns(ref, width, me), dst, local.at[t])
        for t, (ref, width, dst) in enumerate(plan)
    ] + [
        pltpu.make_async_copy(gain_ref, gains_here, local.at[4]),
        pltpu.make_async_copy(seg_ref, segs_ref.at[0], local.at[5]),
    ]
    copies = [
        remote(columns(ref, width, device), dst, send.at[i, t], recv.at[i, t], device)
        for i, device in enumerate(others)
        for t, (ref, width, dst) in enumerate(plan)
    ]
    copies += [
        remote(gain_ref, gains_here, send.at[i, 4], recv.at[i, 4], device)
        for i, device in enumerate(others)
    ]
    copies += [
        remote(seg_ref, segs_ref.at[1 + k], s_send.at[k], s_recv.at[k], device)
        for k, device in enumerate(partners(me)[:3])
    ]
    for copy in own:
        copy.start()
    greet(others)
    for copy in copies:
        copy.start()
    for copy in own + copies:
        copy.wait()


def spread_attention(wq, wk, wv, wo, gain, seg):
    size = 2 * TP
    rows = wq.shape[0]
    cols = (wq.shape[1] + wk.shape[1] + wv.shape[1] + wo.shape[1]) // size
    anywhere = pl.BlockSpec(memory_space=pl.ANY)
    sem = pltpu.SemaphoreType.DMA
    return pl.pallas_call(
        spread_kernel,
        in_specs=[anywhere] * 6,
        out_specs=[anywhere] * 3,
        out_shape=[
            struct((size * rows, cols), bf16),
            struct((size, *gain.shape), f32),
            struct((TP, *seg.shape), jnp.int32),
        ],
        scratch_shapes=[sem((size - 1, 5)), sem((size - 1, 5)), sem((6,)), sem((3,)), sem((3,))],
        compiler_params=pltpu.CompilerParams(collective_id=5, has_side_effects=True),
        name="spread_attention",
    )(wq, wk, wv, wo, gain, seg)


def gather_kernel(
    run, seg_ref, rate_ref, x_ref, gate_ref, up_ref,
    cos_ref, sin_ref, start_ref, x_all, w_all,
    w_ref, flat, wide, xs, x_send, x_recv, w_send, w_recv, local,
):
    me = lax.axis_index("dp")
    size = 2 * TP
    x, y, d, _ = partners(me)
    others = everyone(me)
    length = x_ref.shape[0]
    rows = w_ref.shape[1]
    h = length // 2
    here = pl.ds(pl.multiple_of((me % size) * rows, rows), rows)

    def place(k, offset=0, count=length):
        return x_all.at[pl.ds(k * length + offset, count)]

    own = [
        pltpu.make_async_copy(xs, place(0), local.at[0]),
        pltpu.make_async_copy(w_ref.at[me % size], w_all.at[here], local.at[1]),
    ]
    fills = [
        pltpu.make_async_copy(ref, flat.at[i], local.at[2 + i]) for i, ref in enumerate((gate_ref, up_ref))
    ]
    weights = [
        remote(w_ref.at[device % size], w_all.at[here], w_send.at[i], w_recv.at[i], device)
        for i, device in enumerate(others)
    ]
    to_x = remote(xs, place(1), x_send.at[0], x_recv.at[0], x)
    to_y = remote(xs, place(2), x_send.at[1], x_recv.at[1], y)
    load_x = pltpu.make_async_copy(x_ref, xs, local.at[4])
    low = remote(place(2, 0, h), place(3, 0, h), x_send.at[2], x_recv.at[2], x)
    high = remote(place(1, h, h), place(3, h, h), x_send.at[3], x_recv.at[3], y)
    for copy in [load_x] + fills:
        copy.start()
    greet(others)
    load_x.wait()
    for copy in (to_x, to_y, own[0]):
        copy.start()
    for copy in fills:
        copy.wait()
    half = wide.shape[1] // 2
    values = [flat[i].astype(f32) for i in range(2)]
    for s in range(size):
        for i in range(2):
            for g in range(half // run):
                at = (g * size + s) * run
                wide[:, i * half + g * run : i * half + (g + 1) * run] = values[i][:, at : at + run]
        w_ref[s] = wide[...].astype(bf16)
    for copy in own[1:] + weights:
        copy.start()

    row = lax.broadcasted_iota(jnp.int32, (length, length), 0)
    column = lax.broadcasted_iota(jnp.int32, (length, length), 1)
    for k in range(TP):
        label = jnp.broadcast_to(seg_ref[k].astype(f32), (length, length))
        mine = jnp.sum(jnp.where(row == column, label, 0.0), axis=1, keepdims=True)
        start = jnp.sum(jnp.where(label < mine, 1.0, 0.0), axis=1, keepdims=True)
        position = lax.broadcasted_iota(jnp.int32, (length, 1), 0).astype(f32) - start
        angle = position * rate_ref[0:1, :]
        sl = pl.ds(k * length, length)
        cos_ref[sl, :] = jnp.cos(angle)
        sin_ref[sl, :] = jnp.sin(angle) * rate_ref[1:2, :]
        start_ref[sl, :] = start.astype(jnp.int32)

    to_x.wait_recv()
    high.start()
    to_y.wait_recv()
    low.start()
    for copy in (to_x, to_y):
        copy.wait_send()
    for copy in own + weights + [low, high]:
        copy.wait()


def gather_group(seg, rates, x, gate, up, run):
    size = 2 * TP
    rows, cols = gate.shape[0], 2 * gate.shape[1] // size
    anywhere = pl.BlockSpec(memory_space=pl.ANY)
    vmem = pl.BlockSpec(memory_space=pltpu.VMEM)
    sem = pltpu.SemaphoreType.DMA
    return pl.pallas_call(
        functools.partial(gather_kernel, run),
        in_specs=[vmem] * 2 + [anywhere] * 3,
        out_specs=[vmem] * 3 + [anywhere] * 2,
        out_shape=[
            struct((TP * x.shape[0], HD), f32),
            struct((TP * x.shape[0], HD), f32),
            struct((TP * x.shape[0], 1), jnp.int32),
            struct((TP * x.shape[0], x.shape[1]), bf16),
            struct((size * rows, cols), bf16),
        ],
        scratch_shapes=[
            pltpu.VMEM((size, rows, cols), bf16),
            pltpu.VMEM((2, *gate.shape), bf16),
            pltpu.VMEM((rows, cols), f32),
            pltpu.VMEM(x.shape, bf16),
            sem((4,)), sem((4,)), sem((size - 1,)), sem((size - 1,)), sem((5,)),
        ],
        compiler_params=pltpu.CompilerParams(
            vmem_limit_bytes=60 << 20, collective_id=6, has_side_effects=True
        ),
        name="gather_group",
    )(seg, rates, x, gate, up)


def attend_kernel(
    x_ref, cos_ref, sin_ref, start_ref, ag_ref, mg_ref, qg_ref, kg_ref, all_ref,
    raw_ref, a1_ref, mixed_ref, after_ref, inv_ref, pa_out, pb_out, wo_ref, a2_ref,
    pa_ref, pb_ref, fill, heads, mix, wo, a2, p_send, p_recv, o_send, o_recv, w_send, w_recv, s_send, s_recv, a_send, a_recv, local,
):
    length, width = x_ref.shape
    step = 128
    score_scale = HD ** (-0.5)
    s = pl.program_id(0)
    me = lax.axis_index("dp")
    core = me % 2
    place = (me // 2) % TP
    x, y, d, sibling = partners(me)
    near = (x, y, d)
    cols = 4 * HD
    proj = pa_ref.shape[1]
    block = all_ref.shape[2] - proj
    planes = all_ref.shape[0]
    deep = pa_ref.shape[0] // planes

    def block_of(device):
        return pl.ds(pl.multiple_of((device % (2 * TP)) * block, block), block)

    own_out = wo.at[:, block_of(me)]
    fills = []
    for g in range(planes):
        at = pl.ds(g * deep, deep)
        fills.append(
            pltpu.make_async_copy(
                all_ref.at[g, pl.ds(0, deep), pl.ds(0, proj)], pa_ref.at[at], fill.at[g, 0]
            )
        )
        fills.append(
            pltpu.make_async_copy(
                all_ref.at[g, pl.ds(0, deep), pl.ds(proj, block)], wo.at[at, block_of(me)], fill.at[g, 1]
            )
        )

    tall = wo.shape[0] // 2
    spread_out = [
        remote(own_out, own_out, w_send.at[i], w_recv.at[i], device)
        for i, device in enumerate(near[:2])
    ]

    def passed(device, offset, i, to):
        ref = wo.at[pl.ds(offset, tall), block_of(device)]
        return remote(ref, ref, w_send.at[i], w_recv.at[i], to)

    pass_on = [passed(x, tall, 2, y), passed(y, 0, 3, x)]
    beside = [remote(own_out, own_out, s_send.at[3], s_recv.at[3], sibling)]
    onward = [
        remote(wo.at[:, block_of(device)], wo.at[:, block_of(device)], s_send.at[i], s_recv.at[i], sibling)
        for i, device in enumerate(near)
    ]
    mine = pl.ds(pl.multiple_of(place * cols, cols), cols)
    home = [
        remote(heads.at[i + 1], mix.at[:, mine], o_send.at[i], o_recv.at[i], device)
        for i, device in enumerate(near)
    ]
    h = length // 2
    a2_x = remote(a2.at[0], a2.at[1], a_send.at[0], a_recv.at[0], x)
    a2_y = remote(a2.at[0], a2.at[2], a_send.at[1], a_recv.at[1], y)
    a2_low = remote(a2.at[2, pl.ds(0, h)], a2.at[3, pl.ds(0, h)], a_send.at[2], a_recv.at[2], x)
    a2_high = remote(a2.at[1, pl.ds(h, h)], a2.at[3, pl.ds(h, h)], a_send.at[3], a_recv.at[3], y)
    keep = [
        pltpu.make_async_copy(a2.at[k], a2_ref.at[pl.ds(k * length, length)], local.at[1 + k])
        for k in range(TP)
    ]
    keep_out = pltpu.make_async_copy(wo, wo_ref, local.at[5])
    keep_b = pltpu.make_async_copy(pb_ref, pb_out, local.at[6])
    keep_a = pltpu.make_async_copy(pa_ref, pa_out, local.at[0])
    swap_p = remote(pa_ref, pb_ref, p_send, p_recv, sibling)

    @pl.when(s == 0)
    def _():
        for copy in fills:
            copy.start()
        greet((x, y, d, sibling))
        for copy in fills:
            copy.wait()
        for copy in [swap_p] + spread_out + beside:
            copy.start()
        keep_a.start()

    @pl.when(s == 3)
    def _():
        for i in range(2):
            spread_out[i].wait_recv()
            pass_on[i].start()
            onward[i].start()

    @pl.loop(0, length // step)
    def _(t):
        sl = pl.ds(pl.multiple_of(t * step, step), step)
        v = x_ref[sl, :].astype(f32)
        a1_ref[sl, :] = (v * inverse_rms(v) * ag_ref[...]).astype(bf16)

    which = part_order(s)
    for half, p_ref in ((0, pa_ref), (1, pb_ref)):
        side = core if half == 0 else 1 - core
        if half:

            @pl.when(s == 0)
            def _():
                swap_p.wait_recv()
                keep_b.start()

        raw_ref[:, half * cols : (half + 1) * cols] = dot(a1_ref[...], p_ref[...])
        (q0, q1, k0), value = heads_of(
            raw_ref[:, half * cols : (half + 1) * cols], cos_ref[...], sin_ref[...], qg_ref[...], kg_ref[...]
        )
        for b in range(length // step):
            sl = slice(b * step, (b + 1) * step)
            span = (b + 1) * step
            qs = jnp.concatenate([q0[2][sl], q1[2][sl]], axis=0)
            probs = block_probs(qs, k0[2][:span], start_ref[sl, :], b * step, score_scale)
            mixed = dot(probs.astype(bf16), value[:span]).astype(bf16)
            for g in range(2):
                at = pl.ds(pl.multiple_of((2 * side + g) * HD, HD), HD)
                heads[which, sl, at] = mixed[g * step : (g + 1) * step]

    for at, k in enumerate(ORDER[:3]):

        @pl.when(s == at)
        def _():
            home[k - 1].start()

    @pl.when(s == 3)
    def _():
        mix[:, mine] = heads[0]
        for copy in pass_on:
            copy.wait_recv()
        onward[2].start()
        for copy in home:
            copy.wait_recv()
        for copy in beside + onward:
            copy.wait_recv()
        keep_out.start()

        @pl.loop(0, width // TILE)
        def _(t):
            sl = pl.ds(pl.multiple_of(t * TILE, TILE), TILE)
            after_ref[:, sl] = x_ref[:, sl].astype(f32) + dot(mix[...], wo[:, sl])

        @pl.loop(0, length // step)
        def _(t):
            sl = pl.ds(pl.multiple_of(t * step, step), step)
            v = after_ref[sl, :]
            inverse = inverse_rms(v)
            inv_ref[sl, :] = inverse
            a2[0, sl, :] = (v * inverse * mg_ref[...]).astype(bf16)

        a2_x.start()
        a2_y.start()
        keep[0].start()
        mixed_ref[...] = mix[...]
        a2_x.wait_recv()
        a2_high.start()
        keep[1].start()
        a2_y.wait_recv()
        a2_low.start()
        keep[2].start()
        a2_high.wait_recv()
        a2_low.wait_recv()
        keep[3].start()
        for copy in spread_out + pass_on + beside + onward + home + [a2_x, a2_y, a2_low, a2_high]:
            copy.wait_send()
        swap_p.wait_send()
        for copy in keep + [keep_out, keep_a, keep_b]:
            copy.wait()


def attend_forward(x, cosine, sine, starts, ag, mg, qg, kg, weights, depth, proj, length):
    tokens, width = x.shape
    planes = weights.shape[0]
    total = planes * depth
    anywhere = pl.BlockSpec(memory_space=pl.ANY)

    def in_order(cols):
        return pl.BlockSpec((length, cols), lambda s: (part_order(s), 0))

    return pl.pallas_call(
        attend_kernel,
        grid=(TP,),
        in_specs=[in_order(width)]
        + [in_order(HD), in_order(HD), in_order(1)]
        + [whole_spec(g.shape) for g in (ag, mg, qg, kg)]
        + [anywhere],
        out_specs=[in_order(8 * HD), in_order(width)]
        + [whole_spec((length, width))] * 2
        + [whole_spec((length, 1))]
        + [anywhere] * 4,
        out_shape=[
            struct((tokens, 8 * HD), f32),
            struct((tokens, width), bf16),
            struct((length, width), bf16),
            struct((length, width), f32),
            struct((length, 1), f32),
            struct((total, proj), bf16),
            struct((total, proj), bf16),
            struct((total, width), bf16),
            struct((tokens, width), bf16),
        ],
        scratch_shapes=[
            pltpu.VMEM((total, proj), bf16),
            pltpu.VMEM((total, proj), bf16),
            pltpu.SemaphoreType.DMA((planes, 2)),
            pltpu.VMEM((TP, length, 4 * HD), bf16),
            pltpu.VMEM((length, width), bf16),
            pltpu.VMEM((total, width), bf16),
            pltpu.VMEM((TP, length, width), bf16),
            pltpu.SemaphoreType.DMA,
            pltpu.SemaphoreType.DMA,
            pltpu.SemaphoreType.DMA((3,)),
            pltpu.SemaphoreType.DMA((3,)),
            pltpu.SemaphoreType.DMA((4,)),
            pltpu.SemaphoreType.DMA((4,)),
            pltpu.SemaphoreType.DMA((4,)),
            pltpu.SemaphoreType.DMA((4,)),
            pltpu.SemaphoreType.DMA((4,)),
            pltpu.SemaphoreType.DMA((4,)),
            pltpu.SemaphoreType.DMA((7,)),
        ],
        compiler_params=pltpu.CompilerParams(
            vmem_limit_bytes=56 << 20, collective_id=3, has_side_effects=True
        ),
        cost_estimate=pl.CostEstimate(
            flops=2 * tokens * width * 8 * HD, bytes_accessed=30 << 20, transcendentals=0
        ),
        name="attend_forward",
    )(x, cosine, sine, starts, ag, mg, qg, kg, weights)


def between_kernel(
    grad_ref, after_ref, inv_ref, gain_ref, cot_ref, mix_ref, w_ref,
    sum_ref, dy_ref, dgain_ref, heads_ref, orecv_ref,
    w, heads, oslot, loads, h_send, h_recv, o_send, o_recv,
):
    length, width = after_ref.shape
    step = 128
    me = lax.axis_index("dp")
    core = me % 2
    x, y, d, sibling = partners(me)
    places = (me, x, y, d)
    cols = heads.shape[2]
    block = oslot.shape[2]

    def rows_of(device):
        return pl.ds(pl.multiple_of(((device // 2) % TP) * cols, cols), cols)

    load = [
        pltpu.make_async_copy(w_ref.at[rows_of(device)], w.at[k], loads.at[k])
        for k, device in enumerate(places)
    ]
    home = [
        remote(heads.at[k], heads_ref.at[k], h_send.at[k - 1], h_recv.at[k - 1], places[k])
        for k in range(1, TP)
    ]
    keep = pltpu.make_async_copy(heads.at[0], heads_ref.at[0], loads.at[TP])
    across = [
        remote(oslot.at[k], orecv_ref.at[k], o_send.at[k], o_recv.at[k], sibling) for k in range(TP)
    ]
    for k in ORDER:
        load[k].start()
    greet((x, y, d, sibling))
    dgain_ref[...] = jnp.zeros_like(dgain_ref)

    @pl.loop(0, length // step)
    def _(t):
        sl = pl.ds(pl.multiple_of(t * step, step), step)
        grad, values, inverse = grad_ref[sl, :], after_ref[sl, :], inv_ref[sl, :]
        scaled = grad * gain_ref[...]
        inner = jnp.mean(scaled * values, axis=-1, keepdims=True)
        total = cot_ref[sl, :].astype(f32) + inverse * (scaled - values * inverse * inverse * inner)
        sum_ref[sl, :] = total
        dy_ref[sl, :] = total.astype(bf16)
        dgain_ref[...] += jnp.sum(grad * values * inverse, axis=0, keepdims=True)

    def out_half(k):
        at = ((places[k] // 2) % TP) * 2 + 1 - core
        cut = pl.ds(pl.multiple_of(at * block, block), block)

        @pl.loop(0, oslot.shape[1] // TILE)
        def _(t):
            sl = pl.ds(pl.multiple_of(t * TILE, TILE), TILE)
            oslot[k, sl, :] = dot_tn(mix_ref[:, sl], dy_ref[:, cut]).astype(bf16)

        across[k].start()

    out_half(3)
    for k in ORDER:
        load[k].wait()
        heads[k] = dot_nt(dy_ref[...], w[k]).astype(bf16)
        if k:
            home[k - 1].start()
        else:
            keep.start()
    for k in ORDER[1:]:
        out_half(k)
    for copy in home + across:
        copy.wait()
    keep.wait()


def between(grad, after, inverse, gain, cot, mix, w):
    length, width = after.shape
    cols = w.shape[0] // TP
    block = width // (2 * TP)
    anywhere = pl.BlockSpec(memory_space=pl.ANY)
    vmem = pl.BlockSpec(memory_space=pltpu.VMEM)
    sem = pltpu.SemaphoreType.DMA
    return pl.pallas_call(
        between_kernel,
        in_specs=[vmem] * 6 + [anywhere],
        out_specs=[vmem] * 3 + [anywhere] * 2,
        out_shape=[
            struct((length, width), f32),
            struct((length, width), bf16),
            struct((1, width), f32),
            struct((TP, length, cols), bf16),
            struct((TP, width, block), bf16),
        ],
        scratch_shapes=[
            pltpu.VMEM((TP, cols, width), bf16),
            pltpu.VMEM((TP, length, cols), bf16),
            pltpu.VMEM((TP, width, block), bf16),
            sem((TP + 1,)), sem((3,)), sem((3,)), sem((TP,)), sem((TP,)),
        ],
        compiler_params=pltpu.CompilerParams(
            vmem_limit_bytes=60 << 20, collective_id=9, has_side_effects=True
        ),
        cost_estimate=pl.CostEstimate(
            flops=4 * length * width * w.shape[0], bytes_accessed=24 << 20, transcendentals=0
        ),
        name="between",
    )(grad, after, inverse, gain, cot, mix, w)


def attend_backward(heads, raw, a1, pa, pb, cosine, sine, starts, qg, kg, mix, dy, orecv, length):
    tokens, width = a1.shape
    block = width // (2 * TP)
    anywhere = pl.BlockSpec(memory_space=pl.ANY)
    sem = pltpu.SemaphoreType.DMA

    def in_order(cols):
        return pl.BlockSpec((length, cols), lambda s: (part_order(s), 0))

    def once(v):
        return pl.BlockSpec(v.shape, lambda s: (0, 0), pipeline_mode=pl.Buffered(1))

    return pl.pallas_call(
        attend_back_kernel,
        grid=(TP,),
        in_specs=[pl.BlockSpec(heads.shape, lambda s: (0, 0, 0), pipeline_mode=pl.Buffered(1))]
        + [in_order(c) for c in (8 * HD, width)]
        + [once(w) for w in (pa, pb)]
        + [in_order(HD), in_order(HD), in_order(1)]
        + [whole_spec(v.shape) for v in (qg, kg)]
        + [once(v) for v in (mix, dy)]
        + [anywhere],
        out_specs=[whole_spec((length, width)), whole_spec((width, pa.shape[1] + block))]
        + [whole_spec(v.shape) for v in (qg, kg)]
        + [anywhere],
        out_shape=[struct((length, width), f32), struct((width, pa.shape[1] + block), bf16)]
        + [struct(v.shape, f32) for v in (qg, kg)]
        + [struct((3, width, block), bf16)],
        scratch_shapes=[
            pltpu.VMEM((length, 8 * HD), bf16),
            pltpu.VMEM((length, HD), f32),
            pltpu.VMEM((length, HD), f32),
            pltpu.VMEM(pa.shape, f32),
            pltpu.VMEM(pa.shape, f32),
            pltpu.VMEM(pa.shape, bf16),
            pltpu.VMEM(pa.shape, bf16),
            pltpu.VMEM((TP, width, block), bf16),
            pltpu.VMEM((width, block), bf16),
        ]
        + scatter_scratch(length, width)
        + [sem, sem, sem((4,)), sem((4,)), sem((TP,))],
        compiler_params=pltpu.CompilerParams(
            vmem_limit_bytes=60 << 20, collective_id=2, has_side_effects=True
        ),
        cost_estimate=pl.CostEstimate(
            flops=2 * tokens * width * 8 * HD, bytes_accessed=30 << 20, transcendentals=0
        ),
        name="attend_backward",
    )(heads, raw, a1, pa, pb, cosine, sine, starts, qg, kg, mix, dy, orecv)[:4]


def down_kernel(
    run, hid_ref, da_ref, db_ref, after_ref, rows_ref, gains_ref, near_ref, back_ref, x_ref, ag_ref, down_ref,
    out_ref, gate_ref, up_ref, total_ref, tokens_ref, wide_ref,
    hid, da, db, after, acc, pieces, gains, near, back, xs, down, loads, p_send, p_recv, g_send, g_recv,
    ebuf, rd, rxy, rs_send, rs_recv,
):
    length = after.shape[0]
    fn = da.shape[0]
    size, rows, _ = pieces.shape
    me = lax.axis_index("dp")
    x, y, _, _ = partners(me)
    others = everyone(me)
    scatter = Scatter(acc, ebuf, rd, rxy, rs_send, rs_recv, x, y)

    def block(device):
        return rows_ref.at[pl.ds(pl.multiple_of((device % size) * rows, rows), rows)]

    own = pltpu.make_async_copy(block(me), pieces.at[me % size], loads.at[0])
    copies = [
        remote(block(device), pieces.at[me % size], p_send.at[i], p_recv.at[i], device)
        for i, device in enumerate(others)
    ]
    own_gains = pltpu.make_async_copy(gains_ref.at[me % size], gains.at[me % size], loads.at[5])
    gain_copies = [
        remote(gains_ref.at[device % size], gains.at[me % size], g_send.at[i], g_recv.at[i], device)
        for i, device in enumerate(others)
    ]
    fills = [
        pltpu.make_async_copy(src, dst, loads.at[1 + i])
        for i, (src, dst) in enumerate(((hid_ref, hid), (da_ref, da), (db_ref, db), (after_ref, after)))
    ]
    extra = [
        pltpu.make_async_copy(near_ref, near, loads.at[6]),
        pltpu.make_async_copy(back_ref, back, loads.at[7]),
        pltpu.make_async_copy(x_ref, xs, loads.at[8]),
        pltpu.make_async_copy(down_ref, down, loads.at[9]),
    ]
    for copy in fills:
        copy.start()
    own.start()
    own_gains.start()
    for copy in extra:
        copy.start()
    greet(others)
    for copy in gain_copies:
        copy.start()
    for copy in fills:
        copy.wait()

    def part_of(k):
        sl = slice(k * length, (k + 1) * length)

        def tile_of(cut):
            value = dot(hid[sl, :fn], da[:, cut]) + dot(hid[sl, fn:], db[:, cut])
            return value + after[:, cut] if k == 0 else value

        return tile_of

    for k in ORDER[:3]:
        scatter.add(k, part_of(k))
    for copy in copies:
        copy.start()
    scatter.add(0, part_of(0))
    for copy in extra:
        copy.wait()

    step = 128

    @pl.loop(0, length // step)
    def _(t):
        sl = pl.ds(pl.multiple_of(t * step, step), step)
        values = xs[sl, :].astype(f32)
        inverse = inverse_rms(values)
        scaled = back[sl, :] * ag_ref[...]
        inner = jnp.mean(scaled * values, axis=-1, keepdims=True)
        tokens_ref[sl, :] = (
            near[sl, :] + inverse * (scaled - values * inverse * inverse * inner)
        ).astype(bf16)

    wide_ref[...] = down[...].astype(f32)
    own_gains.wait()
    for copy in gain_copies:
        copy.wait()
    total = jnp.sum(gains[...], axis=0)
    for g in range(total.shape[0]):
        total_ref[g] = total[g : g + 1]
    own.wait()
    for copy in copies:
        copy.wait()
    for source in range(size):
        piece = pieces[source].astype(f32)
        for g in range(fn // run):
            to = (g * size + source) * run
            gate_ref[:, to : to + run] = piece[:, g * run : (g + 1) * run]
            up_ref[:, to : to + run] = piece[:, fn + g * run : fn + (g + 1) * run]
    scatter.finish()
    out_ref[...] = acc[...].astype(bf16)


def down_forward(hid, da, db, after, mlp_rows, gains, near, back, x, ag, down, run):
    length, width = after.shape
    size = 2 * TP
    rows, cols = mlp_rows.shape[0] // size, mlp_rows.shape[1]
    ff = size * cols // 2
    anywhere = pl.BlockSpec(memory_space=pl.ANY)
    vmem = pl.BlockSpec(memory_space=pltpu.VMEM)
    sem = pltpu.SemaphoreType.DMA
    return pl.pallas_call(
        functools.partial(down_kernel, run),
        in_specs=[anywhere] * 9 + [vmem, anywhere],
        out_specs=[vmem] * 6,
        out_shape=[
            struct((length, width), bf16),
            struct((rows, ff), f32),
            struct((rows, ff), f32),
            struct((gains.shape[1], 1, gains.shape[2]), f32),
            struct((length, width), bf16),
            struct(down.shape, f32),
        ],
        scratch_shapes=[
            pltpu.VMEM(hid.shape, bf16),
            pltpu.VMEM(da.shape, bf16),
            pltpu.VMEM(db.shape, bf16),
            pltpu.VMEM(after.shape, f32),
            pltpu.VMEM(after.shape, f32),
            pltpu.VMEM((size, rows, cols), bf16),
            pltpu.VMEM(gains.shape, f32),
            pltpu.VMEM(after.shape, f32),
            pltpu.VMEM(after.shape, f32),
            pltpu.VMEM(x.shape, bf16),
            pltpu.VMEM(down.shape, bf16),
            sem((10,)), sem((size - 1,)), sem((size - 1,)), sem((size - 1,)), sem((size - 1,)),
        ]
        + scatter_scratch(length, width),
        compiler_params=pltpu.CompilerParams(
            vmem_limit_bytes=56 << 20, collective_id=7, has_side_effects=True
        ),
        cost_estimate=pl.CostEstimate(
            flops=2 * length * width * cols, bytes_accessed=30 << 20, transcendentals=0
        ),
        name="down_forward",
    )(hid, da, db, after, mlp_rows, gains, near, back, x, ag, down)


def return_kernel(
    rows_ref, gains_ref, q_ref, k_ref, v_ref, o_ref, total_ref, pieces, gains, send, recv, local, g_send, g_recv,
):
    size, rows, _ = pieces.shape
    me = lax.axis_index("dp")
    others = everyone(me)

    def block(device):
        return rows_ref.at[pl.ds(pl.multiple_of((device % size) * rows, rows), rows)]

    planes = gains.shape[0]
    plane = me // size
    column = [(plane + i) % planes for i in range(1, planes)]
    own = [
        pltpu.make_async_copy(block(me), pieces.at[me % size], local.at[0]),
        pltpu.make_async_copy(gains_ref.at[plane], gains.at[plane], local.at[1]),
    ]
    copies = [
        remote(block(device), pieces.at[me % size], send.at[i], recv.at[i], device)
        for i, device in enumerate(others)
    ]
    copies += [
        remote(gains_ref.at[to], gains.at[plane], g_send.at[i], g_recv.at[i], to * size + me % size)
        for i, to in enumerate(column)
    ]
    for copy in own:
        copy.start()
    greet(others + [to * size + me % size for to in column])
    for copy in copies:
        copy.start()
    for copy in own + copies:
        copy.wait()
    total_ref[...] = jnp.sum(gains[...], axis=0)
    for source in range(size):
        at = 0
        for ref in (q_ref, k_ref, v_ref, o_ref):
            width = ref.shape[1] // size
            ref[:, source * width : (source + 1) * width] = pieces[source, :, at : at + width].astype(f32)
            at += width


def return_attention(attn_rows, gains, widths):
    size = 2 * TP
    rows, cols = attn_rows.shape[0] // size, attn_rows.shape[1]
    sem = pltpu.SemaphoreType.DMA
    return pl.pallas_call(
        return_kernel,
        in_specs=[pl.BlockSpec(memory_space=pl.ANY)] * 2,
        out_specs=[pl.BlockSpec(memory_space=pltpu.VMEM)] * 5,
        out_shape=[struct((rows, w), f32) for w in widths] + [struct(gains.shape[1:], f32)],
        scratch_shapes=[
            pltpu.VMEM((size, rows, cols), bf16),
            pltpu.VMEM(gains.shape, f32),
            sem((size - 1,)), sem((size - 1,)), sem((2,)),
            sem((gains.shape[0] - 1,)), sem((gains.shape[0] - 1,)),
        ],
        compiler_params=pltpu.CompilerParams(collective_id=8, has_side_effects=True),
        name="return_attention",
    )(attn_rows, gains)


def make_body(n):
    m = n // (2 * TP)
    z_groups = [[g * 2 * TP + k for g in range(m)] for k in range(2 * TP)]

    def swap(v, bits):
        return lax.ppermute(v, "dp", [(a, a ^ bits) for a in range(n)])

    def gather_xy(v):
        h = v.shape[0] // 2
        x = swap(v, 2)
        y = swap(v, 4)
        d_low = swap(y[:h], 2)
        d_high = swap(x[h:], 4)
        return [v, x, y, jnp.concatenate([d_low, d_high])]

    def scatter_xy(p0, p1, p2, p3):
        h = p3.shape[0] // 2
        d_low = swap(p3[:h], 4)
        d_high = swap(p3[h:], 2)
        sx = jnp.concatenate([(p1[:h].astype(f32) + d_low.astype(f32)).astype(bf16), p1[h:]])
        sy = jnp.concatenate([p2[:h], (p2[h:].astype(f32) + d_high.astype(f32)).astype(bf16)])
        return p0 + swap(sx, 2).astype(f32) + swap(sy, 4).astype(f32)

    def gather_z(v):
        return lax.all_gather(v, "dp", axis=0, tiled=True, axis_index_groups=z_groups)

    def scatter_z(v):
        return lax.psum_scatter(
            v, "dp", scatter_dimension=0, tiled=True, axis_index_groups=z_groups
        )

    def body(
        tokens,
        segments,
        w_query,
        w_key,
        w_value,
        w_out,
        w_gate,
        w_up,
        w_down,
        attn_gain,
        mlp_gain,
        query_gain,
        key_gain,
        cotangent,
    ):
        me = lax.axis_index("dp")
        core = me % 2
        place = (me // 2) % TP
        length, width = tokens.shape
        rows = w_query.shape[0]
        ffr = w_down.shape[0]

        qn = w_query.shape[1] // (2 * TP)
        kn = w_key.shape[1] // (2 * TP)
        pn = qn + 2 * kn
        hr = query_gain.shape[0]
        gains = jnp.concatenate([attn_gain, mlp_gain, query_gain, key_gain]).astype(f32)
        count = gains.shape[0]
        padded = -(-count // 256) * 256
        attn_in, gains, seg_all = spread_attention(
            w_query, w_key, w_value, w_out, jnp.pad(gains, (0, padded - count))[None], segments
        )

        depth, wide = attn_in.shape
        gain_rows = gains.astype(bf16).reshape(-1, padded)
        below = jnp.pad(gain_rows, ((0, -gain_rows.shape[0] % 16), (0, wide - padded)))
        attn_all = gather_z(jnp.concatenate([attn_in, below])).reshape(m, -1, wide)
        tokens_in, _ = lax.optimization_barrier((tokens, attn_in))

        rate = THETA ** (-(jnp.arange(HD // 2, dtype=f32) * 2.0 / HD))
        sign = jnp.where(jnp.arange(HD) < HD // 2, -1.0, 1.0).astype(f32)
        rates = jnp.stack([jnp.concatenate([rate, rate]), sign])
        cosine, sine, starts, tokens_all, mlp_in = gather_group(
            seg_all, rates, tokens_in, w_gate, w_up, ffr
        )
        mlp_a = gather_z(mlp_in)
        tokens_all, attn_all = lax.optimization_barrier((tokens_all, attn_all))
        gains = attn_all[:, depth : depth + gain_rows.shape[0], :padded].reshape(n, padded)
        attn_scale = gains[:, :rows].reshape(-1).astype(f32)
        mlp_scale = gains[:, rows : 2 * rows].reshape(-1).astype(f32)
        query_scale = gains[:, 2 * rows : 2 * rows + hr].reshape(-1).astype(f32)
        key_scale = gains[:, 2 * rows + hr : count].reshape(-1).astype(f32)

        (
            raw, normed_one, mixed_own, after_attn, inv_two, proj_a, proj_b, out_full, normed_two_all
        ) = attend_forward(
            tokens_all, cosine, sine, starts, attn_scale[None], mlp_scale[None],
            query_scale[None], key_scale[None], attn_all, depth, pn, length,
        )

        inputs = tokens.astype(f32)
        mlp_a, normed_two_all, down_local = lax.optimization_barrier((mlp_a, normed_two_all, w_down))
        down_a = gather_z(down_local)
        fn = down_a.shape[0]

        gate_value, up_value, hidden, mlp_b, grad_all, down_sum = feed_forward(
            normed_two_all, mlp_a, cotangent
        )
        down_rows = scatter_z(down_sum)
        grad_normed_two, mlp_sum, down_b = feed_backward(
            gate_value, up_value, grad_all, down_a, mlp_a, mlp_b, normed_two_all, length
        )
        mlp_rows = scatter_z(mlp_sum)
        grad_normed_two, down_rows = lax.optimization_barrier((grad_normed_two, down_rows))

        grad_after, grad_after_low, mlp_gain_grad, grad_heads, out_other = between(
            grad_normed_two, after_attn, inv_two, mlp_scale[None], cotangent, mixed_own, out_full
        )

        grad_normed_one, attn_sum, query_gain_grad, key_gain_grad = attend_backward(
            grad_heads, raw, normed_one, proj_a, proj_b, cosine, sine, starts,
            query_scale[None], key_scale[None], mixed_own, grad_after_low, out_other, length,
        )
        attn_rows = scatter_z(attn_sum)
        attn_gain_grad = jnp.sum(grad_normed_one * inputs * inverse_rms(inputs), axis=0)

        gain_grads = jnp.concatenate(
            [
                attn_gain_grad.reshape(m, 2 * TP, -1),
                mlp_gain_grad.reshape(m, 2 * TP, -1),
                query_gain_grad.reshape(m, 2 * TP, -1),
                key_gain_grad.reshape(m, 2 * TP, -1),
                jnp.zeros((m, 2 * TP, padded - count), f32),
            ],
            axis=2,
        ).transpose(1, 0, 2)
        output, gate_shard, up_shard, gain_sums, tokens_grad, down_shard = down_forward(
            hidden, down_a, down_b, after_attn, mlp_rows, gain_grads, grad_after, grad_normed_one,
            tokens, attn_scale[None], down_rows, ffr,
        )
        attn_rows, output = lax.optimization_barrier((attn_rows, output))
        query_shard, key_shard, value_shard, out_shard, gain_grads = return_attention(
            attn_rows, gain_sums, [w.shape[1] for w in (w_query, w_key, w_value, w_out)]
        )

        gain_grads = gain_grads[0]

        return (
            output,
            tokens_grad,
            query_shard,
            key_shard,
            value_shard,
            out_shard,
            gate_shard,
            up_shard,
            down_shard,
            gain_grads[:rows],
            gain_grads[rows : 2 * rows],
            gain_grads[2 * rows : 2 * rows + hr],
            gain_grads[2 * rows + hr : count],
        )

    return body


def solution(mesh):
    row = P("dp", None)
    flat = P("dp")
    return jax.shard_map(
        make_body(mesh.shape["dp"]),
        mesh=mesh,
        in_specs=(row,) * 9 + (flat,) * 4 + (row,),
        out_specs=(row,) * 9 + (flat,) * 4,
        check_vma=False,
    )
```

```python
import functools

import jax
import jax.numpy as jnp
from jax import lax
from jax.experimental import pallas as pl
from jax.experimental.pallas import tpu as pltpu
from jax.sharding import PartitionSpec as P

H = 16
KVH = 8
HD = 128
TP = 4

EPS = 1e-06
THETA = 1000000.0

f32 = jnp.float32
bf16 = jnp.bfloat16
MESH = pl.DeviceIdType.MESH


def inverse_rms(values):
    return lax.rsqrt(jnp.mean(values * values, axis=-1, keepdims=True) + EPS)


def dot(a, b):
    return lax.dot_general(a, b, (((1,), (0,)), ((), ())), preferred_element_type=f32)


def dot_tn(a, b):
    return lax.dot_general(a, b, (((0,), (0,)), ((), ())), preferred_element_type=f32)


def dot_nt(a, b):
    return lax.dot_general(a, b, (((1,), (1,)), ((), ())), preferred_element_type=f32)


def turn(v):
    return pltpu.roll(v, HD // 2, 1)


def heads_of(raw, cosine, sine, query_gain, key_gain):
    out = []
    for k, gain in ((0, query_gain), (1, query_gain), (2, key_gain)):
        v = raw[:, k * HD : (k + 1) * HD]
        inverse = inverse_rms(v)
        normed = v * inverse * gain
        out.append((v, inverse, (normed * cosine + turn(normed) * sine).astype(bf16)))
    return out, raw[:, 3 * HD :].astype(bf16)


def block_probs(qs, keys, starts, row0, score_scale):
    size, span = starts.shape[0], keys.shape[0]
    scores = dot_nt(qs, keys) * score_scale
    column = lax.broadcasted_iota(jnp.int32, (size, span), 1)
    row = lax.broadcasted_iota(jnp.int32, (size, span), 0) + row0
    allowed = (column >= starts) & (column <= row)
    allowed = jnp.concatenate([allowed, allowed], axis=0)
    scores = jnp.where(allowed, scores, -1e30)
    power_term = jnp.exp(scores - jnp.max(scores, axis=-1, keepdims=True))
    return power_term / jnp.sum(power_term, axis=-1, keepdims=True)


def partners(me):
    x = me + 2 - 4 * ((me // 2) % 2)
    y = me + 4 - 8 * ((me // 4) % 2)
    d = x + 4 - 8 * ((me // 4) % 2)
    return x, y, d, me + 1 - 2 * (me % 2)


def greet(devices):
    barrier = pltpu.get_barrier_semaphore()
    for device in devices:
        pl.semaphore_signal(barrier, inc=1, device_id=(device,), device_id_type=MESH)
    pl.semaphore_wait(barrier, len(devices))


def remote(src, dst, send, recv, device):
    return pltpu.make_async_remote_copy(
        src_ref=src, dst_ref=dst, send_sem=send, recv_sem=recv, device_id=(device,), device_id_type=MESH
    )


TILE = 512


class Scatter:
    def __init__(self, out, ebuf, rd, rxy, send, recv, x, y):
        self.out, self.ebuf, self.rd, self.rxy = out, ebuf, rd, rxy
        length, width = out.shape
        h = length // 2
        self.half = h
        self.span = width // 2

        def pair(i, src, dst, rows, device):
            copies = []
            for c in range(2):
                cols = pl.ds(c * self.span, self.span)
                copies.append(
                    remote(
                        src[0].at[src[1], pl.ds(src[2], rows), cols],
                        dst[0].at[dst[1], pl.ds(dst[2], rows), cols],
                        send.at[i, c],
                        recv.at[i, c],
                        device,
                    )
                )
            return copies

        self.low = pair(0, (ebuf, 0, 0), (rd, 0, 0), h, y)
        self.high = pair(1, (ebuf, 0, h), (rd, 1, 0), h, x)
        self.to_x = pair(2, (ebuf, 1, 0), (rxy, 0, 0), length, x)
        self.to_y = pair(3, (ebuf, 2, 0), (rxy, 1, 0), length, y)

    def add(self, k, tile_of):
        h = self.half
        tiles = self.span // TILE
        for c in range(2):
            if k == 1:
                self.low[c].wait_recv()
            if k == 2:
                self.high[c].wait_recv()

            @pl.loop(c * tiles, (c + 1) * tiles)
            def _(t):
                sl = pl.ds(pl.multiple_of(t * TILE, TILE), TILE)
                value = tile_of(sl)
                if k == 0:
                    self.out[:, sl] = value
                elif k == 3:
                    self.ebuf[0, :, sl] = value.astype(bf16)
                elif k == 1:
                    self.ebuf[1, :h, sl] = (value[:h] + self.rd[0, :, sl].astype(f32)).astype(bf16)
                    self.ebuf[1, h:, sl] = value[h:].astype(bf16)
                else:
                    self.ebuf[2, :h, sl] = value[:h].astype(bf16)
                    self.ebuf[2, h:, sl] = (value[h:] + self.rd[1, :, sl].astype(f32)).astype(bf16)

            if k == 3:
                self.low[c].start()
                self.high[c].start()
            if k == 1:
                self.to_x[c].start()
            if k == 2:
                self.to_y[c].start()

    def finish(self):
        tiles = self.span // TILE
        for c in range(2):
            self.to_x[c].wait_recv()
            self.to_y[c].wait_recv()

            @pl.loop(c * tiles, (c + 1) * tiles)
            def _(t):
                sl = pl.ds(pl.multiple_of(t * TILE, TILE), TILE)
                self.out[:, sl] += self.rxy[0, :, sl].astype(f32) + self.rxy[1, :, sl].astype(f32)

        for copy in self.low + self.high + self.to_x + self.to_y:
            copy.wait_send()


def scatter_scratch(length, width):
    return [
        pltpu.VMEM((3, length, width), bf16),
        pltpu.VMEM((2, length // 2, width), bf16),
        pltpu.VMEM((2, length, width), bf16),
        pltpu.SemaphoreType.DMA((4, 2)),
        pltpu.SemaphoreType.DMA((4, 2)),
    ]


def attend_back_kernel(
    heads, raw_ref, a1_ref, pa_ref, pb_ref, cos_ref, sin_ref, start_ref, qg_ref, kg_ref, mix_ref, dy_ref, orecv_ref,
    out_ref, sum_ref, dqg_ref, dkg_ref, ogot_ref,
    gp_ref, dk_ref, dv_ref, acc_a, acc_b, cbuf, crecv, oslot, ofetch, dyo,
    ebuf, rd, rxy, rs_send, rs_recv, c_send, c_recv, os_send, os_recv, o_local,
):
    length = a1_ref.shape[0]
    step = 128
    score_scale = HD ** (-0.5)
    s = pl.program_id(0)
    me = lax.axis_index("dp")
    core = me % 2
    x, y, d, sibling = partners(me)
    scatter = Scatter(out_ref, ebuf, rd, rxy, rs_send, rs_recv, x, y)
    across = remote(cbuf, crecv, c_send, c_recv, sibling)
    block = oslot.shape[2]
    tall = oslot.shape[1] // 2
    o_low = remote(
        oslot.at[3, pl.ds(0, tall)], ogot_ref.at[2, pl.ds(0, tall)], os_send.at[2], os_recv.at[2], y
    )
    o_high = remote(
        oslot.at[3, pl.ds(tall, tall)], ogot_ref.at[2, pl.ds(tall, tall)], os_send.at[3], os_recv.at[3], x
    )
    o_home = [
        remote(oslot.at[k], ogot_ref.at[k - 1], os_send.at[k - 1], os_recv.at[k - 1], device)
        for k, device in ((1, x), (2, y))
    ]
    o_back = [
        pltpu.make_async_copy(ogot_ref.at[k - 1], oslot.at[k], o_local.at[k]) for k in range(1, 3)
    ]

    @pl.when(s == 0)
    def _():
        fetch = pltpu.make_async_copy(orecv_ref, oslot, o_local.at[0])
        fetch.start()
        greet((x, y, d, sibling))
        for ref in (acc_a, acc_b, dqg_ref, dkg_ref):
            ref[...] = jnp.zeros_like(ref)
        for k, device in enumerate((me, x, y, d)):
            at = ((device // 2) % TP) * 2 + core
            dyo[:, k * block : (k + 1) * block] = dy_ref[:, pl.ds(pl.multiple_of(at * block, block), block)]
        fetch.wait()

        @pl.loop(0, oslot.shape[1] // TILE)
        def _(t):
            sl = pl.ds(pl.multiple_of(t * TILE, TILE), TILE)
            value = dot_tn(mix_ref[:, sl], dyo[...])
            for k in range(TP):
                oslot[k, sl, :] = (
                    value[:, k * block : (k + 1) * block] + oslot[k, sl, :].astype(f32)
                ).astype(bf16)

        o_low.start()
        o_high.start()

    @pl.when(s == 1)
    def _():
        for copy, k, offset in ((o_low, 1, 0), (o_high, 2, tall)):
            copy.wait_recv()
            fetch = pltpu.make_async_copy(
                ogot_ref.at[2, pl.ds(offset, tall)], ofetch, o_local.at[0]
            )
            fetch.start()
            fetch.wait()

            @pl.loop(0, tall // TILE)
            def _(t):
                sl = pl.ds(pl.multiple_of(t * TILE, TILE), TILE)
                to = pl.ds(pl.multiple_of(offset + t * TILE, TILE), TILE)
                oslot[k, to, :] = (oslot[k, to, :].astype(f32) + ofetch[sl, :].astype(f32)).astype(bf16)

            o_home[k - 1].start()

    which = part_order(s)

    for h in range(2):
        col = h * 4 * HD
        side = core if h == 0 else 1 - core
        cosine, sine = cos_ref[...], sin_ref[...]
        (q0, q1, k0), value = heads_of(
            raw_ref[:, col : col + 4 * HD], cosine, sine, qg_ref[...], kg_ref[...]
        )
        dk_ref[...] = jnp.zeros_like(dk_ref)
        dv_ref[...] = jnp.zeros_like(dv_ref)
        parts = []
        for b in range(length // step):
            sl = slice(b * step, (b + 1) * step)
            span = (b + 1) * step
            qs = jnp.concatenate([q0[2][sl], q1[2][sl]], axis=0)
            gs = jnp.concatenate(
                [
                    heads[which, sl, pl.ds(pl.multiple_of((2 * side + g) * HD, HD), HD)]
                    for g in range(2)
                ],
                axis=0,
            )
            keys, values = k0[2][:span], value[:span]
            probs = block_probs(qs, keys, start_ref[sl, :], b * step, score_scale)
            dv_ref[:span, :] += dot_tn(probs.astype(bf16), gs)
            grad_probs = dot_nt(gs, values)
            delta = jnp.sum(probs * grad_probs, axis=-1, keepdims=True)
            grad_scores = (probs * (grad_probs - delta)).astype(bf16)
            dk_ref[:span, :] += dot_tn(grad_scores, qs)
            parts.append(dot(grad_scores, keys))
        dq0 = jnp.concatenate([p[:step] for p in parts], axis=0) * score_scale
        dq1 = jnp.concatenate([p[step:] for p in parts], axis=0) * score_scale
        for k, (raw, inverse, _), grad, gain_ref, dgain_ref in (
            (0, q0, dq0, qg_ref, dqg_ref),
            (1, q1, dq1, qg_ref, dqg_ref),
            (2, k0, dk_ref[...] * score_scale, kg_ref, dkg_ref),
        ):
            back = grad * cosine + turn(grad * sine)
            scaled = back * gain_ref[...]
            inner = jnp.mean(scaled * raw, axis=-1, keepdims=True)
            gp_ref[:, col + k * HD : col + (k + 1) * HD] = (
                inverse * (scaled - raw * inverse * inverse * inner)
            ).astype(bf16)
            dgain_ref[...] += jnp.sum(back * raw * inverse, axis=0, keepdims=True)
        gp_ref[:, col + 3 * HD : col + 4 * HD] = dv_ref[...].astype(bf16)

    half = 4 * HD

    def tile_of(sl):
        return dot_nt(gp_ref[:, :half], pa_ref[sl, :]) + dot_nt(gp_ref[:, half:], pb_ref[sl, :])

    for at, k in enumerate(ORDER):

        @pl.when(s == at)
        def _():
            scatter.add(k, tile_of)

    @pl.loop(0, acc_a.shape[0] // TILE)
    def _(t):
        sl = pl.ds(pl.multiple_of(t * TILE, TILE), TILE)
        acc_b[sl, :] += dot_tn(a1_ref[:, sl], gp_ref[:, half:])

    @pl.when(s == 3)
    def _():
        cbuf[...] = acc_b[...].astype(bf16)
        across.start()

    @pl.loop(0, acc_a.shape[0] // TILE)
    def _(t):
        sl = pl.ds(pl.multiple_of(t * TILE, TILE), TILE)
        acc_a[sl, :] += dot_tn(a1_ref[:, sl], gp_ref[:, :half])

    @pl.when(s == 3)
    def _():
        proj = acc_a.shape[1]
        across.wait_recv()
        sum_ref[:, :proj] = (acc_a[...] + crecv[...].astype(f32)).astype(bf16)
        o_low.wait_send()
        o_high.wait_send()
        for copy, back in zip(o_home, o_back):
            copy.wait()
            back.start()
        for back in o_back:
            back.wait()

        @pl.loop(0, oslot.shape[1] // TILE)
        def _(t):
            sl = pl.ds(pl.multiple_of(t * TILE, TILE), TILE)
            total = oslot[0, sl, :].astype(f32)
            for k in range(1, 3):
                total += oslot[k, sl, :].astype(f32)
            sum_ref[sl, proj:] = total.astype(bf16)

        scatter.finish()
        across.wait_send()


CHUNK = 256


def feed_kernel(
    a2_ref, wa_ref, g_ref,
    gate_ref, up_ref, hid_ref, wb_ref, ga_ref, sum_ref,
    a2, wa, wb, g, hid, stage, cbuf, crecv, acc,
    loads, x_send, x_recv, g_send, g_recv, s_sem, c_send, c_recv, keeps,
):
    tokens, width = a2.shape
    length = g_ref.shape[0]
    fn = wa.shape[1] // 2
    x, y, d, sibling = partners(lax.axis_index("dp"))
    h = length // 2

    def rows(k, offset=0, size=length):
        return g.at[pl.ds(k * length + offset, size)]

    load_x = pltpu.make_async_copy(a2_ref, a2, loads.at[0])
    load_w = pltpu.make_async_copy(wa_ref, wa, loads.at[1])
    load_g = pltpu.make_async_copy(g_ref, rows(0), loads.at[2])
    swap_w = remote(wa_ref, wb, x_send.at[0], x_recv.at[0], sibling)
    g_x = remote(g_ref, rows(1), g_send.at[0], g_recv.at[0], x)
    g_y = remote(g_ref, rows(2), g_send.at[1], g_recv.at[1], y)
    g_low = remote(rows(2, 0, h), rows(3, 0, h), g_send.at[2], g_recv.at[2], x)
    g_high = remote(rows(1, h, h), rows(3, h, h), g_send.at[3], g_recv.at[3], y)
    keep_w = pltpu.make_async_copy(wb, wb_ref, keeps.at[0])
    keep_g = pltpu.make_async_copy(g, ga_ref, keeps.at[1])
    keep_h = pltpu.make_async_copy(hid, hid_ref, keeps.at[2])

    load_w.start()
    load_x.start()
    load_g.start()
    greet((x, y, d, sibling))
    g_x.start()
    g_y.start()
    swap_w.start()

    per_half = fn // CHUNK
    span = 2 * length
    halves = tokens // span

    def store(i, which, ref):
        half = i // (per_half * halves)
        j = i % (per_half * halves)
        r, c = j // per_half, j % per_half
        return pltpu.make_async_copy(
            stage.at[i % 2, which],
            ref.at[
                pl.ds(pl.multiple_of(r * span, span), span),
                pl.ds(pl.multiple_of((half * per_half + c) * CHUNK, CHUNK), CHUNK),
            ],
            s_sem.at[i % 2, which],
        )

    def run(half, w):
        @pl.loop(0, per_half * halves)
        def _(j):
            i = j + half * per_half * halves

            @pl.when(i >= 2)
            def _():
                store(i - 2, 0, gate_ref).wait()
                store(i - 2, 1, up_ref).wait()

            r, c = j // per_half, j % per_half
            sl = pl.ds(pl.multiple_of(r * span, span), span)
            gate = dot(a2[sl, :], w[:, pl.ds(pl.multiple_of(c * CHUNK, CHUNK), CHUNK)])
            up = dot(a2[sl, :], w[:, pl.ds(pl.multiple_of(fn + c * CHUNK, CHUNK), CHUNK)])
            stage[i % 2, 0] = gate.astype(bf16)
            stage[i % 2, 1] = up.astype(bf16)
            hid[sl, pl.ds(pl.multiple_of((half * per_half + c) * CHUNK, CHUNK), CHUNK)] = (
                gate * jax.nn.sigmoid(gate) * up
            ).astype(bf16)
            store(i, 0, gate_ref).start()
            store(i, 1, up_ref).start()

    load_w.wait()
    load_x.wait()
    run(0, wa)
    swap_w.wait_recv()
    keep_w.start()
    run(1, wb)
    last = 2 * per_half * halves
    for i in (last - 2, last - 1):
        store(i, 0, gate_ref).wait()
        store(i, 1, up_ref).wait()
    keep_h.start()

    g_x.wait_recv()
    g_high.start()
    g_y.wait_recv()
    g_low.start()
    load_g.wait()
    near = pl.ds(0, 3 * length)
    far = pl.ds(3 * length, length)

    @pl.loop(0, 2 * per_half)
    def _(t):
        cols = pl.ds(pl.multiple_of(t * CHUNK, CHUNK), CHUNK)
        acc[t] = dot_tn(hid[near, cols], g[near, :])

    g_low.wait_recv()
    g_high.wait_recv()
    keep_g.start()

    def across(t):
        return remote(cbuf.at[t], crecv.at[t], c_send.at[t], c_recv.at[t], sibling)

    @pl.loop(0, per_half)
    def _(t):
        cols = pl.ds(pl.multiple_of(fn + t * CHUNK, CHUNK), CHUNK)
        cbuf[t] = (acc[per_half + t] + dot_tn(hid[far, cols], g[far, :])).astype(bf16)
        across(t).start()

    @pl.loop(0, per_half)
    def _(t):
        cols = pl.ds(pl.multiple_of(t * CHUNK, CHUNK), CHUNK)
        own = acc[t] + dot_tn(hid[far, cols], g[far, :])
        across(t).wait_recv()
        sum_ref[cols, :] = (own + crecv[t].astype(f32)).astype(bf16)

    for t in range(per_half):
        across(t).wait_send()
    for copy in (swap_w, g_x, g_y, g_low, g_high):
        copy.wait_send()
    for copy in (keep_w, keep_g, keep_h):
        copy.wait()


def feed_forward(a2, wa, g):
    tokens, width = a2.shape
    fn = wa.shape[1] // 2
    length = g.shape[0]
    anywhere = pl.BlockSpec(memory_space=pl.ANY)
    sem = pltpu.SemaphoreType.DMA
    return pl.pallas_call(
        feed_kernel,
        in_specs=[anywhere] * 3,
        out_specs=[anywhere] * 5 + [pl.BlockSpec(memory_space=pltpu.VMEM)],
        out_shape=[
            struct((tokens, 2 * fn), bf16),
            struct((tokens, 2 * fn), bf16),
            struct((tokens, 2 * fn), bf16),
            struct(wa.shape, bf16),
            struct((tokens, width), bf16),
            struct((fn, width), bf16),
        ],
        scratch_shapes=[
            pltpu.VMEM(a2.shape, bf16),
            pltpu.VMEM(wa.shape, bf16),
            pltpu.VMEM(wa.shape, bf16),
            pltpu.VMEM(a2.shape, bf16),
            pltpu.VMEM((tokens, 2 * fn), bf16),
            pltpu.VMEM((2, 2, 2 * length, CHUNK), bf16),
            pltpu.VMEM((fn // CHUNK, CHUNK, width), bf16),
            pltpu.VMEM((fn // CHUNK, CHUNK, width), bf16),
            pltpu.VMEM((2 * fn // CHUNK, CHUNK, width), f32),
            sem((3,)), sem((2,)), sem((2,)), sem((4,)), sem((4,)), sem((2, 2)),
            sem((fn // CHUNK,)), sem((fn // CHUNK,)), sem((3,)),
        ],
        compiler_params=pltpu.CompilerParams(
            vmem_limit_bytes=58 << 20, collective_id=4, has_side_effects=True
        ),
        cost_estimate=pl.CostEstimate(
            flops=4 * tokens * width * fn, bytes_accessed=30 << 20, transcendentals=0
        ),
        name="feed_forward",
    )(a2, wa, g)


def feed_back_kernel(
    gate_ref, up_ref, ga_ref, da_ref, wa_ref, wb_ref, a2_ref,
    out_ref, sum_ref, db_ref, crecv_ref,
    gp, wa, wb, a2, wd, uv, cbuf, cgot, stage, loads, u_sem, c_send, c_recv, g_sem, s_sem,
    d_send, d_recv,
    ebuf, rd, rxy, rs_send, rs_recv,
):
    length = out_ref.shape[0]
    cols = wa.shape[1]
    fn = cols // 2
    rows = cbuf.shape[1]
    tiles = a2.shape[1] // rows
    x, y, d, sibling = partners(lax.axis_index("dp"))
    scatter = Scatter(out_ref, ebuf, rd, rxy, rs_send, rs_recv, x, y)

    def piece(k):
        sl = pl.ds(k * length, length)
        return pltpu.make_async_copy(ga_ref.at[sl], a2.at[sl], loads.at[k])

    load_a = pltpu.make_async_copy(wa_ref, wa, loads.at[4])
    load_b = pltpu.make_async_copy(wb_ref, wb, loads.at[5])
    load_da = pltpu.make_async_copy(da_ref, wd.at[pl.ds(0, fn)], loads.at[6])
    swap_d = remote(da_ref, wd.at[pl.ds(fn, fn)], d_send, d_recv, sibling)
    keep_d = pltpu.make_async_copy(wd.at[pl.ds(fn, fn)], db_ref, loads.at[7])
    load_x = pltpu.make_async_copy(a2_ref, a2, loads.at[8])
    steps = 2 * TP

    def step_of(i):
        return part_order(i // 2), i % 2

    def fetch_uv(i, which, ref):
        part, c = step_of(i)
        return pltpu.make_async_copy(
            ref.at[
                pl.ds(pl.multiple_of(part * length, length), length),
                pl.ds(pl.multiple_of(c * fn, CHUNK), fn),
            ],
            uv.at[i % 2, which],
            u_sem.at[i % 2, which],
        )

    fetch_uv(0, 0, gate_ref).start()
    fetch_uv(0, 1, up_ref).start()
    piece(3).start()
    load_da.start()
    greet((x, y, d, sibling))
    swap_d.start()
    load_a.start()
    load_b.start()
    for k in (1, 2, 0):
        piece(k).start()

    def rows_of(t):
        return pl.ds(pl.multiple_of(t * rows, rows), rows)

    def across(t):
        return remote(
            cbuf.at[t % 2], crecv_ref.at[rows_of(t)], c_send.at[t % 2], c_recv.at[t], sibling
        )

    def fetch(t):
        return pltpu.make_async_copy(crecv_ref.at[rows_of(t)], cgot.at[t % 2], g_sem.at[t % 2])

    def store(t):
        return pltpu.make_async_copy(stage.at[t % 2], sum_ref.at[rows_of(t)], s_sem.at[t % 2])

    def part_of(k):
        sl = slice(k * length, (k + 1) * length)

        def tile_of(cut):
            return dot_nt(gp[sl, :cols], wa[cut, :]) + dot_nt(gp[sl, cols:], wb[cut, :])

        return tile_of

    def inner(first, end):
        @pl.loop(first, end)
        def _(i):
            @pl.when(i + 1 < steps)
            def _():
                fetch_uv(i + 1, 0, gate_ref).start()
                fetch_uv(i + 1, 1, up_ref).start()

            part, half = step_of(i)
            sl = pl.ds(pl.multiple_of(part * length, length), length)
            fetch_uv(i, 0, gate_ref).wait()
            fetch_uv(i, 1, up_ref).wait()
            for at in range(0, fn, CHUNK):
                cut = slice(at, at + CHUNK)
                rows_at = pl.ds(pl.multiple_of(half * fn + at, CHUNK), CHUNK)
                grad_hidden = dot_nt(a2[sl, :], wd[rows_at, :])
                gate = uv[i % 2, 0, :, cut].astype(f32)
                up = uv[i % 2, 1, :, cut].astype(f32)
                sig = jax.nn.sigmoid(gate)
                scaled = grad_hidden * sig
                to = half * cols + at
                gp[sl, pl.ds(pl.multiple_of(to, CHUNK), CHUNK)] = (
                    scaled * up * (1.0 + gate * (1.0 - sig))
                ).astype(bf16)
                gp[sl, pl.ds(pl.multiple_of(to + fn, CHUNK), CHUNK)] = (scaled * gate).astype(bf16)

    piece(3).wait()
    load_da.wait()
    inner(0, 1)
    swap_d.wait_recv()
    keep_d.start()
    inner(1, 2)
    load_a.wait()
    load_b.wait()
    scatter.add(3, part_of(3))
    for k in (1, 2, 0):
        piece(k).wait()
    inner(2, steps)
    load_x.start()
    scatter.add(1, part_of(1))
    scatter.add(2, part_of(2))
    load_x.wait()

    @pl.loop(0, tiles)
    def _(t):
        @pl.when(t >= 2)
        def _():
            across(t - 2).wait_send()

        cbuf[t % 2] = dot_tn(a2[:, rows_of(t)], gp[:, cols:]).astype(bf16)
        across(t).start()

    scatter.add(0, part_of(0))

    @pl.loop(0, tiles)
    def _(t):
        across(t).wait_recv()
        fetch(t).start()

        @pl.when(t >= 2)
        def _():
            store(t - 2).wait()

        own = dot_tn(a2[:, rows_of(t)], gp[:, :cols])
        fetch(t).wait()
        stage[t % 2] = (own + cgot[t % 2].astype(f32)).astype(bf16)
        store(t).start()

    for t in (tiles - 2, tiles - 1):
        store(t).wait()
        across(t).wait_send()
    swap_d.wait_send()
    keep_d.wait()
    scatter.finish()


def feed_backward(gate, up, ga, da, wa, wb, a2, length):
    tokens, width = a2.shape
    cols = wa.shape[1]
    rows = 256
    anywhere = pl.BlockSpec(memory_space=pl.ANY)
    sem = pltpu.SemaphoreType.DMA
    return pl.pallas_call(
        feed_back_kernel,
        in_specs=[anywhere] * 7,
        out_specs=[pl.BlockSpec(memory_space=pltpu.VMEM), anywhere, anywhere, anywhere],
        out_shape=[
            struct((length, width), f32),
            struct(wa.shape, bf16),
            struct(da.shape, bf16),
            struct(wa.shape, bf16),
        ],
        scratch_shapes=[
            pltpu.VMEM((tokens, 2 * cols), bf16),
            pltpu.VMEM(wa.shape, bf16),
            pltpu.VMEM(wb.shape, bf16),
            pltpu.VMEM(a2.shape, bf16),
            pltpu.VMEM((cols, width), bf16),
            pltpu.VMEM((2, 2, length, cols // 2), bf16),
            pltpu.VMEM((2, rows, cols), bf16),
            pltpu.VMEM((2, rows, cols), bf16),
            pltpu.VMEM((2, rows, cols), bf16),
            sem((9,)), sem((2, 2)), sem((2,)), sem((width // rows,)), sem((2,)), sem((2,)),
            sem, sem,
        ]
        + scatter_scratch(length, width),
        compiler_params=pltpu.CompilerParams(
            vmem_limit_bytes=62 << 20, collective_id=1, has_side_effects=True
        ),
        cost_estimate=pl.CostEstimate(
            flops=4 * tokens * width * cols, bytes_accessed=30 << 20, transcendentals=0
        ),
        name="feed_backward",
    )(gate, up, ga, da, wa, wb, a2)[:3]


ORDER = (3, 1, 2, 0)


def part_order(s):
    return 3 - 2 * s + 3 * (s // 2)


def rows_spec(length, cols):
    return pl.BlockSpec((length, cols), lambda s: (s, 0))


def whole_spec(shape):
    return pl.BlockSpec(shape, lambda s: (0, 0))


def struct(shape, dtype):
    return jax.ShapeDtypeStruct(shape, dtype)


def everyone(me):
    size = 2 * TP
    base = me - me % size
    return [base + (me % size + i) % size for i in range(1, size)]


def spread_kernel(
    wq_ref, wk_ref, wv_ref, wo_ref, gain_ref, seg_ref,
    all_ref, gains_ref, segs_ref,
    send, recv, local, s_send, s_recv,
):
    me = lax.axis_index("dp")
    size = 2 * TP
    rows = wq_ref.shape[0]
    here = pl.ds(pl.multiple_of((me % size) * rows, rows), rows)
    plan = []
    at = 0
    for ref in (wq_ref, wk_ref, wv_ref, wo_ref):
        width = ref.shape[1] // size
        plan.append((ref, width, all_ref.at[here, pl.ds(at, width)]))
        at += width

    def columns(ref, width, device):
        return ref.at[:, pl.ds(pl.multiple_of((device % size) * width, width), width)]

    others = everyone(me)
    gains_here = gains_ref.at[me % size]
    own = [
        pltpu.make_async_copy(columns(ref, width, me), dst, local.at[t])
        for t, (ref, width, dst) in enumerate(plan)
    ] + [
        pltpu.make_async_copy(gain_ref, gains_here, local.at[4]),
        pltpu.make_async_copy(seg_ref, segs_ref.at[0], local.at[5]),
    ]
    copies = [
        remote(columns(ref, width, device), dst, send.at[i, t], recv.at[i, t], device)
        for i, device in enumerate(others)
        for t, (ref, width, dst) in enumerate(plan)
    ]
    copies += [
        remote(gain_ref, gains_here, send.at[i, 4], recv.at[i, 4], device)
        for i, device in enumerate(others)
    ]
    copies += [
        remote(seg_ref, segs_ref.at[1 + k], s_send.at[k], s_recv.at[k], device)
        for k, device in enumerate(partners(me)[:3])
    ]
    for copy in own:
        copy.start()
    greet(others)
    for copy in copies:
        copy.start()
    for copy in own + copies:
        copy.wait()


def spread_attention(wq, wk, wv, wo, gain, seg):
    size = 2 * TP
    rows = wq.shape[0]
    cols = (wq.shape[1] + wk.shape[1] + wv.shape[1] + wo.shape[1]) // size
    anywhere = pl.BlockSpec(memory_space=pl.ANY)
    sem = pltpu.SemaphoreType.DMA
    return pl.pallas_call(
        spread_kernel,
        in_specs=[anywhere] * 6,
        out_specs=[anywhere] * 3,
        out_shape=[
            struct((size * rows, cols), bf16),
            struct((size, *gain.shape), f32),
            struct((TP, *seg.shape), jnp.int32),
        ],
        scratch_shapes=[sem((size - 1, 5)), sem((size - 1, 5)), sem((6,)), sem((3,)), sem((3,))],
        compiler_params=pltpu.CompilerParams(collective_id=5, has_side_effects=True),
        name="spread_attention",
    )(wq, wk, wv, wo, gain, seg)


def gather_kernel(
    run, seg_ref, rate_ref, x_ref, gate_ref, up_ref,
    cos_ref, sin_ref, start_ref, x_all, w_all,
    w_ref, flat, wide, xs, x_send, x_recv, w_send, w_recv, local,
):
    me = lax.axis_index("dp")
    size = 2 * TP
    x, y, d, _ = partners(me)
    others = everyone(me)
    length = x_ref.shape[0]
    rows = w_ref.shape[1]
    h = length // 2
    here = pl.ds(pl.multiple_of((me % size) * rows, rows), rows)

    def place(k, offset=0, count=length):
        return x_all.at[pl.ds(k * length + offset, count)]

    own = [
        pltpu.make_async_copy(xs, place(0), local.at[0]),
        pltpu.make_async_copy(w_ref.at[me % size], w_all.at[here], local.at[1]),
    ]
    fills = [
        pltpu.make_async_copy(ref, flat.at[i], local.at[2 + i]) for i, ref in enumerate((gate_ref, up_ref))
    ]
    weights = [
        remote(w_ref.at[device % size], w_all.at[here], w_send.at[i], w_recv.at[i], device)
        for i, device in enumerate(others)
    ]
    to_x = remote(xs, place(1), x_send.at[0], x_recv.at[0], x)
    to_y = remote(xs, place(2), x_send.at[1], x_recv.at[1], y)
    load_x = pltpu.make_async_copy(x_ref, xs, local.at[4])
    low = remote(place(2, 0, h), place(3, 0, h), x_send.at[2], x_recv.at[2], x)
    high = remote(place(1, h, h), place(3, h, h), x_send.at[3], x_recv.at[3], y)
    for copy in [load_x] + fills:
        copy.start()
    greet(others)
    load_x.wait()
    for copy in (to_x, to_y, own[0]):
        copy.start()
    for copy in fills:
        copy.wait()
    half = wide.shape[1] // 2
    values = [flat[i].astype(f32) for i in range(2)]
    for s in range(size):
        for i in range(2):
            for g in range(half // run):
                at = (g * size + s) * run
                wide[:, i * half + g * run : i * half + (g + 1) * run] = values[i][:, at : at + run]
        w_ref[s] = wide[...].astype(bf16)
    for copy in own[1:] + weights:
        copy.start()

    row = lax.broadcasted_iota(jnp.int32, (length, length), 0)
    column = lax.broadcasted_iota(jnp.int32, (length, length), 1)
    for k in range(TP):
        label = jnp.broadcast_to(seg_ref[k].astype(f32), (length, length))
        mine = jnp.sum(jnp.where(row == column, label, 0.0), axis=1, keepdims=True)
        start = jnp.sum(jnp.where(label < mine, 1.0, 0.0), axis=1, keepdims=True)
        position = lax.broadcasted_iota(jnp.int32, (length, 1), 0).astype(f32) - start
        angle = position * rate_ref[0:1, :]
        sl = pl.ds(k * length, length)
        cos_ref[sl, :] = jnp.cos(angle)
        sin_ref[sl, :] = jnp.sin(angle) * rate_ref[1:2, :]
        start_ref[sl, :] = start.astype(jnp.int32)

    to_x.wait_recv()
    high.start()
    to_y.wait_recv()
    low.start()
    for copy in (to_x, to_y):
        copy.wait_send()
    for copy in own + weights + [low, high]:
        copy.wait()


def gather_group(seg, rates, x, gate, up, run):
    size = 2 * TP
    rows, cols = gate.shape[0], 2 * gate.shape[1] // size
    anywhere = pl.BlockSpec(memory_space=pl.ANY)
    vmem = pl.BlockSpec(memory_space=pltpu.VMEM)
    sem = pltpu.SemaphoreType.DMA
    return pl.pallas_call(
        functools.partial(gather_kernel, run),
        in_specs=[vmem] * 2 + [anywhere] * 3,
        out_specs=[vmem] * 3 + [anywhere] * 2,
        out_shape=[
            struct((TP * x.shape[0], HD), f32),
            struct((TP * x.shape[0], HD), f32),
            struct((TP * x.shape[0], 1), jnp.int32),
            struct((TP * x.shape[0], x.shape[1]), bf16),
            struct((size * rows, cols), bf16),
        ],
        scratch_shapes=[
            pltpu.VMEM((size, rows, cols), bf16),
            pltpu.VMEM((2, *gate.shape), bf16),
            pltpu.VMEM((rows, cols), f32),
            pltpu.VMEM(x.shape, bf16),
            sem((4,)), sem((4,)), sem((size - 1,)), sem((size - 1,)), sem((5,)),
        ],
        compiler_params=pltpu.CompilerParams(
            vmem_limit_bytes=60 << 20, collective_id=6, has_side_effects=True
        ),
        name="gather_group",
    )(seg, rates, x, gate, up)


def attend_kernel(
    x_ref, cos_ref, sin_ref, start_ref, ag_ref, mg_ref, qg_ref, kg_ref, all_ref,
    raw_ref, a1_ref, mixed_ref, after_ref, inv_ref, pa_out, pb_out, wo_ref, a2_ref,
    pa_ref, pb_ref, fill, heads, mix, wo, a2, p_send, p_recv, o_send, o_recv, w_send, w_recv, s_send, s_recv, a_send, a_recv, local,
):
    length, width = x_ref.shape
    step = 128
    score_scale = HD ** (-0.5)
    s = pl.program_id(0)
    me = lax.axis_index("dp")
    core = me % 2
    place = (me // 2) % TP
    x, y, d, sibling = partners(me)
    near = (x, y, d)
    cols = 4 * HD
    proj = pa_ref.shape[1]
    block = all_ref.shape[2] - proj
    planes = all_ref.shape[0]
    deep = pa_ref.shape[0] // planes

    def block_of(device):
        return pl.ds(pl.multiple_of((device % (2 * TP)) * block, block), block)

    own_out = wo.at[:, block_of(me)]
    fills = []
    for g in range(planes):
        at = pl.ds(g * deep, deep)
        fills.append(
            pltpu.make_async_copy(
                all_ref.at[g, pl.ds(0, deep), pl.ds(0, proj)], pa_ref.at[at], fill.at[g, 0]
            )
        )
        fills.append(
            pltpu.make_async_copy(
                all_ref.at[g, pl.ds(0, deep), pl.ds(proj, block)], wo.at[at, block_of(me)], fill.at[g, 1]
            )
        )

    tall = wo.shape[0] // 2
    spread_out = [
        remote(own_out, own_out, w_send.at[i], w_recv.at[i], device)
        for i, device in enumerate(near[:2])
    ]

    def passed(device, offset, i, to):
        ref = wo.at[pl.ds(offset, tall), block_of(device)]
        return remote(ref, ref, w_send.at[i], w_recv.at[i], to)

    pass_on = [passed(x, tall, 2, y), passed(y, 0, 3, x)]
    beside = [remote(own_out, own_out, s_send.at[3], s_recv.at[3], sibling)]
    onward = [
        remote(wo.at[:, block_of(device)], wo.at[:, block_of(device)], s_send.at[i], s_recv.at[i], sibling)
        for i, device in enumerate(near)
    ]
    mine = pl.ds(pl.multiple_of(place * cols, cols), cols)
    home = [
        remote(heads.at[i + 1], mix.at[:, mine], o_send.at[i], o_recv.at[i], device)
        for i, device in enumerate(near)
    ]
    h = length // 2
    a2_x = remote(a2.at[0], a2.at[1], a_send.at[0], a_recv.at[0], x)
    a2_y = remote(a2.at[0], a2.at[2], a_send.at[1], a_recv.at[1], y)
    a2_low = remote(a2.at[2, pl.ds(0, h)], a2.at[3, pl.ds(0, h)], a_send.at[2], a_recv.at[2], x)
    a2_high = remote(a2.at[1, pl.ds(h, h)], a2.at[3, pl.ds(h, h)], a_send.at[3], a_recv.at[3], y)
    keep = [
        pltpu.make_async_copy(a2.at[k], a2_ref.at[pl.ds(k * length, length)], local.at[1 + k])
        for k in range(TP)
    ]
    keep_out = pltpu.make_async_copy(wo, wo_ref, local.at[5])
    keep_b = pltpu.make_async_copy(pb_ref, pb_out, local.at[6])
    keep_a = pltpu.make_async_copy(pa_ref, pa_out, local.at[0])
    swap_p = remote(pa_ref, pb_ref, p_send, p_recv, sibling)

    @pl.when(s == 0)
    def _():
        for copy in fills:
            copy.start()
        greet((x, y, d, sibling))
        for copy in fills:
            copy.wait()
        for copy in [swap_p] + spread_out + beside:
            copy.start()
        keep_a.start()

    @pl.when(s == 3)
    def _():
        for i in range(2):
            spread_out[i].wait_recv()
            pass_on[i].start()
            onward[i].start()

    @pl.loop(0, length // step)
    def _(t):
        sl = pl.ds(pl.multiple_of(t * step, step), step)
        v = x_ref[sl, :].astype(f32)
        a1_ref[sl, :] = (v * inverse_rms(v) * ag_ref[...]).astype(bf16)

    which = part_order(s)
    for half, p_ref in ((0, pa_ref), (1, pb_ref)):
        side = core if half == 0 else 1 - core
        if half:

            @pl.when(s == 0)
            def _():
                swap_p.wait_recv()
                keep_b.start()

        raw_ref[:, half * cols : (half + 1) * cols] = dot(a1_ref[...], p_ref[...])
        (q0, q1, k0), value = heads_of(
            raw_ref[:, half * cols : (half + 1) * cols], cos_ref[...], sin_ref[...], qg_ref[...], kg_ref[...]
        )
        for b in range(length // step):
            sl = slice(b * step, (b + 1) * step)
            span = (b + 1) * step
            qs = jnp.concatenate([q0[2][sl], q1[2][sl]], axis=0)
            probs = block_probs(qs, k0[2][:span], start_ref[sl, :], b * step, score_scale)
            mixed = dot(probs.astype(bf16), value[:span]).astype(bf16)
            for g in range(2):
                at = pl.ds(pl.multiple_of((2 * side + g) * HD, HD), HD)
                heads[which, sl, at] = mixed[g * step : (g + 1) * step]

    for at, k in enumerate(ORDER[:3]):

        @pl.when(s == at)
        def _():
            home[k - 1].start()

    @pl.when(s == 3)
    def _():
        mix[:, mine] = heads[0]
        for copy in pass_on:
            copy.wait_recv()
        onward[2].start()
        for copy in home:
            copy.wait_recv()
        for copy in beside + onward:
            copy.wait_recv()
        keep_out.start()

        @pl.loop(0, width // TILE)
        def _(t):
            sl = pl.ds(pl.multiple_of(t * TILE, TILE), TILE)
            after_ref[:, sl] = x_ref[:, sl].astype(f32) + dot(mix[...], wo[:, sl])

        @pl.loop(0, length // step)
        def _(t):
            sl = pl.ds(pl.multiple_of(t * step, step), step)
            v = after_ref[sl, :]
            inverse = inverse_rms(v)
            inv_ref[sl, :] = inverse
            a2[0, sl, :] = (v * inverse * mg_ref[...]).astype(bf16)

        a2_x.start()
        a2_y.start()
        keep[0].start()
        mixed_ref[...] = mix[...]
        a2_x.wait_recv()
        a2_high.start()
        keep[1].start()
        a2_y.wait_recv()
        a2_low.start()
        keep[2].start()
        a2_high.wait_recv()
        a2_low.wait_recv()
        keep[3].start()
        for copy in spread_out + pass_on + beside + onward + home + [a2_x, a2_y, a2_low, a2_high]:
            copy.wait_send()
        swap_p.wait_send()
        for copy in keep + [keep_out, keep_a, keep_b]:
            copy.wait()


def attend_forward(x, cosine, sine, starts, ag, mg, qg, kg, weights, depth, proj, length):
    tokens, width = x.shape
    planes = weights.shape[0]
    total = planes * depth
    anywhere = pl.BlockSpec(memory_space=pl.ANY)

    def in_order(cols):
        return pl.BlockSpec((length, cols), lambda s: (part_order(s), 0))

    return pl.pallas_call(
        attend_kernel,
        grid=(TP,),
        in_specs=[in_order(width)]
        + [in_order(HD), in_order(HD), in_order(1)]
        + [whole_spec(g.shape) for g in (ag, mg, qg, kg)]
        + [anywhere],
        out_specs=[in_order(8 * HD), in_order(width)]
        + [whole_spec((length, width))] * 2
        + [whole_spec((length, 1))]
        + [anywhere] * 4,
        out_shape=[
            struct((tokens, 8 * HD), f32),
            struct((tokens, width), bf16),
            struct((length, width), bf16),
            struct((length, width), f32),
            struct((length, 1), f32),
            struct((total, proj), bf16),
            struct((total, proj), bf16),
            struct((total, width), bf16),
            struct((tokens, width), bf16),
        ],
        scratch_shapes=[
            pltpu.VMEM((total, proj), bf16),
            pltpu.VMEM((total, proj), bf16),
            pltpu.SemaphoreType.DMA((planes, 2)),
            pltpu.VMEM((TP, length, 4 * HD), bf16),
            pltpu.VMEM((length, width), bf16),
            pltpu.VMEM((total, width), bf16),
            pltpu.VMEM((TP, length, width), bf16),
            pltpu.SemaphoreType.DMA,
            pltpu.SemaphoreType.DMA,
            pltpu.SemaphoreType.DMA((3,)),
            pltpu.SemaphoreType.DMA((3,)),
            pltpu.SemaphoreType.DMA((4,)),
            pltpu.SemaphoreType.DMA((4,)),
            pltpu.SemaphoreType.DMA((4,)),
            pltpu.SemaphoreType.DMA((4,)),
            pltpu.SemaphoreType.DMA((4,)),
            pltpu.SemaphoreType.DMA((4,)),
            pltpu.SemaphoreType.DMA((7,)),
        ],
        compiler_params=pltpu.CompilerParams(
            vmem_limit_bytes=56 << 20, collective_id=3, has_side_effects=True
        ),
        cost_estimate=pl.CostEstimate(
            flops=2 * tokens * width * 8 * HD, bytes_accessed=30 << 20, transcendentals=0
        ),
        name="attend_forward",
    )(x, cosine, sine, starts, ag, mg, qg, kg, weights)


def between_kernel(
    grad_ref, after_ref, inv_ref, gain_ref, cot_ref, mix_ref, w_ref,
    sum_ref, dy_ref, dgain_ref, heads_ref, orecv_ref,
    w, heads, oslot, dyo, loads, h_send, h_recv, o_send, o_recv,
):
    length, width = after_ref.shape
    step = 128
    me = lax.axis_index("dp")
    core = me % 2
    x, y, d, sibling = partners(me)
    places = (me, x, y, d)
    cols = heads.shape[2]
    block = oslot.shape[2]

    def rows_of(device):
        return pl.ds(pl.multiple_of(((device // 2) % TP) * cols, cols), cols)

    load = [
        pltpu.make_async_copy(w_ref.at[rows_of(device)], w.at[k], loads.at[k])
        for k, device in enumerate(places)
    ]
    home = [
        remote(heads.at[k], heads_ref.at[k], h_send.at[k - 1], h_recv.at[k - 1], places[k])
        for k in range(1, TP)
    ]
    keep = pltpu.make_async_copy(heads.at[0], heads_ref.at[0], loads.at[TP])
    def across(t):
        sl = pl.ds(pl.multiple_of(t * TILE, TILE), TILE)
        return remote(oslot.at[:, sl], orecv_ref.at[:, sl], o_send.at[t], o_recv.at[t], sibling)

    for k in ORDER:
        load[k].start()
    greet((x, y, d, sibling))
    dgain_ref[...] = jnp.zeros_like(dgain_ref)

    @pl.loop(0, length // step)
    def _(t):
        sl = pl.ds(pl.multiple_of(t * step, step), step)
        grad, values, inverse = grad_ref[sl, :], after_ref[sl, :], inv_ref[sl, :]
        scaled = grad * gain_ref[...]
        inner = jnp.mean(scaled * values, axis=-1, keepdims=True)
        total = cot_ref[sl, :].astype(f32) + inverse * (scaled - values * inverse * inverse * inner)
        sum_ref[sl, :] = total
        dy_ref[sl, :] = total.astype(bf16)
        dgain_ref[...] += jnp.sum(grad * values * inverse, axis=0, keepdims=True)

    for k in ORDER:
        load[k].wait()
        heads[k] = dot_nt(dy_ref[...], w[k]).astype(bf16)
        if k:
            home[k - 1].start()
        else:
            keep.start()
    for k in range(TP):
        at = ((places[k] // 2) % TP) * 2 + 1 - core
        dyo[:, k * block : (k + 1) * block] = dy_ref[:, pl.ds(pl.multiple_of(at * block, block), block)]

    tiles = oslot.shape[1] // TILE

    @pl.loop(0, tiles)
    def _(t):
        sl = pl.ds(pl.multiple_of(t * TILE, TILE), TILE)
        value = dot_tn(mix_ref[:, sl], dyo[...])
        for k in range(TP):
            oslot[k, sl, :] = value[:, k * block : (k + 1) * block].astype(bf16)
        across(t).start()

    for copy in home:
        copy.wait()
    for t in range(tiles):
        across(t).wait()
    keep.wait()


def between(grad, after, inverse, gain, cot, mix, w):
    length, width = after.shape
    cols = w.shape[0] // TP
    block = width // (2 * TP)
    anywhere = pl.BlockSpec(memory_space=pl.ANY)
    vmem = pl.BlockSpec(memory_space=pltpu.VMEM)
    sem = pltpu.SemaphoreType.DMA
    return pl.pallas_call(
        between_kernel,
        in_specs=[vmem] * 6 + [anywhere],
        out_specs=[vmem] * 3 + [anywhere] * 2,
        out_shape=[
            struct((length, width), f32),
            struct((length, width), bf16),
            struct((1, width), f32),
            struct((TP, length, cols), bf16),
            struct((TP, width, block), bf16),
        ],
        scratch_shapes=[
            pltpu.VMEM((TP, cols, width), bf16),
            pltpu.VMEM((TP, length, cols), bf16),
            pltpu.VMEM((TP, width, block), bf16),
            pltpu.VMEM((length, TP * block), bf16),
            sem((TP + 1,)), sem((3,)), sem((3,)), sem((width // TILE,)), sem((width // TILE,)),
        ],
        compiler_params=pltpu.CompilerParams(
            vmem_limit_bytes=60 << 20, collective_id=9, has_side_effects=True
        ),
        cost_estimate=pl.CostEstimate(
            flops=4 * length * width * w.shape[0], bytes_accessed=24 << 20, transcendentals=0
        ),
        name="between",
    )(grad, after, inverse, gain, cot, mix, w)


def attend_backward(heads, raw, a1, pa, pb, cosine, sine, starts, qg, kg, mix, dy, orecv, length):
    tokens, width = a1.shape
    block = width // (2 * TP)
    anywhere = pl.BlockSpec(memory_space=pl.ANY)
    sem = pltpu.SemaphoreType.DMA

    def in_order(cols):
        return pl.BlockSpec((length, cols), lambda s: (part_order(s), 0))

    def once(v):
        return pl.BlockSpec(v.shape, lambda s: (0, 0), pipeline_mode=pl.Buffered(1))

    return pl.pallas_call(
        attend_back_kernel,
        grid=(TP,),
        in_specs=[pl.BlockSpec(heads.shape, lambda s: (0, 0, 0), pipeline_mode=pl.Buffered(1))]
        + [in_order(c) for c in (8 * HD, width)]
        + [once(w) for w in (pa, pb)]
        + [in_order(HD), in_order(HD), in_order(1)]
        + [whole_spec(v.shape) for v in (qg, kg)]
        + [once(v) for v in (mix, dy)]
        + [anywhere],
        out_specs=[whole_spec((length, width)), whole_spec((width, pa.shape[1] + block))]
        + [whole_spec(v.shape) for v in (qg, kg)]
        + [anywhere],
        out_shape=[struct((length, width), f32), struct((width, pa.shape[1] + block), bf16)]
        + [struct(v.shape, f32) for v in (qg, kg)]
        + [struct((3, width, block), bf16)],
        scratch_shapes=[
            pltpu.VMEM((length, 8 * HD), bf16),
            pltpu.VMEM((length, HD), f32),
            pltpu.VMEM((length, HD), f32),
            pltpu.VMEM(pa.shape, f32),
            pltpu.VMEM(pa.shape, f32),
            pltpu.VMEM(pa.shape, bf16),
            pltpu.VMEM(pa.shape, bf16),
            pltpu.VMEM((TP, width, block), bf16),
            pltpu.VMEM((width // 2, block), bf16),
            pltpu.VMEM((length, TP * block), bf16),
        ]
        + scatter_scratch(length, width)
        + [sem, sem, sem((4,)), sem((4,)), sem((TP,))],
        compiler_params=pltpu.CompilerParams(
            vmem_limit_bytes=60 << 20, collective_id=2, has_side_effects=True
        ),
        cost_estimate=pl.CostEstimate(
            flops=2 * tokens * width * 8 * HD, bytes_accessed=30 << 20, transcendentals=0
        ),
        name="attend_backward",
    )(heads, raw, a1, pa, pb, cosine, sine, starts, qg, kg, mix, dy, orecv)[:4]


def down_kernel(
    run, hid_ref, da_ref, db_ref, after_ref, rows_ref, gains_ref, near_ref, back_ref, x_ref, ag_ref, down_ref,
    out_ref, gate_ref, up_ref, total_ref, tokens_ref, wide_ref,
    hid, da, db, after, acc, pieces, gains, near, back, xs, down, loads, p_send, p_recv, g_send, g_recv,
    ebuf, rd, rxy, rs_send, rs_recv,
):
    length = after.shape[0]
    fn = da.shape[0]
    size, rows, _ = pieces.shape
    me = lax.axis_index("dp")
    x, y, _, _ = partners(me)
    others = everyone(me)
    scatter = Scatter(acc, ebuf, rd, rxy, rs_send, rs_recv, x, y)

    def block(device):
        return rows_ref.at[pl.ds(pl.multiple_of((device % size) * rows, rows), rows)]

    own = pltpu.make_async_copy(block(me), pieces.at[me % size], loads.at[0])
    copies = [
        remote(block(device), pieces.at[me % size], p_send.at[i], p_recv.at[i], device)
        for i, device in enumerate(others)
    ]
    own_gains = pltpu.make_async_copy(gains_ref.at[me % size], gains.at[me % size], loads.at[5])
    gain_copies = [
        remote(gains_ref.at[device % size], gains.at[me % size], g_send.at[i], g_recv.at[i], device)
        for i, device in enumerate(others)
    ]
    fills = [
        pltpu.make_async_copy(src, dst, loads.at[1 + i])
        for i, (src, dst) in enumerate(((hid_ref, hid), (da_ref, da), (db_ref, db), (after_ref, after)))
    ]
    extra = [
        pltpu.make_async_copy(near_ref, near, loads.at[6]),
        pltpu.make_async_copy(back_ref, back, loads.at[7]),
        pltpu.make_async_copy(x_ref, xs, loads.at[8]),
        pltpu.make_async_copy(down_ref, down, loads.at[9]),
    ]
    for copy in fills:
        copy.start()
    own.start()
    own_gains.start()
    for copy in extra:
        copy.start()
    greet(others)
    for copy in gain_copies:
        copy.start()
    for copy in fills:
        copy.wait()

    def part_of(k):
        sl = slice(k * length, (k + 1) * length)

        def tile_of(cut):
            value = dot(hid[sl, :fn], da[:, cut]) + dot(hid[sl, fn:], db[:, cut])
            return value + after[:, cut] if k == 0 else value

        return tile_of

    for k in ORDER[:3]:
        scatter.add(k, part_of(k))
    for copy in copies:
        copy.start()
    scatter.add(0, part_of(0))
    for copy in extra:
        copy.wait()

    step = 128

    @pl.loop(0, length // step)
    def _(t):
        sl = pl.ds(pl.multiple_of(t * step, step), step)
        values = xs[sl, :].astype(f32)
        inverse = inverse_rms(values)
        scaled = back[sl, :] * ag_ref[...]
        inner = jnp.mean(scaled * values, axis=-1, keepdims=True)
        tokens_ref[sl, :] = (
            near[sl, :] + inverse * (scaled - values * inverse * inverse * inner)
        ).astype(bf16)

    wide_ref[...] = down[...].astype(f32)
    own_gains.wait()
    for copy in gain_copies:
        copy.wait()
    total = jnp.sum(gains[...], axis=0)
    for g in range(total.shape[0]):
        total_ref[g] = total[g : g + 1]
    own.wait()
    for copy in copies:
        copy.wait()
    for source in range(size):
        piece = pieces[source].astype(f32)
        for g in range(fn // run):
            to = (g * size + source) * run
            gate_ref[:, to : to + run] = piece[:, g * run : (g + 1) * run]
            up_ref[:, to : to + run] = piece[:, fn + g * run : fn + (g + 1) * run]
    scatter.finish()
    out_ref[...] = acc[...].astype(bf16)


def down_forward(hid, da, db, after, mlp_rows, gains, near, back, x, ag, down, run):
    length, width = after.shape
    size = 2 * TP
    rows, cols = mlp_rows.shape[0] // size, mlp_rows.shape[1]
    ff = size * cols // 2
    anywhere = pl.BlockSpec(memory_space=pl.ANY)
    vmem = pl.BlockSpec(memory_space=pltpu.VMEM)
    sem = pltpu.SemaphoreType.DMA
    return pl.pallas_call(
        functools.partial(down_kernel, run),
        in_specs=[anywhere] * 9 + [vmem, anywhere],
        out_specs=[vmem] * 6,
        out_shape=[
            struct((length, width), bf16),
            struct((rows, ff), f32),
            struct((rows, ff), f32),
            struct((gains.shape[1], 1, gains.shape[2]), f32),
            struct((length, width), bf16),
            struct(down.shape, f32),
        ],
        scratch_shapes=[
            pltpu.VMEM(hid.shape, bf16),
            pltpu.VMEM(da.shape, bf16),
            pltpu.VMEM(db.shape, bf16),
            pltpu.VMEM(after.shape, f32),
            pltpu.VMEM(after.shape, f32),
            pltpu.VMEM((size, rows, cols), bf16),
            pltpu.VMEM(gains.shape, f32),
            pltpu.VMEM(after.shape, f32),
            pltpu.VMEM(after.shape, f32),
            pltpu.VMEM(x.shape, bf16),
            pltpu.VMEM(down.shape, bf16),
            sem((10,)), sem((size - 1,)), sem((size - 1,)), sem((size - 1,)), sem((size - 1,)),
        ]
        + scatter_scratch(length, width),
        compiler_params=pltpu.CompilerParams(
            vmem_limit_bytes=56 << 20, collective_id=7, has_side_effects=True
        ),
        cost_estimate=pl.CostEstimate(
            flops=2 * length * width * cols, bytes_accessed=30 << 20, transcendentals=0
        ),
        name="down_forward",
    )(hid, da, db, after, mlp_rows, gains, near, back, x, ag, down)


def return_kernel(
    rows_ref, gains_ref, q_ref, k_ref, v_ref, o_ref, total_ref, pieces, gains, send, recv, local, g_send, g_recv,
):
    size, rows, _ = pieces.shape
    me = lax.axis_index("dp")
    others = everyone(me)

    def block(device):
        return rows_ref.at[pl.ds(pl.multiple_of((device % size) * rows, rows), rows)]

    planes = gains.shape[0]
    plane = me // size
    column = [(plane + i) % planes for i in range(1, planes)]
    own = [
        pltpu.make_async_copy(block(me), pieces.at[me % size], local.at[0]),
        pltpu.make_async_copy(gains_ref.at[plane], gains.at[plane], local.at[1]),
    ]
    copies = [
        remote(block(device), pieces.at[me % size], send.at[i], recv.at[i], device)
        for i, device in enumerate(others)
    ]
    copies += [
        remote(gains_ref.at[to], gains.at[plane], g_send.at[i], g_recv.at[i], to * size + me % size)
        for i, to in enumerate(column)
    ]
    for copy in own:
        copy.start()
    greet(others + [to * size + me % size for to in column])
    for copy in copies:
        copy.start()
    for copy in own + copies:
        copy.wait()
    total_ref[...] = jnp.sum(gains[...], axis=0)
    for source in range(size):
        at = 0
        for ref in (q_ref, k_ref, v_ref, o_ref):
            width = ref.shape[1] // size
            ref[:, source * width : (source + 1) * width] = pieces[source, :, at : at + width].astype(f32)
            at += width


def return_attention(attn_rows, gains, widths):
    size = 2 * TP
    rows, cols = attn_rows.shape[0] // size, attn_rows.shape[1]
    sem = pltpu.SemaphoreType.DMA
    return pl.pallas_call(
        return_kernel,
        in_specs=[pl.BlockSpec(memory_space=pl.ANY)] * 2,
        out_specs=[pl.BlockSpec(memory_space=pltpu.VMEM)] * 5,
        out_shape=[struct((rows, w), f32) for w in widths] + [struct(gains.shape[1:], f32)],
        scratch_shapes=[
            pltpu.VMEM((size, rows, cols), bf16),
            pltpu.VMEM(gains.shape, f32),
            sem((size - 1,)), sem((size - 1,)), sem((2,)),
            sem((gains.shape[0] - 1,)), sem((gains.shape[0] - 1,)),
        ],
        compiler_params=pltpu.CompilerParams(collective_id=8, has_side_effects=True),
        name="return_attention",
    )(attn_rows, gains)


def make_body(n):
    m = n // (2 * TP)
    z_groups = [[g * 2 * TP + k for g in range(m)] for k in range(2 * TP)]

    def swap(v, bits):
        return lax.ppermute(v, "dp", [(a, a ^ bits) for a in range(n)])

    def gather_xy(v):
        h = v.shape[0] // 2
        x = swap(v, 2)
        y = swap(v, 4)
        d_low = swap(y[:h], 2)
        d_high = swap(x[h:], 4)
        return [v, x, y, jnp.concatenate([d_low, d_high])]

    def scatter_xy(p0, p1, p2, p3):
        h = p3.shape[0] // 2
        d_low = swap(p3[:h], 4)
        d_high = swap(p3[h:], 2)
        sx = jnp.concatenate([(p1[:h].astype(f32) + d_low.astype(f32)).astype(bf16), p1[h:]])
        sy = jnp.concatenate([p2[:h], (p2[h:].astype(f32) + d_high.astype(f32)).astype(bf16)])
        return p0 + swap(sx, 2).astype(f32) + swap(sy, 4).astype(f32)

    def gather_z(v):
        return lax.all_gather(v, "dp", axis=0, tiled=True, axis_index_groups=z_groups)

    def scatter_z(v):
        return lax.psum_scatter(
            v, "dp", scatter_dimension=0, tiled=True, axis_index_groups=z_groups
        )

    def body(
        tokens,
        segments,
        w_query,
        w_key,
        w_value,
        w_out,
        w_gate,
        w_up,
        w_down,
        attn_gain,
        mlp_gain,
        query_gain,
        key_gain,
        cotangent,
    ):
        me = lax.axis_index("dp")
        core = me % 2
        place = (me // 2) % TP
        length, width = tokens.shape
        rows = w_query.shape[0]
        ffr = w_down.shape[0]

        qn = w_query.shape[1] // (2 * TP)
        kn = w_key.shape[1] // (2 * TP)
        pn = qn + 2 * kn
        hr = query_gain.shape[0]
        gains = jnp.concatenate([attn_gain, mlp_gain, query_gain, key_gain]).astype(f32)
        count = gains.shape[0]
        padded = -(-count // 256) * 256
        attn_in, gains, seg_all = spread_attention(
            w_query, w_key, w_value, w_out, jnp.pad(gains, (0, padded - count))[None], segments
        )

        depth, wide = attn_in.shape
        gain_rows = gains.astype(bf16).reshape(-1, padded)
        below = jnp.pad(gain_rows, ((0, -gain_rows.shape[0] % 16), (0, wide - padded)))
        attn_all = gather_z(jnp.concatenate([attn_in, below])).reshape(m, -1, wide)
        tokens_in, _ = lax.optimization_barrier((tokens, attn_in))

        rate = THETA ** (-(jnp.arange(HD // 2, dtype=f32) * 2.0 / HD))
        sign = jnp.where(jnp.arange(HD) < HD // 2, -1.0, 1.0).astype(f32)
        rates = jnp.stack([jnp.concatenate([rate, rate]), sign])
        cosine, sine, starts, tokens_all, mlp_in = gather_group(
            seg_all, rates, tokens_in, w_gate, w_up, ffr
        )
        mlp_a = gather_z(mlp_in)
        tokens_all, attn_all = lax.optimization_barrier((tokens_all, attn_all))
        gains = attn_all[:, depth : depth + gain_rows.shape[0], :padded].reshape(n, padded)
        attn_scale = gains[:, :rows].reshape(-1).astype(f32)
        mlp_scale = gains[:, rows : 2 * rows].reshape(-1).astype(f32)
        query_scale = gains[:, 2 * rows : 2 * rows + hr].reshape(-1).astype(f32)
        key_scale = gains[:, 2 * rows + hr : count].reshape(-1).astype(f32)

        (
            raw, normed_one, mixed_own, after_attn, inv_two, proj_a, proj_b, out_full, normed_two_all
        ) = attend_forward(
            tokens_all, cosine, sine, starts, attn_scale[None], mlp_scale[None],
            query_scale[None], key_scale[None], attn_all, depth, pn, length,
        )

        inputs = tokens.astype(f32)
        mlp_a, normed_two_all, down_local = lax.optimization_barrier((mlp_a, normed_two_all, w_down))
        down_a = gather_z(down_local)
        fn = down_a.shape[0]

        gate_value, up_value, hidden, mlp_b, grad_all, down_sum = feed_forward(
            normed_two_all, mlp_a, cotangent
        )
        down_rows = scatter_z(down_sum)
        grad_normed_two, mlp_sum, down_b = feed_backward(
            gate_value, up_value, grad_all, down_a, mlp_a, mlp_b, normed_two_all, length
        )
        mlp_rows = scatter_z(mlp_sum)
        grad_normed_two, down_rows = lax.optimization_barrier((grad_normed_two, down_rows))

        grad_after, grad_after_low, mlp_gain_grad, grad_heads, out_other = between(
            grad_normed_two, after_attn, inv_two, mlp_scale[None], cotangent, mixed_own, out_full
        )

        grad_normed_one, attn_sum, query_gain_grad, key_gain_grad = attend_backward(
            grad_heads, raw, normed_one, proj_a, proj_b, cosine, sine, starts,
            query_scale[None], key_scale[None], mixed_own, grad_after_low, out_other, length,
        )
        attn_rows = scatter_z(attn_sum)
        attn_gain_grad = jnp.sum(grad_normed_one * inputs * inverse_rms(inputs), axis=0)

        gain_grads = jnp.concatenate(
            [
                attn_gain_grad.reshape(m, 2 * TP, -1),
                mlp_gain_grad.reshape(m, 2 * TP, -1),
                query_gain_grad.reshape(m, 2 * TP, -1),
                key_gain_grad.reshape(m, 2 * TP, -1),
                jnp.zeros((m, 2 * TP, padded - count), f32),
            ],
            axis=2,
        ).transpose(1, 0, 2)
        output, gate_shard, up_shard, gain_sums, tokens_grad, down_shard = down_forward(
            hidden, down_a, down_b, after_attn, mlp_rows, gain_grads, grad_after, grad_normed_one,
            tokens, attn_scale[None], down_rows, ffr,
        )
        attn_rows, output = lax.optimization_barrier((attn_rows, output))
        query_shard, key_shard, value_shard, out_shard, gain_grads = return_attention(
            attn_rows, gain_sums, [w.shape[1] for w in (w_query, w_key, w_value, w_out)]
        )

        gain_grads = gain_grads[0]

        return (
            output,
            tokens_grad,
            query_shard,
            key_shard,
            value_shard,
            out_shard,
            gate_shard,
            up_shard,
            down_shard,
            gain_grads[:rows],
            gain_grads[rows : 2 * rows],
            gain_grads[2 * rows : 2 * rows + hr],
            gain_grads[2 * rows + hr : count],
        )

    return body


def solution(mesh):
    row = P("dp", None)
    flat = P("dp")
    return jax.shard_map(
        make_body(mesh.shape["dp"]),
        mesh=mesh,
        in_specs=(row,) * 9 + (flat,) * 4 + (row,),
        out_specs=(row,) * 9 + (flat,) * 4,
        check_vma=False,
    )
```
